32 devices in a mesh: wide: 8 (over z, y), narrow: 4 (over x, core).
Axes of the slice: x: 2, y: 2, z: 4, core: 2. Of those that a mesh axis runs over, the one named last changes fastest.
Arguments:
- hidden: bfloat16 [4, 2048, 768], P('narrow', 'wide'), may hold values from -6 to 6
- doc_start: int32 [4, 2048], P('narrow', 'wide'), may hold values from 0 to 1, as said below
- expert_choice: int32 [2, 4, 2048], P(None, 'narrow', 'wide'), may hold values from 0 to 15, as said below
- slot_index: int32 [2, 4, 2048], P(None, 'narrow', 'wide'), may hold values from -1 to 19, as said below
- norm_mix: float32 [2, 768], replicated, may hold values from 0.1 to 1.9
- in_weight: bfloat16 [2, 768, 3072], replicated, may hold values from -0.21875 to 0.21875
- conv_weight: float32 [2, 4, 1536], replicated, may hold values from -3 to 3
- conv_bias: float32 [2, 1536], replicated, may hold values from -3 to 3
- state_weight: bfloat16 [2, 1536, 80], replicated, may hold values from -0.15625 to 0.15625
- step_weight: bfloat16 [2, 48, 1536], replicated, may hold values from -0.875 to 0.875
- step_bias: float32 [2, 1536], replicated, may hold values from -4 to -2
- decay_log: float32 [2, 16, 1536], replicated, may hold values from -11.6 to 0.5
- skip_weight: float32 [2, 1536], replicated, may hold values from 0.5 to 1.5
- out_weight: bfloat16 [2, 1536, 768], replicated, may hold values from -0.15625 to 0.15625
- norm_expert: float32 [2, 768], replicated, may hold values from 0.1 to 1.9
- router: bfloat16 [2, 768, 16], replicated, may hold values from -0.15625 to 0.15625
- expert_up: bfloat16 [2, 16, 768, 3072], P(None, 'narrow', None, 'wide'), may hold values from -0.21875 to 0.21875
- expert_down: bfloat16 [2, 16, 3072, 768], P(None, 'narrow', 'wide'), may hold values from -4 to 4
- cotangent: bfloat16 [4, 2048, 768], P('narrow', 'wide'), may hold values from -6 to 6
Outputs:
- output: bfloat16 [4, 2048, 768], P('narrow', 'wide')
- hidden_input_gradient: float32 [4, 2048, 768], P('narrow', 'wide')
- grad_norm_mix: float32 [2, 768], P(None, ('wide', 'narrow'))
- grad_in_weight: float32 [2, 768, 3072], P(None, None, ('wide', 'narrow'))
- grad_conv_weight: float32 [2, 4, 1536], P(None, None, ('wide', 'narrow'))
- grad_conv_bias: float32 [2, 1536], P(None, ('wide', 'narrow'))
- grad_state_weight: float32 [2, 1536, 80], P(None, ('wide', 'narrow'))
- grad_step_weight: float32 [2, 48, 1536], P(None, None, ('wide', 'narrow'))
- grad_step_bias: float32 [2, 1536], P(None, ('wide', 'narrow'))
- grad_decay_log: float32 [2, 16, 1536], P(None, None, ('wide', 'narrow'))
- grad_skip_weight: float32 [2, 1536], P(None, ('wide', 'narrow'))
- grad_out_weight: float32 [2, 1536, 768], P(None, ('wide', 'narrow'))
- grad_norm_expert: float32 [2, 768], P(None, ('wide', 'narrow'))
- grad_router: float32 [2, 768, 16], P(None, ('wide', 'narrow'))
- grad_expert_up: float32 [2, 16, 768, 3072], P(None, 'narrow', None, 'wide')
- grad_expert_down: float32 [2, 16, 3072, 768], P(None, 'narrow', 'wide')
The draws below stay inside these ranges and needn't reach their ends.
Inputs may be any that keep to these rules, and one draw needn't show every extreme that they name: `doc_start`: position 0 of every sequence starts a document; in one sequence, drawn from the seed, no other position does. `expert_choice`: in every layer and every aligned block of 256 tokens of a sequence, some expert is named by more than 20 tokens. `slot_index`: A token's slot is the number of earlier tokens of its aligned block of 256 with the same expert in the same layer, or -1 where that number is 20 or more.
All inputs are finite; a program needn't handle non-finite values.
Results may differ from the reference program's by a relative error of at most 0.02.
The reference program's roundings to bfloat16 on the way count: a program that leaves them out, or rounds other values in their place, can miss the bound.
Values may be sent and summed in bfloat16 or wider, within the bound.
A program may use at most 256 MiB of HBM per device.

```python
import jax
import jax.numpy as jnp
from jax import lax

D = 768
DI = 1536
NS = 16
KC = 4
RK = 48
FF = 3072
LAYERS = 2
TOK_DEV = 256
BLOCK = 16
EXPERTS = 16
CAP = 20
SEQ = 2048
SEQS = 4
RB = 80
N_WIDE = 8
DEVICES = 32


def route_draw(key):
    key = jax.random.fold_in(key, 71)
    first, second, third, fourth = jax.random.split(key, 4)
    shape = (LAYERS, SEQS, SEQ // TOK_DEV, TOK_DEV)
    scores = jax.random.randint(first, (LAYERS, EXPERTS), 0, 1 << 20) * EXPERTS + jnp.arange(EXPERTS, dtype=jnp.int32)
    order = jnp.argsort(scores, axis=1).astype(jnp.int32)
    raw = jnp.minimum(jax.random.randint(second, shape, 0, EXPERTS), jax.random.randint(third, shape, 0, EXPERTS))
    chosen = jnp.take_along_axis(order, raw.reshape(LAYERS, -1), axis=1).reshape(shape)
    ranking = jax.random.randint(fourth, shape, 0, 1 << 16) * TOK_DEV + jnp.arange(TOK_DEV, dtype=jnp.int32)
    ranks = jnp.argsort(jnp.argsort(ranking, axis=3), axis=3)
    chosen = jnp.where(ranks <= CAP, order[:, 0][:, None, None, None], chosen).astype(jnp.int32)
    onehot = (chosen[..., None] == jnp.arange(EXPERTS, dtype=jnp.int32)).astype(jnp.int32)
    earlier = jnp.cumsum(onehot, axis=3) - onehot
    slot = jnp.sum(earlier * onehot, axis=4)
    slot = jnp.where(slot < CAP, slot, -1).astype(jnp.int32)
    return (chosen.reshape(LAYERS, SEQS, SEQ), slot.reshape(LAYERS, SEQS, SEQ))


def draw_expert_choice(key, part):
    routes = route_draw(key)
    return routes[0]


def draw_slot_index(key, part):
    routes = route_draw(key)
    return routes[1]


def draw_doc_start(key, part):
    key = jax.random.fold_in(key, 5)
    first, second = jax.random.split(key)
    marks = (jax.random.randint(first, (SEQS, SEQ), 0, 2 * TOK_DEV) == 0).astype(jnp.int32)
    whole = jax.random.randint(second, (), 0, SEQS)
    marks = jnp.where(jnp.arange(SEQS, dtype=jnp.int32)[:, None] == whole, 0, marks)
    return marks.at[:, 0].set(1).astype(jnp.int32)


def draw_decay_log(key, part):
    key = jax.random.fold_in(key, 9)
    first, second = jax.random.split(key)
    share = 0.5
    pick = jax.random.uniform(first, (LAYERS, 1, DI), jnp.float32)
    level = jax.random.uniform(second, (LAYERS, NS, DI), jnp.float32)
    slow = jnp.log(1e-05) + level * (jnp.log(0.0001) - jnp.log(1e-05))
    fast = jnp.log(0.3) + level * (jnp.log(1.5) - jnp.log(0.3))
    return jnp.where(pick < share, slow, fast).astype(jnp.float32)


def level_of(own_key, extent, cuts, low, high):
    factor_of, own = 1.0, jax.random.fold_in(own_key, 6)
    for dim, parts in cuts:
        steps = jnp.exp(jax.random.uniform(jax.random.fold_in(own, dim), (parts,), jnp.float32, low / len(cuts), high / len(cuts)))
        factor_of = factor_of * jnp.repeat(steps, extent[dim] // parts).reshape([-1 if axis == dim else 1 for axis in range(len(extent))])
    return factor_of


def scatter_about(rng, extent, scale, most, cuts=(), kind=jnp.bfloat16):
    entries = scale * jax.random.normal(rng, extent, jnp.float32)
    if cuts:
        entries = entries * level_of(rng, extent, cuts, -0.22, 0.18)
    return jnp.clip(entries, -most, most).astype(kind)


def setup_inputs(seed: int = 0) -> dict:
    keys = jax.random.split(jax.random.key(seed), 20)
    return {
        "hidden": scatter_about(keys[0], (SEQS, SEQ, D), 1.0, 6.0, ((0, 4), (1, 8))),
        "doc_start": draw_doc_start(jax.random.fold_in(keys[19], 71), 0),
        "expert_choice": draw_expert_choice(jax.random.fold_in(keys[19], 71), 0),
        "slot_index": draw_slot_index(jax.random.fold_in(keys[19], 71), 0),
        "norm_mix": jnp.clip(1.0 + 0.18 * jax.random.normal(keys[4], (LAYERS, D), jnp.float32), 0.1, 1.9),
        "in_weight": scatter_about(keys[5], (LAYERS, D, 2 * DI), D ** -0.5, 0.21875),
        "conv_weight": scatter_about(keys[6], (LAYERS, KC, DI), 0.5, 3.0, (), jnp.float32),
        "conv_bias": scatter_about(keys[7], (LAYERS, DI), 0.3, 3.0, (), jnp.float32),
        "state_weight": scatter_about(keys[8], (LAYERS, DI, RB), DI ** -0.5, 0.15625),
        "step_weight": scatter_about(keys[9], (LAYERS, RK, DI), RK ** -0.5, 0.875),
        "step_bias": jnp.clip(jax.random.uniform(keys[10], (LAYERS, DI), jnp.float32, -4.0, -2.0), -4.0, -2.0),
        "decay_log": draw_decay_log(jax.random.fold_in(keys[19], 71), 0),
        "skip_weight": jnp.clip(jax.random.uniform(keys[12], (LAYERS, DI), jnp.float32, 0.5, 1.5), 0.5, 1.5),
        "out_weight": scatter_about(keys[13], (LAYERS, DI, D), DI ** -0.5, 0.15625),
        "norm_expert": jnp.clip(1.0 + 0.18 * jax.random.normal(keys[14], (LAYERS, D), jnp.float32), 0.1, 1.9),
        "router": scatter_about(keys[15], (LAYERS, D, EXPERTS), (2 * D) ** -0.5, 0.15625),
        "expert_up": scatter_about(keys[16], (LAYERS, EXPERTS, D, FF), D ** -0.5, 0.21875, ((1, 4), (3, 8))),
        "expert_down": scatter_about(keys[17], (LAYERS, EXPERTS, FF, D), 2 ** -0.5, 4.0, ((1, 4), (2, 8))),
        "cotangent": scatter_about(keys[18], (SEQS, SEQ, D), 1.0, 6.0, ((0, 4), (1, 8))),
    }


@jax.custom_vjp
def low(v):
    return lax.optimization_barrier(v.astype(jnp.bfloat16)).astype(jnp.float32)

@jax.custom_vjp
def low_back(v):
    return v

def low_keep(v):
    return (low(v), None)

def low_pass(kept, grad):
    return (grad,)

def back_keep(v):
    return (v, None)

def back_low(kept, grad):
    return (low(grad),)
low.defvjp(low_keep, low_pass)
low_back.defvjp(back_keep, back_low)
EPS = 1e-05
TOP_PRECISION = lax.Precision.HIGHEST

def rms_scale(values, gain):
    return values * lax.rsqrt(lax.optimization_barrier(jnp.mean(values * values, axis=-1, keepdims=True)) + EPS) * gain

def project(left_operand, right_operand):
    return jnp.einsum('axz,zf->axf', left_operand, right_operand, precision=TOP_PRECISION)

def conv_mix(inner_value, starts, kernel, shift_bias):
    width = kernel.shape[0]
    length = inner_value.shape[1]
    padded_value = jnp.pad(inner_value, ((0, 0), (width - 1, 0), (0, 0)))
    padded_start = jnp.pad(starts, ((0, 0), (width - 1, 0)))
    total = shift_bias + kernel[0] * inner_value
    alive = jnp.ones_like(starts)
    for offset in range(1, width):
        alive = alive * (1.0 - padded_start[:, width - offset:width - offset + length])
        total = total + kernel[offset] * padded_value[:, width - 1 - offset:width - 1 - offset + length] * alive[:, :, None]
    return total

def selective_scan(step_size, input_map, output_map, activated, starts, decay_rate):

    def block_combiner(state, pieces):

        def token_fn(carry, item):
            size_now, input_now, output_now, value_now, start_now = item
            decay = jnp.exp(size_now[:, None, :] * decay_rate) * (1.0 - start_now)[:, None, None]
            carry = decay * carry + (size_now * value_now)[:, None, :] * input_now[:, :, None]
            return (carry, lax.optimization_barrier(jnp.sum(output_now[:, :, None] * carry, axis=1)))
        return lax.scan(token_fn, state, pieces)

    def to_blocks(values):
        moved = jnp.moveaxis(values, 1, 0)
        return moved.reshape((SEQ // BLOCK, BLOCK) + moved.shape[1:])
    pieces = tuple((to_blocks(values) for values in (step_size, input_map, output_map, activated, starts)))
    initial = jnp.zeros((step_size.shape[0],) + decay_rate.shape, jnp.float32)
    final_state, outputs = lax.scan(jax.checkpoint(block_combiner), initial, pieces)
    outputs = outputs.reshape((SEQ,) + outputs.shape[2:])
    return jnp.moveaxis(outputs, 0, 1)

def mamba_layer(current, starts, weights):
    norm_mix, in_weight, conv_weight, conv_bias, state_weight, step_weight, step_bias, decay_log, skip_weight, out_weight = weights
    normed = low(rms_scale(current, norm_mix))
    projected = low_back(project(normed, in_weight))
    inner_value = projected[..., :DI]
    inner_gate = projected[..., DI:]
    activated = low(jax.nn.silu(conv_mix(inner_value, starts, conv_weight, conv_bias)))
    selection = low_back(project(activated, state_weight))
    step_linear = low_back(project(low(selection[..., :RK]), step_weight))
    step_size = jax.nn.softplus(step_linear + step_bias)
    input_map = selection[..., RK:RK + NS]
    output_map = selection[..., RK + NS:]
    decay_rate = -jnp.exp(decay_log)
    mixer_out = selective_scan(step_size, input_map, output_map, activated, starts, decay_rate) + skip_weight * activated
    gated = low(mixer_out * jax.nn.silu(inner_gate))
    return current + low_back(project(gated, out_weight))

def expert_block(pieces):
    rows, up_matrix, down_matrix = pieces
    pre_act = low_back(jnp.dot(rows, up_matrix, precision=TOP_PRECISION))
    hidden_rows = low(jax.nn.gelu(pre_act, approximate=False))
    return low_back(low(jnp.dot(hidden_rows, down_matrix, precision=TOP_PRECISION)))

def expert_layer(current, chosen_row, slot_row, norm_expert, router, expert_up, expert_down):
    routed = low(rms_scale(current, norm_expert))
    logits = low_back(project(routed, router))
    shares = jax.nn.softmax(logits, axis=-1)
    gate = jnp.take_along_axis(shares, chosen_row[..., None], axis=-1)[..., 0]
    keep = (slot_row >= 0).astype(jnp.float32)
    per_expert = DEVICES * CAP
    source = jnp.arange(SEQS, dtype=jnp.int32)[:, None] * N_WIDE + jnp.arange(SEQ, dtype=jnp.int32)[None, :] // TOK_DEV
    place = jnp.where(slot_row >= 0, chosen_row * per_expert + source * CAP + slot_row, EXPERTS * per_expert)
    place = place.astype(jnp.int32).reshape(-1)
    sent = low_back(routed).reshape(-1, D)
    buffer = jnp.zeros((EXPERTS * per_expert + 1, D), jnp.float32).at[place].set(sent)[:-1]
    outputs = lax.map(jax.checkpoint(expert_block), (buffer.reshape(EXPERTS, per_expert, D), expert_up, expert_down))
    table = jnp.concatenate([outputs.reshape(-1, D), jnp.zeros((1, D), jnp.float32)], axis=0)
    returned = table[place].reshape(current.shape)
    return current + (keep * gate)[..., None] * returned

def forward(hidden, mamba_weights, expert_weights, starts, expert_choice, slot_index):
    current = hidden
    for layer in range(LAYERS):
        current = mamba_layer(current, starts, [weight[layer] for weight in mamba_weights])
        norm_expert, router, expert_up, expert_down = [weight[layer] for weight in expert_weights]
        current = expert_layer(current, expert_choice[layer], slot_index[layer], norm_expert, router, expert_up, expert_down)
    return current

def reference(hidden, doc_start, expert_choice, slot_index, norm_mix, in_weight, conv_weight, conv_bias, state_weight, step_weight, step_bias, decay_log, skip_weight, out_weight, norm_expert, router, expert_up, expert_down, cotangent):
    starts = doc_start.astype(jnp.float32)
    mamba_weights = tuple((weight.astype(jnp.float32) for weight in (norm_mix, in_weight, conv_weight, conv_bias, state_weight, step_weight, step_bias, decay_log, skip_weight, out_weight)))
    expert_weights = tuple((weight.astype(jnp.float32) for weight in (norm_expert, router, expert_up, expert_down)))

    def run(inputs, mamba_set, expert_set):
        return forward(inputs, mamba_set, expert_set, starts, expert_choice, slot_index)
    final, pullback = jax.vjp(run, hidden.astype(jnp.float32), mamba_weights, expert_weights)
    hidden_input_gradient, mamba_grads, expert_grads = pullback(cotangent.astype(jnp.float32))
    return (final.astype(jnp.bfloat16), hidden_input_gradient, mamba_grads[0], mamba_grads[1], mamba_grads[2], mamba_grads[3], mamba_grads[4], mamba_grads[5], mamba_grads[6], mamba_grads[7], mamba_grads[8], mamba_grads[9], expert_grads[0], expert_grads[1], expert_grads[2], expert_grads[3])
```

```python
import functools

import jax
import jax.numpy as jnp
from jax import lax
from jax.experimental import pallas as pl
from jax.experimental.pallas import tpu as pltpu
from jax.sharding import PartitionSpec as P

EPS = 1e-05
CHUNKS = 8
LANES = 128
LOG2E = 1.4426950408889634
RESET = 1e9
MIB = 1024 * 1024
MESH = pl.DeviceIdType.MESH
VMEM = pltpu.VMEM


def to_steps(values):
    steps = values.shape[0] // CHUNKS
    return jnp.swapaxes(values.reshape((CHUNKS, steps) + values.shape[1:]), 0, 1)


def to_tokens(values):
    moved = jnp.swapaxes(values, 0, 1)
    return moved.reshape((-1,) + values.shape[2:])


def rms_scale(values, gain):
    return values * lax.rsqrt(jnp.mean(values * values, axis=-1, keepdims=True) + EPS) * gain


def rms_back(values, gain, grad):
    scale = lax.rsqrt(jnp.mean(values * values, axis=-1, keepdims=True) + EPS)
    weighted = grad * gain
    inner = jnp.mean(weighted * values, axis=-1, keepdims=True)
    return (
        scale * weighted - values * (scale * scale * scale) * inner,
        jnp.sum(grad * values * scale, axis=0),
    )


def dot_nn(left, right):
    return lax.dot_general(left, right, (((1,), (0,)), ((), ())), preferred_element_type=jnp.float32)


def dot_nt(left, right):
    return lax.dot_general(left, right, (((1,), (1,)), ((), ())), preferred_element_type=jnp.float32)


def dot_tn(left, right):
    return lax.dot_general(left, right, (((0,), (0,)), ((), ())), preferred_element_type=jnp.float32)


def passed_along(x, by):
    size = lax.axis_size("wide")
    return lax.ppermute(x, "wide", [(i, i + by) for i in range(size) if 0 <= i + by < size])


def with_rim(values, rim):
    count = rim.shape[0]
    tail = values[values.shape[0] - count :, : CHUNKS - 1]
    return jnp.concatenate([jnp.concatenate([rim[:, None], tail], axis=1), values], axis=0)


def keep_masks(starts, taps):
    extended = with_rim(starts[..., None], jnp.zeros((taps - 1, 1), jnp.float32))
    steps = starts.shape[0]
    alive = jnp.ones(starts.shape + (1,), jnp.float32)
    masks = []
    for offset in range(1, taps):
        back = taps - offset
        alive = alive * (1.0 - extended[back : back + steps])
        masks.append(alive)
    return jnp.broadcast_to(jnp.stack(masks), (taps - 1,) + starts.shape + (LANES,))


def rim_keep(starts, count):
    tail = 1.0 - starts[starts.shape[0] - count :, CHUNKS - 1]
    later = jnp.cumprod(tail[::-1])[::-1]
    return jnp.concatenate([later[1:], jnp.ones((1,), jnp.float32)])


def microseconds(count):
    return pl.CostEstimate(flops=int(count * 1.0e9), transcendentals=0, bytes_accessed=1000000)


def plain_call(kernel, grid, in_specs, out_specs, out_shapes, scratch, args, cost):
    return pl.pallas_call(
        kernel,
        grid=grid,
        in_specs=in_specs,
        out_specs=out_specs,
        out_shape=out_shapes,
        scratch_shapes=scratch,
        compiler_params=pltpu.CompilerParams(
            dimension_semantics=("arbitrary",), vmem_limit_bytes=48 * MIB
        ),
        cost_estimate=microseconds(cost),
    )(*args)


def shaped(shape, kind=jnp.float32):
    return jax.ShapeDtypeStruct(shape, kind)


def slab(steps, first=0):
    return pl.BlockSpec((steps, CHUNKS, LANES), lambda c: (0, 0, first + c))


def rows_of(count):
    return pl.BlockSpec((count, LANES), lambda c: (0, c))


def layer_rows(layer, count):
    return pl.BlockSpec((None, count, LANES), lambda c: (layer, 0, c))


def layer_columns(layer, count):
    return pl.BlockSpec((None, LANES, count), lambda c: (layer, c, 0))


def layer_whole(layer, shape):
    return pl.BlockSpec((None,) + shape, lambda c: (layer,) + (0,) * len(shape))


def whole(shape):
    return pl.BlockSpec(shape, lambda c: (0,) * len(shape))


ANYWHERE = pl.BlockSpec(memory_space=pl.ANY)


def spread_columns(selection_ref, first, states, out_ref):
    def one(step, carry):
        tile = selection_ref[step]
        for n in range(states):
            out_ref[step, n] = jnp.broadcast_to(tile[:, first + n : first + n + 1], (CHUNKS, LANES))
        return carry

    lax.fori_loop(0, selection_ref.shape[0], one, 0)


def rate_rows(rate):
    return [jnp.broadcast_to(rate[n : n + 1, :], (CHUNKS, LANES)) for n in range(rate.shape[0])]


def rates_of(decay_log):
    return -jnp.exp(decay_log) * LOG2E


def two_steps(ref, pair, lanes=slice(None)):
    both = ref[pl.ds(pl.multiple_of(pair * 2 * CHUNKS, 2 * CHUNKS), 2 * CHUNKS), lanes]
    both = both.astype(jnp.float32)
    return both[:CHUNKS], both[CHUNKS:]


def chunk_links(found, sizes, rates, reverse):
    place = lax.broadcasted_iota(jnp.int32, (CHUNKS, LANES), 0)
    if reverse:
        place = CHUNKS - 1 - place
    last = 0 if reverse else CHUNKS - 1

    def shifted(values, by):
        turned = pltpu.roll(values, CHUNKS - by if reverse else by, axis=0)
        return jnp.where(place >= by, turned, 0.0)

    lengths = [sizes]
    for by in (1, 2, 4):
        lengths.append(lengths[-1] + shifted(lengths[-1], by))
    links, totals = [], []
    for n, rate in enumerate(rates):
        level = found[n]
        for index, by in enumerate((1, 2, 4)):
            level = level + jnp.exp2(lengths[index] * rate) * shifted(level, by)
        links.append(shifted(level, 1))
        totals.append(level[last : last + 1])
    return links, totals, shifted(lengths[-1], 1), lengths[-1][last : last + 1]


def conv_slab(extended, step, mask_ref, kernel_ref, bias, taps):
    total = bias + kernel_ref[0:1, :] * extended[step + taps - 1]
    tiles = total.shape[1] // LANES
    for offset in range(1, taps):
        mask = mask_ref[offset - 1, step]
        mask = jnp.concatenate([mask] * tiles, axis=1) if tiles > 1 else mask
        total = total + kernel_ref[offset : offset + 1, :] * (
            extended[step + taps - 1 - offset] * mask
        )
    return total


def extend(value_ref, rim_ref, extended, taps):
    steps = value_ref.shape[0]
    place = lax.broadcasted_iota(jnp.int32, value_ref.shape[1:], 0)
    for j in range(taps - 1):
        turned = pltpu.roll(value_ref[steps - taps + 1 + j], 1, axis=0)
        extended[j] = jnp.where(place == 0, rim_ref[j : j + 1, :], turned)
    extended[taps - 1 :] = value_ref[...]


def front_kernel(dims, value_ref, rim_ref, mask_ref, reset_ref, conv_ref, conv_bias_ref, state_ref,
                 step_ref, step_bias_ref, decay_ref,
                 act_ref, selection_ref, size_ref, link_ref, link_size_ref, total_ref, total_size_ref,
                 extended, maps):
    taps, rank, states, steps, channels = dims
    extend(value_ref, rim_ref, extended, taps)
    bias = conv_bias_ref[...]

    def conv_pair(pair, carry):
        both = []
        for step in (2 * pair, 2 * pair + 1):
            both.append(jax.nn.silu(conv_slab(extended, step, mask_ref, conv_ref, bias, taps)))
        at = pl.ds(pl.multiple_of(pair * 2 * CHUNKS, 2 * CHUNKS), 2 * CHUNKS)
        act_ref[at, :] = jnp.concatenate(both, axis=0).astype(jnp.bfloat16)
        return carry

    lax.fori_loop(0, steps // 2, conv_pair, 0)
    selection = dot_nn(act_ref[...], state_ref[...])
    selection_ref[...] = selection.reshape(steps, CHUNKS, selection.shape[1])
    rank_low = selection[:, :rank].astype(jnp.bfloat16)

    def size_tile(c, carry):
        lanes = pl.ds(pl.multiple_of(c * 256, 256), 256)
        linear = dot_nn(rank_low, step_ref[:, lanes]) + step_bias_ref[:, lanes]
        size_ref[:, :, lanes] = jax.nn.softplus(linear).reshape(steps, CHUNKS, 256)
        return carry

    lax.fori_loop(0, channels // 256, size_tile, 0)
    spread_columns(selection_ref, rank, states, maps)

    def end_tile(c, carry):
        lanes = pl.ds(pl.multiple_of(c * LANES, LANES), LANES)
        rates = rate_rows(rates_of(decay_ref[:, lanes]))

        def one(pair, carry):
            levels, length = list(carry[:states]), carry[states]
            acts = two_steps(act_ref, pair, lanes)
            for half in (0, 1):
                step = 2 * pair + half
                size = size_ref[step, :, lanes]
                value = size * acts[half]
                size = size + reset_ref[step]
                for n in range(states):
                    levels[n] = jnp.exp2(size * rates[n]) * levels[n] + value * maps[step, n]
                length = length + size
            return tuple(levels) + (length,)

        zero = jnp.zeros((CHUNKS, LANES), jnp.float32)
        found = lax.fori_loop(0, steps // 2, one, (zero,) * (states + 1))
        links, totals, link_size, total_size = chunk_links(found, found[states], rates, False)
        link_size_ref[:, lanes] = link_size
        total_size_ref[:, lanes] = total_size
        for n in range(states):
            link_ref[n, :, lanes] = links[n]
            total_ref[n : n + 1, lanes] = totals[n]
        return carry

    lax.fori_loop(0, channels // LANES, end_tile, 0)


def mixer_front(layer, projected, rim, masks, reset, conv_weight, conv_bias, state_weight, step_weight,
                step_bias, decay_log):
    steps = projected.shape[0]
    channels = conv_weight.shape[2]
    taps, rank, states = conv_weight.shape[1], step_weight.shape[1], decay_log.shape[1]
    columns = state_weight.shape[2]
    value = pl.BlockSpec((steps, CHUNKS, channels), lambda c: (0, 0, 0))
    shapes = [
        shaped((steps * CHUNKS, channels), jnp.bfloat16),
        shaped((steps, CHUNKS, columns)),
        shaped((steps, CHUNKS, channels)),
        shaped((states, CHUNKS, channels)),
        shaped((CHUNKS, channels)),
        shaped((states, channels)),
        shaped((1, channels)),
    ]
    return plain_call(
        functools.partial(front_kernel, (taps, rank, states, steps, channels)),
        (1,),
        [value, whole(rim.shape), whole(masks.shape), whole(reset.shape),
         layer_whole(layer, conv_weight.shape[1:]), layer_whole(layer, conv_bias.shape[1:]),
         layer_whole(layer, state_weight.shape[1:]), layer_whole(layer, step_weight.shape[1:]),
         layer_whole(layer, step_bias.shape[1:]), layer_whole(layer, decay_log.shape[1:])],
        [whole(s.shape) for s in shapes],
        shapes,
        [VMEM((steps + taps - 1, CHUNKS, channels), jnp.float32),
         VMEM((steps, states, CHUNKS, LANES), jnp.float32)],
        (projected, rim, masks, reset, conv_weight, conv_bias, state_weight, step_weight, step_bias,
         decay_log),
        18,
    )


def run_kernel(dims, size_ref, act_ref, selection_ref, reset_ref, decay_ref, link_ref, link_size_ref,
               entering_ref, gate_ref, skip_ref, out_weight_ref, current_ref, norm_ref, router_ref, fill_ref,
               mixed_ref, gated_ref, begin_ref, middle_ref, routed_ref, logits_ref, outbound_ref,
               in_maps, out_maps):
    rank, states, steps, tiles = dims

    @pl.when(pl.program_id(0) == 0)
    def _():
        spread_columns(selection_ref, rank, states, in_maps)
        spread_columns(selection_ref, rank + states, states, out_maps)
        middle_ref[...] = current_ref[...]

    rates = rate_rows(rates_of(decay_ref[...]))
    link_size = link_size_ref[...]
    skip = skip_ref[...]
    begin = []
    for n in range(states):
        first = link_ref[n] + jnp.exp2(link_size * rates[n]) * entering_ref[n : n + 1, :]
        begin_ref[n] = first
        begin.append(first)

    def one(pair, carry):
        levels = list(carry)
        acts = two_steps(act_ref, pair)
        both = []
        for half in (0, 1):
            step = 2 * pair + half
            size = size_ref[step]
            value = size * acts[half]
            size = size + reset_ref[step]
            sums = [skip * acts[half], None]
            for n in range(states):
                levels[n] = jnp.exp2(size * rates[n]) * levels[n] + value * in_maps[step, n]
                term = out_maps[step, n] * levels[n]
                sums[n % 2] = term if sums[n % 2] is None else sums[n % 2] + term
            mixed = sums[0] + sums[1]
            mixed_ref[step] = mixed
            both.append(mixed * jax.nn.silu(gate_ref[step]))
        at = pl.ds(pl.multiple_of(pair * 2 * CHUNKS, 2 * CHUNKS), 2 * CHUNKS)
        gated_ref[at, :] = jnp.concatenate(both, axis=0).astype(jnp.bfloat16)
        return tuple(levels)

    lax.fori_loop(0, steps // 2, one, tuple(begin))
    middle_ref[...] += dot_nn(gated_ref[...], out_weight_ref[...])

    @pl.when(pl.program_id(0) == tiles - 1)
    def _():
        routed = rms_scale(middle_ref[...], norm_ref[...]).astype(jnp.bfloat16)
        routed_ref[...] = routed
        logits_ref[...] = dot_nn(routed, router_ref[...])
        outbound_ref[...] = dot_nn(fill_ref[...], routed).astype(jnp.bfloat16)


def mixer_run(layer, size, act, selection, reset, decay_log, link, link_size, entering, projected, skip_weight,
              out_weight, current, norm_expert, router, fill):
    steps, _, channels = size.shape
    tokens = steps * CHUNKS
    states, width, experts = decay_log.shape[1], current.shape[1], router.shape[2]
    rank = selection.shape[2] - 2 * states
    tiles = channels // LANES
    low = jnp.bfloat16
    maps = VMEM((steps, states, CHUNKS, LANES), jnp.float32)
    return plain_call(
        functools.partial(run_kernel, (rank, states, steps, tiles)),
        (tiles,),
        [slab(steps), rows_of(tokens), whole(selection.shape), whole(reset.shape),
         layer_rows(layer, states), slab(states), rows_of(CHUNKS), rows_of(states), slab(steps, tiles),
         layer_rows(layer, 1), layer_columns(layer, width), whole(current.shape),
         layer_whole(layer, (1, width)), layer_whole(layer, (width, experts)), whole(fill.shape)],
        [slab(steps), rows_of(tokens), slab(states), whole((tokens, width)), whole((tokens, width)),
         whole((tokens, experts)), whole((fill.shape[0], width))],
        [
            shaped((steps, CHUNKS, channels)),
            shaped((tokens, channels), low),
            shaped((states, CHUNKS, channels)),
            shaped((tokens, width)),
            shaped((tokens, width), low),
            shaped((tokens, experts)),
            shaped((fill.shape[0], width), low),
        ],
        [maps, maps],
        (size, act, selection, reset, decay_log, link, link_size, entering, projected, skip_weight, out_weight,
         current, norm_expert, router, fill),
        22,
    )


def turn_kernel(dims, grad_ref, out_weight_ref, gate_ref, mixed_ref, act_ref, gated_ref, size_ref,
                selection_ref, reset_ref, decay_ref,
                grad_y_ref, grad_gate_ref, grad_skip_ref, grad_out_ref, link_ref, link_size_ref, total_ref,
                total_size_ref, maps, held):
    rank, states, steps = dims

    @pl.when(pl.program_id(0) == 0)
    def _():
        spread_columns(selection_ref, rank + states, states, maps)

    grad = grad_ref[...]
    grad_out_ref[...] = dot_tn(gated_ref[...], grad).astype(jnp.bfloat16)
    held[...] = dot_nt(grad, out_weight_ref[...]).reshape(steps, CHUNKS, LANES)
    rates = rate_rows(rates_of(decay_ref[...]))

    def one(at, carry):
        levels, length, skip = list(carry[:states]), carry[states], carry[states + 1]
        pair = steps // 2 - 1 - at
        acts = two_steps(act_ref, pair)
        both = [None, None]
        for half in (1, 0):
            step = 2 * pair + half
            gate = gate_ref[step]
            share = jax.nn.sigmoid(gate)
            gated = held[step]
            grad_y = gated * (gate * share)
            both[half] = gated * mixed_ref[step] * (share * (1.0 + gate * (1.0 - share)))
            grad_y_ref[step] = grad_y
            skip = skip + grad_y * acts[half]
            size = size_ref[step] + reset_ref[step]
            for n in range(states):
                levels[n] = jnp.exp2(size * rates[n]) * (levels[n] + grad_y * maps[step, n])
            length = length + size
        rows = pl.ds(pl.multiple_of(pair * 2 * CHUNKS, 2 * CHUNKS), 2 * CHUNKS)
        grad_gate_ref[rows, :] = jnp.concatenate(both, axis=0).astype(jnp.bfloat16)
        return tuple(levels) + (length, skip)

    zero = jnp.zeros((CHUNKS, LANES), jnp.float32)
    found = lax.fori_loop(0, steps // 2, one, (zero,) * (states + 2))
    grad_skip_ref[...] = jnp.sum(found[states + 1], axis=0, keepdims=True)
    links, totals, link_size, total_size = chunk_links(found, found[states], rates, True)
    link_size_ref[...] = link_size
    total_size_ref[...] = total_size
    for n in range(states):
        link_ref[n] = links[n]
        total_ref[n : n + 1, :] = totals[n]


def mixer_turn(layer, grad_low, out_weight, projected, mixed, act, gated, size, selection, reset, decay_log):
    steps, _, channels = size.shape
    tokens = steps * CHUNKS
    states, width = decay_log.shape[1], grad_low.shape[1]
    rank = selection.shape[2] - 2 * states
    tiles = channels // LANES
    low = jnp.bfloat16
    return plain_call(
        functools.partial(turn_kernel, (rank, states, steps)),
        (tiles,),
        [whole(grad_low.shape), layer_columns(layer, width), slab(steps, tiles), slab(steps), rows_of(tokens),
         rows_of(tokens), slab(steps), whole(selection.shape), whole(reset.shape), layer_rows(layer, states)],
        [slab(steps), rows_of(tokens), rows_of(1), pl.BlockSpec((LANES, width), lambda c: (c, 0)),
         slab(states), rows_of(CHUNKS), rows_of(states), rows_of(1)],
        [
            shaped((steps, CHUNKS, channels)),
            shaped((tokens, channels), low),
            shaped((1, channels)),
            shaped((channels, width), low),
            shaped((states, CHUNKS, channels)),
            shaped((CHUNKS, channels)),
            shaped((states, channels)),
            shaped((1, channels)),
        ],
        [VMEM((steps, states, CHUNKS, LANES), jnp.float32), VMEM((steps, CHUNKS, LANES), jnp.float32)],
        (grad_low, out_weight, projected, mixed, act, gated, size, selection, reset, decay_log),
        14,
    )


def back_kernel(dims, size_ref, act_ref, grad_ref, decay_ref, selection_ref, reset_ref, begin_ref, link_ref,
                link_size_ref, entering_ref, step_ref, step_bias_ref, skip_ref,
                grad_act_ref, grad_decay_ref, grad_bias_ref, grad_step_ref, grad_selection_ref,
                in_maps, out_maps, levels, decays, grad_in, grad_out, grad_size, grad_rate, grad_rank):
    rank, states, steps, tiles = dims
    tokens = steps * CHUNKS

    @pl.when(pl.program_id(0) == 0)
    def _():
        spread_columns(selection_ref, rank, states, in_maps)
        spread_columns(selection_ref, rank + states, states, out_maps)
        grad_in[...] = jnp.zeros_like(grad_in)
        grad_out[...] = jnp.zeros_like(grad_out)
        grad_rank[...] = jnp.zeros_like(grad_rank)

    true_rates = -jnp.exp(decay_ref[...])
    rates = rate_rows(true_rates * LOG2E)
    skip = skip_ref[...]
    begin = []
    for n in range(states):
        levels[0, n] = begin_ref[n]
        begin.append(begin_ref[n])

    def ahead(pair, carry):
        now = list(carry)
        acts = two_steps(act_ref, pair)
        for half in (0, 1):
            step = 2 * pair + half
            size = size_ref[step]
            value = size * acts[half]
            size = size + reset_ref[step]
            for n in range(states):
                decay = jnp.exp2(size * rates[n])
                decays[step, n] = decay
                now[n] = decay * now[n] + value * in_maps[step, n]
                levels[step + 1, n] = now[n]
        return tuple(now)

    lax.fori_loop(0, steps // 2, ahead, tuple(begin))
    link_size = link_size_ref[...]
    tail = []
    for n in range(states):
        tail.append(link_ref[n] + jnp.exp2(link_size * rates[n]) * entering_ref[n : n + 1, :])
        grad_rate[n] = jnp.zeros((CHUNKS, LANES), jnp.float32)

    def retreat(at, carry):
        passed = list(carry)
        pair = steps // 2 - 1 - at
        acts = two_steps(act_ref, pair)
        for half in (1, 0):
            step = 2 * pair + half
            plain = size_ref[step]
            act = acts[half]
            grad = grad_ref[step]
            value = plain * act
            by_rate = jnp.zeros((CHUNKS, LANES), jnp.float32)
            by_input = jnp.zeros((CHUNKS, LANES), jnp.float32)
            for n in range(states):
                lanes = slice(n * LANES, (n + 1) * LANES)
                back = out_maps[step, n] * grad + passed[n]
                grad_out[step, :, lanes] += grad * levels[step + 1, n]
                grad_in[step, :, lanes] += back * value
                by_input = by_input + back * in_maps[step, n]
                passed[n] = decays[step, n] * back
                pull = passed[n] * levels[step, n]
                by_rate = by_rate + pull * rates[n]
                grad_rate[n] += pull * plain
            grad_size[step] = by_rate * (1.0 / LOG2E) + act * by_input
            grad_act_ref[step] = plain * by_input + grad * skip
        return tuple(passed)

    lax.fori_loop(0, steps // 2, retreat, tuple(tail))
    for n in range(states):
        grad_decay_ref[n : n + 1, :] = (
            jnp.sum(grad_rate[n], axis=0, keepdims=True) * true_rates[n : n + 1, :]
        )
    rank_low = selection_ref[...].reshape(tokens, selection_ref.shape[2])[:, :rank].astype(jnp.bfloat16)
    linear = dot_nn(rank_low, step_ref[...]) + step_bias_ref[...]
    grad_linear = grad_size[...].reshape(tokens, LANES) * jax.nn.sigmoid(linear)
    grad_bias_ref[...] = jnp.sum(grad_linear, axis=0, keepdims=True)
    grad_low = grad_linear.astype(jnp.bfloat16)
    grad_step_ref[...] = dot_tn(rank_low, grad_low)
    grad_rank[...] += dot_nt(grad_low, step_ref[...])

    @pl.when(pl.program_id(0) == tiles - 1)
    def _():
        size = states * LANES
        row = lax.broadcasted_iota(jnp.int32, (size, states), 0)
        column = lax.broadcasted_iota(jnp.int32, (size, states), 1)
        pick = ((row >= column * LANES) & (row < (column + 1) * LANES)).astype(jnp.float32)
        pick = pick.astype(jnp.bfloat16)
        found = [grad_rank[...]]
        for ref in (grad_in, grad_out):
            full = ref[...].reshape(tokens, size)
            high = full.astype(jnp.bfloat16)
            rest = (full - high.astype(jnp.float32)).astype(jnp.bfloat16)
            found.append(dot_nn(high, pick) + dot_nn(rest, pick))
        grad_selection_ref[...] = jnp.concatenate(found, axis=1).astype(jnp.bfloat16)


def mixer_back(layer, size, act, grad_y, decay_log, selection, reset, begin, link, link_size, entering,
               step_weight, step_bias, skip_weight):
    steps, _, channels = size.shape
    tokens = steps * CHUNKS
    states = decay_log.shape[1]
    columns = selection.shape[2]
    rank = columns - 2 * states
    tiles = channels // LANES
    f32 = jnp.float32
    maps = VMEM((steps, states, CHUNKS, LANES), f32)
    return plain_call(
        functools.partial(back_kernel, (rank, states, steps, tiles)),
        (tiles,),
        [slab(steps), rows_of(tokens), slab(steps), layer_rows(layer, states), whole(selection.shape),
         whole(reset.shape), slab(states), slab(states), rows_of(CHUNKS), rows_of(states),
         layer_rows(layer, rank), layer_rows(layer, 1), layer_rows(layer, 1)],
        [slab(steps), rows_of(states), rows_of(1), rows_of(rank), whole((tokens, columns))],
        [
            shaped((steps, CHUNKS, channels)),
            shaped((states, channels)),
            shaped((1, channels)),
            shaped((rank, channels)),
            shaped((tokens, columns), jnp.bfloat16),
        ],
        [maps, maps, VMEM((steps + 1, states, CHUNKS, LANES), f32), maps,
         VMEM((steps, CHUNKS, states * LANES), f32), VMEM((steps, CHUNKS, states * LANES), f32),
         VMEM((steps, CHUNKS, LANES), f32), VMEM((states, CHUNKS, LANES), f32), VMEM((tokens, rank), f32)],
        (size, act, grad_y, decay_log, selection, reset, begin, link, link_size, entering, step_weight,
         step_bias, skip_weight),
        35,
    )


def conv_back_kernel(dims, grad_act_ref, grad_selection_ref, state_ref, value_ref, rim_ref, mask_ref,
                     conv_ref, conv_bias_ref, act_ref, grad_step_ref, grad_decay_ref, grad_bias_ref,
                     grad_skip_ref, grad_value_ref, edge_ref, rim_grad_ref, channel_ref,
                     extended, passed):
    taps, states, steps = dims
    tokens = steps * CHUNKS
    extend(value_ref, rim_ref, extended, taps)
    bias = conv_bias_ref[...]
    grad_selection = grad_selection_ref[...]
    from_selection = dot_nt(grad_selection, state_ref[...]).reshape(steps, CHUNKS, LANES)
    passed[:steps] = grad_act_ref[...] + from_selection
    passed[steps:] = jnp.zeros((taps - 1, CHUNKS, LANES), jnp.float32)
    zero = jnp.zeros((CHUNKS, LANES), jnp.float32)

    def ahead(step, carry):
        convolved = conv_slab(extended, step, mask_ref, conv_ref, bias, taps)
        share = jax.nn.sigmoid(convolved)
        grad = passed[step] * (share * (1.0 + convolved * (1.0 - share)))
        passed[step] = grad
        new = [carry[0] + grad, carry[1] + grad * extended[step + taps - 1]]
        for offset in range(1, taps):
            kept = grad * mask_ref[offset - 1, step]
            new.append(carry[offset + 1] + kept * extended[step + taps - 1 - offset])
        return tuple(new)

    sums = lax.fori_loop(0, steps, ahead, (zero,) * (taps + 1), unroll=4)

    def reach(step, last):
        total = zero
        for offset in range(last):
            at = step + offset
            part = conv_ref[offset : offset + 1, :] * passed[at]
            if offset:
                part = part * mask_ref[offset - 1, at]
            total = total + part
        return total

    def back(pair, carry):
        both = [reach(2 * pair + half, taps) for half in (0, 1)]
        rows = pl.ds(pl.multiple_of(pair * 2 * CHUNKS, 2 * CHUNKS), 2 * CHUNKS)
        grad_value_ref[rows, :] = jnp.concatenate(both, axis=0).astype(jnp.bfloat16)
        return carry

    safe = (steps - taps + 1) // 2
    lax.fori_loop(0, safe, back, 0, unroll=2)
    place = lax.broadcasted_iota(jnp.int32, (CHUNKS, LANES), 0)
    ends = {}
    for j in range(taps - 1):
        before = zero
        for offset in range(taps - 1 - j, taps):
            at = j - taps + 1 + offset
            before = before + conv_ref[offset : offset + 1, :] * (
                passed[at] * mask_ref[offset - 1, at]
            )
        rim_grad_ref[j : j + 1, :] = before[0:1]
        ends[steps - taps + 1 + j] = jnp.where(
            place < CHUNKS - 1, pltpu.roll(before, CHUNKS - 1, axis=0), 0.0
        )
    for pair in range(safe, steps // 2):
        both = []
        for step in (2 * pair, 2 * pair + 1):
            total = reach(step, min(taps, steps - step))
            if step in ends:
                total = total + ends[step]
                j = step - steps + taps - 1
                edge_ref[j : j + 1, :] = total[CHUNKS - 1 : CHUNKS]
            both.append(total)
        grad_value_ref[2 * pair * CHUNKS : (2 * pair + 2) * CHUNKS, :] = jnp.concatenate(
            both, axis=0
        ).astype(jnp.bfloat16)
    small = jnp.zeros((CHUNKS, LANES), jnp.float32)
    rows = [jnp.sum(part, axis=0, keepdims=True) for part in sums[1:] + sums[:1]]
    rows += [grad_bias_ref[...], grad_skip_ref[...]]
    for index, row in enumerate(rows):
        small = jnp.where(place == index, row, small)
    grad_state = dot_tn(grad_selection, act_ref[...])
    parts = [grad_state, grad_step_ref[...], grad_decay_ref[...], small]
    used = sum(part.shape[0] for part in parts)
    parts.append(jnp.zeros((2 * LANES - used, LANES), jnp.float32))
    channel_ref[...] = jnp.concatenate(parts, axis=0).T.astype(jnp.bfloat16)


def mixer_conv_back(layer, grad_act, grad_selection, state_weight, projected, rim, masks, conv_weight,
                    conv_bias, act, grad_step, grad_decay, grad_bias, grad_skip):
    steps, _, channels = grad_act.shape
    tokens = steps * CHUNKS
    taps, columns = conv_weight.shape[1], state_weight.shape[2]
    states, rank = grad_decay.shape[0], grad_step.shape[0]
    tiles = channels // LANES
    f32 = jnp.float32
    return plain_call(
        functools.partial(conv_back_kernel, (taps, states, steps)),
        (tiles,),
        [slab(steps), whole(grad_selection.shape), layer_columns(layer, columns), slab(steps),
         rows_of(taps - 1), whole(masks.shape), layer_rows(layer, taps), layer_rows(layer, 1),
         rows_of(tokens), rows_of(rank), rows_of(states), rows_of(1), rows_of(1)],
        [rows_of(tokens), rows_of(taps - 1), rows_of(taps - 1),
         pl.BlockSpec((LANES, 2 * LANES), lambda c: (c, 0))],
        [
            shaped((tokens, channels), jnp.bfloat16),
            shaped((taps - 1, channels)),
            shaped((taps - 1, channels)),
            shaped((channels, 2 * LANES), jnp.bfloat16),
        ],
        [VMEM((steps + taps - 1, CHUNKS, LANES), f32), VMEM((steps + taps - 1, CHUNKS, LANES), f32)],
        (grad_act, grad_selection, state_weight, projected, rim, masks, conv_weight, conv_bias, act, grad_step,
         grad_decay, grad_bias, grad_skip),
        10,
    )


def link_kernel(layer, count, reverse, total_ref, size_ref, decay_ref, out_ref,
                mine, mine_length, near, near_length, both, both_length, far, far_length,
                send, recv, send_length, recv_length):
    here = lax.axis_index("wide")
    group = lax.axis_index("narrow")
    pairs = count // 2
    pair, side = here // 2, lax.rem(here, 2)
    partner = here + 1 - 2 * side
    others = [lax.rem(pair + k, pairs) for k in range(1, pairs)]
    f32 = jnp.float32
    barrier = pltpu.get_barrier_semaphore()
    pl.semaphore_signal(barrier, inc=1, device_id=(partner, group), device_id_type=MESH)
    for other in others:
        pl.semaphore_signal(barrier, inc=1, device_id=(2 * other + side, group), device_id_type=MESH)
    mine[...] = total_ref[...].astype(mine.dtype)
    mine_length[...] = size_ref[...]
    rate = rates_of(decay_ref[layer])
    pl.semaphore_wait(barrier, pairs)

    def hand(index, source, source_length, target, target_length, window):
        copies = []
        for src, dst, out, back in (
            (source, target, send, recv), (source_length, target_length, send_length, recv_length)):
            copies.append(pltpu.make_async_remote_copy(
                src_ref=src, dst_ref=dst, send_sem=out.at[index], recv_sem=back.at[index],
                device_id=(window, group), device_id_type=MESH))
            copies[-1].start()
        return copies

    first = hand(0, mine, mine_length, near, near_length, partner)
    for copy in first:
        copy.wait_recv()
    second_here = (side == 0) if reverse else (side == 1)
    own, own_length = total_ref[...], size_ref[...]
    met, met_length = near[...].astype(f32), near_length[...]
    late_length = jnp.where(second_here, own_length, met_length)
    early = jnp.where(second_here, met, own)
    late = jnp.where(second_here, own, met)
    both[...] = (jnp.exp2(late_length * rate) * early + late).astype(both.dtype)
    both_length[...] = own_length + met_length
    sent = []
    for k, other in enumerate(others):
        sent.append(hand(
            1 + k, both, both_length, far.at[pair], far_length.at[pair], 2 * other + side))
    for copies in sent:
        for copy in copies:
            copy.wait_recv()
    level = jnp.zeros(own.shape, f32)
    for at in range(pairs - 1, -1, -1) if reverse else range(pairs):
        valid = (pair < at) if reverse else (pair > at)
        step = jnp.exp2(far_length[at] * rate) * level + far[at].astype(f32)
        level = jnp.where(valid, step, level)
    step = jnp.exp2(met_length * rate) * level + met
    out_ref[...] = jnp.where(second_here, step, level)
    for copies in [first] + sent:
        for copy in copies:
            copy.wait_send()


def handed_on(layer, total, size, decay_log, reverse, identity):
    count = lax.axis_size("wide")
    pairs = count // 2
    states, channels = total.shape
    f32, low = jnp.float32, jnp.bfloat16
    dma = pltpu.SemaphoreType.DMA((pairs,))
    return pl.pallas_call(
        functools.partial(link_kernel, layer, count, reverse),
        out_shape=jax.ShapeDtypeStruct((states, channels), f32),
        in_specs=[pl.BlockSpec(memory_space=VMEM)] * 3,
        out_specs=pl.BlockSpec(memory_space=VMEM),
        scratch_shapes=[
            VMEM((states, channels), low),
            VMEM((1, channels), f32),
            VMEM((states, channels), low),
            VMEM((1, channels), f32),
            VMEM((states, channels), low),
            VMEM((1, channels), f32),
            VMEM((pairs, states, channels), low),
            VMEM((pairs, 1, channels), f32),
            dma, dma, dma, dma,
        ],
        compiler_params=pltpu.CompilerParams(
            collective_id=identity, has_side_effects=True, vmem_limit_bytes=16 * MIB
        ),
        cost_estimate=microseconds(12),
    )(total, size, decay_log)


def gelu_parts(values):
    bell = 0.5 * (1.0 + lax.erf(values * 0.7071067811865476))
    return bell


def expert_kernel(dims, backward, layer, *refs):
    count, groups, experts, block, share, width, hidden = dims
    if backward:
        (out_ref, perm_ref, up_hbm, down_hbm, pre_hbm, ret_ref, rows_hbm, low_hbm,
         arrived, rows, pre, low, part, got, final, landed, up, down,
         there_send, there_recv, gather_send, gather_recv, sum_send, sum_recv,
         back_send, back_recv, local) = refs
    else:
        (out_ref, perm_ref, up_hbm, down_hbm, ret_ref, rows_hbm, pre_hbm, low_hbm,
         arrived, rows, pre, low, part, got, final, landed, up, down,
         there_send, there_recv, gather_send, gather_recv, sum_send, sum_recv,
         back_send, back_recv, local) = refs
    here = lax.axis_index("wide")
    group = lax.axis_index("narrow")
    half = count // 2

    def window_of(position):
        position = lax.rem(position + 2 * count, count)
        upper = position // half
        return 2 * position * (1 - upper) + (2 * (count - 1 - position) + 1) * upper

    odd = lax.rem(here, 2)
    spot = (here // 2) * (1 - odd) + (count - 1 - here // 2) * odd
    ring = (window_of(spot + 1), window_of(spot - 1))
    peers = [lax.rem(group + k, groups) for k in range(1, groups)]

    loads = [
        pltpu.make_async_copy(up_hbm.at[layer], up, local.at[0]),
        pltpu.make_async_copy(down_hbm.at[layer], down, local.at[1]),
    ]
    if backward:
        loads.append(pltpu.make_async_copy(pre_hbm, pre, local.at[2]))
    for load in loads:
        load.start()

    barrier = pltpu.get_barrier_semaphore()
    for window in ring:
        pl.semaphore_signal(barrier, inc=1, device_id=(window, group), device_id_type=MESH)
    for peer in peers:
        pl.semaphore_signal(barrier, inc=1, device_id=(here, peer), device_id_type=MESH)
    pl.semaphore_wait(barrier, groups + 1)

    there = []
    for k, peer in enumerate(peers):
        there.append(pltpu.make_async_remote_copy(
            src_ref=out_ref.at[peer], dst_ref=arrived.at[group], send_sem=there_send.at[k],
            recv_sem=there_recv.at[k], device_id=(here, peer), device_id_type=MESH))
        there[-1].start()
    arrived[group] = out_ref[group]
    for copy in there:
        copy.wait_recv()
    flat = arrived[...].reshape(groups * block, width)
    own = dot_nn(perm_ref[...], flat).astype(jnp.bfloat16).reshape(experts, share, width)

    def span(window):
        return pl.ds(pl.multiple_of(window * share, 16), share)

    rows[:, span(here), :] = own

    def compute(windows):
        def one(e, carry):
            x = jnp.concatenate([rows[e, span(w), :] for w in windows], axis=0)
            if backward:
                grad_hidden = dot_nt(x, down[e])
                before = jnp.concatenate([pre[e, span(w), :] for w in windows], axis=0)
                slope = gelu_parts(before) + before * (
                    0.3989422804014327 * jnp.exp(-0.5 * before * before)
                )
                middle = (grad_hidden * slope).astype(jnp.bfloat16)
                y = dot_nt(middle, up[e])
            else:
                before = dot_nn(x, up[e])
                middle = (before * gelu_parts(before)).astype(jnp.bfloat16)
                y = dot_nn(middle, down[e])
            y = y.astype(jnp.bfloat16)
            for index, w in enumerate(windows):
                piece = slice(index * share, (index + 1) * share)
                if not backward:
                    pre[e, span(w), :] = before[piece]
                low[e, span(w), :] = middle[piece]
                part[e, span(w), :] = y[piece]
            return carry

        lax.fori_loop(0, experts, one, 0)

    cut = experts // 2
    halves = (pl.ds(0, cut), pl.ds(cut, experts - cut))
    gathers = []

    def parts_at(step):
        return [(way, sign, piece) for piece in (0, 1) for way, sign in ((0, 1), (1, -1))
                if step < half or piece == way]

    def hop(step, way, sign, piece):
        origin = window_of(spot - sign * (step - 1))
        return pltpu.make_async_remote_copy(
            src_ref=rows.at[halves[piece], span(origin), :], dst_ref=rows.at[halves[piece], span(origin), :],
            send_sem=gather_send.at[way, step - 1, piece], recv_sem=gather_recv.at[way, step - 1, piece],
            device_id=(ring[way], group), device_id_type=MESH)

    def pass_on(step, way, sign, piece):
        copy = hop(step, way, sign, piece)
        copy.start()
        gathers.append(copy)

    for way, sign, piece in parts_at(1):
        pass_on(1, way, sign, piece)
    for load in loads:
        load.wait()
    compute([here])
    for step in range(1, half + 1):
        for way, sign, piece in parts_at(step):
            hop(step, way, sign, piece).wait_recv()
            if step < half and (way, sign, piece) in parts_at(step + 1):
                pass_on(step + 1, way, sign, piece)
        if step < half:
            compute([window_of(spot - step), window_of(spot + step)])
        else:
            compute([window_of(spot + half)])

    saves = [
        pltpu.make_async_copy(rows, rows_hbm, local.at[3]),
        pltpu.make_async_copy(low, low_hbm, local.at[4]),
    ]
    if not backward:
        saves.append(pltpu.make_async_copy(pre, pre_hbm, local.at[2]))
    for save in saves:
        save.start()

    sums, last = [], {}
    for step in range(half):
        for which in (0, 1):
            for way, sign in ((0, 1), (1, -1)):
                if step == 0 and which != way:
                    continue
                window = window_of(spot + sign * (half - step))
                held = halves[which]
                if (way, which) in last:
                    last[way, which].wait_recv()
                    part[held, span(window), :] = (
                        part[held, span(window), :].astype(jnp.float32)
                        + got[way, step - 1, held].astype(jnp.float32)
                    ).astype(jnp.bfloat16)
                copy = pltpu.make_async_remote_copy(
                    src_ref=part.at[held, span(window), :], dst_ref=got.at[way, step, held],
                    send_sem=sum_send.at[way, step, which], recv_sem=sum_recv.at[way, step, which],
                    device_id=(ring[way], group), device_id_type=MESH)
                copy.start()
                sums.append(copy)
                last[way, which] = copy
    total = part[:, span(here), :].astype(jnp.float32)
    for way in (0, 1):
        for which in (0, 1):
            last[way, which].wait_recv()
        total = total + got[way, half - 1].astype(jnp.float32)
    packed = total.astype(jnp.bfloat16).reshape(experts * share, width)
    final[...] = dot_tn(perm_ref[...], packed).astype(jnp.bfloat16).reshape(groups, block, width)

    home = []
    for k, peer in enumerate(peers):
        home.append(pltpu.make_async_remote_copy(
            src_ref=final.at[peer], dst_ref=landed.at[group], send_sem=back_send.at[k],
            recv_sem=back_recv.at[k], device_id=(here, peer), device_id_type=MESH))
        home[-1].start()
    ret_ref[group] = final[group]
    for k, copy in enumerate(home):
        copy.wait_recv()
    for k in range(1, groups):
        source = lax.rem(group + groups - k, groups)
        ret_ref[source] = landed[source]
    for copy in there + gathers + sums + home:
        copy.wait_send()
    for save in saves:
        save.wait()


def expert_pass(outbound, perm, expert_up, expert_down, pre, layer, identity):
    count, groups = lax.axis_size("wide"), lax.axis_size("narrow")
    backward = pre is not None
    _, block, width = outbound.shape
    _, experts, _, hidden = expert_up.shape
    share = perm.shape[0] // experts
    half = count // 2
    total = count * share
    low, f32 = jnp.bfloat16, jnp.float32
    dims = (count, groups, experts, block, share, width, hidden)
    anywhere, inside = pl.BlockSpec(memory_space=pl.ANY), pl.BlockSpec(memory_space=VMEM)
    saved_rows = jax.ShapeDtypeStruct((experts, total, width), low)
    saved_low = jax.ShapeDtypeStruct((experts, total, hidden), low)
    saved_pre = jax.ShapeDtypeStruct((experts, total, hidden), f32)
    back = jax.ShapeDtypeStruct((groups, block, width), low)
    dma = pltpu.SemaphoreType.DMA
    args = (outbound, perm, expert_up, expert_down) + ((pre,) if backward else ())
    outs = [back, saved_rows] + ([] if backward else [saved_pre]) + [saved_low]
    return pl.pallas_call(
        functools.partial(expert_kernel, dims, backward, layer),
        out_shape=outs,
        in_specs=[inside, inside] + [anywhere] * (len(args) - 2),
        out_specs=[inside] + [anywhere] * (len(outs) - 1),
        scratch_shapes=[
            VMEM((groups, block, width), low),
            VMEM((experts, total, width), low),
            VMEM((experts, total, hidden), f32),
            VMEM((experts, total, hidden), low),
            VMEM((experts, total, width), low),
            VMEM((2, half, experts, share, width), low),
            VMEM((groups, block, width), low),
            VMEM((groups, block, width), low),
            VMEM((experts, width, hidden), low),
            VMEM((experts, hidden, width), low),
            dma((groups - 1,)), dma((groups - 1,)),
            dma((2, half, 2)), dma((2, half, 2)),
            dma((2, half, 2)), dma((2, half, 2)),
            dma((groups - 1,)), dma((groups - 1,)),
            dma((5,)),
        ],
        compiler_params=pltpu.CompilerParams(
            collective_id=identity, has_side_effects=True, vmem_limit_bytes=56 * MIB
        ),
        cost_estimate=microseconds(95),
    )(*args)


def expert_order(experts, groups, block, capacity):
    share = groups * capacity
    row = jnp.arange(experts * share, dtype=jnp.int32)
    expert, rest = row // share, row % share
    source = (rest // capacity) * block + expert * capacity + rest % capacity
    return (source[:, None] == jnp.arange(groups * block, dtype=jnp.int32)[None, :]).astype(jnp.bfloat16)


def sum_kernel(dims, *refs):
    count, lines, sizes, first_rows, width = dims
    total = len(sizes)
    arrays, out_ref = refs[:total], refs[total]
    (own, near, over, spun, spun_first, home, core_send, core_recv, load, over_send, over_recv,
     spin_send, spin_recv, spin_first_send, spin_first_recv, home_send, home_recv) = refs[total + 1 :]
    rows = sum(sizes)
    later = rows - first_rows
    here = lax.axis_index("wide")
    group = lax.axis_index("narrow")
    line, core = group // 2, lax.rem(group, 2)
    half = count // 2
    low, f32 = jnp.bfloat16, jnp.float32

    def window_of(position):
        position = lax.rem(position + 2 * count, count)
        upper = position // half
        return 2 * position * (1 - upper) + (2 * (count - 1 - position) + 1) * upper

    odd = lax.rem(here, 2)
    spot = (here // 2) * (1 - odd) + (count - 1 - here // 2) * odd
    ring = (window_of(spot + 1), window_of(spot - 1))
    peer = 2 * line + 1 - core
    lines_away = [lax.rem(line + k, lines) for k in range(1, lines)]

    barrier = pltpu.get_barrier_semaphore()
    for window in ring:
        pl.semaphore_signal(barrier, inc=1, device_id=(window, group), device_id_type=MESH)
    pl.semaphore_signal(barrier, inc=1, device_id=(here, peer), device_id_type=MESH)
    for other in lines_away:
        pl.semaphore_signal(barrier, inc=1, device_id=(here, 2 * other + core), device_id_type=MESH)
    pl.semaphore_wait(barrier, 2 + lines)

    order = [spot + half]
    for away in range(half - 1, 0, -1):
        order += [spot + away, spot - away]
    order = [window_of(position) for position in order + [spot]]
    sent, held = [], []
    for k, window in enumerate(order):
        held.append([])
        start = 0
        for i, size in enumerate(sizes):
            place = pl.ds(start, size)
            start += size
            copy = pltpu.make_async_remote_copy(
                src_ref=arrays[i].at[window, :, 1 - core], dst_ref=near.at[window, :, place],
                send_sem=core_send.at[k, i], recv_sem=core_recv.at[k, i],
                device_id=(here, peer), device_id_type=MESH)
            copy.start()
            mine = pltpu.make_async_copy(
                arrays[i].at[window, :, core], own.at[window, :, place], load.at[k, i])
            mine.start()
            sent.append(copy)
            held[-1].append((copy, mine))

    ahead, behind = pl.ds(0, first_rows), pl.ds(first_rows, later)
    cut_first = first_rows // 32 * 16
    cut_later = later // 32 * 16
    parts_first = (pl.ds(0, cut_first), pl.ds(cut_first, first_rows - cut_first))
    parts_later = (
        pl.ds(first_rows, cut_later), pl.ds(first_rows + cut_later, later - cut_later))
    parts_got = (pl.ds(0, cut_later), pl.ds(cut_later, later - cut_later))

    def meet(k):
        window = order[k]
        for copy, mine in held[k]:
            copy.wait_recv()
            mine.wait()

        def one(at, carry):
            place = pl.ds(pl.multiple_of(at * 16, 16), 16)
            for x in range(lines):
                own[window, x, place] = (
                    own[window, x, place].astype(f32) + near[window, x, place].astype(f32)
                ).astype(low)
            return carry

        lax.fori_loop(0, rows // 16, one, 0)
        for j, other in enumerate(lines_away):
            copy = pltpu.make_async_remote_copy(
                src_ref=own.at[window, other, ahead], dst_ref=over.at[j, window],
                send_sem=over_send.at[j, k], recv_sem=over_recv.at[j, k],
                device_id=(here, 2 * other + core), device_id_type=MESH)
            copy.start()
            sent.append(copy)
            crossing[k].append(copy)

    crossing = [[] for _ in order]

    def spin_later(step):
        for way, sign in ((0, 1), (1, -1)):
            window = window_of(spot + sign * (half - step))
            if step == 0:
                which, got_which = parts_later[way], parts_got[way]
            else:
                which, got_which = behind, pl.ds(0, later)
                add_which, add_got = (
                    (parts_later[way], parts_got[way]) if step == 1 else (which, got_which))
                turns[way][-1].wait_recv()
                own[window, :, add_which] = (
                    own[window, :, add_which].astype(f32)
                    + spun[way, step - 1, :, add_got].astype(f32)
                ).astype(low)
            copy = pltpu.make_async_remote_copy(
                src_ref=own.at[window, :, which], dst_ref=spun.at[way, step, :, got_which],
                send_sem=spin_send.at[way, step], recv_sem=spin_recv.at[way, step],
                device_id=(ring[way], group), device_id_type=MESH)
            copy.start()
            sent.append(copy)
            turns[way].append(copy)

    turns = ([], [])
    meet(0)
    spin_later(0)
    for step in range(1, half):
        meet(2 * step - 1)
        meet(2 * step)
        spin_later(step)
    meet(len(order) - 1)
    summed = own[here, :, behind].astype(f32)
    for way in (0, 1):
        turns[way][-1].wait_recv()
        summed = summed + spun[way, half - 1].astype(f32)
    own[here, :, behind] = summed.astype(low)
    homes = []
    for j, other in enumerate(lines_away):
        copy = pltpu.make_async_remote_copy(
            src_ref=own.at[here, other, behind], dst_ref=home.at[j],
            send_sem=home_send.at[j], recv_sem=home_recv.at[j],
            device_id=(here, 2 * other + core), device_id_type=MESH)
        copy.start()
        sent.append(copy)
        homes.append(copy)

    def cross(k):
        window = order[k]
        value = own[window, line, ahead].astype(f32)
        for j, copy in enumerate(crossing[k]):
            copy.wait_recv()
            value = value + over[j, window].astype(f32)
        return value

    first_turns = ([], [])

    def spin_first(step):
        for way, sign in ((0, 1), (1, -1)):
            k = 0 if step == 0 else 2 * step - 1 + way
            window = order[k]
            if step or way == 0:
                own[window, line, ahead] = cross(k).astype(low)
            if step == 0:
                which = parts_first[way]
            else:
                which = ahead
                add_which = parts_first[way] if step == 1 else which
                first_turns[way][-1].wait_recv()
                own[window, line, add_which] = (
                    own[window, line, add_which].astype(f32)
                    + spun_first[way, step - 1, add_which].astype(f32)
                ).astype(low)
            copy = pltpu.make_async_remote_copy(
                src_ref=own.at[window, line, which], dst_ref=spun_first.at[way, step, which],
                send_sem=spin_first_send.at[way, step], recv_sem=spin_first_recv.at[way, step],
                device_id=(ring[way], group), device_id_type=MESH)
            copy.start()
            sent.append(copy)
            first_turns[way].append(copy)

    for step in range(half):
        spin_first(step)
    summed = cross(len(order) - 1)
    for way in (0, 1):
        first_turns[way][-1].wait_recv()
        summed = summed + spun_first[way, half - 1].astype(f32)
    out_ref[ahead, :] = summed
    value = own[here, line, behind].astype(f32)
    for j, copy in enumerate(homes):
        copy.wait_recv()
        value = value + home[j].astype(f32)
    out_ref[behind, :] = value
    for copy in sent:
        copy.wait_send()


def summed_shares(arrays, identity):
    count, groups = lax.axis_size("wide"), lax.axis_size("narrow")
    lines, half = groups // 2, count // 2
    width = arrays[0].shape[2]
    if any(array.shape[1] % 16 for array in arrays):
        packed = jnp.concatenate(arrays, axis=1)
        arrays = [jnp.pad(packed, ((0, 0), (0, -packed.shape[1] % 16), (0, 0)))]
    sizes = tuple(array.shape[1] for array in arrays)
    rows = sum(sizes)
    first = max(32, rows * 11 // 20 // 16 * 16)
    later = rows - first
    low = jnp.bfloat16
    dma = pltpu.SemaphoreType.DMA
    return pl.pallas_call(
        functools.partial(sum_kernel, (count, lines, sizes, first, width)),
        out_shape=jax.ShapeDtypeStruct((rows, width), jnp.float32),
        in_specs=[ANYWHERE] * len(arrays),
        out_specs=pl.BlockSpec(memory_space=VMEM),
        scratch_shapes=[
            VMEM((count, lines, rows, width), low),
            VMEM((count, lines, rows, width), low),
            VMEM((lines - 1, count, first, width), low),
            VMEM((2, half, lines, later, width), low),
            VMEM((2, half, first, width), low),
            VMEM((lines - 1, later, width), low),
            dma((count, len(arrays))), dma((count, len(arrays))), dma((count, len(arrays))),
            dma((lines - 1, count)), dma((lines - 1, count)),
            dma((2, half)), dma((2, half)),
            dma((2, half)), dma((2, half)),
            dma((lines - 1,)), dma((lines - 1,)),
        ],
        compiler_params=pltpu.CompilerParams(
            collective_id=identity, has_side_effects=True, vmem_limit_bytes=56 * MIB
        ),
        cost_estimate=microseconds(60),
    )(*[array.reshape(count, lines, 2, array.shape[1], width) for array in arrays])


def weights_kernel(experts, *refs):
    first, second, (up_ref, down_ref) = refs[:4], refs[4:8], refs[8:]
    for layer, (rows, pre, hidden, grad) in enumerate((first, second)):
        @pl.when(pl.program_id(0) // experts == layer)
        def _():
            up_ref[...] = dot_tn(rows[...], pre[...])
            down_ref[...] = dot_tn(hidden[...], grad[...])


def expert_weights(kept):
    experts, total, width = kept[0][0].shape
    hidden = kept[0][1].shape[2]
    f32 = jnp.float32
    specs = []
    for layer in (0, 1):
        for columns in (width, hidden, hidden, width):
            if layer == 0:
                place = lambda i: (jnp.minimum(i, experts - 1), 0, 0)
            else:
                place = lambda i: (jnp.maximum(i - experts, 0), 0, 0)
            specs.append(pl.BlockSpec((None, total, columns), place))
    outs = [
        pl.BlockSpec((None, None, width, hidden), lambda i: (i // experts, i % experts, 0, 0)),
        pl.BlockSpec((None, None, hidden, width), lambda i: (i // experts, i % experts, 0, 0)),
    ]
    return plain_call(
        functools.partial(weights_kernel, experts),
        (2 * experts,),
        specs,
        outs,
        [shaped((2, experts, width, hidden), f32), shaped((2, experts, hidden, width), f32)],
        [],
        tuple(kept[0]) + tuple(kept[1]),
        15,
    )


def on_device(
    hidden,
    doc_start,
    expert_choice,
    slot_index,
    norm_mix,
    in_weight,
    conv_weight,
    conv_bias,
    state_weight,
    step_weight,
    step_bias,
    decay_log,
    skip_weight,
    out_weight,
    norm_expert,
    router,
    expert_up,
    expert_down,
    cotangent,
):
    layers = in_weight.shape[0]
    tokens = hidden.shape[1]
    width = hidden.shape[2]
    inner = skip_weight.shape[1]
    rank = step_weight.shape[1]
    states = decay_log.shape[1]
    experts = router.shape[2]
    taps = conv_weight.shape[1]
    steps = tokens // CHUNKS
    both = ("wide", "narrow")
    groups = lax.axis_size("narrow")
    devices = lax.axis_size("wide") * groups
    per_group = experts // groups
    capacity = max(2, 5 * tokens // (4 * experts))
    block = -(-per_group * capacity // 16) * 16
    low, f32 = jnp.bfloat16, jnp.float32
    starts = to_steps(doc_start[0]).astype(f32)
    masks = keep_masks(starts, taps)
    keep_mask = rim_keep(starts, taps - 1)[:, None]
    reset = jnp.broadcast_to((starts * RESET)[..., None], starts.shape + (LANES,))
    order = expert_order(per_group, groups, block, capacity)
    conv_bias, step_bias, skip_weight, norm_expert = (
        values[:, None, :] for values in (conv_bias, step_bias, skip_weight, norm_expert))
    current = to_steps(hidden[0]).reshape(tokens, width).astype(f32)
    saved = []

    def cube(values):
        return values.reshape(steps, CHUNKS, values.shape[-1])

    fills, onehots, keeps = [], [], []
    for layer in range(layers):
        chosen = to_steps(expert_choice[layer, 0]).reshape(tokens)
        slot_row = to_steps(slot_index[layer, 0]).reshape(tokens)
        kept = slot_row >= 0
        place = (chosen // per_group) * block + (chosen % per_group) * capacity + slot_row
        place = jnp.where(kept, place, -1)
        fills.append(
            (place[None, :] == jnp.arange(groups * block, dtype=jnp.int32)[:, None]).astype(low))
        onehots.append((chosen[:, None] == jnp.arange(experts, dtype=jnp.int32)[None, :]).astype(f32))
        keeps.append(kept.astype(f32)[:, None])

    for layer in range(layers):
        begin = current
        normed = rms_scale(current, norm_mix[layer]).astype(low)
        projected = cube(dot_nn(normed, in_weight[layer]))
        rim = passed_along(projected[steps - taps + 1 :, CHUNKS - 1, :inner] * keep_mask, 1)
        act, selection, size, link, link_size, total, total_size = mixer_front(
            layer, projected, rim, masks, reset, conv_weight, conv_bias, state_weight, step_weight, step_bias,
            decay_log)
        entering = handed_on(layer, total, total_size, decay_log, False, layer)
        mixed, gated, begins, middle, routed, logits, outbound = mixer_run(
            layer, size, act, selection, reset, decay_log, link, link_size, entering, projected, skip_weight,
            out_weight, current, norm_expert, router, fills[layer])
        returned, kept_rows, pre_act, hidden_low = expert_pass(
            outbound.reshape(groups, block, width), order, expert_up, expert_down, None, layer, 4 + layer)
        shares = jax.nn.softmax(logits, axis=-1)
        gate = jnp.sum(shares * onehots[layer], axis=1, keepdims=True)
        back_rows = dot_tn(fills[layer], returned.reshape(groups * block, width))
        current = middle + (keeps[layer] * gate) * back_rows
        saved.append(dict(
            begin=begin, normed=normed, projected=projected, rim=rim, act=act, selection=selection, size=size,
            begins=begins, mixed=mixed, gated=gated, middle=middle, routed=routed, shares=shares, gate=gate,
            kept_rows=kept_rows, pre_act=pre_act, hidden_low=hidden_low, back_rows=back_rows))
    output = to_tokens(cube(current.astype(low)))[None]
    grad = to_steps(cotangent[0]).reshape(tokens, width).astype(f32)
    packed = [None] * layers
    expert_kept = [None] * layers
    per_device = inner // devices
    norm_device = width // devices
    fold = width // (2 * LANES)
    spare = 160
    for layer in range(layers - 1, -1, -1):
        entry = saved[layer]
        fill, keep, gate = fills[layer], keeps[layer], entry["gate"]
        grad_rows_low = ((keep * gate) * grad).astype(low)
        grad_gate = keep * jnp.sum(grad * entry["back_rows"], axis=1, keepdims=True)
        outbound = dot_nn(fill, grad_rows_low).astype(low).reshape(groups, block, width)
        inbound, grad_rows, grad_pre = expert_pass(
            outbound, order, expert_up, expert_down, entry["pre_act"], layer, 6 + layer)
        expert_kept[layer] = (entry["kept_rows"], grad_pre, entry["hidden_low"], grad_rows)
        grad_sent = dot_tn(fill, inbound.reshape(groups * block, width))
        grad_logits_low = ((grad_gate * gate) * (onehots[layer] - entry["shares"])).astype(low)
        grad_router = dot_tn(entry["routed"], grad_logits_low)
        grad_routed = grad_sent + dot_nt(grad_logits_low, router[layer])
        grad_middle, grad_norm_expert = rms_back(entry["middle"], norm_expert[layer], grad_routed)
        grad = grad + grad_middle
        grad_low = grad.astype(low)
        grad_y, grad_igate, grad_skip, grad_out, link, link_size, total, total_size = mixer_turn(
            layer, grad_low, out_weight, entry["projected"], entry["mixed"], entry["act"], entry["gated"],
            entry["size"], entry["selection"], reset, decay_log)
        entering = handed_on(layer, total, total_size, decay_log, True, 2 + layer)
        grad_act, grad_decay, grad_bias, grad_step, grad_selection = mixer_back(
            layer, entry["size"], entry["act"], grad_y, decay_log, entry["selection"], reset,
            entry["begins"], link, link_size, entering, step_weight, step_bias, skip_weight)
        grad_value, edge, rim_grad, channel = mixer_conv_back(
            layer, grad_act, grad_selection, state_weight, entry["projected"], entry["rim"], masks, conv_weight,
            conv_bias, entry["act"], grad_step, grad_decay, grad_bias, grad_skip)
        edge = edge + passed_along(rim_grad, -1) * keep_mask
        grad_value = cube(grad_value).at[steps - taps + 1 :, CHUNKS - 1].set(edge.astype(low))
        grad_value = grad_value.reshape(tokens, inner)
        grad_projected = jnp.concatenate([grad_value, grad_igate], axis=1)
        grad_in = dot_tn(grad_projected, entry["normed"]).astype(low)
        grad_normed = dot_nt(grad_projected, in_weight[layer])
        grad_begin, grad_norm_mix = rms_back(entry["begin"], norm_mix[layer], grad_normed)
        grad = grad + grad_begin
        feature = jnp.concatenate(
            [grad_router, grad_norm_mix[:, None], grad_norm_expert.reshape(width, 1)], axis=1)
        feature = jnp.pad(
            feature.reshape(devices, norm_device, experts + 2).astype(low),
            ((0, 0), (0, per_device - norm_device), (spare, 2 * LANES - spare - experts - 2)))
        channel = channel.reshape(devices, per_device, 2 * LANES) + feature
        channel = jnp.swapaxes(channel.reshape(devices, fold, per_device // fold, 2 * LANES), 1, 2)
        packed[layer] = [
            grad_in.reshape(devices, -1, width),
            grad_out.reshape(devices, -1, width),
            channel.reshape(devices, -1, width),
        ]
    up_grads, down_grads = expert_weights(expert_kept)
    sums = summed_shares([part for parts in packed for part in parts], 8)
    bounds = [0]
    for part in packed[0]:
        bounds.append(bounds[-1] + part.shape[1])
    sums = sums[: layers * bounds[-1]].reshape(layers, bounds[-1], width)
    grad_in, grad_out, mine = (sums[:, bounds[i] : bounds[i + 1]] for i in range(3))
    mine = mine.reshape(layers, per_device // fold, fold, 2 * LANES)
    mine = jnp.swapaxes(mine, 1, 2).reshape(layers, per_device, 2 * LANES)
    feature = mine[:, :norm_device, spare : spare + experts + 2]
    fields = jnp.swapaxes(mine, 1, 2)
    bounds = [0]
    for count in (rank + 2 * states, rank, states, taps, 1, 1, 1):
        bounds.append(bounds[-1] + count)
    fields = [fields[:, bounds[i] : bounds[i + 1]] for i in range(7)]
    shared = (
        feature[:, :, experts],
        jnp.swapaxes(grad_in, 1, 2),
        fields[3],
        fields[4][:, 0],
        mine[:, :, : bounds[1]],
        fields[1],
        fields[5][:, 0],
        fields[2],
        fields[6][:, 0],
        grad_out,
        feature[:, :, experts + 1],
        feature[:, :, :experts],
    )
    output_grad = to_tokens(cube(grad))[None]
    return (output, output_grad, *shared, up_grads, down_grads)


def solution(mesh):
    both = ("wide", "narrow")
    placed = (
        P("narrow", "wide", None),
        P("narrow", "wide"),
        P(None, "narrow", "wide"),
        P(None, "narrow", "wide"),
    ) + (P(),) * 12 + (
        P(None, "narrow", None, "wide"),
        P(None, "narrow", "wide", None),
        P("narrow", "wide", None),
    )
    return jax.shard_map(
        on_device,
        mesh=mesh,
        in_specs=placed,
        out_specs=(
            P("narrow", "wide", None),
            P("narrow", "wide", None),
            P(None, both),
            P(None, None, both),
            P(None, None, both),
            P(None, both),
            P(None, both, None),
            P(None, None, both),
            P(None, both),
            P(None, None, both),
            P(None, both),
            P(None, both, None),
            P(None, both),
            P(None, both, None),
            P(None, "narrow", None, "wide"),
            P(None, "narrow", "wide", None),
        ),
        check_vma=False,
    )
```

```python
import functools

import jax
import jax.numpy as jnp
from jax import lax
from jax.experimental import pallas as pl
from jax.experimental.pallas import tpu as pltpu
from jax.sharding import PartitionSpec as P

EPS = 1e-05
CHUNKS = 8
LANES = 128
LOG2E = 1.4426950408889634
RESET = 1e9
MIB = 1024 * 1024
MESH = pl.DeviceIdType.MESH
VMEM = pltpu.VMEM


def to_steps(values):
    steps = values.shape[0] // CHUNKS
    return jnp.swapaxes(values.reshape((CHUNKS, steps) + values.shape[1:]), 0, 1)


def to_tokens(values):
    moved = jnp.swapaxes(values, 0, 1)
    return moved.reshape((-1,) + values.shape[2:])


def rms_scale(values, gain):
    return values * lax.rsqrt(jnp.mean(values * values, axis=-1, keepdims=True) + EPS) * gain


def rms_back(values, gain, grad):
    scale = lax.rsqrt(jnp.mean(values * values, axis=-1, keepdims=True) + EPS)
    weighted = grad * gain
    inner = jnp.mean(weighted * values, axis=-1, keepdims=True)
    return (
        scale * weighted - values * (scale * scale * scale) * inner,
        jnp.sum(grad * values * scale, axis=0),
    )


def dot_nn(left, right):
    return lax.dot_general(left, right, (((1,), (0,)), ((), ())), preferred_element_type=jnp.float32)


def dot_nt(left, right):
    return lax.dot_general(left, right, (((1,), (1,)), ((), ())), preferred_element_type=jnp.float32)


def dot_tn(left, right):
    return lax.dot_general(left, right, (((0,), (0,)), ((), ())), preferred_element_type=jnp.float32)


def passed_along(x, by):
    size = lax.axis_size("wide")
    return lax.ppermute(x, "wide", [(i, i + by) for i in range(size) if 0 <= i + by < size])


def with_rim(values, rim):
    count = rim.shape[0]
    tail = values[values.shape[0] - count :, : CHUNKS - 1]
    return jnp.concatenate([jnp.concatenate([rim[:, None], tail], axis=1), values], axis=0)


def keep_masks(starts, taps):
    extended = with_rim(starts[..., None], jnp.zeros((taps - 1, 1), jnp.float32))
    steps = starts.shape[0]
    alive = jnp.ones(starts.shape + (1,), jnp.float32)
    masks = []
    for offset in range(1, taps):
        back = taps - offset
        alive = alive * (1.0 - extended[back : back + steps])
        masks.append(alive)
    return jnp.broadcast_to(jnp.stack(masks), (taps - 1,) + starts.shape + (LANES,))


def rim_keep(starts, count):
    tail = 1.0 - starts[starts.shape[0] - count :, CHUNKS - 1]
    later = jnp.cumprod(tail[::-1])[::-1]
    return jnp.concatenate([later[1:], jnp.ones((1,), jnp.float32)])


def microseconds(count):
    return pl.CostEstimate(flops=int(count * 1.5e8), transcendentals=0, bytes_accessed=10000)


def plain_call(kernel, grid, in_specs, out_specs, out_shapes, scratch, args, cost):
    return pl.pallas_call(
        kernel,
        grid=grid,
        in_specs=in_specs,
        out_specs=out_specs,
        out_shape=out_shapes,
        scratch_shapes=scratch,
        compiler_params=pltpu.CompilerParams(
            dimension_semantics=("arbitrary",), vmem_limit_bytes=60 * MIB
        ),
        cost_estimate=microseconds(cost),
    )(*args)


def shaped(shape, kind=jnp.float32):
    return jax.ShapeDtypeStruct(shape, kind)


def slab(steps, first=0):
    return pl.BlockSpec((steps, CHUNKS, LANES), lambda c: (0, 0, first + c))


def rows_of(count):
    return pl.BlockSpec((count, LANES), lambda c: (0, c))


def layer_rows(layer, count):
    return pl.BlockSpec((None, count, LANES), lambda c: (layer, 0, c))


def layer_columns(layer, count):
    return pl.BlockSpec((None, LANES, count), lambda c: (layer, c, 0))


def layer_whole(layer, shape):
    return pl.BlockSpec((None,) + shape, lambda c: (layer,) + (0,) * len(shape))


def whole(shape):
    return pl.BlockSpec(shape, lambda c: (0,) * len(shape))


ANYWHERE = pl.BlockSpec(memory_space=pl.ANY)


def spread_columns(selection_ref, first, states, out_ref):
    def one(step, carry):
        tile = selection_ref[step]
        for n in range(states):
            out_ref[step, n] = jnp.broadcast_to(tile[:, first + n : first + n + 1], (CHUNKS, LANES))
        return carry

    lax.fori_loop(0, selection_ref.shape[0], one, 0, unroll=8)


def rate_rows(rate):
    return [jnp.broadcast_to(rate[n : n + 1, :], (CHUNKS, LANES)) for n in range(rate.shape[0])]


def rates_of(decay_log):
    return -jnp.exp(decay_log) * LOG2E


def two_steps(ref, pair, lanes=slice(None)):
    both = ref[pl.ds(pl.multiple_of(pair * 2 * CHUNKS, 2 * CHUNKS), 2 * CHUNKS), lanes]
    both = both.astype(jnp.float32)
    return both[:CHUNKS], both[CHUNKS:]


def chunk_links(found, sizes, rates, reverse):
    place = lax.broadcasted_iota(jnp.int32, (CHUNKS, LANES), 0)
    if reverse:
        place = CHUNKS - 1 - place
    last = 0 if reverse else CHUNKS - 1

    def shifted(values, by):
        turned = pltpu.roll(values, CHUNKS - by if reverse else by, axis=0)
        return jnp.where(place >= by, turned, 0.0)

    lengths = [sizes]
    for by in (1, 2, 4):
        lengths.append(lengths[-1] + shifted(lengths[-1], by))
    links, totals = [], []
    for n, rate in enumerate(rates):
        level = found[n]
        for index, by in enumerate((1, 2, 4)):
            level = level + jnp.exp2(lengths[index] * rate) * shifted(level, by)
        links.append(shifted(level, 1))
        totals.append(level[last : last + 1])
    return links, totals, shifted(lengths[-1], 1), lengths[-1][last : last + 1]


def conv_slab(extended, step, mask_ref, kernel_ref, bias, taps):
    total = bias + kernel_ref[0:1, :] * extended[step + taps - 1]
    tiles = total.shape[1] // LANES
    for offset in range(1, taps):
        mask = mask_ref[offset - 1, step]
        mask = jnp.concatenate([mask] * tiles, axis=1) if tiles > 1 else mask
        total = total + kernel_ref[offset : offset + 1, :] * (
            extended[step + taps - 1 - offset] * mask
        )
    return total


def extend(value_ref, rim_ref, extended, taps):
    steps = value_ref.shape[0]
    place = lax.broadcasted_iota(jnp.int32, value_ref.shape[1:], 0)
    for j in range(taps - 1):
        turned = pltpu.roll(value_ref[steps - taps + 1 + j], 1, axis=0)
        extended[j] = jnp.where(place == 0, rim_ref[j : j + 1, :], turned)
    extended[taps - 1 :] = value_ref[...]


def front_kernel(dims, value_ref, rim_ref, mask_ref, reset_ref, conv_ref, conv_bias_ref, state_ref,
                 step_ref, step_bias_ref, decay_ref,
                 act_ref, selection_ref, size_ref, link_ref, link_size_ref, total_ref, total_size_ref,
                 extended, maps):
    taps, rank, states, steps, channels = dims
    extend(value_ref, rim_ref, extended, taps)
    bias = conv_bias_ref[...]

    def conv_pair(pair, carry):
        both = []
        for step in (2 * pair, 2 * pair + 1):
            both.append(jax.nn.silu(conv_slab(extended, step, mask_ref, conv_ref, bias, taps)))
        at = pl.ds(pl.multiple_of(pair * 2 * CHUNKS, 2 * CHUNKS), 2 * CHUNKS)
        act_ref[at, :] = jnp.concatenate(both, axis=0).astype(jnp.bfloat16)
        return carry

    lax.fori_loop(0, steps // 2, conv_pair, 0)
    selection = dot_nn(act_ref[...], state_ref[...])
    selection_ref[...] = selection.reshape(steps, CHUNKS, selection.shape[1])
    rank_low = selection[:, :rank].astype(jnp.bfloat16)

    def size_tile(c, carry):
        lanes = pl.ds(pl.multiple_of(c * 256, 256), 256)
        linear = dot_nn(rank_low, step_ref[:, lanes]) + step_bias_ref[:, lanes]
        size_ref[:, :, lanes] = jax.nn.softplus(linear).reshape(steps, CHUNKS, 256)
        return carry

    lax.fori_loop(0, channels // 256, size_tile, 0)
    spread_columns(selection_ref, rank, states, maps)

    def end_tile(c, carry):
        lanes = pl.ds(pl.multiple_of(c * LANES, LANES), LANES)
        rates = rate_rows(rates_of(decay_ref[:, lanes]))

        def one(pair, carry):
            levels, length = list(carry[:states]), carry[states]
            acts = two_steps(act_ref, pair, lanes)
            for half in (0, 1):
                step = 2 * pair + half
                size = size_ref[step, :, lanes]
                value = size * acts[half]
                size = size + reset_ref[step]
                for n in range(states):
                    levels[n] = jnp.exp2(size * rates[n]) * levels[n] + value * maps[step, n]
                length = length + size
            return tuple(levels) + (length,)

        zero = jnp.zeros((CHUNKS, LANES), jnp.float32)
        found = lax.fori_loop(0, steps // 2, one, (zero,) * (states + 1), unroll=2)
        links, totals, link_size, total_size = chunk_links(found, found[states], rates, False)
        link_size_ref[:, lanes] = link_size
        total_size_ref[:, lanes] = total_size
        for n in range(states):
            link_ref[n, :, lanes] = links[n]
            total_ref[n : n + 1, lanes] = totals[n]
        return carry

    lax.fori_loop(0, channels // LANES, end_tile, 0)


def mixer_front(layer, projected, rim, masks, reset, conv_weight, conv_bias, state_weight, step_weight,
                step_bias, decay_log):
    steps = projected.shape[0]
    channels = conv_weight.shape[2]
    taps, rank, states = conv_weight.shape[1], step_weight.shape[1], decay_log.shape[1]
    columns = state_weight.shape[2]
    value = pl.BlockSpec((steps, CHUNKS, channels), lambda c: (0, 0, 0))
    shapes = [
        shaped((steps * CHUNKS, channels), jnp.bfloat16),
        shaped((steps, CHUNKS, columns)),
        shaped((steps, CHUNKS, channels)),
        shaped((states, CHUNKS, channels)),
        shaped((CHUNKS, channels)),
        shaped((states, channels)),
        shaped((1, channels)),
    ]
    return plain_call(
        functools.partial(front_kernel, (taps, rank, states, steps, channels)),
        (1,),
        [value, whole(rim.shape), whole(masks.shape), whole(reset.shape),
         layer_whole(layer, conv_weight.shape[1:]), layer_whole(layer, conv_bias.shape[1:]),
         layer_whole(layer, state_weight.shape[1:]), layer_whole(layer, step_weight.shape[1:]),
         layer_whole(layer, step_bias.shape[1:]), layer_whole(layer, decay_log.shape[1:])],
        [whole(s.shape) for s in shapes],
        shapes,
        [VMEM((steps + taps - 1, CHUNKS, channels), jnp.float32),
         VMEM((steps, states, CHUNKS, LANES), jnp.float32)],
        (projected, rim, masks, reset, conv_weight, conv_bias, state_weight, step_weight, step_bias,
         decay_log),
        18,
    )


def run_kernel(dims, size_ref, act_ref, selection_ref, reset_ref, decay_ref, link_ref, link_size_ref,
               entering_ref, gate_ref, skip_ref, out_weight_ref, current_ref, norm_ref, router_ref, fill_ref,
               mixed_ref, gated_ref, begin_ref, middle_ref, routed_ref, logits_ref, outbound_ref,
               in_maps, out_maps):
    rank, states, steps, tiles = dims

    @pl.when(pl.program_id(0) == 0)
    def _():
        spread_columns(selection_ref, rank, states, in_maps)
        spread_columns(selection_ref, rank + states, states, out_maps)
        middle_ref[...] = current_ref[...]

    rates = rate_rows(rates_of(decay_ref[...]))
    link_size = link_size_ref[...]
    skip = skip_ref[...]
    begin = []
    for n in range(states):
        first = link_ref[n] + jnp.exp2(link_size * rates[n]) * entering_ref[n : n + 1, :]
        begin_ref[n] = first
        begin.append(first)

    def one(pair, carry):
        levels = list(carry)
        acts = two_steps(act_ref, pair)
        both = []
        for half in (0, 1):
            step = 2 * pair + half
            size = size_ref[step]
            value = size * acts[half]
            size = size + reset_ref[step]
            sums = [skip * acts[half], None]
            for n in range(states):
                levels[n] = jnp.exp2(size * rates[n]) * levels[n] + value * in_maps[step, n]
                term = out_maps[step, n] * levels[n]
                sums[n % 2] = term if sums[n % 2] is None else sums[n % 2] + term
            mixed = sums[0] + sums[1]
            mixed_ref[step] = mixed
            both.append(mixed * jax.nn.silu(gate_ref[step]))
        at = pl.ds(pl.multiple_of(pair * 2 * CHUNKS, 2 * CHUNKS), 2 * CHUNKS)
        gated_ref[at, :] = jnp.concatenate(both, axis=0).astype(jnp.bfloat16)
        return tuple(levels)

    lax.fori_loop(0, steps // 2, one, tuple(begin), unroll=2)
    middle_ref[...] += dot_nn(gated_ref[...], out_weight_ref[...])

    @pl.when(pl.program_id(0) == tiles - 1)
    def _():
        routed = rms_scale(middle_ref[...], norm_ref[...]).astype(jnp.bfloat16)
        routed_ref[...] = routed
        logits_ref[...] = dot_nn(routed, router_ref[...])
        outbound_ref[...] = dot_nn(fill_ref[...], routed).astype(jnp.bfloat16)


def mixer_run(layer, size, act, selection, reset, decay_log, link, link_size, entering, projected, skip_weight,
              out_weight, current, norm_expert, router, fill):
    steps, _, channels = size.shape
    tokens = steps * CHUNKS
    states, width, experts = decay_log.shape[1], current.shape[1], router.shape[2]
    rank = selection.shape[2] - 2 * states
    tiles = channels // LANES
    low = jnp.bfloat16
    maps = VMEM((steps, states, CHUNKS, LANES), jnp.float32)
    return plain_call(
        functools.partial(run_kernel, (rank, states, steps, tiles)),
        (tiles,),
        [slab(steps), rows_of(tokens), whole(selection.shape), whole(reset.shape),
         layer_rows(layer, states), slab(states), rows_of(CHUNKS), rows_of(states), slab(steps, tiles),
         layer_rows(layer, 1), layer_columns(layer, width), whole(current.shape),
         layer_whole(layer, (1, width)), layer_whole(layer, (width, experts)), whole(fill.shape)],
        [slab(steps), rows_of(tokens), slab(states), whole((tokens, width)), whole((tokens, width)),
         whole((tokens, experts)), whole((fill.shape[0], width))],
        [
            shaped((steps, CHUNKS, channels)),
            shaped((tokens, channels), low),
            shaped((states, CHUNKS, channels)),
            shaped((tokens, width)),
            shaped((tokens, width), low),
            shaped((tokens, experts)),
            shaped((fill.shape[0], width), low),
        ],
        [maps, maps],
        (size, act, selection, reset, decay_log, link, link_size, entering, projected, skip_weight, out_weight,
         current, norm_expert, router, fill),
        22,
    )


def turn_kernel(dims, grad_ref, out_weight_ref, gate_ref, mixed_ref, act_ref, gated_ref, size_ref,
                selection_ref, reset_ref, decay_ref,
                grad_y_ref, grad_gate_ref, grad_skip_ref, grad_out_ref, link_ref, link_size_ref, total_ref,
                total_size_ref, maps, held):
    rank, states, steps = dims

    @pl.when(pl.program_id(0) == 0)
    def _():
        spread_columns(selection_ref, rank + states, states, maps)

    grad = grad_ref[...]
    grad_out_ref[...] = dot_tn(gated_ref[...], grad).astype(jnp.bfloat16)
    held[...] = dot_nt(grad, out_weight_ref[...]).reshape(steps, CHUNKS, LANES)
    rates = rate_rows(rates_of(decay_ref[...]))

    def one(at, carry):
        levels, length, skip = list(carry[:states]), carry[states], carry[states + 1]
        pair = steps // 2 - 1 - at
        acts = two_steps(act_ref, pair)
        both = [None, None]
        for half in (1, 0):
            step = 2 * pair + half
            gate = gate_ref[step]
            share = jax.nn.sigmoid(gate)
            gated = held[step]
            grad_y = gated * (gate * share)
            both[half] = gated * mixed_ref[step] * (share * (1.0 + gate * (1.0 - share)))
            grad_y_ref[step] = grad_y
            skip = skip + grad_y * acts[half]
            size = size_ref[step] + reset_ref[step]
            for n in range(states):
                levels[n] = jnp.exp2(size * rates[n]) * (levels[n] + grad_y * maps[step, n])
            length = length + size
        rows = pl.ds(pl.multiple_of(pair * 2 * CHUNKS, 2 * CHUNKS), 2 * CHUNKS)
        grad_gate_ref[rows, :] = jnp.concatenate(both, axis=0).astype(jnp.bfloat16)
        return tuple(levels) + (length, skip)

    zero = jnp.zeros((CHUNKS, LANES), jnp.float32)
    found = lax.fori_loop(0, steps // 2, one, (zero,) * (states + 2), unroll=2)
    grad_skip_ref[...] = jnp.sum(found[states + 1], axis=0, keepdims=True)
    links, totals, link_size, total_size = chunk_links(found, found[states], rates, True)
    link_size_ref[...] = link_size
    total_size_ref[...] = total_size
    for n in range(states):
        link_ref[n] = links[n]
        total_ref[n : n + 1, :] = totals[n]


def mixer_turn(layer, grad_low, out_weight, projected, mixed, act, gated, size, selection, reset, decay_log):
    steps, _, channels = size.shape
    tokens = steps * CHUNKS
    states, width = decay_log.shape[1], grad_low.shape[1]
    rank = selection.shape[2] - 2 * states
    tiles = channels // LANES
    low = jnp.bfloat16
    return plain_call(
        functools.partial(turn_kernel, (rank, states, steps)),
        (tiles,),
        [whole(grad_low.shape), layer_columns(layer, width), slab(steps, tiles), slab(steps), rows_of(tokens),
         rows_of(tokens), slab(steps), whole(selection.shape), whole(reset.shape), layer_rows(layer, states)],
        [slab(steps), rows_of(tokens), rows_of(1), pl.BlockSpec((LANES, width), lambda c: (c, 0)),
         slab(states), rows_of(CHUNKS), rows_of(states), rows_of(1)],
        [
            shaped((steps, CHUNKS, channels)),
            shaped((tokens, channels), low),
            shaped((1, channels)),
            shaped((channels, width), low),
            shaped((states, CHUNKS, channels)),
            shaped((CHUNKS, channels)),
            shaped((states, channels)),
            shaped((1, channels)),
        ],
        [VMEM((steps, states, CHUNKS, LANES), jnp.float32), VMEM((steps, CHUNKS, LANES), jnp.float32)],
        (grad_low, out_weight, projected, mixed, act, gated, size, selection, reset, decay_log),
        14,
    )


def back_kernel(dims, size_ref, act_ref, grad_ref, decay_ref, selection_ref, reset_ref, begin_ref, link_ref,
                link_size_ref, entering_ref, step_ref, step_bias_ref, skip_ref,
                grad_act_ref, grad_decay_ref, grad_bias_ref, grad_step_ref, grad_selection_ref,
                in_maps, out_maps, levels, decays, grad_in, grad_out, grad_size, grad_rate, grad_all):
    rank, states, steps, tiles = dims
    tokens = steps * CHUNKS

    @pl.when(pl.program_id(0) == 0)
    def _():
        spread_columns(selection_ref, rank, states, in_maps)
        spread_columns(selection_ref, rank + states, states, out_maps)
        grad_in[...] = jnp.zeros_like(grad_in)
        grad_out[...] = jnp.zeros_like(grad_out)

    true_rates = -jnp.exp(decay_ref[...])
    rates = rate_rows(true_rates * LOG2E)
    skip = skip_ref[...]
    begin = []
    for n in range(states):
        levels[0, n] = begin_ref[n]
        begin.append(begin_ref[n])

    def ahead(pair, carry):
        now = list(carry)
        acts = two_steps(act_ref, pair)
        for half in (0, 1):
            step = 2 * pair + half
            size = size_ref[step]
            value = size * acts[half]
            size = size + reset_ref[step]
            for n in range(states):
                decay = jnp.exp2(size * rates[n])
                decays[step, n] = decay
                now[n] = decay * now[n] + value * in_maps[step, n]
                levels[step + 1, n] = now[n]
        return tuple(now)

    lax.fori_loop(0, steps // 2, ahead, tuple(begin), unroll=2)
    link_size = link_size_ref[...]
    tail = []
    for n in range(states):
        tail.append(link_ref[n] + jnp.exp2(link_size * rates[n]) * entering_ref[n : n + 1, :])
        grad_rate[n] = jnp.zeros((CHUNKS, LANES), jnp.float32)

    def retreat(at, carry):
        passed = list(carry)
        pair = steps // 2 - 1 - at
        acts = two_steps(act_ref, pair)
        for half in (1, 0):
            step = 2 * pair + half
            plain = size_ref[step]
            act = acts[half]
            grad = grad_ref[step]
            value = plain * act
            by_rate = jnp.zeros((CHUNKS, LANES), jnp.float32)
            by_input = jnp.zeros((CHUNKS, LANES), jnp.float32)
            for n in range(states):
                lanes = slice(n * LANES, (n + 1) * LANES)
                back = out_maps[step, n] * grad + passed[n]
                grad_out[step, :, lanes] += grad * levels[step + 1, n]
                grad_in[step, :, lanes] += back * value
                by_input = by_input + back * in_maps[step, n]
                passed[n] = decays[step, n] * back
                pull = passed[n] * levels[step, n]
                by_rate = by_rate + pull * rates[n]
                grad_rate[n] += pull * plain
            grad_size[step] = by_rate * (1.0 / LOG2E) + act * by_input
            grad_act_ref[step] = plain * by_input + grad * skip
        return tuple(passed)

    lax.fori_loop(0, steps // 2, retreat, tuple(tail), unroll=2)
    for n in range(states):
        grad_decay_ref[n : n + 1, :] = (
            jnp.sum(grad_rate[n], axis=0, keepdims=True) * true_rates[n : n + 1, :]
        )
    tile = pl.program_id(0)
    grad_all[:, pl.ds(pl.multiple_of(tile * LANES, LANES), LANES)] = grad_size[...].reshape(tokens, LANES)

    @pl.when(pl.program_id(0) == tiles - 1)
    def _():
        rank_low = selection_ref[...].reshape(tokens, selection_ref.shape[2])[:, :rank].astype(jnp.bfloat16)
        linear = dot_nn(rank_low, step_ref[...]) + step_bias_ref[...]
        grad_linear = grad_all[...] * jax.nn.sigmoid(linear)
        grad_bias_ref[...] = jnp.sum(grad_linear, axis=0, keepdims=True)
        grad_low = grad_linear.astype(jnp.bfloat16)
        grad_step_ref[...] = dot_tn(rank_low, grad_low)
        grad_rank = dot_nt(grad_low, step_ref[...])
        size = states * LANES
        row = lax.broadcasted_iota(jnp.int32, (size, states), 0)
        column = lax.broadcasted_iota(jnp.int32, (size, states), 1)
        pick = ((row >= column * LANES) & (row < (column + 1) * LANES)).astype(jnp.float32)
        pick = pick.astype(jnp.bfloat16)
        found = [grad_rank]
        for ref in (grad_in, grad_out):
            full = ref[...].reshape(tokens, size)
            high = full.astype(jnp.bfloat16)
            rest = (full - high.astype(jnp.float32)).astype(jnp.bfloat16)
            found.append(dot_nn(high, pick) + dot_nn(rest, pick))
        grad_selection_ref[...] = jnp.concatenate(found, axis=1).astype(jnp.bfloat16)


def mixer_back(layer, size, act, grad_y, decay_log, selection, reset, begin, link, link_size, entering,
               step_weight, step_bias, skip_weight):
    steps, _, channels = size.shape
    tokens = steps * CHUNKS
    states = decay_log.shape[1]
    columns = selection.shape[2]
    rank = columns - 2 * states
    tiles = channels // LANES
    f32 = jnp.float32
    maps = VMEM((steps, states, CHUNKS, LANES), f32)
    return plain_call(
        functools.partial(back_kernel, (rank, states, steps, tiles)),
        (tiles,),
        [slab(steps), rows_of(tokens), slab(steps), layer_rows(layer, states), whole(selection.shape),
         whole(reset.shape), slab(states), slab(states), rows_of(CHUNKS), rows_of(states),
         layer_whole(layer, (rank, channels)), layer_whole(layer, (1, channels)), layer_rows(layer, 1)],
        [slab(steps), rows_of(states), whole((1, channels)), whole((rank, channels)),
         whole((tokens, columns))],
        [
            shaped((steps, CHUNKS, channels)),
            shaped((states, channels)),
            shaped((1, channels)),
            shaped((rank, channels)),
            shaped((tokens, columns), jnp.bfloat16),
        ],
        [maps, maps, VMEM((steps + 1, states, CHUNKS, LANES), f32), maps,
         VMEM((steps, CHUNKS, states * LANES), f32), VMEM((steps, CHUNKS, states * LANES), f32),
         VMEM((steps, CHUNKS, LANES), f32), VMEM((states, CHUNKS, LANES), f32), VMEM((tokens, channels), f32)],
        (size, act, grad_y, decay_log, selection, reset, begin, link, link_size, entering, step_weight,
         step_bias, skip_weight),
        35,
    )


def conv_back_kernel(dims, grad_act_ref, grad_selection_ref, state_ref, value_ref, rim_ref, mask_ref,
                     conv_ref, conv_bias_ref, act_ref, grad_step_ref, grad_decay_ref, grad_bias_ref,
                     grad_skip_ref, grad_value_ref, edge_ref, rim_grad_ref, channel_ref,
                     extended, passed):
    taps, states, steps = dims
    tokens = steps * CHUNKS
    extend(value_ref, rim_ref, extended, taps)
    bias = conv_bias_ref[...]
    grad_selection = grad_selection_ref[...]
    from_selection = dot_nt(grad_selection, state_ref[...]).reshape(steps, CHUNKS, LANES)
    passed[:steps] = grad_act_ref[...] + from_selection
    passed[steps:] = jnp.zeros((taps - 1, CHUNKS, LANES), jnp.float32)
    zero = jnp.zeros((CHUNKS, LANES), jnp.float32)

    def ahead(step, carry):
        convolved = conv_slab(extended, step, mask_ref, conv_ref, bias, taps)
        share = jax.nn.sigmoid(convolved)
        grad = passed[step] * (share * (1.0 + convolved * (1.0 - share)))
        passed[step] = grad
        new = [carry[0] + grad, carry[1] + grad * extended[step + taps - 1]]
        for offset in range(1, taps):
            kept = grad * mask_ref[offset - 1, step]
            new.append(carry[offset + 1] + kept * extended[step + taps - 1 - offset])
        return tuple(new)

    sums = lax.fori_loop(0, steps, ahead, (zero,) * (taps + 1), unroll=4)

    def reach(step, last):
        total = zero
        for offset in range(last):
            at = step + offset
            part = conv_ref[offset : offset + 1, :] * passed[at]
            if offset:
                part = part * mask_ref[offset - 1, at]
            total = total + part
        return total

    def back(pair, carry):
        both = [reach(2 * pair + half, taps) for half in (0, 1)]
        rows = pl.ds(pl.multiple_of(pair * 2 * CHUNKS, 2 * CHUNKS), 2 * CHUNKS)
        grad_value_ref[rows, :] = jnp.concatenate(both, axis=0).astype(jnp.bfloat16)
        return carry

    safe = (steps - taps + 1) // 2
    lax.fori_loop(0, safe, back, 0, unroll=2)
    place = lax.broadcasted_iota(jnp.int32, (CHUNKS, LANES), 0)
    ends = {}
    for j in range(taps - 1):
        before = zero
        for offset in range(taps - 1 - j, taps):
            at = j - taps + 1 + offset
            before = before + conv_ref[offset : offset + 1, :] * (
                passed[at] * mask_ref[offset - 1, at]
            )
        rim_grad_ref[j : j + 1, :] = before[0:1]
        ends[steps - taps + 1 + j] = jnp.where(
            place < CHUNKS - 1, pltpu.roll(before, CHUNKS - 1, axis=0), 0.0
        )
    for pair in range(safe, steps // 2):
        both = []
        for step in (2 * pair, 2 * pair + 1):
            total = reach(step, min(taps, steps - step))
            if step in ends:
                total = total + ends[step]
                j = step - steps + taps - 1
                edge_ref[j : j + 1, :] = total[CHUNKS - 1 : CHUNKS]
            both.append(total)
        grad_value_ref[2 * pair * CHUNKS : (2 * pair + 2) * CHUNKS, :] = jnp.concatenate(
            both, axis=0
        ).astype(jnp.bfloat16)
    small = jnp.zeros((CHUNKS, LANES), jnp.float32)
    rows = [jnp.sum(part, axis=0, keepdims=True) for part in sums[1:] + sums[:1]]
    rows += [grad_bias_ref[...], grad_skip_ref[...]]
    for index, row in enumerate(rows):
        small = jnp.where(place == index, row, small)
    grad_state = dot_tn(grad_selection, act_ref[...])
    parts = [grad_state, grad_step_ref[...], grad_decay_ref[...], small]
    used = sum(part.shape[0] for part in parts)
    parts.append(jnp.zeros((2 * LANES - used, LANES), jnp.float32))
    channel_ref[...] = jnp.concatenate(parts, axis=0).T.astype(jnp.bfloat16)


def mixer_conv_back(layer, grad_act, grad_selection, state_weight, projected, rim, masks, conv_weight,
                    conv_bias, act, grad_step, grad_decay, grad_bias, grad_skip):
    steps, _, channels = grad_act.shape
    tokens = steps * CHUNKS
    taps, columns = conv_weight.shape[1], state_weight.shape[2]
    states, rank = grad_decay.shape[0], grad_step.shape[0]
    tiles = channels // LANES
    f32 = jnp.float32
    return plain_call(
        functools.partial(conv_back_kernel, (taps, states, steps)),
        (tiles,),
        [slab(steps), whole(grad_selection.shape), layer_columns(layer, columns), slab(steps),
         rows_of(taps - 1), whole(masks.shape), layer_rows(layer, taps), layer_rows(layer, 1),
         rows_of(tokens), rows_of(rank), rows_of(states), rows_of(1), rows_of(1)],
        [rows_of(tokens), rows_of(taps - 1), rows_of(taps - 1),
         pl.BlockSpec((LANES, 2 * LANES), lambda c: (c, 0))],
        [
            shaped((tokens, channels), jnp.bfloat16),
            shaped((taps - 1, channels)),
            shaped((taps - 1, channels)),
            shaped((channels, 2 * LANES), jnp.bfloat16),
        ],
        [VMEM((steps + taps - 1, CHUNKS, LANES), f32), VMEM((steps + taps - 1, CHUNKS, LANES), f32)],
        (grad_act, grad_selection, state_weight, projected, rim, masks, conv_weight, conv_bias, act, grad_step,
         grad_decay, grad_bias, grad_skip),
        10,
    )


def link_kernel(layer, count, reverse, total_ref, size_ref, decay_ref, out_ref,
                mine, mine_length, near, near_length, both, both_length, far, far_length,
                send, recv, send_length, recv_length):
    here = lax.axis_index("wide")
    group = lax.axis_index("narrow")
    pairs = count // 2
    pair, side = here // 2, lax.rem(here, 2)
    partner = here + 1 - 2 * side
    others = [lax.rem(pair + k, pairs) for k in range(1, pairs)]
    f32 = jnp.float32
    barrier = pltpu.get_barrier_semaphore()
    pl.semaphore_signal(barrier, inc=1, device_id=(partner, group), device_id_type=MESH)
    for other in others:
        pl.semaphore_signal(barrier, inc=1, device_id=(2 * other + side, group), device_id_type=MESH)
    mine[...] = total_ref[...].astype(mine.dtype)
    mine_length[...] = size_ref[...]
    rate = rates_of(decay_ref[layer])
    pl.semaphore_wait(barrier, pairs)

    def hand(index, source, source_length, target, target_length, window):
        copies = []
        for src, dst, out, back in (
            (source, target, send, recv), (source_length, target_length, send_length, recv_length)):
            copies.append(pltpu.make_async_remote_copy(
                src_ref=src, dst_ref=dst, send_sem=out.at[index], recv_sem=back.at[index],
                device_id=(window, group), device_id_type=MESH))
            copies[-1].start()
        return copies

    first = hand(0, mine, mine_length, near, near_length, partner)
    for copy in first:
        copy.wait_recv()
    second_here = (side == 0) if reverse else (side == 1)
    own, own_length = total_ref[...], size_ref[...]
    met, met_length = near[...].astype(f32), near_length[...]
    late_length = jnp.where(second_here, own_length, met_length)
    early = jnp.where(second_here, met, own)
    late = jnp.where(second_here, own, met)
    both[...] = (jnp.exp2(late_length * rate) * early + late).astype(both.dtype)
    both_length[...] = own_length + met_length
    sent = []
    for k, other in enumerate(others):
        sent.append(hand(
            1 + k, both, both_length, far.at[pair], far_length.at[pair], 2 * other + side))
    for copies in sent:
        for copy in copies:
            copy.wait_recv()
    level = jnp.zeros(own.shape, f32)
    for at in range(pairs - 1, -1, -1) if reverse else range(pairs):
        valid = (pair < at) if reverse else (pair > at)
        step = jnp.exp2(far_length[at] * rate) * level + far[at].astype(f32)
        level = jnp.where(valid, step, level)
    step = jnp.exp2(met_length * rate) * level + met
    out_ref[...] = jnp.where(second_here, step, level)
    for copies in [first] + sent:
        for copy in copies:
            copy.wait_send()


def handed_on(layer, total, size, decay_log, reverse, identity):
    count = lax.axis_size("wide")
    pairs = count // 2
    states, channels = total.shape
    f32, low = jnp.float32, jnp.bfloat16
    dma = pltpu.SemaphoreType.DMA((pairs,))
    return pl.pallas_call(
        functools.partial(link_kernel, layer, count, reverse),
        out_shape=jax.ShapeDtypeStruct((states, channels), f32),
        in_specs=[pl.BlockSpec(memory_space=VMEM)] * 3,
        out_specs=pl.BlockSpec(memory_space=VMEM),
        scratch_shapes=[
            VMEM((states, channels), low),
            VMEM((1, channels), f32),
            VMEM((states, channels), low),
            VMEM((1, channels), f32),
            VMEM((states, channels), low),
            VMEM((1, channels), f32),
            VMEM((pairs, states, channels), low),
            VMEM((pairs, 1, channels), f32),
            dma, dma, dma, dma,
        ],
        compiler_params=pltpu.CompilerParams(
            collective_id=identity, has_side_effects=True, vmem_limit_bytes=60 * MIB
        ),
        cost_estimate=microseconds(12),
    )(total, size, decay_log)


def bell(values):
    return 0.5 * (1.0 + lax.erf(values * 0.7071067811865476))


def expert_kernel(dims, backward, *refs):
    count, groups, members, block, share, width, hidden = dims
    folded = folds(width, hidden)
    out_ref, perm_ref, *refs = refs
    weight_refs, refs = (refs[:1], refs[1:]) if folded else (refs[:2], refs[2:])
    if backward:
        pre_hbm, ret_ref, rows_hbm, low_hbm, *scratch = refs
    else:
        ret_ref, rows_hbm, pre_hbm, low_hbm, *scratch = refs
    (arrived, own, rows, pre, low, part, got, final, landed, up, down, total,
     there_send, there_recv, row_send, row_recv, sum_send, sum_recv, back_send, back_recv, local) = scratch
    f32, bf16 = jnp.float32, jnp.bfloat16
    here = lax.axis_index("wide")
    group = lax.axis_index("narrow")
    quads = count // members
    quad, member = here // members, lax.rem(here, members)
    peers = [lax.rem(group + k, groups) for k in range(1, groups)]

    fold = max(folded, 1)
    loads = [pltpu.make_async_copy(weight_refs[0].at[:, pl.ds(0, width)], up, local.at[0])]
    for f in range(folded):
        loads.append(pltpu.make_async_copy(
            weight_refs[0].at[:, pl.ds(width + f * hidden, hidden)],
            down.at[:, :, pl.ds(f * hidden, hidden)], local.at[1 + f]))
    if not folded:
        loads.append(pltpu.make_async_copy(weight_refs[1], down, local.at[1]))
    if backward:
        loads.append(pltpu.make_async_copy(pre_hbm, pre, local.at[1 + fold]))
    for load in loads:
        load.start()

    def window_at(away, turn):
        return lax.rem(quad + away, quads) * members + lax.rem(member + turn, members)

    barrier = pltpu.get_barrier_semaphore()
    for peer in peers:
        pl.semaphore_signal(barrier, inc=1, device_id=(here, peer), device_id_type=MESH)
    for away in range(quads):
        for turn in range(members):
            if away or turn:
                pl.semaphore_signal(
                    barrier, inc=1, device_id=(window_at(away, turn), group), device_id_type=MESH)
    pl.semaphore_wait(barrier, groups - 1 + count - 1)

    there = []
    for k, peer in enumerate(peers):
        there.append(pltpu.make_async_remote_copy(
            src_ref=out_ref.at[peer], dst_ref=arrived.at[group], send_sem=there_send.at[k],
            recv_sem=there_recv.at[k], device_id=(here, peer), device_id_type=MESH))
        there[-1].start()
    arrived[group] = out_ref[group]
    for copy in there:
        copy.wait_recv()
    flat = arrived[...].reshape(groups * block, width)
    own[...] = dot_nn(perm_ref[...], flat).astype(bf16).reshape(members, share, width)

    def span(window):
        return pl.ds(pl.multiple_of(window * share, 16), share)

    sent = []

    def carry(away, turn):
        window = window_at(away, turn)
        copy = pltpu.make_async_remote_copy(
            src_ref=own.at[lax.rem(member + turn, members)], dst_ref=rows.at[span(here), :],
            send_sem=row_send.at[away, turn], recv_sem=row_recv.at[away, turn],
            device_id=(window, group), device_id_type=MESH)
        copy.start()
        sent.append(copy)

    for turn in range(members):
        for away in list(range(1, quads)) + [0]:
            if away or turn:
                carry(away, turn)
    rows[span(here), :] = own[member]

    def arrive(away, turn):
        window = lax.rem(quad + quads - away, quads) * members + lax.rem(member + members - turn, members)
        pltpu.make_async_remote_copy(
            src_ref=own.at[member], dst_ref=rows.at[span(window), :],
            send_sem=row_send.at[away, turn], recv_sem=row_recv.at[away, turn],
            device_id=(window, group), device_id_type=MESH).wait_recv()
        return window

    def compute(windows):
        size = len(windows) * share

        def one(s, carry):
            x = jnp.concatenate([rows[span(w), :] for w in windows], axis=0)
            if backward:
                grad_hidden = dot_nt(x, down[s])
                before = jnp.concatenate([pre[s, span(w), :] for w in windows], axis=0)
                slope = bell(before) + before * (0.3989422804014327 * jnp.exp(-0.5 * before * before))
                middle = (grad_hidden * slope).astype(bf16)
                y = dot_nt(middle, up[s])
            else:
                before = dot_nn(x, up[s])
                middle = (before * bell(before)).astype(bf16)
                y = dot_nn(middle, down[s])
            for index, w in enumerate(windows):
                piece = slice(index * share, (index + 1) * share)
                if not backward:
                    pre[s, span(w), :] = before[piece]
                low[s, span(w), :] = middle[piece]

            @pl.when(s == 0)
            def _():
                total[:size] = y

            @pl.when(s > 0)
            def _():
                total[:size] += y

            return carry

        lax.fori_loop(0, members, one, 0)
        for index, w in enumerate(windows):
            part[w] = total[index * share : (index + 1) * share].astype(bf16)

    def give_back(away, turn, window):
        copy = pltpu.make_async_remote_copy(
            src_ref=part.at[window], dst_ref=got.at[here],
            send_sem=sum_send.at[away, turn], recv_sem=sum_recv.at[away, turn],
            device_id=(window, group), device_id_type=MESH)
        copy.start()
        sent.append(copy)

    for load in loads:
        load.wait()
    windows = [here] + [arrive(0, turn) for turn in range(1, members)]
    compute(windows)
    for turn in range(1, members):
        give_back(0, turn, windows[turn])
    got[here] = part[here]
    for away in range(1, quads):
        for first in range(0, members, 2):
            windows = [arrive(away, turn) for turn in (first, first + 1)]
            compute(windows)
            for turn in (first, first + 1):
                give_back(away, turn, windows[turn - first])

    saves = [
        pltpu.make_async_copy(rows, rows_hbm, local.at[2 + fold]),
        pltpu.make_async_copy(low, low_hbm, local.at[3 + fold]),
    ]
    if not backward:
        saves.append(pltpu.make_async_copy(pre, pre_hbm, local.at[1 + fold]))
    for save in saves:
        save.start()

    for away in range(quads):
        for turn in range(members):
            if away or turn:
                window = window_at(away, turn)
                pltpu.make_async_remote_copy(
                    src_ref=part.at[here], dst_ref=got.at[window],
                    send_sem=sum_send.at[away, turn], recv_sem=sum_recv.at[away, turn],
                    device_id=(window, group), device_id_type=MESH).wait_recv()
    summed = got[pl.ds(0, members)].astype(f32)
    for q in range(1, quads):
        summed = summed + got[pl.ds(q * members, members)].astype(f32)
    packed = summed.astype(bf16).reshape(members * share, width)
    final[...] = dot_tn(perm_ref[...], packed).astype(bf16).reshape(groups, block, width)

    home = []
    for k, peer in enumerate(peers):
        home.append(pltpu.make_async_remote_copy(
            src_ref=final.at[peer], dst_ref=landed.at[group], send_sem=back_send.at[k],
            recv_sem=back_recv.at[k], device_id=(here, peer), device_id_type=MESH))
        home[-1].start()
    ret_ref[group] = final[group]
    for copy in home:
        copy.wait_recv()
    for k in range(1, groups):
        source = lax.rem(group + groups - k, groups)
        ret_ref[source] = landed[source]
    for copy in there + sent + home:
        copy.wait_send()
    for save in saves:
        save.wait()


def expert_pass(outbound, perm, weights, pre, identity):
    count, groups = lax.axis_size("wide"), lax.axis_size("narrow")
    backward = pre is not None
    _, block, width = outbound.shape
    members, _, hidden = weights[0].shape
    share = perm.shape[0] // members
    quads = count // members
    total = count * share
    low, f32 = jnp.bfloat16, jnp.float32
    dims = (count, groups, members, block, share, width, hidden)
    inside = pl.BlockSpec(memory_space=VMEM)
    args = (outbound, perm) + tuple(weights) + ((pre,) if backward else ())
    outs = [shaped((groups, block, width), low), shaped((total, width), low)]
    outs += ([] if backward else [shaped((members, total, hidden))]) + [shaped((members, total, hidden), low)]
    dma = pltpu.SemaphoreType.DMA
    return pl.pallas_call(
        functools.partial(expert_kernel, dims, backward),
        out_shape=outs,
        in_specs=[inside, inside] + [ANYWHERE] * (len(args) - 2),
        out_specs=[inside] + [ANYWHERE] * (len(outs) - 1),
        scratch_shapes=[
            VMEM((groups, block, width), low),
            VMEM((members, share, width), low),
            VMEM((total, width), low),
            VMEM((members, total, hidden), f32),
            VMEM((members, total, hidden), low),
            VMEM((count, share, width), low),
            VMEM((count, share, width), low),
            VMEM((groups, block, width), low),
            VMEM((groups, block, width), low),
            VMEM((members, width, hidden), low),
            VMEM((members, hidden, width), low),
            VMEM((members * share, width), f32),
            dma((groups - 1,)), dma((groups - 1,)),
            dma((quads, members)), dma((quads, members)),
            dma((quads, members)), dma((quads, members)),
            dma((groups - 1,)), dma((groups - 1,)),
            dma((4 + max(folds(width, hidden), 1),)),
        ],
        compiler_params=pltpu.CompilerParams(
            collective_id=identity, has_side_effects=True, vmem_limit_bytes=60 * MIB
        ),
        cost_estimate=microseconds(65),
    )(*args)


def expert_order(experts, groups, block, capacity):
    share = groups * capacity
    row = jnp.arange(experts * share, dtype=jnp.int32)
    expert, rest = row // share, row % share
    source = (rest // capacity) * block + expert * capacity + rest % capacity
    return (source[:, None] == jnp.arange(groups * block, dtype=jnp.int32)[None, :]).astype(jnp.bfloat16)


def between_members(arrays):
    count, members = lax.axis_size("wide"), arrays[0].shape[0]
    quads = [list(range(first, first + members)) for first in range(0, count, members)]
    return [
        lax.all_to_all(values, "wide", split_axis=0, concat_axis=0, tiled=True, axis_index_groups=quads)
        for values in arrays
    ]


def folds(width, hidden):
    return 0 if hidden % LANES else width // hidden


def pack_kernel(up_ref, down_ref, out_ref):
    width, hidden = up_ref.shape
    out_ref[:width] = up_ref[...]
    for f in range(width // hidden):
        out_ref[width + f * hidden : width + (f + 1) * hidden] = down_ref[:, f * hidden : (f + 1) * hidden]


def packed_weights(layer, up, down):
    _, experts, width, hidden = up.shape
    if not folds(width, hidden):
        return [up[layer], down[layer]]
    return [plain_call(
        pack_kernel,
        (experts,),
        [pl.BlockSpec((None, None, width, hidden), lambda e: (layer, e, 0, 0)),
         pl.BlockSpec((None, None, hidden, width), lambda e: (layer, e, 0, 0))],
        pl.BlockSpec((None, 2 * width, hidden), lambda e: (e, 0, 0)),
        shaped((experts, 2 * width, hidden), up.dtype),
        [],
        (up, down),
        4,
    )]


def weights_kernel(rows_ref, pre_ref, hidden_ref, grad_ref, *out_refs):
    width, hidden = rows_ref.shape[1], pre_ref.shape[1]
    low = jnp.bfloat16
    up = dot_tn(rows_ref[...], pre_ref[...]).astype(low)
    down = dot_tn(hidden_ref[...], grad_ref[...]).astype(low)
    if len(out_refs) == 2:
        out_refs[0][...], out_refs[1][...] = up, down
        return
    out_refs[0][:width] = up
    for f in range(width // hidden):
        out_refs[0][width + f * hidden : width + (f + 1) * hidden] = down[:, f * hidden : (f + 1) * hidden]


def expert_weights(rows, pre, hidden_rows, grad_rows):
    total, width = rows.shape
    members, _, hidden = pre.shape
    slices = pl.BlockSpec((None, total, hidden), lambda s: (s, 0, 0))
    sizes = [(2 * width, hidden)] if folds(width, hidden) else [(width, hidden), (hidden, width)]
    return plain_call(
        weights_kernel,
        (members,),
        [whole((total, width)), slices, slices, whole((total, width))],
        [pl.BlockSpec((None,) + size, lambda s: (s, 0, 0)) for size in sizes],
        [shaped((members,) + size, jnp.bfloat16) for size in sizes],
        [],
        (rows, pre, hidden_rows, grad_rows),
        6,
    )


def widen_kernel(experts, *refs):
    up_ref, down_ref = refs[-2:]
    refs = refs[:-2]
    width, hidden = up_ref.shape
    for layer in (0, 1):
        @pl.when(pl.program_id(0) // experts == layer)
        def _():
            if len(refs) == 4:
                up_ref[...] = refs[2 * layer][...].astype(jnp.float32)
                down_ref[...] = refs[2 * layer + 1][...].astype(jnp.float32)
                return
            up_ref[...] = refs[layer][:width].astype(jnp.float32)
            for f in range(width // hidden):
                down_ref[:, f * hidden : (f + 1) * hidden] = refs[layer][
                    width + f * hidden : width + (f + 1) * hidden].astype(jnp.float32)


def widened(first, second, width, hidden):
    experts = first[0].shape[0]
    specs = []
    for layer, arrays in enumerate((first, second)):
        for array in arrays:
            if layer == 0:
                place = lambda i: (jnp.minimum(i, experts - 1), 0, 0)
            else:
                place = lambda i: (jnp.maximum(i - experts, 0), 0, 0)
            specs.append(pl.BlockSpec((None,) + array.shape[1:], place))
    return plain_call(
        functools.partial(widen_kernel, experts),
        (2 * experts,),
        specs,
        [pl.BlockSpec((None, None, width, hidden), lambda i: (i // experts, i % experts, 0, 0)),
         pl.BlockSpec((None, None, hidden, width), lambda i: (i // experts, i % experts, 0, 0))],
        [shaped((2, experts, width, hidden)), shaped((2, experts, hidden, width))],
        [],
        tuple(first) + tuple(second),
        9,
    )


def sum_kernel(dims, *refs):
    count, lines, sizes, first_rows, width = dims
    total = len(sizes)
    arrays, out_ref = refs[:total], refs[total]
    (own, near, over, spun, spun_first, home, core_send, core_recv, load, over_send, over_recv,
     spin_send, spin_recv, spin_first_send, spin_first_recv, home_send, home_recv) = refs[total + 1 :]
    rows = sum(sizes)
    later = rows - first_rows
    here = lax.axis_index("wide")
    group = lax.axis_index("narrow")
    line, core = group // 2, lax.rem(group, 2)
    half = count // 2
    low, f32 = jnp.bfloat16, jnp.float32

    def window_of(position):
        position = lax.rem(position + 2 * count, count)
        upper = position // half
        return 2 * position * (1 - upper) + (2 * (count - 1 - position) + 1) * upper

    odd = lax.rem(here, 2)
    spot = (here // 2) * (1 - odd) + (count - 1 - here // 2) * odd
    ring = (window_of(spot + 1), window_of(spot - 1))
    peer = 2 * line + 1 - core
    lines_away = [lax.rem(line + k, lines) for k in range(1, lines)]

    barrier = pltpu.get_barrier_semaphore()
    for window in ring:
        pl.semaphore_signal(barrier, inc=1, device_id=(window, group), device_id_type=MESH)
    pl.semaphore_signal(barrier, inc=1, device_id=(here, peer), device_id_type=MESH)
    for other in lines_away:
        pl.semaphore_signal(barrier, inc=1, device_id=(here, 2 * other + core), device_id_type=MESH)
    pl.semaphore_wait(barrier, 2 + lines)

    order = [spot + half]
    for away in range(half - 1, 0, -1):
        order += [spot + away, spot - away]
    order = [window_of(position) for position in order + [spot]]
    sent, held = [], []
    for k, window in enumerate(order):
        held.append([])
        start = 0
        for i, size in enumerate(sizes):
            place = pl.ds(start, size)
            start += size
            copy = pltpu.make_async_remote_copy(
                src_ref=arrays[i].at[window, :, 1 - core], dst_ref=near.at[window, :, place],
                send_sem=core_send.at[k, i], recv_sem=core_recv.at[k, i],
                device_id=(here, peer), device_id_type=MESH)
            copy.start()
            mine = pltpu.make_async_copy(
                arrays[i].at[window, :, core], own.at[window, :, place], load.at[k, i])
            mine.start()
            sent.append(copy)
            held[-1].append((copy, mine))

    ahead, behind = pl.ds(0, first_rows), pl.ds(first_rows, later)
    cut_first = first_rows // 32 * 16
    cut_later = later // 32 * 16
    parts_first = (pl.ds(0, cut_first), pl.ds(cut_first, first_rows - cut_first))
    parts_later = (
        pl.ds(first_rows, cut_later), pl.ds(first_rows + cut_later, later - cut_later))
    parts_got = (pl.ds(0, cut_later), pl.ds(cut_later, later - cut_later))

    def meet(k):
        window = order[k]
        for copy, mine in held[k]:
            copy.wait_recv()
            mine.wait()

        def one(at, carry):
            place = pl.ds(pl.multiple_of(at * 16, 16), 16)
            for x in range(lines):
                own[window, x, place] = (
                    own[window, x, place].astype(f32) + near[window, x, place].astype(f32)
                ).astype(low)
            return carry

        lax.fori_loop(0, rows // 16, one, 0)
        for j, other in enumerate(lines_away):
            copy = pltpu.make_async_remote_copy(
                src_ref=own.at[window, other, ahead], dst_ref=over.at[j, window],
                send_sem=over_send.at[j, k], recv_sem=over_recv.at[j, k],
                device_id=(here, 2 * other + core), device_id_type=MESH)
            copy.start()
            sent.append(copy)
            crossing[k].append(copy)

    crossing = [[] for _ in order]

    def spin_later(step):
        for way, sign in ((0, 1), (1, -1)):
            window = window_of(spot + sign * (half - step))
            if step == 0:
                which, got_which = parts_later[way], parts_got[way]
            else:
                which, got_which = behind, pl.ds(0, later)
                add_which, add_got = (
                    (parts_later[way], parts_got[way]) if step == 1 else (which, got_which))
                turns[way][-1].wait_recv()
                own[window, :, add_which] = (
                    own[window, :, add_which].astype(f32)
                    + spun[way, step - 1, :, add_got].astype(f32)
                ).astype(low)
            copy = pltpu.make_async_remote_copy(
                src_ref=own.at[window, :, which], dst_ref=spun.at[way, step, :, got_which],
                send_sem=spin_send.at[way, step], recv_sem=spin_recv.at[way, step],
                device_id=(ring[way], group), device_id_type=MESH)
            copy.start()
            sent.append(copy)
            turns[way].append(copy)

    turns = ([], [])
    meet(0)
    spin_later(0)
    for step in range(1, half):
        meet(2 * step - 1)
        meet(2 * step)
        spin_later(step)
    meet(len(order) - 1)
    summed = own[here, :, behind].astype(f32)
    for way in (0, 1):
        turns[way][-1].wait_recv()
        summed = summed + spun[way, half - 1].astype(f32)
    own[here, :, behind] = summed.astype(low)
    homes = []
    for j, other in enumerate(lines_away):
        copy = pltpu.make_async_remote_copy(
            src_ref=own.at[here, other, behind], dst_ref=home.at[j],
            send_sem=home_send.at[j], recv_sem=home_recv.at[j],
            device_id=(here, 2 * other + core), device_id_type=MESH)
        copy.start()
        sent.append(copy)
        homes.append(copy)

    def cross(k):
        window = order[k]
        value = own[window, line, ahead].astype(f32)
        for j, copy in enumerate(crossing[k]):
            copy.wait_recv()
            value = value + over[j, window].astype(f32)
        return value

    first_turns = ([], [])

    def spin_first(step):
        for way, sign in ((0, 1), (1, -1)):
            k = 0 if step == 0 else 2 * step - 1 + way
            window = order[k]
            if step or way == 0:
                own[window, line, ahead] = cross(k).astype(low)
            if step == 0:
                which = parts_first[way]
            else:
                which = ahead
                add_which = parts_first[way] if step == 1 else which
                first_turns[way][-1].wait_recv()
                own[window, line, add_which] = (
                    own[window, line, add_which].astype(f32)
                    + spun_first[way, step - 1, add_which].astype(f32)
                ).astype(low)
            copy = pltpu.make_async_remote_copy(
                src_ref=own.at[window, line, which], dst_ref=spun_first.at[way, step, which],
                send_sem=spin_first_send.at[way, step], recv_sem=spin_first_recv.at[way, step],
                device_id=(ring[way], group), device_id_type=MESH)
            copy.start()
            sent.append(copy)
            first_turns[way].append(copy)

    for step in range(half):
        spin_first(step)
    summed = cross(len(order) - 1)
    for way in (0, 1):
        first_turns[way][-1].wait_recv()
        summed = summed + spun_first[way, half - 1].astype(f32)
    out_ref[ahead, :] = summed
    value = own[here, line, behind].astype(f32)
    for j, copy in enumerate(homes):
        copy.wait_recv()
        value = value + home[j].astype(f32)
    out_ref[behind, :] = value
    for copy in sent:
        copy.wait_send()


def summed_shares(arrays, identity):
    count, groups = lax.axis_size("wide"), lax.axis_size("narrow")
    lines, half = groups // 2, count // 2
    width = arrays[0].shape[2]
    if any(array.shape[1] % 16 for array in arrays):
        packed = jnp.concatenate(arrays, axis=1)
        arrays = [jnp.pad(packed, ((0, 0), (0, -packed.shape[1] % 16), (0, 0)))]
    sizes = tuple(array.shape[1] for array in arrays)
    rows = sum(sizes)
    first = max(32, rows * 11 // 20 // 16 * 16)
    later = rows - first
    low = jnp.bfloat16
    dma = pltpu.SemaphoreType.DMA
    return pl.pallas_call(
        functools.partial(sum_kernel, (count, lines, sizes, first, width)),
        out_shape=jax.ShapeDtypeStruct((rows, width), jnp.float32),
        in_specs=[ANYWHERE] * len(arrays),
        out_specs=pl.BlockSpec(memory_space=VMEM),
        scratch_shapes=[
            VMEM((count, lines, rows, width), low),
            VMEM((count, lines, rows, width), low),
            VMEM((lines - 1, count, first, width), low),
            VMEM((2, half, lines, later, width), low),
            VMEM((2, half, first, width), low),
            VMEM((lines - 1, later, width), low),
            dma((count, len(arrays))), dma((count, len(arrays))), dma((count, len(arrays))),
            dma((lines - 1, count)), dma((lines - 1, count)),
            dma((2, half)), dma((2, half)),
            dma((2, half)), dma((2, half)),
            dma((lines - 1,)), dma((lines - 1,)),
        ],
        compiler_params=pltpu.CompilerParams(
            collective_id=identity, has_side_effects=True, vmem_limit_bytes=60 * MIB
        ),
        cost_estimate=microseconds(60),
    )(*[array.reshape(count, lines, 2, array.shape[1], width) for array in arrays])


def on_device(
    hidden,
    doc_start,
    expert_choice,
    slot_index,
    norm_mix,
    in_weight,
    conv_weight,
    conv_bias,
    state_weight,
    step_weight,
    step_bias,
    decay_log,
    skip_weight,
    out_weight,
    norm_expert,
    router,
    expert_up,
    expert_down,
    cotangent,
):
    layers = in_weight.shape[0]
    tokens = hidden.shape[1]
    width = hidden.shape[2]
    inner = skip_weight.shape[1]
    rank = step_weight.shape[1]
    states = decay_log.shape[1]
    experts = router.shape[2]
    taps = conv_weight.shape[1]
    steps = tokens // CHUNKS
    both = ("wide", "narrow")
    groups = lax.axis_size("narrow")
    devices = lax.axis_size("wide") * groups
    per_group = experts // groups
    capacity = max(2, 5 * tokens // (4 * experts))
    block = -(-per_group * capacity // 16) * 16
    low, f32 = jnp.bfloat16, jnp.float32
    starts = to_steps(doc_start[0]).astype(f32)
    masks = keep_masks(starts, taps)
    keep_mask = rim_keep(starts, taps - 1)[:, None]
    reset = jnp.broadcast_to((starts * RESET)[..., None], starts.shape + (LANES,))
    order = expert_order(per_group, groups, block, capacity)
    conv_bias, step_bias, skip_weight, norm_expert = (
        values[:, None, :] for values in (conv_bias, step_bias, skip_weight, norm_expert))
    current = to_steps(hidden[0]).reshape(tokens, width).astype(f32)
    saved = []

    def cube(values):
        return values.reshape(steps, CHUNKS, values.shape[-1])

    fills, onehots, keeps = [], [], []
    for layer in range(layers):
        chosen = to_steps(expert_choice[layer, 0]).reshape(tokens)
        slot_row = to_steps(slot_index[layer, 0]).reshape(tokens)
        kept = slot_row >= 0
        place = (chosen // per_group) * block + (chosen % per_group) * capacity + slot_row
        place = jnp.where(kept, place, -1)
        fills.append(
            (place[None, :] == jnp.arange(groups * block, dtype=jnp.int32)[:, None]).astype(low))
        onehots.append((chosen[:, None] == jnp.arange(experts, dtype=jnp.int32)[None, :]).astype(f32))
        keeps.append(kept.astype(f32)[:, None])

    tail = passed_along(hidden[0, tokens - taps + 1 :] * keep_mask.astype(low), 1)
    weights = [None] * layers
    ready, tail = lax.optimization_barrier((packed_weights(0, expert_up, expert_down), tail))
    weights[0] = between_members(ready)
    for layer in range(layers):
        begin = current
        normed = rms_scale(current, norm_mix[layer]).astype(low)
        projected = cube(dot_nn(normed, in_weight[layer]))
        if layer == 0:
            before = rms_scale(tail.astype(f32), norm_mix[layer]).astype(low)
            rim = dot_nn(before, in_weight[layer, :, :inner])
        else:
            rim = passed_along(projected[steps - taps + 1 :, CHUNKS - 1, :inner] * keep_mask, 1)
        act, selection, size, link, link_size, total, total_size = mixer_front(
            layer, projected, rim, masks, reset, conv_weight, conv_bias, state_weight, step_weight, step_bias,
            decay_log)
        entering = handed_on(layer, total, total_size, decay_log, False, layer)
        if layer + 1 < layers:
            ready, entering = lax.optimization_barrier(
                (packed_weights(layer + 1, expert_up, expert_down), entering))
            weights[layer + 1] = between_members(ready)
        mixed, gated, begins, middle, routed, logits, outbound = mixer_run(
            layer, size, act, selection, reset, decay_log, link, link_size, entering, projected, skip_weight,
            out_weight, current, norm_expert, router, fills[layer])
        returned, kept_rows, pre_act, hidden_low = expert_pass(
            outbound.reshape(groups, block, width), order, weights[layer], None, 4 + layer)
        shares = jax.nn.softmax(logits, axis=-1)
        gate = jnp.sum(shares * onehots[layer], axis=1, keepdims=True)
        back_rows = dot_tn(fills[layer], returned.reshape(groups * block, width))
        current = middle + (keeps[layer] * gate) * back_rows
        saved.append(dict(
            begin=begin, normed=normed, projected=projected, rim=rim, act=act, selection=selection, size=size,
            begins=begins, mixed=mixed, gated=gated, middle=middle, routed=routed, shares=shares, gate=gate,
            kept_rows=kept_rows, pre_act=pre_act, hidden_low=hidden_low, back_rows=back_rows))
    output = to_tokens(cube(current.astype(low)))[None]
    grad = to_steps(cotangent[0]).reshape(tokens, width).astype(f32)
    packed = [None] * layers
    expert_grads = [None] * layers
    per_device = inner // devices
    norm_device = width // devices
    fold = width // (2 * LANES)
    spare = 160
    for layer in range(layers - 1, -1, -1):
        entry = saved[layer]
        fill, keep, gate = fills[layer], keeps[layer], entry["gate"]
        grad_rows_low = ((keep * gate) * grad).astype(low)
        grad_gate = keep * jnp.sum(grad * entry["back_rows"], axis=1, keepdims=True)
        outbound = dot_nn(fill, grad_rows_low).astype(low).reshape(groups, block, width)
        inbound, grad_rows, grad_pre = expert_pass(
            outbound, order, weights[layer], entry["pre_act"], 6 + layer)
        ready = expert_weights(entry["kept_rows"], grad_pre, entry["hidden_low"], grad_rows)
        grad_sent = dot_tn(fill, inbound.reshape(groups * block, width))
        grad_logits_low = ((grad_gate * gate) * (onehots[layer] - entry["shares"])).astype(low)
        grad_router = dot_tn(entry["routed"], grad_logits_low)
        grad_routed = grad_sent + dot_nt(grad_logits_low, router[layer])
        grad_middle, grad_norm_expert = rms_back(entry["middle"], norm_expert[layer], grad_routed)
        grad = grad + grad_middle
        grad_low = grad.astype(low)
        grad_y, grad_igate, grad_skip, grad_out, link, link_size, total, total_size = mixer_turn(
            layer, grad_low, out_weight, entry["projected"], entry["mixed"], entry["act"], entry["gated"],
            entry["size"], entry["selection"], reset, decay_log)
        entering = handed_on(layer, total, total_size, decay_log, True, 2 + layer)
        ready, entering = lax.optimization_barrier((ready, entering))
        expert_grads[layer] = between_members(ready)
        grad_act, grad_decay, grad_bias, grad_step, grad_selection = mixer_back(
            layer, entry["size"], entry["act"], grad_y, decay_log, entry["selection"], reset,
            entry["begins"], link, link_size, entering, step_weight, step_bias, skip_weight)
        grad_value, edge, rim_grad, channel = mixer_conv_back(
            layer, grad_act, grad_selection, state_weight, entry["projected"], entry["rim"], masks, conv_weight,
            conv_bias, entry["act"], grad_step, grad_decay, grad_bias, grad_skip)
        edge = edge + passed_along(rim_grad, -1) * keep_mask
        grad_value = cube(grad_value).at[steps - taps + 1 :, CHUNKS - 1].set(edge.astype(low))
        grad_value = grad_value.reshape(tokens, inner)
        grad_projected = jnp.concatenate([grad_value, grad_igate], axis=1)
        grad_in = dot_tn(grad_projected, entry["normed"]).astype(low)
        grad_normed = dot_nt(grad_projected, in_weight[layer])
        grad_begin, grad_norm_mix = rms_back(entry["begin"], norm_mix[layer], grad_normed)
        grad = grad + grad_begin
        feature = jnp.concatenate(
            [grad_router, grad_norm_mix[:, None], grad_norm_expert.reshape(width, 1)], axis=1)
        feature = jnp.pad(
            feature.reshape(devices, norm_device, experts + 2).astype(low),
            ((0, 0), (0, per_device - norm_device), (spare, 2 * LANES - spare - experts - 2)))
        channel = channel.reshape(devices, per_device, 2 * LANES) + feature
        channel = jnp.swapaxes(channel.reshape(devices, fold, per_device // fold, 2 * LANES), 1, 2)
        packed[layer] = [
            grad_in.reshape(devices, -1, width),
            grad_out.reshape(devices, -1, width),
            channel.reshape(devices, -1, width),
        ]
    up_grads, down_grads = widened(*expert_grads, width, expert_up.shape[3])
    sums = summed_shares([part for parts in packed for part in parts], 8)
    bounds = [0]
    for part in packed[0]:
        bounds.append(bounds[-1] + part.shape[1])
    sums = sums[: layers * bounds[-1]].reshape(layers, bounds[-1], width)
    grad_in, grad_out, mine = (sums[:, bounds[i] : bounds[i + 1]] for i in range(3))
    mine = mine.reshape(layers, per_device // fold, fold, 2 * LANES)
    mine = jnp.swapaxes(mine, 1, 2).reshape(layers, per_device, 2 * LANES)
    feature = mine[:, :norm_device, spare : spare + experts + 2]
    fields = jnp.swapaxes(mine, 1, 2)
    bounds = [0]
    for count in (rank + 2 * states, rank, states, taps, 1, 1, 1):
        bounds.append(bounds[-1] + count)
    fields = [fields[:, bounds[i] : bounds[i + 1]] for i in range(7)]
    shared = (
        feature[:, :, experts],
        jnp.swapaxes(grad_in, 1, 2),
        fields[3],
        fields[4][:, 0],
        mine[:, :, : bounds[1]],
        fields[1],
        fields[5][:, 0],
        fields[2],
        fields[6][:, 0],
        grad_out,
        feature[:, :, experts + 1],
        feature[:, :, :experts],
    )
    output_grad = to_tokens(cube(grad))[None]
    return (output, output_grad, *shared, up_grads, down_grads)


def solution(mesh):
    both = ("wide", "narrow")
    placed = (
        P("narrow", "wide", None),
        P("narrow", "wide"),
        P(None, "narrow", "wide"),
        P(None, "narrow", "wide"),
    ) + (P(),) * 12 + (
        P(None, "narrow", None, "wide"),
        P(None, "narrow", "wide", None),
        P("narrow", "wide", None),
    )
    return jax.shard_map(
        on_device,
        mesh=mesh,
        in_specs=placed,
        out_specs=(
            P("narrow", "wide", None),
            P("narrow", "wide", None),
            P(None, both),
            P(None, None, both),
            P(None, None, both),
            P(None, both),
            P(None, both, None),
            P(None, None, both),
            P(None, both),
            P(None, None, both),
            P(None, both),
            P(None, both, None),
            P(None, both),
            P(None, both, None),
            P(None, "narrow", None, "wide"),
            P(None, "narrow", "wide", None),
        ),
        check_vma=False,
    )
```

```python
import functools

import jax
import jax.numpy as jnp
from jax import lax
from jax.experimental import pallas as pl
from jax.experimental.pallas import tpu as pltpu
from jax.sharding import PartitionSpec as P

EPS = 1e-05
CHUNKS = 8
LANES = 128
LOG2E = 1.4426950408889634
RESET = 1e9
MIB = 1024 * 1024
MESH = pl.DeviceIdType.MESH
VMEM = pltpu.VMEM


def to_steps(values):
    steps = values.shape[0] // CHUNKS
    return jnp.swapaxes(values.reshape((CHUNKS, steps) + values.shape[1:]), 0, 1)


def to_tokens(values):
    moved = jnp.swapaxes(values, 0, 1)
    return moved.reshape((-1,) + values.shape[2:])


def rms_scale(values, gain):
    return values * lax.rsqrt(jnp.mean(values * values, axis=-1, keepdims=True) + EPS) * gain


def rms_back(values, gain, grad):
    scale = lax.rsqrt(jnp.mean(values * values, axis=-1, keepdims=True) + EPS)
    weighted = grad * gain
    inner = jnp.mean(weighted * values, axis=-1, keepdims=True)
    return (
        scale * weighted - values * (scale * scale * scale) * inner,
        jnp.sum(grad * values * scale, axis=0),
    )


def dot_nn(left, right):
    return lax.dot_general(left, right, (((1,), (0,)), ((), ())), preferred_element_type=jnp.float32)


def dot_nt(left, right):
    return lax.dot_general(left, right, (((1,), (1,)), ((), ())), preferred_element_type=jnp.float32)


def dot_tn(left, right):
    return lax.dot_general(left, right, (((0,), (0,)), ((), ())), preferred_element_type=jnp.float32)


def passed_along(x, by):
    size = lax.axis_size("wide")
    return lax.ppermute(x, "wide", [(i, i + by) for i in range(size) if 0 <= i + by < size])


def with_rim(values, rim):
    count = rim.shape[0]
    tail = values[values.shape[0] - count :, : CHUNKS - 1]
    return jnp.concatenate([jnp.concatenate([rim[:, None], tail], axis=1), values], axis=0)


def keep_masks(starts, taps):
    extended = with_rim(starts[..., None], jnp.zeros((taps - 1, 1), jnp.float32))
    steps = starts.shape[0]
    alive = jnp.ones(starts.shape + (1,), jnp.float32)
    masks = []
    for offset in range(1, taps):
        back = taps - offset
        alive = alive * (1.0 - extended[back : back + steps])
        masks.append(alive)
    return jnp.broadcast_to(jnp.stack(masks), (taps - 1,) + starts.shape + (LANES,))


def rim_keep(starts, count):
    tail = 1.0 - starts[starts.shape[0] - count :, CHUNKS - 1]
    later = jnp.cumprod(tail[::-1])[::-1]
    return jnp.concatenate([later[1:], jnp.ones((1,), jnp.float32)])


def microseconds(count):
    return pl.CostEstimate(flops=int(count * 1.5e8), transcendentals=0, bytes_accessed=10000)


def plain_call(kernel, grid, in_specs, out_specs, out_shapes, scratch, args, cost, aliases=None):
    return pl.pallas_call(
        kernel,
        grid=grid,
        in_specs=in_specs,
        out_specs=out_specs,
        out_shape=out_shapes,
        scratch_shapes=scratch,
        input_output_aliases=aliases or {},
        compiler_params=pltpu.CompilerParams(
            dimension_semantics=("arbitrary",), vmem_limit_bytes=60 * MIB
        ),
        cost_estimate=microseconds(cost),
    )(*args)


def shaped(shape, kind=jnp.float32):
    return jax.ShapeDtypeStruct(shape, kind)


def slab(steps, first=0):
    return pl.BlockSpec((steps, CHUNKS, LANES), lambda c: (0, 0, first + c))


def rows_of(count):
    return pl.BlockSpec((count, LANES), lambda c: (0, c))


def layer_rows(layer, count):
    return pl.BlockSpec((None, count, LANES), lambda c: (layer, 0, c))


def layer_columns(layer, count):
    return pl.BlockSpec((None, LANES, count), lambda c: (layer, c, 0))


def layer_whole(layer, shape):
    return pl.BlockSpec((None,) + shape, lambda c: (layer,) + (0,) * len(shape))


def whole(shape):
    return pl.BlockSpec(shape, lambda c: (0,) * len(shape))


ANYWHERE = pl.BlockSpec(memory_space=pl.ANY)


def spread_columns(selection_ref, first, states, out_ref):
    def one(step, carry):
        tile = selection_ref[step]
        for n in range(states):
            out_ref[step, n] = jnp.broadcast_to(tile[:, first + n : first + n + 1], (CHUNKS, LANES))
        return carry

    lax.fori_loop(0, selection_ref.shape[0], one, 0, unroll=8)


def rate_rows(rate):
    return [jnp.broadcast_to(rate[n : n + 1, :], (CHUNKS, LANES)) for n in range(rate.shape[0])]


def rates_of(decay_log):
    return -jnp.exp(decay_log) * LOG2E


def two_steps(ref, pair, lanes=slice(None)):
    both = ref[pl.ds(pl.multiple_of(pair * 2 * CHUNKS, 2 * CHUNKS), 2 * CHUNKS), lanes]
    both = both.astype(jnp.float32)
    return both[:CHUNKS], both[CHUNKS:]


def chunk_links(found, sizes, rates, reverse):
    place = lax.broadcasted_iota(jnp.int32, (CHUNKS, LANES), 0)
    if reverse:
        place = CHUNKS - 1 - place
    last = 0 if reverse else CHUNKS - 1

    def shifted(values, by):
        turned = pltpu.roll(values, CHUNKS - by if reverse else by, axis=0)
        return jnp.where(place >= by, turned, 0.0)

    lengths = [sizes]
    for by in (1, 2, 4):
        lengths.append(lengths[-1] + shifted(lengths[-1], by))
    links, totals = [], []
    for n, rate in enumerate(rates):
        level = found[n]
        for index, by in enumerate((1, 2, 4)):
            level = level + jnp.exp2(lengths[index] * rate) * shifted(level, by)
        links.append(shifted(level, 1))
        totals.append(level[last : last + 1])
    return links, totals, shifted(lengths[-1], 1), lengths[-1][last : last + 1]


def conv_slab(extended, step, mask_ref, kernel_ref, bias, taps):
    total = bias + kernel_ref[0:1, :] * extended[step + taps - 1]
    tiles = total.shape[1] // LANES
    for offset in range(1, taps):
        mask = mask_ref[offset - 1, step]
        mask = jnp.concatenate([mask] * tiles, axis=1) if tiles > 1 else mask
        total = total + kernel_ref[offset : offset + 1, :] * (
            extended[step + taps - 1 - offset] * mask
        )
    return total


def extend(value_ref, rim_ref, extended, taps):
    steps = value_ref.shape[0]
    place = lax.broadcasted_iota(jnp.int32, value_ref.shape[1:], 0)
    for j in range(taps - 1):
        turned = pltpu.roll(value_ref[steps - taps + 1 + j], 1, axis=0)
        extended[j] = jnp.where(place == 0, rim_ref[j : j + 1, :], turned)
    extended[taps - 1 :] = value_ref[...]


def front_kernel(dims, value_ref, rim_ref, mask_ref, reset_ref, conv_ref, conv_bias_ref, state_ref,
                 step_ref, step_bias_ref, decay_ref,
                 act_ref, selection_ref, size_ref, link_ref, link_size_ref, total_ref, total_size_ref,
                 extended, maps, sized, pushed):
    taps, rank, states, steps, channels = dims
    extend(value_ref, rim_ref, extended, taps)
    bias = conv_bias_ref[...]

    def conv_pair(pair, carry):
        both = []
        for step in (2 * pair, 2 * pair + 1):
            both.append(jax.nn.silu(conv_slab(extended, step, mask_ref, conv_ref, bias, taps)))
        at = pl.ds(pl.multiple_of(pair * 2 * CHUNKS, 2 * CHUNKS), 2 * CHUNKS)
        act_ref[at, :] = jnp.concatenate(both, axis=0).astype(jnp.bfloat16)
        return carry

    lax.fori_loop(0, steps // 2, conv_pair, 0)
    selection = dot_nn(act_ref[...], state_ref[...])
    selection_ref[...] = selection.reshape(steps, CHUNKS, selection.shape[1])
    rank_low = selection[:, :rank].astype(jnp.bfloat16)

    def size_tile(c, carry):
        lanes = pl.ds(pl.multiple_of(c * 256, 256), 256)
        linear = dot_nn(rank_low, step_ref[:, lanes]) + step_bias_ref[:, lanes]
        size_ref[:, :, lanes] = jax.nn.softplus(linear).reshape(steps, CHUNKS, 256)
        return carry

    lax.fori_loop(0, channels // 256, size_tile, 0)
    spread_columns(selection_ref, rank, states, maps)

    def end_tile(c, carry):
        lanes = pl.ds(pl.multiple_of(c * LANES, LANES), LANES)
        rates = rate_rows(rates_of(decay_ref[:, lanes]))
        size = size_ref[:, :, lanes]
        pushed[...] = size * act_ref[:, lanes].astype(jnp.float32).reshape(size.shape)
        sized[...] = size + reset_ref[...]

        def one(step, carry):
            size, value = sized[step], pushed[step]
            new = []
            for n in range(states):
                new.append(jnp.exp2(size * rates[n]) * carry[n] + value * maps[step, n])
            return tuple(new) + (carry[states] + size,)

        zero = jnp.zeros((CHUNKS, LANES), jnp.float32)
        found = lax.fori_loop(0, steps, one, (zero,) * (states + 1), unroll=4)
        links, totals, link_size, total_size = chunk_links(found, found[states], rates, False)
        link_size_ref[:, lanes] = link_size
        total_size_ref[:, lanes] = total_size
        for n in range(states):
            link_ref[n, :, lanes] = links[n]
            total_ref[n : n + 1, lanes] = totals[n]
        return carry

    lax.fori_loop(0, channels // LANES, end_tile, 0)


def mixer_front(layer, projected, rim, masks, reset, conv_weight, conv_bias, state_weight, step_weight,
                step_bias, decay_log):
    steps = projected.shape[0]
    channels = conv_weight.shape[2]
    taps, rank, states = conv_weight.shape[1], step_weight.shape[1], decay_log.shape[1]
    columns = state_weight.shape[2]
    value = pl.BlockSpec((steps, CHUNKS, channels), lambda c: (0, 0, 0))
    shapes = [
        shaped((steps * CHUNKS, channels), jnp.bfloat16),
        shaped((steps, CHUNKS, columns)),
        shaped((steps, CHUNKS, channels)),
        shaped((states, CHUNKS, channels)),
        shaped((CHUNKS, channels)),
        shaped((states, channels)),
        shaped((1, channels)),
    ]
    return plain_call(
        functools.partial(front_kernel, (taps, rank, states, steps, channels)),
        (1,),
        [value, whole(rim.shape), whole(masks.shape), whole(reset.shape),
         layer_whole(layer, conv_weight.shape[1:]), layer_whole(layer, conv_bias.shape[1:]),
         layer_whole(layer, state_weight.shape[1:]), layer_whole(layer, step_weight.shape[1:]),
         layer_whole(layer, step_bias.shape[1:]), layer_whole(layer, decay_log.shape[1:])],
        [whole(s.shape) for s in shapes],
        shapes,
        [VMEM((steps + taps - 1, CHUNKS, channels), jnp.float32),
         VMEM((steps, states, CHUNKS, LANES), jnp.float32),
         VMEM((steps, CHUNKS, LANES), jnp.float32), VMEM((steps, CHUNKS, LANES), jnp.float32)],
        (projected, rim, masks, reset, conv_weight, conv_bias, state_weight, step_weight, step_bias,
         decay_log),
        18,
    )


def run_kernel(dims, size_ref, act_ref, selection_ref, reset_ref, decay_ref, link_ref, link_size_ref,
               entering_ref, gate_ref, skip_ref, out_weight_ref, current_ref, norm_ref, router_ref, fill_ref,
               mixed_ref, gated_ref, begin_ref, middle_ref, routed_ref, logits_ref, outbound_ref,
               in_maps, out_maps, sized, pushed):
    rank, states, steps, tiles = dims

    @pl.when(pl.program_id(0) == 0)
    def _():
        spread_columns(selection_ref, rank, states, in_maps)
        spread_columns(selection_ref, rank + states, states, out_maps)
        middle_ref[...] = current_ref[...]

    rates = rate_rows(rates_of(decay_ref[...]))
    link_size = link_size_ref[...]
    skip = skip_ref[...]
    begin = []
    for n in range(states):
        first = link_ref[n] + jnp.exp2(link_size * rates[n]) * entering_ref[n : n + 1, :]
        begin_ref[n] = first
        begin.append(first)

    size = size_ref[...]
    act = act_ref[...].astype(jnp.float32).reshape(size.shape)
    pushed[...] = size * act
    sized[...] = size + reset_ref[...]

    def one(step, carry):
        size, value = sized[step], pushed[step]
        new = []
        sums = [None, None]
        for n in range(states):
            level = jnp.exp2(size * rates[n]) * carry[n] + value * in_maps[step, n]
            new.append(level)
            term = out_maps[step, n] * level
            sums[n % 2] = term if sums[n % 2] is None else sums[n % 2] + term
        mixed_ref[step] = sums[0] + sums[1]
        return tuple(new)

    lax.fori_loop(0, steps, one, tuple(begin), unroll=4)
    mixed = mixed_ref[...] + skip * act
    mixed_ref[...] = mixed
    gated = mixed * jax.nn.silu(gate_ref[...])
    gated_ref[...] = gated.reshape(steps * CHUNKS, LANES).astype(jnp.bfloat16)
    middle_ref[...] += dot_nn(gated_ref[...], out_weight_ref[...])

    @pl.when(pl.program_id(0) == tiles - 1)
    def _():
        routed = rms_scale(middle_ref[...], norm_ref[...]).astype(jnp.bfloat16)
        routed_ref[...] = routed
        logits_ref[...] = dot_nn(routed, router_ref[...])
        outbound_ref[...] = dot_nn(fill_ref[...], routed).astype(jnp.bfloat16)


def mixer_run(layer, size, act, selection, reset, decay_log, link, link_size, entering, projected, skip_weight,
              out_weight, current, norm_expert, router, fill):
    steps, _, channels = size.shape
    tokens = steps * CHUNKS
    states, width, experts = decay_log.shape[1], current.shape[1], router.shape[2]
    rank = selection.shape[2] - 2 * states
    tiles = channels // LANES
    low = jnp.bfloat16
    maps = VMEM((steps, states, CHUNKS, LANES), jnp.float32)
    return plain_call(
        functools.partial(run_kernel, (rank, states, steps, tiles)),
        (tiles,),
        [slab(steps), rows_of(tokens), whole(selection.shape), whole(reset.shape),
         layer_rows(layer, states), slab(states), rows_of(CHUNKS), rows_of(states), slab(steps, tiles),
         layer_rows(layer, 1), layer_columns(layer, width), whole(current.shape),
         layer_whole(layer, (1, width)), layer_whole(layer, (width, experts)), whole(fill.shape)],
        [slab(steps), rows_of(tokens), slab(states), whole((tokens, width)), whole((tokens, width)),
         whole((tokens, experts)), whole((fill.shape[0], width))],
        [
            shaped((steps, CHUNKS, channels)),
            shaped((tokens, channels), low),
            shaped((states, CHUNKS, channels)),
            shaped((tokens, width)),
            shaped((tokens, width), low),
            shaped((tokens, experts)),
            shaped((fill.shape[0], width), low),
        ],
        [maps, maps] + [VMEM((steps, CHUNKS, LANES), jnp.float32)] * 2,
        (size, act, selection, reset, decay_log, link, link_size, entering, projected, skip_weight, out_weight,
         current, norm_expert, router, fill),
        22,
    )


def turn_kernel(dims, grad_ref, out_weight_ref, gate_ref, mixed_ref, act_ref, gated_ref, size_ref,
                selection_ref, reset_ref, decay_ref,
                grad_y_ref, grad_gate_ref, grad_skip_ref, grad_out_ref, link_ref, link_size_ref, total_ref,
                total_size_ref, maps, sized):
    rank, states, steps = dims

    @pl.when(pl.program_id(0) == 0)
    def _():
        spread_columns(selection_ref, rank + states, states, maps)

    grad = grad_ref[...]
    grad_out_ref[...] = dot_tn(gated_ref[...], grad).astype(jnp.bfloat16)
    gated = dot_nt(grad, out_weight_ref[...]).reshape(steps, CHUNKS, LANES)
    gate = gate_ref[...]
    share = jax.nn.sigmoid(gate)
    grad_y = gated * (gate * share)
    grad_y_ref[...] = grad_y
    grad_gate = gated * mixed_ref[...] * (share * (1.0 + gate * (1.0 - share)))
    grad_gate_ref[...] = grad_gate.reshape(steps * CHUNKS, LANES).astype(jnp.bfloat16)
    by_skip = grad_y * act_ref[...].astype(jnp.float32).reshape(steps, CHUNKS, LANES)
    grad_skip_ref[...] = jnp.sum(jnp.sum(by_skip, axis=0), axis=0, keepdims=True)
    sized[...] = size_ref[...] + reset_ref[...]
    rates = rate_rows(rates_of(decay_ref[...]))

    def one(at, carry):
        step = steps - 1 - at
        size, grad_y = sized[step], grad_y_ref[step]
        new = []
        for n in range(states):
            new.append(jnp.exp2(size * rates[n]) * (carry[n] + grad_y * maps[step, n]))
        return tuple(new) + (carry[states] + size,)

    zero = jnp.zeros((CHUNKS, LANES), jnp.float32)
    found = lax.fori_loop(0, steps, one, (zero,) * (states + 1), unroll=4)
    links, totals, link_size, total_size = chunk_links(found, found[states], rates, True)
    link_size_ref[...] = link_size
    total_size_ref[...] = total_size
    for n in range(states):
        link_ref[n] = links[n]
        total_ref[n : n + 1, :] = totals[n]


def mixer_turn(layer, grad_low, out_weight, projected, mixed, act, gated, size, selection, reset, decay_log):
    steps, _, channels = size.shape
    tokens = steps * CHUNKS
    states, width = decay_log.shape[1], grad_low.shape[1]
    rank = selection.shape[2] - 2 * states
    tiles = channels // LANES
    low = jnp.bfloat16
    return plain_call(
        functools.partial(turn_kernel, (rank, states, steps)),
        (tiles,),
        [whole(grad_low.shape), layer_columns(layer, width), slab(steps, tiles), slab(steps), rows_of(tokens),
         rows_of(tokens), slab(steps), whole(selection.shape), whole(reset.shape), layer_rows(layer, states)],
        [slab(steps), pl.BlockSpec((tokens, LANES), lambda c: (0, tiles + c)), rows_of(1),
         pl.BlockSpec((LANES, width), lambda c: (c, 0)),
         slab(states), rows_of(CHUNKS), rows_of(states), rows_of(1)],
        [
            shaped((steps, CHUNKS, channels)),
            shaped((tokens, 2 * channels), low),
            shaped((1, channels)),
            shaped((channels, width), low),
            shaped((states, CHUNKS, channels)),
            shaped((CHUNKS, channels)),
            shaped((states, channels)),
            shaped((1, channels)),
        ],
        [VMEM((steps, states, CHUNKS, LANES), jnp.float32), VMEM((steps, CHUNKS, LANES), jnp.float32)],
        (grad_low, out_weight, projected, mixed, act, gated, size, selection, reset, decay_log),
        14,
    )


def back_kernel(dims, size_ref, act_ref, grad_ref, decay_ref, selection_ref, reset_ref, begin_ref, link_ref,
                link_size_ref, entering_ref, step_ref, step_bias_ref, skip_ref,
                grad_act_ref, grad_decay_ref, grad_bias_ref, grad_step_ref, grad_selection_ref,
                in_maps, out_maps, levels, decays, grad_in, grad_out, grad_size, grad_rate, grad_all, sized, pushed, acted):
    rank, states, steps, tiles = dims
    tokens = steps * CHUNKS

    @pl.when(pl.program_id(0) == 0)
    def _():
        spread_columns(selection_ref, rank, states, in_maps)
        spread_columns(selection_ref, rank + states, states, out_maps)
        grad_in[...] = jnp.zeros_like(grad_in)
        grad_out[...] = jnp.zeros_like(grad_out)

    true_rates = -jnp.exp(decay_ref[...])
    rates = rate_rows(true_rates * LOG2E)
    skip = skip_ref[...]
    begin = []
    for n in range(states):
        levels[0, n] = begin_ref[n]
        begin.append(begin_ref[n])

    size = size_ref[...]
    act = act_ref[...].astype(jnp.float32).reshape(size.shape)
    acted[...] = act
    pushed[...] = size * act
    sized[...] = size + reset_ref[...]

    def ahead(step, carry):
        size, value = sized[step], pushed[step]
        new = []
        for n in range(states):
            decay = jnp.exp2(size * rates[n])
            decays[step, n] = decay
            level = decay * carry[n] + value * in_maps[step, n]
            levels[step + 1, n] = level
            new.append(level)
        return tuple(new)

    lax.fori_loop(0, steps, ahead, tuple(begin), unroll=4)
    link_size = link_size_ref[...]
    tail = []
    for n in range(states):
        tail.append(link_ref[n] + jnp.exp2(link_size * rates[n]) * entering_ref[n : n + 1, :])
        grad_rate[n] = jnp.zeros((CHUNKS, LANES), jnp.float32)

    def retreat(at, carry):
        step = steps - 1 - at
        plain, act, grad, value = size_ref[step], acted[step], grad_ref[step], pushed[step]
        by_rate = jnp.zeros((CHUNKS, LANES), jnp.float32)
        by_input = jnp.zeros((CHUNKS, LANES), jnp.float32)
        new = []
        for n in range(states):
            lanes = slice(n * LANES, (n + 1) * LANES)
            back = out_maps[step, n] * grad + carry[n]
            grad_out[step, :, lanes] += grad * levels[step + 1, n]
            grad_in[step, :, lanes] += back * value
            by_input = by_input + back * in_maps[step, n]
            passed = decays[step, n] * back
            new.append(passed)
            pull = passed * levels[step, n]
            by_rate = by_rate + pull * rates[n]
            grad_rate[n] += pull * plain
        grad_size[step] = by_rate * (1.0 / LOG2E) + act * by_input
        grad_act_ref[step] = plain * by_input + grad * skip
        return tuple(new)

    lax.fori_loop(0, steps, retreat, tuple(tail), unroll=2)
    for n in range(states):
        grad_decay_ref[n : n + 1, :] = (
            jnp.sum(grad_rate[n], axis=0, keepdims=True) * true_rates[n : n + 1, :]
        )
    tile = pl.program_id(0)
    grad_all[:, pl.ds(pl.multiple_of(tile * LANES, LANES), LANES)] = grad_size[...].reshape(tokens, LANES)

    @pl.when(pl.program_id(0) == tiles - 1)
    def _():
        rank_low = selection_ref[...].reshape(tokens, selection_ref.shape[2])[:, :rank].astype(jnp.bfloat16)
        linear = dot_nn(rank_low, step_ref[...]) + step_bias_ref[...]
        grad_linear = grad_all[...] * jax.nn.sigmoid(linear)
        grad_bias_ref[...] = jnp.sum(grad_linear, axis=0, keepdims=True)
        grad_low = grad_linear.astype(jnp.bfloat16)
        grad_step_ref[...] = dot_tn(rank_low, grad_low)
        grad_rank = dot_nt(grad_low, step_ref[...])
        size = states * LANES
        row = lax.broadcasted_iota(jnp.int32, (size, states), 0)
        column = lax.broadcasted_iota(jnp.int32, (size, states), 1)
        pick = ((row >= column * LANES) & (row < (column + 1) * LANES)).astype(jnp.float32)
        pick = pick.astype(jnp.bfloat16)
        found = [grad_rank]
        for ref in (grad_in, grad_out):
            full = ref[...].reshape(tokens, size)
            high = full.astype(jnp.bfloat16)
            rest = (full - high.astype(jnp.float32)).astype(jnp.bfloat16)
            found.append(dot_nn(high, pick) + dot_nn(rest, pick))
        grad_selection_ref[...] = jnp.concatenate(found, axis=1).astype(jnp.bfloat16)


def mixer_back(layer, size, act, grad_y, decay_log, selection, reset, begin, link, link_size, entering,
               step_weight, step_bias, skip_weight):
    steps, _, channels = size.shape
    tokens = steps * CHUNKS
    states = decay_log.shape[1]
    columns = selection.shape[2]
    rank = columns - 2 * states
    tiles = channels // LANES
    f32 = jnp.float32
    maps = VMEM((steps, states, CHUNKS, LANES), f32)
    return plain_call(
        functools.partial(back_kernel, (rank, states, steps, tiles)),
        (tiles,),
        [slab(steps), rows_of(tokens), slab(steps), layer_rows(layer, states), whole(selection.shape),
         whole(reset.shape), slab(states), slab(states), rows_of(CHUNKS), rows_of(states),
         layer_whole(layer, (rank, channels)), layer_whole(layer, (1, channels)), layer_rows(layer, 1)],
        [slab(steps), rows_of(states), whole((1, channels)), whole((rank, channels)),
         whole((tokens, columns))],
        [
            shaped((steps, CHUNKS, channels)),
            shaped((states, channels)),
            shaped((1, channels)),
            shaped((rank, channels)),
            shaped((tokens, columns), jnp.bfloat16),
        ],
        [maps, maps, VMEM((steps + 1, states, CHUNKS, LANES), f32), maps,
         VMEM((steps, CHUNKS, states * LANES), f32), VMEM((steps, CHUNKS, states * LANES), f32),
         VMEM((steps, CHUNKS, LANES), f32), VMEM((states, CHUNKS, LANES), f32), VMEM((tokens, channels), f32)]
        + [VMEM((steps, CHUNKS, LANES), f32)] * 3,
        (size, act, grad_y, decay_log, selection, reset, begin, link, link_size, entering, step_weight,
         step_bias, skip_weight),
        35,
    )


def conv_back_kernel(dims, grad_act_ref, grad_selection_ref, state_ref, value_ref, rim_ref, mask_ref,
                     conv_ref, conv_bias_ref, act_ref, grad_step_ref, grad_decay_ref, grad_bias_ref,
                     grad_skip_ref, half_ref, grad_value_ref, edge_ref, rim_grad_ref, channel_ref,
                     extended, passed):
    taps, states, steps = dims
    tokens = steps * CHUNKS
    extend(value_ref, rim_ref, extended, taps)
    bias = conv_bias_ref[...]
    grad_selection = grad_selection_ref[...]
    from_selection = dot_nt(grad_selection, state_ref[...]).reshape(steps, CHUNKS, LANES)
    passed[:steps] = grad_act_ref[...] + from_selection
    passed[steps:] = jnp.zeros((taps - 1, CHUNKS, LANES), jnp.float32)
    zero = jnp.zeros((CHUNKS, LANES), jnp.float32)

    def ahead(step, carry):
        convolved = conv_slab(extended, step, mask_ref, conv_ref, bias, taps)
        share = jax.nn.sigmoid(convolved)
        grad = passed[step] * (share * (1.0 + convolved * (1.0 - share)))
        passed[step] = grad
        new = [carry[0] + grad, carry[1] + grad * extended[step + taps - 1]]
        for offset in range(1, taps):
            kept = grad * mask_ref[offset - 1, step]
            new.append(carry[offset + 1] + kept * extended[step + taps - 1 - offset])
        return tuple(new)

    sums = lax.fori_loop(0, steps, ahead, (zero,) * (taps + 1), unroll=4)

    def reach(step, last):
        total = zero
        for offset in range(last):
            at = step + offset
            part = conv_ref[offset : offset + 1, :] * passed[at]
            if offset:
                part = part * mask_ref[offset - 1, at]
            total = total + part
        return total

    def back(pair, carry):
        both = [reach(2 * pair + half, taps) for half in (0, 1)]
        rows = pl.ds(pl.multiple_of(pair * 2 * CHUNKS, 2 * CHUNKS), 2 * CHUNKS)
        grad_value_ref[rows, :] = jnp.concatenate(both, axis=0).astype(jnp.bfloat16)
        return carry

    safe = (steps - taps + 1) // 2
    lax.fori_loop(0, safe, back, 0, unroll=2)
    place = lax.broadcasted_iota(jnp.int32, (CHUNKS, LANES), 0)
    ends = {}
    for j in range(taps - 1):
        before = zero
        for offset in range(taps - 1 - j, taps):
            at = j - taps + 1 + offset
            before = before + conv_ref[offset : offset + 1, :] * (
                passed[at] * mask_ref[offset - 1, at]
            )
        rim_grad_ref[j : j + 1, :] = before[0:1]
        ends[steps - taps + 1 + j] = jnp.where(
            place < CHUNKS - 1, pltpu.roll(before, CHUNKS - 1, axis=0), 0.0
        )
    for pair in range(safe, steps // 2):
        both = []
        for step in (2 * pair, 2 * pair + 1):
            total = reach(step, min(taps, steps - step))
            if step in ends:
                total = total + ends[step]
                j = step - steps + taps - 1
                edge_ref[j : j + 1, :] = total[CHUNKS - 1 : CHUNKS]
            both.append(total)
        grad_value_ref[2 * pair * CHUNKS : (2 * pair + 2) * CHUNKS, :] = jnp.concatenate(
            both, axis=0
        ).astype(jnp.bfloat16)
    small = jnp.zeros((CHUNKS, LANES), jnp.float32)
    rows = [jnp.sum(part, axis=0, keepdims=True) for part in sums[1:] + sums[:1]]
    rows += [grad_bias_ref[...], grad_skip_ref[...]]
    for index, row in enumerate(rows):
        small = jnp.where(place == index, row, small)
    grad_state = dot_tn(grad_selection, act_ref[...])
    parts = [grad_state, grad_step_ref[...], grad_decay_ref[...], small]
    used = sum(part.shape[0] for part in parts)
    parts.append(jnp.zeros((2 * LANES - used, LANES), jnp.float32))
    channel_ref[...] = jnp.concatenate(parts, axis=0).T.astype(jnp.bfloat16)


def mixer_conv_back(layer, grad_act, grad_selection, state_weight, projected, rim, masks, conv_weight,
                    conv_bias, act, grad_step, grad_decay, grad_bias, grad_skip, halved):
    steps, _, channels = grad_act.shape
    tokens = steps * CHUNKS
    taps, columns = conv_weight.shape[1], state_weight.shape[2]
    states, rank = grad_decay.shape[0], grad_step.shape[0]
    tiles = channels // LANES
    f32 = jnp.float32
    return plain_call(
        functools.partial(conv_back_kernel, (taps, states, steps)),
        (tiles,),
        [slab(steps), whole(grad_selection.shape), layer_columns(layer, columns), slab(steps),
         rows_of(taps - 1), whole(masks.shape), layer_rows(layer, taps), layer_rows(layer, 1),
         rows_of(tokens), rows_of(rank), rows_of(states), rows_of(1), rows_of(1), ANYWHERE],
        [rows_of(tokens), rows_of(taps - 1), rows_of(taps - 1),
         pl.BlockSpec((LANES, 2 * LANES), lambda c: (c, 0))],
        [
            shaped((tokens, 2 * channels), jnp.bfloat16),
            shaped((taps - 1, channels)),
            shaped((taps - 1, channels)),
            shaped((channels, 2 * LANES), jnp.bfloat16),
        ],
        [VMEM((steps + taps - 1, CHUNKS, LANES), f32), VMEM((steps + taps - 1, CHUNKS, LANES), f32)],
        (grad_act, grad_selection, state_weight, projected, rim, masks, conv_weight, conv_bias, act, grad_step,
         grad_decay, grad_bias, grad_skip, halved),
        10,
        {13: 0},
    )


def link_kernel(layer, count, reverse, total_ref, size_ref, decay_ref, out_ref,
                mine, mine_length, near, near_length, both, both_length, far, far_length,
                send, recv, send_length, recv_length):
    here = lax.axis_index("wide")
    group = lax.axis_index("narrow")
    pairs = count // 2
    pair, side = here // 2, lax.rem(here, 2)
    partner = here + 1 - 2 * side
    others = [lax.rem(pair + k, pairs) for k in range(1, pairs)]
    f32 = jnp.float32
    barrier = pltpu.get_barrier_semaphore()
    pl.semaphore_signal(barrier, inc=1, device_id=(partner, group), device_id_type=MESH)
    for other in others:
        pl.semaphore_signal(barrier, inc=1, device_id=(2 * other + side, group), device_id_type=MESH)
    mine[...] = total_ref[...].astype(mine.dtype)
    mine_length[...] = size_ref[...]
    rate = rates_of(decay_ref[layer])
    pl.semaphore_wait(barrier, pairs)

    def hand(index, source, source_length, target, target_length, window):
        copies = []
        for src, dst, out, back in (
            (source, target, send, recv), (source_length, target_length, send_length, recv_length)):
            copies.append(pltpu.make_async_remote_copy(
                src_ref=src, dst_ref=dst, send_sem=out.at[index], recv_sem=back.at[index],
                device_id=(window, group), device_id_type=MESH))
            copies[-1].start()
        return copies

    first = hand(0, mine, mine_length, near, near_length, partner)
    for copy in first:
        copy.wait_recv()
    second_here = (side == 0) if reverse else (side == 1)
    own, own_length = total_ref[...], size_ref[...]
    met, met_length = near[...].astype(f32), near_length[...]
    late_length = jnp.where(second_here, own_length, met_length)
    early = jnp.where(second_here, met, own)
    late = jnp.where(second_here, own, met)
    both[...] = (jnp.exp2(late_length * rate) * early + late).astype(both.dtype)
    both_length[...] = own_length + met_length
    sent = []
    for k, other in enumerate(others):
        sent.append(hand(
            1 + k, both, both_length, far.at[pair], far_length.at[pair], 2 * other + side))
    for copies in sent:
        for copy in copies:
            copy.wait_recv()
    level = jnp.zeros(own.shape, f32)
    for at in range(pairs - 1, -1, -1) if reverse else range(pairs):
        valid = (pair < at) if reverse else (pair > at)
        step = jnp.exp2(far_length[at] * rate) * level + far[at].astype(f32)
        level = jnp.where(valid, step, level)
    step = jnp.exp2(met_length * rate) * level + met
    out_ref[...] = jnp.where(second_here, step, level)
    for copies in [first] + sent:
        for copy in copies:
            copy.wait_send()


def handed_on(layer, total, size, decay_log, reverse, identity):
    count = lax.axis_size("wide")
    pairs = count // 2
    states, channels = total.shape
    f32, low = jnp.float32, jnp.bfloat16
    dma = pltpu.SemaphoreType.DMA((pairs,))
    return pl.pallas_call(
        functools.partial(link_kernel, layer, count, reverse),
        out_shape=jax.ShapeDtypeStruct((states, channels), f32),
        in_specs=[pl.BlockSpec(memory_space=VMEM)] * 3,
        out_specs=pl.BlockSpec(memory_space=VMEM),
        scratch_shapes=[
            VMEM((states, channels), low),
            VMEM((1, channels), f32),
            VMEM((states, channels), low),
            VMEM((1, channels), f32),
            VMEM((states, channels), low),
            VMEM((1, channels), f32),
            VMEM((pairs, states, channels), low),
            VMEM((pairs, 1, channels), f32),
            dma, dma, dma, dma,
        ],
        compiler_params=pltpu.CompilerParams(
            collective_id=identity, has_side_effects=True, vmem_limit_bytes=60 * MIB
        ),
        cost_estimate=microseconds(12),
    )(total, size, decay_log)


def bell(values):
    return 0.5 * (1.0 + lax.erf(values * 0.7071067811865476))


def expert_kernel(dims, backward, *refs):
    count, groups, members, block, share, width, hidden = dims
    if backward:
        out_ref, perm_ref, up_hbm, down_hbm, pre_hbm, ret_ref, rows_hbm, low_hbm, *scratch = refs
    else:
        out_ref, perm_ref, up_hbm, down_hbm, ret_ref, rows_hbm, pre_hbm, low_hbm, *scratch = refs
    (arrived, own, rows, pre, low, part, got, final, landed, up, down, total,
     there_send, there_recv, row_send, row_recv, sum_send, sum_recv, back_send, back_recv, local) = scratch
    f32, bf16 = jnp.float32, jnp.bfloat16
    here = lax.axis_index("wide")
    group = lax.axis_index("narrow")
    quads = count // members
    quad, member = here // members, lax.rem(here, members)
    lines = groups // 2
    line, core = group // 2, lax.rem(group, 2)
    near_group = group + 1 - 2 * core
    others = [(2 * away + c, 2 * lax.rem(line + away, lines) + c) for away in range(1, lines) for c in (0, 1)]
    early = 2 * (share // groups) // 16 * 16
    head, tail = pl.ds(0, early), pl.ds(early, share - early)

    loads = [
        pltpu.make_async_copy(up_hbm, up, local.at[0]),
        pltpu.make_async_copy(down_hbm, down, local.at[1]),
    ]
    if backward:
        loads.append(pltpu.make_async_copy(pre_hbm, pre, local.at[2]))
    for load in loads:
        load.start()

    def window_at(away, turn):
        return lax.rem(quad + away, quads) * members + lax.rem(member + turn, members)

    barrier = pltpu.get_barrier_semaphore()
    for peer in [near_group] + [other for _, other in others]:
        pl.semaphore_signal(barrier, inc=1, device_id=(here, peer), device_id_type=MESH)
    for away in range(quads):
        for turn in range(members):
            if away or turn:
                pl.semaphore_signal(
                    barrier, inc=1, device_id=(window_at(away, turn), group), device_id_type=MESH)
    pl.semaphore_wait(barrier, groups - 1 + count - 1)

    there = []

    def hand_over(k, source, target, send, recv):
        if k:
            place, peer = others[k - 1]
            away = place // 2
            landing, signal = (lines - away) * 2 + core, 2 * away - 1 + core
        else:
            peer, landing, signal = near_group, core, 0
        copy = pltpu.make_async_remote_copy(
            src_ref=source, dst_ref=target.at[landing], send_sem=send.at[k], recv_sem=recv.at[signal],
            device_id=(here, peer), device_id_type=MESH)
        copy.start()
        return copy

    def taken(k, target, send, recv):
        pltpu.make_async_remote_copy(
            src_ref=out_ref.at[group], dst_ref=target.at[0], send_sem=send.at[k], recv_sem=recv.at[k],
            device_id=(here, near_group), device_id_type=MESH).wait_recv()

    there = [hand_over(0, out_ref.at[near_group], arrived, there_send, there_recv)]
    for k, (_, other) in enumerate(others):
        there.append(hand_over(1 + k, out_ref.at[other], arrived, there_send, there_recv))
    arrived[core] = out_ref[group]

    def span(window, part=None):
        start, size = (0, share) if part is None else ((0, early), (early, share - early))[part]
        return pl.ds(pl.multiple_of(window * share + start, 16), size)

    sent = []
    ways = [(away, turn) for turn in range(members) for away in list(range(1, quads)) + [0] if away or turn]

    def carry(away, turn, part):
        window = window_at(away, turn)
        copy = pltpu.make_async_remote_copy(
            src_ref=own.at[lax.rem(member + turn, members), (head, tail)[part]],
            dst_ref=rows.at[span(here, part), :],
            send_sem=row_send.at[away, turn, part], recv_sem=row_recv.at[away, turn, part],
            device_id=(window, group), device_id_type=MESH)
        copy.start()
        sent.append(copy)

    taken(0, arrived, there_send, there_recv)
    order = perm_ref[...].reshape(members, share, groups * block)
    first = arrived[pl.ds(0, 2)].reshape(2 * block, width)
    own[:, head] = dot_nn(
        order[:, :early, : 2 * block].reshape(members * early, 2 * block), first
    ).astype(bf16).reshape(members, early, width)
    for away, turn in ways:
        carry(away, turn, 0)
    for k in range(1, groups - 1):
        taken(k, arrived, there_send, there_recv)
    own[:, tail] = dot_nn(
        order[:, early:].reshape(members * (share - early), groups * block),
        arrived[...].reshape(groups * block, width),
    ).astype(bf16).reshape(members, share - early, width)
    for away, turn in ways:
        carry(away, turn, 1)
    rows[span(here), :] = own[member]

    def arrive(away, turn):
        window = lax.rem(quad + quads - away, quads) * members + lax.rem(member + members - turn, members)
        for part in (0, 1):
            pltpu.make_async_remote_copy(
                src_ref=own.at[member, (head, tail)[part]], dst_ref=rows.at[span(window, part), :],
                send_sem=row_send.at[away, turn, part], recv_sem=row_recv.at[away, turn, part],
                device_id=(window, group), device_id_type=MESH).wait_recv()
        return window

    def compute(windows):
        size = len(windows) * share

        def one(s, carry):
            x = jnp.concatenate([rows[span(w), :] for w in windows], axis=0)
            if backward:
                grad_hidden = dot_nt(x, down[s])
                before = jnp.concatenate([pre[s, span(w), :] for w in windows], axis=0)
                slope = bell(before) + before * (0.3989422804014327 * jnp.exp(-0.5 * before * before))
                middle = (grad_hidden * slope).astype(bf16)
                y = dot_nt(middle, up[s])
            else:
                before = dot_nn(x, up[s])
                middle = (before * bell(before)).astype(bf16)
                y = dot_nn(middle, down[s])
            for index, w in enumerate(windows):
                piece = slice(index * share, (index + 1) * share)
                if not backward:
                    pre[s, span(w), :] = before[piece]
                low[s, span(w), :] = middle[piece]

            @pl.when(s == 0)
            def _():
                total[:size] = y

            @pl.when(s > 0)
            def _():
                total[:size] += y

            return carry

        lax.fori_loop(0, members, one, 0)
        for index, w in enumerate(windows):
            part[w] = total[index * share : (index + 1) * share].astype(bf16)

    def give_back(away, turn, window, part):
        copy = pltpu.make_async_remote_copy(
            src_ref=part_rows(window, part), dst_ref=got.at[here, (head, tail)[part]],
            send_sem=sum_send.at[away, turn, part], recv_sem=sum_recv.at[away, turn, part],
            device_id=(window, group), device_id_type=MESH)
        copy.start()
        sent.append(copy)

    def part_rows(window, which):
        return part.at[window, (head, tail)[which]]

    for load in loads:
        load.wait()
    windows = [here] + [arrive(0, turn) for turn in range(1, members)]
    compute(windows)
    for which in (1, 0):
        for turn in range(1, members):
            give_back(0, turn, windows[turn], which)
    got[here] = part[here]
    late = []
    for away in range(1, quads):
        for first in range(0, members, 2):
            windows = [arrive(away, turn) for turn in (first, first + 1)]
            compute(windows)
            for turn in (first, first + 1):
                give_back(away, turn, windows[turn - first], 1)
                late.append((away, turn, windows[turn - first]))
    for away, turn, window in late:
        give_back(away, turn, window, 0)

    saves = [
        pltpu.make_async_copy(rows, rows_hbm, local.at[3]),
        pltpu.make_async_copy(low, low_hbm, local.at[4]),
    ]
    if not backward:
        saves.append(pltpu.make_async_copy(pre, pre_hbm, local.at[2]))
    for save in saves:
        save.start()

    def returned(which):
        for away, turn in ways:
            window = window_at(away, turn)
            pltpu.make_async_remote_copy(
                src_ref=part_rows(here, which), dst_ref=got.at[window, (head, tail)[which]],
                send_sem=sum_send.at[away, turn, which], recv_sem=sum_recv.at[away, turn, which],
                device_id=(window, group), device_id_type=MESH).wait_recv()
        place = (head, tail)[which]
        summed = got[pl.ds(0, members), place].astype(f32)
        for q in range(1, quads):
            summed = summed + got[pl.ds(q * members, members), place].astype(f32)
        return summed.astype(bf16)

    later = returned(1)
    rest = groups - 2
    final[pl.ds(2, rest)] = dot_tn(
        order[:, early:, 2 * block :].reshape(members * (share - early), rest * block),
        later.reshape(members * (share - early), width),
    ).astype(bf16).reshape(rest, block, width)
    home = []
    for k, (place, _) in enumerate(others):
        home.append(hand_over(1 + k, final.at[place], landed, back_send, back_recv))
    sooner = returned(0)
    final[pl.ds(0, 2)] = (
        dot_tn(order[:, :early, : 2 * block].reshape(members * early, 2 * block),
               sooner.reshape(members * early, width))
        + dot_tn(order[:, early:, : 2 * block].reshape(members * (share - early), 2 * block),
                 later.reshape(members * (share - early), width))
    ).astype(bf16).reshape(2, block, width)
    home.append(hand_over(0, final.at[1 - core], landed, back_send, back_recv))
    ret_ref[group] = final[core]
    for k in range(groups - 1):
        taken(k, landed, back_send, back_recv)
    ret_ref[near_group] = landed[1 - core]
    for place, other in others:
        ret_ref[other] = landed[place]
    for copy in there + sent + home:
        copy.wait_send()
    for save in saves:
        save.wait()


def expert_pass(outbound, perm, weights, pre, identity):
    count, groups = lax.axis_size("wide"), lax.axis_size("narrow")
    backward = pre is not None
    _, block, width = outbound.shape
    members, _, hidden = weights[0].shape
    share = perm.shape[0] // members
    quads = count // members
    total = count * share
    low, f32 = jnp.bfloat16, jnp.float32
    dims = (count, groups, members, block, share, width, hidden)
    inside = pl.BlockSpec(memory_space=VMEM)
    args = (outbound, perm) + tuple(weights) + ((pre,) if backward else ())
    outs = [shaped((groups, block, width), low), shaped((total, width), low)]
    outs += ([] if backward else [shaped((members, total, hidden))]) + [shaped((members, total, hidden), low)]
    dma = pltpu.SemaphoreType.DMA
    return pl.pallas_call(
        functools.partial(expert_kernel, dims, backward),
        out_shape=outs,
        in_specs=[inside, inside] + [ANYWHERE] * (len(args) - 2),
        out_specs=[inside] + [ANYWHERE] * (len(outs) - 1),
        scratch_shapes=[
            VMEM((groups, block, width), low),
            VMEM((members, share, width), low),
            VMEM((total, width), low),
            VMEM((members, total, hidden), f32),
            VMEM((members, total, hidden), low),
            VMEM((count, share, width), low),
            VMEM((count, share, width), low),
            VMEM((groups, block, width), low),
            VMEM((groups, block, width), low),
            VMEM((members, width, hidden), low),
            VMEM((members, hidden, width), low),
            VMEM((members * share, width), f32),
            dma((groups - 1,)), dma((groups - 1,)),
            dma((quads, members, 2)), dma((quads, members, 2)),
            dma((quads, members, 2)), dma((quads, members, 2)),
            dma((groups - 1,)), dma((groups - 1,)),
            dma((5,)),
        ],
        compiler_params=pltpu.CompilerParams(
            collective_id=identity, has_side_effects=True, vmem_limit_bytes=60 * MIB
        ),
        cost_estimate=microseconds(65),
    )(*args)


def expert_order(experts, groups, block, capacity):
    share = groups * capacity
    row = jnp.arange(experts * share, dtype=jnp.int32)
    expert, rest = row // share, row % share
    source = (rest // capacity) * block + expert * capacity + rest % capacity
    return (source[:, None] == jnp.arange(groups * block, dtype=jnp.int32)[None, :]).astype(jnp.bfloat16)


def between_members(arrays):
    count, members = lax.axis_size("wide"), arrays[0].shape[0]
    quads = [list(range(first, first + members)) for first in range(0, count, members)]
    return [
        lax.all_to_all(values, "wide", split_axis=0, concat_axis=0, tiled=True, axis_index_groups=quads)
        for values in arrays
    ]


def slice_kernel(layer, from_ref, to_ref, held, got, put):
    count = held.shape[0]
    incoming = [pltpu.make_async_copy(from_ref.at[layer, e], held.at[e], got.at[e]) for e in range(count)]
    outgoing = [pltpu.make_async_copy(held.at[e], to_ref.at[e], put.at[e]) for e in range(count)]
    for copy in incoming:
        copy.start()
    for into, out in zip(incoming, outgoing):
        into.wait()
        out.start()
    for out in outgoing:
        out.wait()


def layer_of(values, layer):
    shape = values.shape[1:]
    return pl.pallas_call(
        functools.partial(slice_kernel, layer),
        out_shape=shaped(shape, values.dtype),
        in_specs=[ANYWHERE],
        out_specs=ANYWHERE,
        scratch_shapes=[
            VMEM(shape, values.dtype), pltpu.SemaphoreType.DMA(shape[:1]), pltpu.SemaphoreType.DMA(shape[:1])],
        compiler_params=pltpu.CompilerParams(vmem_limit_bytes=60 * MIB),
        cost_estimate=microseconds(2),
    )(values)


def folds(width, hidden):
    return 0 if hidden % LANES else width // hidden


def weights_kernel(rows_ref, pre_ref, hidden_ref, grad_ref, *out_refs):
    width, hidden = rows_ref.shape[1], pre_ref.shape[1]
    low = jnp.bfloat16
    up = dot_tn(rows_ref[...], pre_ref[...]).astype(low)
    down = dot_tn(hidden_ref[...], grad_ref[...]).astype(low)
    if len(out_refs) == 2:
        out_refs[0][...], out_refs[1][...] = up, down
        return
    out_refs[0][:width] = up
    for f in range(width // hidden):
        out_refs[0][width + f * hidden : width + (f + 1) * hidden] = down[:, f * hidden : (f + 1) * hidden]


def expert_weights(rows, pre, hidden_rows, grad_rows):
    total, width = rows.shape
    members, _, hidden = pre.shape
    slices = pl.BlockSpec((None, total, hidden), lambda s: (s, 0, 0))
    sizes = [(2 * width, hidden)] if folds(width, hidden) else [(width, hidden), (hidden, width)]
    return plain_call(
        weights_kernel,
        (members,),
        [whole((total, width)), slices, slices, whole((total, width))],
        [pl.BlockSpec((None,) + size, lambda s: (s, 0, 0)) for size in sizes],
        [shaped((members,) + size, jnp.bfloat16) for size in sizes],
        [],
        (rows, pre, hidden_rows, grad_rows),
        6,
    )


def widen_kernel(experts, *refs):
    up_ref, down_ref = refs[-2:]
    refs = refs[:-2]
    width, hidden = up_ref.shape
    for layer in (0, 1):
        @pl.when(pl.program_id(0) // experts == layer)
        def _():
            if len(refs) == 4:
                up_ref[...] = refs[2 * layer][...].astype(jnp.float32)
                down_ref[...] = refs[2 * layer + 1][...].astype(jnp.float32)
                return
            up_ref[...] = refs[layer][:width].astype(jnp.float32)
            for f in range(width // hidden):
                down_ref[:, f * hidden : (f + 1) * hidden] = refs[layer][
                    width + f * hidden : width + (f + 1) * hidden].astype(jnp.float32)


def widened(first, second, width, hidden):
    experts = first[0].shape[0]
    specs = []
    for layer, arrays in enumerate((first, second)):
        for array in arrays:
            if layer == 0:
                place = lambda i: (jnp.minimum(i, experts - 1), 0, 0)
            else:
                place = lambda i: (jnp.maximum(i - experts, 0), 0, 0)
            specs.append(pl.BlockSpec((None,) + array.shape[1:], place))
    return plain_call(
        functools.partial(widen_kernel, experts),
        (2 * experts,),
        specs,
        [pl.BlockSpec((None, None, width, hidden), lambda i: (i // experts, i % experts, 0, 0)),
         pl.BlockSpec((None, None, hidden, width), lambda i: (i // experts, i % experts, 0, 0))],
        [shaped((2, experts, width, hidden)), shaped((2, experts, hidden, width))],
        [],
        tuple(first) + tuple(second),
        9,
    )


def sum_kernel(dims, *refs):
    count, lines, sizes, first_rows, width = dims
    total = len(sizes)
    arrays, out_ref = refs[:total], refs[total]
    (own, near, over, spun, spun_first, home, core_send, core_recv, load, over_send, over_recv,
     spin_send, spin_recv, spin_first_send, spin_first_recv, home_send, home_recv) = refs[total + 1 :]
    rows = sum(sizes)
    later = rows - first_rows
    here = lax.axis_index("wide")
    group = lax.axis_index("narrow")
    line, core = group // 2, lax.rem(group, 2)
    half = count // 2
    low, f32 = jnp.bfloat16, jnp.float32

    def window_of(position):
        position = lax.rem(position + 2 * count, count)
        upper = position // half
        return 2 * position * (1 - upper) + (2 * (count - 1 - position) + 1) * upper

    odd = lax.rem(here, 2)
    spot = (here // 2) * (1 - odd) + (count - 1 - here // 2) * odd
    ring = (window_of(spot + 1), window_of(spot - 1))
    peer = 2 * line + 1 - core
    lines_away = [lax.rem(line + k, lines) for k in range(1, lines)]

    barrier = pltpu.get_barrier_semaphore()
    for window in ring:
        pl.semaphore_signal(barrier, inc=1, device_id=(window, group), device_id_type=MESH)
    pl.semaphore_signal(barrier, inc=1, device_id=(here, peer), device_id_type=MESH)
    for other in lines_away:
        pl.semaphore_signal(barrier, inc=1, device_id=(here, 2 * other + core), device_id_type=MESH)
    pl.semaphore_wait(barrier, 2 + lines)

    order = [spot + half]
    for away in range(half - 1, 0, -1):
        order += [spot + away, spot - away]
    order = [window_of(position) for position in order + [spot]]
    sent, held = [], []
    for k, window in enumerate(order):
        held.append([])
        start = 0
        for i, size in enumerate(sizes):
            place = pl.ds(start, size)
            start += size
            copy = pltpu.make_async_remote_copy(
                src_ref=arrays[i].at[window, :, 1 - core], dst_ref=near.at[window, :, place],
                send_sem=core_send.at[k, i], recv_sem=core_recv.at[k, i],
                device_id=(here, peer), device_id_type=MESH)
            copy.start()
            mine = pltpu.make_async_copy(
                arrays[i].at[window, :, core], own.at[window, :, place], load.at[k, i])
            mine.start()
            sent.append(copy)
            held[-1].append((copy, mine))

    ahead, behind = pl.ds(0, first_rows), pl.ds(first_rows, later)
    cut_first = first_rows // 32 * 16
    cut_later = later // 32 * 16
    parts_first = (pl.ds(0, cut_first), pl.ds(cut_first, first_rows - cut_first))
    parts_later = (
        pl.ds(first_rows, cut_later), pl.ds(first_rows + cut_later, later - cut_later))
    parts_got = (pl.ds(0, cut_later), pl.ds(cut_later, later - cut_later))

    def meet(k):
        window = order[k]
        for copy, mine in held[k]:
            copy.wait_recv()
            mine.wait()

        def one(at, carry):
            place = pl.ds(pl.multiple_of(at * 16, 16), 16)
            for x in range(lines):
                own[window, x, place] = (
                    own[window, x, place].astype(f32) + near[window, x, place].astype(f32)
                ).astype(low)
            return carry

        lax.fori_loop(0, rows // 16, one, 0)
        for j, other in enumerate(lines_away):
            copy = pltpu.make_async_remote_copy(
                src_ref=own.at[window, other, ahead], dst_ref=over.at[j, window],
                send_sem=over_send.at[j, k], recv_sem=over_recv.at[j, k],
                device_id=(here, 2 * other + core), device_id_type=MESH)
            copy.start()
            sent.append(copy)
            crossing[k].append(copy)

    crossing = [[] for _ in order]

    def spin_later(step):
        for way, sign in ((0, 1), (1, -1)):
            window = window_of(spot + sign * (half - step))
            if step == 0:
                which, got_which = parts_later[way], parts_got[way]
                if not (later - cut_later if way else cut_later):
                    continue
            else:
                which, got_which = behind, pl.ds(0, later)
                add_which, add_got = (
                    (parts_later[way], parts_got[way]) if step == 1 else (which, got_which))
                if turns[way]:
                    turns[way][-1].wait_recv()
                    own[window, :, add_which] = (
                        own[window, :, add_which].astype(f32)
                        + spun[way, step - 1, :, add_got].astype(f32)
                    ).astype(low)
            copy = pltpu.make_async_remote_copy(
                src_ref=own.at[window, :, which], dst_ref=spun.at[way, step, :, got_which],
                send_sem=spin_send.at[way, step], recv_sem=spin_recv.at[way, step],
                device_id=(ring[way], group), device_id_type=MESH)
            copy.start()
            sent.append(copy)
            turns[way].append(copy)

    def cross(k):
        window = order[k]
        value = own[window, line, ahead].astype(f32)
        for j, copy in enumerate(crossing[k]):
            copy.wait_recv()
            value = value + over[j, window].astype(f32)
        return value

    first_turns = ([], [])

    def spin_first(step):
        for way, sign in ((0, 1), (1, -1)):
            k = 0 if step == 0 else 2 * step - 1 + way
            window = order[k]
            if step or way == 0:
                own[window, line, ahead] = cross(k).astype(low)
            if step == 0:
                which = parts_first[way]
            else:
                which = ahead
                add_which = parts_first[way] if step == 1 else which
                first_turns[way][-1].wait_recv()
                own[window, line, add_which] = (
                    own[window, line, add_which].astype(f32)
                    + spun_first[way, step - 1, add_which].astype(f32)
                ).astype(low)
            copy = pltpu.make_async_remote_copy(
                src_ref=own.at[window, line, which], dst_ref=spun_first.at[way, step, which],
                send_sem=spin_first_send.at[way, step], recv_sem=spin_first_recv.at[way, step],
                device_id=(ring[way], group), device_id_type=MESH)
            copy.start()
            sent.append(copy)
            first_turns[way].append(copy)

    turns = ([], [])
    meet(0)
    spin_later(0)
    for step in range(1, half):
        meet(2 * step - 1)
        meet(2 * step)
        spin_first(step - 1)
        spin_later(step)
    meet(len(order) - 1)
    spin_first(half - 1)
    summed = own[here, :, behind].astype(f32)
    for way in (0, 1):
        turns[way][-1].wait_recv()
        summed = summed + spun[way, half - 1].astype(f32)
    own[here, :, behind] = summed.astype(low)
    homes = []
    for j, other in enumerate(lines_away):
        copy = pltpu.make_async_remote_copy(
            src_ref=own.at[here, other, behind], dst_ref=home.at[j],
            send_sem=home_send.at[j], recv_sem=home_recv.at[j],
            device_id=(here, 2 * other + core), device_id_type=MESH)
        copy.start()
        sent.append(copy)
        homes.append(copy)

    summed = cross(len(order) - 1)
    for way in (0, 1):
        first_turns[way][-1].wait_recv()
        summed = summed + spun_first[way, half - 1].astype(f32)
    out_ref[ahead, :] = summed
    value = own[here, line, behind].astype(f32)
    for j, copy in enumerate(homes):
        copy.wait_recv()
        value = value + home[j].astype(f32)
    out_ref[behind, :] = value
    for copy in sent:
        copy.wait_send()


def summed_shares(arrays, identity):
    count, groups = lax.axis_size("wide"), lax.axis_size("narrow")
    lines, half = groups // 2, count // 2
    width = arrays[0].shape[2]
    if any(array.shape[1] % 16 for array in arrays):
        packed = jnp.concatenate(arrays, axis=1)
        arrays = [jnp.pad(packed, ((0, 0), (0, -packed.shape[1] % 16), (0, 0)))]
    sizes = tuple(array.shape[1] for array in arrays)
    rows = sum(sizes)
    first = max(32, rows * 11 // 20 // 16 * 16)
    later = rows - first
    low = jnp.bfloat16
    dma = pltpu.SemaphoreType.DMA
    return pl.pallas_call(
        functools.partial(sum_kernel, (count, lines, sizes, first, width)),
        out_shape=jax.ShapeDtypeStruct((rows, width), jnp.float32),
        in_specs=[ANYWHERE] * len(arrays),
        out_specs=pl.BlockSpec(memory_space=VMEM),
        scratch_shapes=[
            VMEM((count, lines, rows, width), low),
            VMEM((count, lines, rows, width), low),
            VMEM((lines - 1, count, first, width), low),
            VMEM((2, half, lines, later, width), low),
            VMEM((2, half, first, width), low),
            VMEM((lines - 1, later, width), low),
            dma((count, len(arrays))), dma((count, len(arrays))), dma((count, len(arrays))),
            dma((lines - 1, count)), dma((lines - 1, count)),
            dma((2, half)), dma((2, half)),
            dma((2, half)), dma((2, half)),
            dma((lines - 1,)), dma((lines - 1,)),
        ],
        compiler_params=pltpu.CompilerParams(
            collective_id=identity, has_side_effects=True, vmem_limit_bytes=60 * MIB
        ),
        cost_estimate=microseconds(60),
    )(*[array.reshape(count, lines, 2, array.shape[1], width) for array in arrays])


def inward_kernel(dims, grad_ref, weight_ref, edge_ref, handed_ref, normed_ref, begin_ref, gain_ref, passed_ref,
                  out_ref, channel_ref, router_ref, expert_ref, packed_ref, new_ref, rows, features):
    blocks, wide, tall, held, fold, marks, spare, steps = dims
    owners, count, _ = packed_ref.shape
    f32, low = jnp.float32, jnp.bfloat16
    step = pl.program_id(0)
    tokens = grad_ref.shape[0]
    last = edge_ref.shape[0]
    value = lax.rem(step, blocks) < blocks // 2
    place = lax.broadcasted_iota(jnp.int32, grad_ref.shape, 0)
    block = grad_ref[...].astype(f32)
    edge = edge_ref[...] + handed_ref[...]
    for j in range(last):
        row = (steps - last + j) * CHUNKS + CHUNKS - 1
        block = jnp.where(jnp.logical_and(place == row, value), edge[j : j + 1], block)
    block = block.astype(low)

    @pl.when(step == 0)
    def _():
        new_ref[...] = jnp.zeros_like(new_ref)
        rows[...] = jnp.zeros_like(rows)

    @pl.when(step < blocks)
    def _():
        new_ref[...] += dot_nt(block, weight_ref[...])

    @pl.when(step == blocks - 1)
    def _():
        grad, norm_grad = rms_back(begin_ref[...], gain_ref[...], new_ref[...])
        new_ref[...] = passed_ref[...] + grad
        experts = router_ref.shape[1]
        lane = lax.broadcasted_iota(jnp.int32, (experts, 2 * LANES), 1)
        row = lax.broadcasted_iota(jnp.int32, (experts, 2 * LANES), 0)
        pick = (lane == row + spare).astype(f32).astype(low)
        lane = lax.broadcasted_iota(jnp.int32, (2, 2 * LANES), 1)
        row = lax.broadcasted_iota(jnp.int32, (2, 2 * LANES), 0)
        pick_norms = (lane == row + spare + experts).astype(f32).astype(low)
        norms = jnp.concatenate([norm_grad[None], expert_ref[...]], axis=0).astype(low)
        features[...] = dot_nn(router_ref[...].astype(low), pick) + dot_tn(norms, pick_norms)

    @pl.when(step >= blocks)
    def _():
        grad = dot_tn(block, normed_ref[...])
        passed = out_ref[...]
        channel = channel_ref[...].astype(f32)
        start = pl.multiple_of((step - blocks) * owners * marks, 8)
        mine = features[pl.ds(start, owners * marks), :]
        thin = held // fold
        whole_tiles = not any(size % 16 for size in (wide, tall, thin))
        target = packed_ref if whole_tiles else rows
        kind = target.dtype
        for k in range(owners):
            target[k, :wide] = grad[k * wide : (k + 1) * wide].astype(kind)
            target[k, wide : wide + tall] = passed[k * tall : (k + 1) * tall].astype(kind)
            small = channel[k * held : (k + 1) * held]
            extra = mine[k * marks : (k + 1) * marks]
            small = small + jnp.concatenate([extra, jnp.zeros((held - marks, 2 * LANES), f32)], axis=0)
            for f in range(fold):
                target[k, wide + tall : wide + tall + thin, f * 2 * LANES : (f + 1) * 2 * LANES] = small[
                    f * thin : (f + 1) * thin].astype(kind)
            if whole_tiles and count > wide + tall + thin:
                packed_ref[k, wide + tall + thin :] = jnp.zeros((count - wide - tall - thin, grad.shape[1]), kind)
        if not whole_tiles:
            packed_ref[...] = rows[...].astype(low)


def mixer_inward(layer, grad_projected, in_weight, edge, handed, normed, begin, gain, passed, grad_out, channel,
                 grad_router, grad_expert, devices, spare):
    tokens, columns = grad_projected.shape
    width = normed.shape[1]
    wide, tall = columns // devices, grad_out.shape[0] // devices
    held, marks = channel.shape[0] // devices, width // devices
    fold = width // (2 * LANES)
    count = wide + tall + held // fold
    count += -count % 16
    owners = 1
    while owners * wide % LANES:
        owners *= 2
    blocks = devices // owners
    span = owners * wide
    taps = edge.shape[0]
    inner = edge.shape[1] // span

    def at(i):
        return jnp.maximum(i - blocks, 0)

    return plain_call(
        functools.partial(inward_kernel, (blocks, wide, tall, held, fold, marks, spare, tokens // CHUNKS)),
        (2 * blocks,),
        [pl.BlockSpec((tokens, span), lambda i: (0, i % blocks)),
         pl.BlockSpec((None, width, span), lambda i: (layer, 0, jnp.minimum(i, blocks - 1))),
         pl.BlockSpec((taps, span), lambda i: (0, jnp.minimum(i % blocks, inner - 1))),
         pl.BlockSpec((taps, span), lambda i: (0, jnp.minimum(i % blocks, inner - 1))),
         whole(normed.shape), whole(begin.shape), layer_whole(layer, (1, width)), whole(passed.shape),
         pl.BlockSpec((owners * tall, width), lambda i: (at(i), 0)),
         pl.BlockSpec((owners * held, 2 * LANES), lambda i: (at(i), 0)),
         whole(grad_router.shape), whole(grad_expert.shape)],
        [pl.BlockSpec((owners, count, width), lambda i: (at(i), 0, 0)), whole((tokens, width))],
        [shaped((devices, count, width), jnp.bfloat16), shaped((tokens, width))],
        [VMEM((owners, count, width), jnp.float32), VMEM((width, 2 * LANES), jnp.float32)],
        (grad_projected, in_weight, edge, handed, normed, begin, gain, passed, grad_out, channel, grad_router,
         grad_expert),
        9,
    )


def unfold_kernel(dims, *refs):
    layers, wide, tall, held, fold, marks, spare, sizes = dims
    inputs, outs = refs[:layers], refs[layers:]
    (in_ref, out_ref, state_ref, step_ref, decay_ref, conv_ref, conv_bias_ref, step_bias_ref, skip_ref,
     router_ref, mix_ref, expert_ref) = outs
    thin = held // fold
    for layer in range(layers):
        whole_rows = inputs[layer][...].astype(jnp.float32)
        in_ref[layer] = whole_rows[:wide]
        out_ref[layer] = whole_rows[wide : wide + tall]
        mine = whole_rows[wide + tall : wide + tall + thin]
        channel = jnp.concatenate(
            [mine[:, f * 2 * LANES : (f + 1) * 2 * LANES] for f in range(fold)], axis=0)
        state_ref[layer] = channel[:, : sizes[0]]
        turned = channel.T
        bounds = [0]
        for size in sizes:
            bounds.append(bounds[-1] + size)
        pieces = [turned[bounds[i] : bounds[i + 1]] for i in range(7)]
        step_ref[layer] = pieces[1]
        decay_ref[layer] = pieces[2]
        conv_ref[layer] = pieces[3]
        conv_bias_ref[layer : layer + 1] = pieces[4]
        step_bias_ref[layer : layer + 1] = pieces[5]
        skip_ref[layer : layer + 1] = pieces[6]
        experts = router_ref.shape[1]
        router_ref[layer] = turned[spare : spare + experts, :marks]
        mix_ref[layer : layer + 1] = turned[spare + experts : spare + experts + 1, :marks]
        expert_ref[layer : layer + 1] = turned[spare + experts + 1 : spare + experts + 2, :marks]


def unfolded(sums, wide, tall, held, marks, experts, spare, sizes):
    layers, width = len(sums), sums[0].shape[1]
    fold = width // (2 * LANES)
    shapes = [
        (wide, width), (tall, width), (held, sizes[0]), (sizes[1], held), (sizes[2], held), (sizes[3], held),
        (held,), (held,), (held,), (experts, marks), (marks,), (marks,),
    ]
    inside = pl.BlockSpec(memory_space=VMEM)
    return pl.pallas_call(
        functools.partial(unfold_kernel, (layers, wide, tall, held, fold, marks, spare, sizes)),
        out_shape=[shaped((layers,) + shape) for shape in shapes],
        in_specs=[inside] * layers,
        out_specs=[inside] * len(shapes),
        compiler_params=pltpu.CompilerParams(vmem_limit_bytes=60 * MIB),
        cost_estimate=microseconds(3),
    )(*sums)


def on_device(
    hidden,
    doc_start,
    expert_choice,
    slot_index,
    norm_mix,
    in_weight,
    conv_weight,
    conv_bias,
    state_weight,
    step_weight,
    step_bias,
    decay_log,
    skip_weight,
    out_weight,
    norm_expert,
    router,
    expert_up,
    expert_down,
    cotangent,
):
    layers = in_weight.shape[0]
    tokens = hidden.shape[1]
    width = hidden.shape[2]
    inner = skip_weight.shape[1]
    rank = step_weight.shape[1]
    states = decay_log.shape[1]
    experts = router.shape[2]
    taps = conv_weight.shape[1]
    steps = tokens // CHUNKS
    both = ("wide", "narrow")
    groups = lax.axis_size("narrow")
    devices = lax.axis_size("wide") * groups
    per_group = experts // groups
    capacity = max(2, 5 * tokens // (4 * experts))
    block = -(-per_group * capacity // 16) * 16
    low, f32 = jnp.bfloat16, jnp.float32
    starts = to_steps(doc_start[0]).astype(f32)
    masks = keep_masks(starts, taps)
    keep_mask = rim_keep(starts, taps - 1)[:, None]
    reset = jnp.broadcast_to((starts * RESET)[..., None], starts.shape + (LANES,))
    order = expert_order(per_group, groups, block, capacity)
    norm_mix, conv_bias, step_bias, skip_weight, norm_expert = (
        values[:, None, :] for values in (norm_mix, conv_bias, step_bias, skip_weight, norm_expert))
    current = to_steps(hidden[0]).reshape(tokens, width).astype(f32)
    saved = []

    def cube(values):
        return values.reshape(steps, CHUNKS, values.shape[-1])

    fills, onehots, keeps = [], [], []
    for layer in range(layers):
        chosen = to_steps(expert_choice[layer, 0]).reshape(tokens)
        slot_row = to_steps(slot_index[layer, 0]).reshape(tokens)
        kept = slot_row >= 0
        place = (chosen // per_group) * block + (chosen % per_group) * capacity + slot_row
        place = jnp.where(kept, place, -1)
        fills.append(
            (place[None, :] == jnp.arange(groups * block, dtype=jnp.int32)[:, None]).astype(low))
        onehots.append((chosen[:, None] == jnp.arange(experts, dtype=jnp.int32)[None, :]).astype(f32))
        keeps.append(kept.astype(f32)[:, None])

    tail = passed_along(hidden[0, tokens - taps + 1 :] * keep_mask.astype(low), 1)
    weights = [None] * layers
    ready, tail = lax.optimization_barrier((layer_of(expert_up, 0), tail))
    weights[0] = between_members([ready])
    for layer in range(layers):
        begin = current
        normed = rms_scale(current, norm_mix[layer]).astype(low)
        projected = cube(dot_nn(normed, in_weight[layer]))
        if layer == 0:
            before = rms_scale(tail.astype(f32), norm_mix[layer]).astype(low)
            rim = dot_nn(before, in_weight[layer, :, :inner])
        else:
            rim = passed_along(projected[steps - taps + 1 :, CHUNKS - 1, :inner] * keep_mask, 1)
        act, selection, size, link, link_size, total, total_size = mixer_front(
            layer, projected, rim, masks, reset, conv_weight, conv_bias, state_weight, step_weight, step_bias,
            decay_log)
        if layer == 0:
            total, fills, order = lax.optimization_barrier((total, fills, order))
        total, ready = lax.optimization_barrier((total, layer_of(expert_down, layer)))
        entering = handed_on(layer, total, total_size, decay_log, False, layer)
        ready, entering = lax.optimization_barrier((ready, entering))
        weights[layer] += between_members([ready])
        mixed, gated, begins, middle, routed, logits, outbound = mixer_run(
            layer, size, act, selection, reset, decay_log, link, link_size, entering, projected, skip_weight,
            out_weight, current, norm_expert, router, fills[layer])
        if layer + 1 < layers:
            ready, outbound = lax.optimization_barrier((layer_of(expert_up, layer + 1), outbound))
            weights[layer + 1] = between_members([ready])
        returned, kept_rows, pre_act, hidden_low = expert_pass(
            outbound.reshape(groups, block, width), order, weights[layer], None, 4 + layer)
        shares = jax.nn.softmax(logits, axis=-1)
        gate = jnp.sum(shares * onehots[layer], axis=1, keepdims=True)
        back_rows = dot_tn(fills[layer], returned.reshape(groups * block, width))
        current = middle + (keeps[layer] * gate) * back_rows
        saved.append(dict(
            begin=begin, normed=normed, projected=projected, rim=rim, act=act, selection=selection, size=size,
            begins=begins, mixed=mixed, gated=gated, middle=middle, routed=routed, shares=shares, gate=gate,
            kept_rows=kept_rows, pre_act=pre_act, hidden_low=hidden_low, back_rows=back_rows))
    output = to_tokens(cube(current.astype(low)))[None]
    grad = to_steps(cotangent[0]).reshape(tokens, width).astype(f32)
    sums = [None] * layers
    expert_grads = [None] * layers
    per_device = inner // devices
    norm_device = width // devices
    spare = 160
    for layer in range(layers - 1, -1, -1):
        entry = saved[layer]
        fill, keep, gate = fills[layer], keeps[layer], entry["gate"]
        grad_rows_low = ((keep * gate) * grad).astype(low)
        grad_gate = keep * jnp.sum(grad * entry["back_rows"], axis=1, keepdims=True)
        outbound = dot_nn(fill, grad_rows_low).astype(low).reshape(groups, block, width)
        inbound, grad_rows, grad_pre = expert_pass(
            outbound, order, weights[layer], entry["pre_act"], 6 + layer)
        ready = expert_weights(entry["kept_rows"], grad_pre, entry["hidden_low"], grad_rows)
        grad_sent = dot_tn(fill, inbound.reshape(groups * block, width))
        grad_logits_low = ((grad_gate * gate) * (onehots[layer] - entry["shares"])).astype(low)
        grad_router = dot_tn(entry["routed"], grad_logits_low)
        grad_routed = grad_sent + dot_nt(grad_logits_low, router[layer])
        grad_middle, grad_norm_expert = rms_back(entry["middle"], norm_expert[layer], grad_routed)
        grad = grad + grad_middle
        grad_low = grad.astype(low)
        grad_y, grad_igate, grad_skip, grad_out, link, link_size, total, total_size = mixer_turn(
            layer, grad_low, out_weight, entry["projected"], entry["mixed"], entry["act"], entry["gated"],
            entry["size"], entry["selection"], reset, decay_log)
        entering = handed_on(layer, total, total_size, decay_log, True, 2 + layer)
        ready, entering = lax.optimization_barrier((ready, entering))
        expert_grads[layer] = between_members(ready)
        grad_act, grad_decay, grad_bias, grad_step, grad_selection = mixer_back(
            layer, entry["size"], entry["act"], grad_y, decay_log, entry["selection"], reset,
            entry["begins"], link, link_size, entering, step_weight, step_bias, skip_weight)
        grad_projected, edge, rim_grad, channel = mixer_conv_back(
            layer, grad_act, grad_selection, state_weight, entry["projected"], entry["rim"], masks, conv_weight,
            conv_bias, entry["act"], grad_step, grad_decay, grad_bias, grad_skip, grad_igate)
        handed = passed_along(rim_grad, -1) * keep_mask
        blocks, grad = mixer_inward(
            layer, grad_projected, in_weight, edge, handed, entry["normed"], entry["begin"], norm_mix, grad,
            grad_out, channel, grad_router, grad_norm_expert.reshape(1, width), devices, spare)
        if layer:
            blocks, grad = lax.optimization_barrier((blocks, grad))
            rows = blocks.shape[1]
            sums[layer] = lax.psum_scatter(
                blocks.reshape(devices * rows, width), both, scatter_dimension=0, tiled=True)
        else:
            sums[layer] = summed_shares([blocks], 8)
    (grad_in, grad_out, grad_state, grad_step, grad_decay, grad_conv, grad_conv_bias, grad_step_bias, grad_skip,
     grad_router, grad_norm_mix, grad_norm_expert) = unfolded(
        sums, 2 * inner // devices, per_device, per_device, norm_device, experts, spare,
        (rank + 2 * states, rank, states, taps, 1, 1, 1))
    shared = (
        grad_norm_mix, jnp.swapaxes(grad_in, 1, 2), grad_conv, grad_conv_bias, grad_state, grad_step,
        grad_step_bias, grad_decay, grad_skip, grad_out, grad_norm_expert, jnp.swapaxes(grad_router, 1, 2))
    up_grads, down_grads = widened(*expert_grads, width, expert_up.shape[3])
    output_grad = to_tokens(cube(grad))[None]
    return (output, output_grad, *shared, up_grads, down_grads)


def solution(mesh):
    both = ("wide", "narrow")
    placed = (
        P("narrow", "wide", None),
        P("narrow", "wide"),
        P(None, "narrow", "wide"),
        P(None, "narrow", "wide"),
    ) + (P(),) * 12 + (
        P(None, "narrow", None, "wide"),
        P(None, "narrow", "wide", None),
        P("narrow", "wide", None),
    )
    return jax.shard_map(
        on_device,
        mesh=mesh,
        in_specs=placed,
        out_specs=(
            P("narrow", "wide", None),
            P("narrow", "wide", None),
            P(None, both),
            P(None, None, both),
            P(None, None, both),
            P(None, both),
            P(None, both, None),
            P(None, None, both),
            P(None, both),
            P(None, None, both),
            P(None, both),
            P(None, both, None),
            P(None, both),
            P(None, both, None),
            P(None, "narrow", None, "wide"),
            P(None, "narrow", "wide", None),
        ),
        check_vma=False,
    )
```

```python
import functools

import jax
import jax.numpy as jnp
from jax import lax
from jax.experimental import pallas as pl
from jax.experimental.pallas import tpu as pltpu
from jax.sharding import PartitionSpec as P

EPS = 1e-05
CHUNKS = 8
LANES = 128
LOG2E = 1.4426950408889634
RESET = 1e9
MIB = 1024 * 1024
MESH = pl.DeviceIdType.MESH
VMEM = pltpu.VMEM


def to_steps(values):
    steps = values.shape[0] // CHUNKS
    return jnp.swapaxes(values.reshape((CHUNKS, steps) + values.shape[1:]), 0, 1)


def to_tokens(values):
    moved = jnp.swapaxes(values, 0, 1)
    return moved.reshape((-1,) + values.shape[2:])


def rms_scale(values, gain):
    return values * lax.rsqrt(jnp.mean(values * values, axis=-1, keepdims=True) + EPS) * gain


def rms_back(values, gain, grad):
    scale = lax.rsqrt(jnp.mean(values * values, axis=-1, keepdims=True) + EPS)
    weighted = grad * gain
    inner = jnp.mean(weighted * values, axis=-1, keepdims=True)
    return (
        scale * weighted - values * (scale * scale * scale) * inner,
        jnp.sum(grad * values * scale, axis=0),
    )


def dot_nn(left, right):
    return lax.dot_general(left, right, (((1,), (0,)), ((), ())), preferred_element_type=jnp.float32)


def dot_nt(left, right):
    return lax.dot_general(left, right, (((1,), (1,)), ((), ())), preferred_element_type=jnp.float32)


def dot_tn(left, right):
    return lax.dot_general(left, right, (((0,), (0,)), ((), ())), preferred_element_type=jnp.float32)


def passed_along(x, by):
    size = lax.axis_size("wide")
    return lax.ppermute(x, "wide", [(i, i + by) for i in range(size) if 0 <= i + by < size])


def tables_kernel(dims, doc_ref, choice_ref, slot_ref, reset_ref, mask_ref, *outs):
    layers, taps, per_group, block, capacity = dims
    tokens = doc_ref.shape[1]
    steps = tokens // CHUNKS
    f32, low = jnp.float32, jnp.bfloat16
    fills, onehots, keeps = outs[:layers], outs[layers : 2 * layers], outs[2 * layers :]
    rows = [doc_ref[...]] + [choice_ref[l] for l in range(layers)] + [slot_ref[l] for l in range(layers)]
    rows = jnp.concatenate([row.astype(f32) for row in rows], axis=0)
    rows = jnp.concatenate([rows, jnp.zeros((CHUNKS - rows.shape[0], tokens), f32)], axis=0).astype(low)
    place = lax.broadcasted_iota(jnp.int32, (tokens, tokens), 1)
    token = (place & (CHUNKS - 1)) * steps + lax.shift_right_logical(place, 3)
    order = (lax.broadcasted_iota(jnp.int32, (tokens, tokens), 0) == token).astype(f32).astype(low)
    along = dot_nn(rows, order)
    down = lax.dot_general(order, rows, (((0,), (1,)), ((), ())), preferred_element_type=f32)

    starts = jnp.broadcast_to(down[:, 0:1], (tokens, LANES)).reshape(steps, CHUNKS, LANES)
    reset_ref[...] = starts * RESET
    chunk = lax.broadcasted_iota(jnp.int32, (CHUNKS, LANES), 0)
    mask_ref[0] = 1.0 - starts
    for offset in range(2, taps):
        mask_ref[offset - 1, offset - 1 :] = mask_ref[offset - 2, offset - 1 :] * (
            1.0 - starts[: steps - offset + 1])
        for i in range(offset - 1):
            before = jnp.where(chunk == 0, 0.0, pltpu.roll(starts[steps - offset + 1 + i], 1, axis=0))
            mask_ref[offset - 1, i] = mask_ref[offset - 2, i] * (1.0 - before)

    for l in range(layers):
        chosen, slot = along[1 + l : 2 + l], along[1 + layers + l : 2 + layers + l]
        group = jnp.floor((chosen + 0.5) * (1.0 / per_group))
        spot = group * block + (chosen - group * per_group) * capacity + slot
        spot = jnp.where(slot >= 0.0, spot, -1.0).astype(jnp.int32)
        fills[l][...] = (
            lax.broadcasted_iota(jnp.int32, fills[l].shape, 0) == spot).astype(f32).astype(low)
        picked = down[:, 1 + l : 2 + l].astype(jnp.int32)
        onehots[l][...] = (lax.broadcasted_iota(jnp.int32, onehots[l].shape, 1) == picked).astype(f32)
        keeps[l][...] = jnp.where(down[:, 1 + layers + l : 2 + layers + l] >= 0.0, 1.0, 0.0)


def tables(doc_start, expert_choice, slot_index, taps, experts, groups, block, capacity):
    layers = expert_choice.shape[0]
    tokens = doc_start.shape[1]
    steps = tokens // CHUNKS
    f32 = jnp.float32
    shapes = [shaped((steps, CHUNKS, LANES)), shaped((taps - 1, steps, CHUNKS, LANES))]
    shapes += [shaped((groups * block, tokens), jnp.bfloat16)] * layers
    shapes += [shaped((tokens, experts))] * layers + [shaped((tokens, 1))] * layers
    inside = pl.BlockSpec(memory_space=VMEM)
    reset, masks, *rest = pl.pallas_call(
        functools.partial(tables_kernel, (layers, taps, experts // groups, block, capacity)),
        out_shape=shapes,
        in_specs=[inside] * 3,
        out_specs=[inside] * len(shapes),
        compiler_params=pltpu.CompilerParams(vmem_limit_bytes=60 * MIB),
        cost_estimate=microseconds(3),
    )(doc_start, expert_choice, slot_index)
    return reset, masks, rest[:layers], rest[layers : 2 * layers], rest[2 * layers :]


def rim_keep(doc_start, count):
    tail = 1.0 - doc_start[doc_start.shape[0] - count :].astype(jnp.float32)
    later = jnp.cumprod(tail[::-1])[::-1]
    return jnp.concatenate([later[1:], jnp.ones((1,), jnp.float32)])


TILE = 2 * LANES


def each_part(body):
    def one(at, carry):
        body(pl.ds(pl.multiple_of(at * LANES, LANES), LANES))
        return carry

    lax.fori_loop(0, TILE // LANES, one, 0)


def microseconds(count):
    return pl.CostEstimate(flops=int(count * 1.5e8), transcendentals=0, bytes_accessed=10000)


def plain_call(kernel, grid, in_specs, out_specs, out_shapes, scratch, args, cost, aliases=None):
    return pl.pallas_call(
        kernel,
        grid=grid,
        in_specs=in_specs,
        out_specs=out_specs,
        out_shape=out_shapes,
        scratch_shapes=scratch,
        input_output_aliases=aliases or {},
        compiler_params=pltpu.CompilerParams(
            dimension_semantics=("arbitrary",), vmem_limit_bytes=60 * MIB
        ),
        cost_estimate=microseconds(cost),
    )(*args)


def shaped(shape, kind=jnp.float32):
    return jax.ShapeDtypeStruct(shape, kind)


def slab(steps, first=0):
    return pl.BlockSpec((steps, CHUNKS, TILE), lambda c: (0, 0, first + c))


def rows_of(count):
    return pl.BlockSpec((count, TILE), lambda c: (0, c))


def layer_rows(layer, count):
    return pl.BlockSpec((None, count, TILE), lambda c: (layer, 0, c))


def layer_columns(layer, count):
    return pl.BlockSpec((None, TILE, count), lambda c: (layer, c, 0))


def layer_whole(layer, shape):
    return pl.BlockSpec((None,) + shape, lambda c: (layer,) + (0,) * len(shape))


def whole(shape):
    return pl.BlockSpec(shape, lambda c: (0,) * len(shape))


ANYWHERE = pl.BlockSpec(memory_space=pl.ANY)


def spread_columns(selection_ref, first, states, out_ref):
    def one(step, carry):
        tile = selection_ref[step]
        for n in range(states):
            out_ref[step, n] = jnp.broadcast_to(tile[:, first + n : first + n + 1], (CHUNKS, LANES))
        return carry

    lax.fori_loop(0, selection_ref.shape[0], one, 0, unroll=8)


def rate_rows(rate):
    return [jnp.broadcast_to(rate[n : n + 1, :], (CHUNKS, LANES)) for n in range(rate.shape[0])]


def rates_of(decay_log):
    return -jnp.exp(decay_log) * LOG2E


def two_steps(ref, pair, lanes=slice(None)):
    both = ref[pl.ds(pl.multiple_of(pair * 2 * CHUNKS, 2 * CHUNKS), 2 * CHUNKS), lanes]
    both = both.astype(jnp.float32)
    return both[:CHUNKS], both[CHUNKS:]


def chunk_links(found, sizes, rates, reverse):
    place = lax.broadcasted_iota(jnp.int32, (CHUNKS, LANES), 0)
    if reverse:
        place = CHUNKS - 1 - place
    last = 0 if reverse else CHUNKS - 1

    def shifted(values, by):
        turned = pltpu.roll(values, CHUNKS - by if reverse else by, axis=0)
        return jnp.where(place >= by, turned, 0.0)

    lengths = [sizes]
    for by in (1, 2, 4):
        lengths.append(lengths[-1] + shifted(lengths[-1], by))
    links, totals = [], []
    for n, rate in enumerate(rates):
        level = found[n]
        for index, by in enumerate((1, 2, 4)):
            level = level + jnp.exp2(lengths[index] * rate) * shifted(level, by)
        links.append(shifted(level, 1))
        totals.append(level[last : last + 1])
    return links, totals, shifted(lengths[-1], 1), lengths[-1][last : last + 1]


def conv_slab(extended, step, mask_ref, kernel_ref, bias, taps):
    total = bias + kernel_ref[0:1, :] * extended[step + taps - 1]
    tiles = total.shape[1] // LANES
    for offset in range(1, taps):
        mask = mask_ref[offset - 1, step]
        mask = jnp.concatenate([mask] * tiles, axis=1) if tiles > 1 else mask
        total = total + kernel_ref[offset : offset + 1, :] * (
            extended[step + taps - 1 - offset] * mask
        )
    return total


def extend(value_ref, rim_ref, extended, taps):
    steps = value_ref.shape[0]
    place = lax.broadcasted_iota(jnp.int32, value_ref.shape[1:], 0)
    for j in range(taps - 1):
        turned = pltpu.roll(value_ref[steps - taps + 1 + j], 1, axis=0)
        extended[j] = jnp.where(place == 0, rim_ref[j : j + 1, :], turned)
    extended[taps - 1 :] = value_ref[...]


def front_kernel(dims, value_ref, rim_ref, mask_ref, reset_ref, conv_ref, conv_bias_ref, state_ref,
                 step_ref, step_bias_ref, decay_ref,
                 act_ref, selection_ref, size_ref, link_ref, link_size_ref, total_ref, total_size_ref,
                 extended, maps, sized, pushed):
    taps, rank, states, steps, channels = dims
    extend(value_ref, rim_ref, extended, taps)
    bias = conv_bias_ref[...]

    def conv_pair(pair, carry):
        both = []
        for step in (2 * pair, 2 * pair + 1):
            both.append(jax.nn.silu(conv_slab(extended, step, mask_ref, conv_ref, bias, taps)))
        at = pl.ds(pl.multiple_of(pair * 2 * CHUNKS, 2 * CHUNKS), 2 * CHUNKS)
        act_ref[at, :] = jnp.concatenate(both, axis=0).astype(jnp.bfloat16)
        return carry

    lax.fori_loop(0, steps // 2, conv_pair, 0)
    selection = dot_nn(act_ref[...], state_ref[...])
    selection_ref[...] = selection.reshape(steps, CHUNKS, selection.shape[1])
    rank_low = selection[:, :rank].astype(jnp.bfloat16)

    def size_tile(c, carry):
        lanes = pl.ds(pl.multiple_of(c * 256, 256), 256)
        linear = dot_nn(rank_low, step_ref[:, lanes]) + step_bias_ref[:, lanes]
        size_ref[:, :, lanes] = jax.nn.softplus(linear).reshape(steps, CHUNKS, 256)
        return carry

    lax.fori_loop(0, channels // 256, size_tile, 0)
    spread_columns(selection_ref, rank, states, maps)

    def end_tile(c, carry):
        lanes = pl.ds(pl.multiple_of(c * LANES, LANES), LANES)
        rates = rate_rows(rates_of(decay_ref[:, lanes]))
        size = size_ref[:, :, lanes]
        pushed[...] = size * act_ref[:, lanes].astype(jnp.float32).reshape(size.shape)
        sized[...] = size + reset_ref[...]

        def one(step, carry):
            size, value = sized[step], pushed[step]
            new = []
            for n in range(states):
                new.append(jnp.exp2(size * rates[n]) * carry[n] + value * maps[step, n])
            return tuple(new) + (carry[states] + size,)

        zero = jnp.zeros((CHUNKS, LANES), jnp.float32)
        found = lax.fori_loop(0, steps, one, (zero,) * (states + 1), unroll=4)
        links, totals, link_size, total_size = chunk_links(found, found[states], rates, False)
        link_size_ref[:, lanes] = link_size
        total_size_ref[:, lanes] = total_size
        for n in range(states):
            link_ref[n, :, lanes] = links[n]
            total_ref[n : n + 1, lanes] = totals[n]
        return carry

    lax.fori_loop(0, channels // LANES, end_tile, 0)


def mixer_front(layer, projected, rim, masks, reset, conv_weight, conv_bias, state_weight, step_weight,
                step_bias, decay_log):
    steps = projected.shape[0]
    channels = conv_weight.shape[2]
    taps, rank, states = conv_weight.shape[1], step_weight.shape[1], decay_log.shape[1]
    columns = state_weight.shape[2]
    value = pl.BlockSpec((steps, CHUNKS, channels), lambda c: (0, 0, 0))
    shapes = [
        shaped((steps * CHUNKS, channels), jnp.bfloat16),
        shaped((steps, CHUNKS, columns)),
        shaped((steps, CHUNKS, channels)),
        shaped((states, CHUNKS, channels)),
        shaped((CHUNKS, channels)),
        shaped((states, channels)),
        shaped((1, channels)),
    ]
    return plain_call(
        functools.partial(front_kernel, (taps, rank, states, steps, channels)),
        (1,),
        [value, whole(rim.shape), whole(masks.shape), whole(reset.shape),
         layer_whole(layer, conv_weight.shape[1:]), layer_whole(layer, conv_bias.shape[1:]),
         layer_whole(layer, state_weight.shape[1:]), layer_whole(layer, step_weight.shape[1:]),
         layer_whole(layer, step_bias.shape[1:]), layer_whole(layer, decay_log.shape[1:])],
        [whole(s.shape) for s in shapes],
        shapes,
        [VMEM((steps + taps - 1, CHUNKS, channels), jnp.float32),
         VMEM((steps, states, CHUNKS, LANES), jnp.float32),
         VMEM((steps, CHUNKS, LANES), jnp.float32), VMEM((steps, CHUNKS, LANES), jnp.float32)],
        (projected, rim, masks, reset, conv_weight, conv_bias, state_weight, step_weight, step_bias,
         decay_log),
        18,
    )


def run_kernel(dims, size_ref, act_ref, selection_ref, reset_ref, decay_ref, link_ref, link_size_ref,
               entering_ref, gate_ref, skip_ref, out_weight_ref, current_ref, norm_ref, router_ref, fill_ref,
               mixed_ref, gated_ref, begin_ref, middle_ref, routed_ref, logits_ref, outbound_ref,
               in_maps, out_maps, pushed):
    rank, states, steps, tiles = dims

    @pl.when(pl.program_id(0) == 0)
    def _():
        spread_columns(selection_ref, rank, states, in_maps)
        spread_columns(selection_ref, rank + states, states, out_maps)
        middle_ref[...] = current_ref[...]

    size = size_ref[...]
    act = act_ref[...].astype(jnp.float32).reshape(size.shape)
    pushed[...] = size * act

    def scan(lanes):
        rates = rate_rows(rates_of(decay_ref[:, lanes]))
        link_size = link_size_ref[:, lanes]
        begin = []
        for n in range(states):
            first = link_ref[n, :, lanes] + jnp.exp2(link_size * rates[n]) * entering_ref[n : n + 1, lanes]
            begin_ref[n, :, lanes] = first
            begin.append(first)

        def one(step, carry):
            size, value = size_ref[step, :, lanes] + reset_ref[step], pushed[step, :, lanes]
            new = []
            sums = [None, None]
            for n in range(states):
                level = jnp.exp2(size * rates[n]) * carry[n] + value * in_maps[step, n]
                new.append(level)
                term = out_maps[step, n] * level
                sums[n % 2] = term if sums[n % 2] is None else sums[n % 2] + term
            mixed_ref[step, :, lanes] = sums[0] + sums[1]
            return tuple(new)

        lax.fori_loop(0, steps, one, tuple(begin), unroll=4)

    each_part(scan)
    mixed = mixed_ref[...] + skip_ref[...] * act
    mixed_ref[...] = mixed
    gated = mixed * jax.nn.silu(gate_ref[...])
    gated_ref[...] = gated.reshape(steps * CHUNKS, TILE).astype(jnp.bfloat16)
    middle_ref[...] += dot_nn(gated_ref[...], out_weight_ref[...])

    @pl.when(pl.program_id(0) == tiles - 1)
    def _():
        routed = rms_scale(middle_ref[...], norm_ref[...]).astype(jnp.bfloat16)
        routed_ref[...] = routed
        logits_ref[...] = dot_nn(routed, router_ref[...])
        outbound_ref[...] = dot_nn(fill_ref[...], routed).astype(jnp.bfloat16)


def mixer_run(layer, size, act, selection, reset, decay_log, link, link_size, entering, projected, skip_weight,
              out_weight, current, norm_expert, router, fill):
    steps, _, channels = size.shape
    tokens = steps * CHUNKS
    states, width, experts = decay_log.shape[1], current.shape[1], router.shape[2]
    rank = selection.shape[2] - 2 * states
    tiles = channels // TILE
    low = jnp.bfloat16
    maps = VMEM((steps, states, CHUNKS, LANES), jnp.float32)
    return plain_call(
        functools.partial(run_kernel, (rank, states, steps, tiles)),
        (tiles,),
        [slab(steps), rows_of(tokens), whole(selection.shape), whole(reset.shape),
         layer_rows(layer, states), slab(states), rows_of(CHUNKS), rows_of(states), slab(steps, tiles),
         layer_rows(layer, 1), layer_columns(layer, width), whole(current.shape),
         layer_whole(layer, (1, width)), layer_whole(layer, (width, experts)), whole(fill.shape)],
        [slab(steps), rows_of(tokens), slab(states), whole((tokens, width)), whole((tokens, width)),
         whole((tokens, experts)), whole((fill.shape[0], width))],
        [
            shaped((steps, CHUNKS, channels)),
            shaped((tokens, channels), low),
            shaped((states, CHUNKS, channels)),
            shaped((tokens, width)),
            shaped((tokens, width), low),
            shaped((tokens, experts)),
            shaped((fill.shape[0], width), low),
        ],
        [maps, maps, VMEM((steps, CHUNKS, TILE), jnp.float32)],
        (size, act, selection, reset, decay_log, link, link_size, entering, projected, skip_weight, out_weight,
         current, norm_expert, router, fill),
        22,
    )


def turn_kernel(dims, grad_ref, out_weight_ref, gate_ref, mixed_ref, act_ref, gated_ref, size_ref,
                selection_ref, reset_ref, decay_ref,
                grad_y_ref, grad_gate_ref, grad_skip_ref, grad_out_ref, link_ref, link_size_ref, total_ref,
                total_size_ref, maps):
    rank, states, steps = dims

    @pl.when(pl.program_id(0) == 0)
    def _():
        spread_columns(selection_ref, rank + states, states, maps)

    grad = grad_ref[...]
    grad_out_ref[...] = dot_tn(gated_ref[...], grad).astype(jnp.bfloat16)
    gated = dot_nt(grad, out_weight_ref[...]).reshape(steps, CHUNKS, TILE)
    gate = gate_ref[...]
    share = jax.nn.sigmoid(gate)
    grad_y = gated * (gate * share)
    grad_y_ref[...] = grad_y
    grad_gate = gated * mixed_ref[...] * (share * (1.0 + gate * (1.0 - share)))
    grad_gate_ref[...] = grad_gate.reshape(steps * CHUNKS, TILE).astype(jnp.bfloat16)
    by_skip = grad_y * act_ref[...].astype(jnp.float32).reshape(steps, CHUNKS, TILE)
    grad_skip_ref[...] = jnp.sum(jnp.sum(by_skip, axis=0), axis=0, keepdims=True)

    def scan(lanes):
        rates = rate_rows(rates_of(decay_ref[:, lanes]))

        def one(at, carry):
            step = steps - 1 - at
            size, grad_y = size_ref[step, :, lanes] + reset_ref[step], grad_y_ref[step, :, lanes]
            new = []
            for n in range(states):
                new.append(jnp.exp2(size * rates[n]) * (carry[n] + grad_y * maps[step, n]))
            return tuple(new) + (carry[states] + size,)

        zero = jnp.zeros((CHUNKS, LANES), jnp.float32)
        found = lax.fori_loop(0, steps, one, (zero,) * (states + 1), unroll=4)
        links, totals, link_size, total_size = chunk_links(found, found[states], rates, True)
        link_size_ref[:, lanes] = link_size
        total_size_ref[:, lanes] = total_size
        for n in range(states):
            link_ref[n, :, lanes] = links[n]
            total_ref[n : n + 1, lanes] = totals[n]

    each_part(scan)


def mixer_turn(layer, grad_low, out_weight, projected, mixed, act, gated, size, selection, reset, decay_log):
    steps, _, channels = size.shape
    tokens = steps * CHUNKS
    states, width = decay_log.shape[1], grad_low.shape[1]
    rank = selection.shape[2] - 2 * states
    tiles = channels // TILE
    low = jnp.bfloat16
    return plain_call(
        functools.partial(turn_kernel, (rank, states, steps)),
        (tiles,),
        [whole(grad_low.shape), layer_columns(layer, width), slab(steps, tiles), slab(steps), rows_of(tokens),
         rows_of(tokens), slab(steps), whole(selection.shape), whole(reset.shape), layer_rows(layer, states)],
        [slab(steps), pl.BlockSpec((tokens, TILE), lambda c: (0, tiles + c)), rows_of(1),
         pl.BlockSpec((TILE, width), lambda c: (c, 0)),
         slab(states), rows_of(CHUNKS), rows_of(states), rows_of(1)],
        [
            shaped((steps, CHUNKS, channels)),
            shaped((tokens, 2 * channels), low),
            shaped((1, channels)),
            shaped((channels, width), low),
            shaped((states, CHUNKS, channels)),
            shaped((CHUNKS, channels)),
            shaped((states, channels)),
            shaped((1, channels)),
        ],
        [VMEM((steps, states, CHUNKS, LANES), jnp.float32)],
        (grad_low, out_weight, projected, mixed, act, gated, size, selection, reset, decay_log),
        14,
    )


def back_kernel(dims, size_ref, act_ref, grad_ref, decay_ref, selection_ref, reset_ref, begin_ref, link_ref,
                link_size_ref, entering_ref, step_ref, step_bias_ref, skip_ref,
                grad_act_ref, grad_decay_ref, grad_bias_ref, grad_step_ref, grad_selection_ref,
                in_maps, out_maps, levels, decays, grad_in, grad_out, grad_size, grad_rate, grad_all, pushed, acted):
    rank, states, steps, tiles = dims
    tokens = steps * CHUNKS

    @pl.when(pl.program_id(0) == 0)
    def _():
        spread_columns(selection_ref, rank, states, in_maps)
        spread_columns(selection_ref, rank + states, states, out_maps)
        grad_in[...] = jnp.zeros_like(grad_in)
        grad_out[...] = jnp.zeros_like(grad_out)

    skip = skip_ref[...]
    size = size_ref[...]
    act = act_ref[...].astype(jnp.float32).reshape(size.shape)
    acted[...] = act
    pushed[...] = size * act

    def scan(lanes):
        true_rates = -jnp.exp(decay_ref[:, lanes])
        rates = rate_rows(true_rates * LOG2E)
        begin = []
        for n in range(states):
            levels[0, n] = begin_ref[n, :, lanes]
            begin.append(begin_ref[n, :, lanes])

        def ahead(step, carry):
            size, value = size_ref[step, :, lanes] + reset_ref[step], pushed[step, :, lanes]
            new = []
            for n in range(states):
                decay = jnp.exp2(size * rates[n])
                decays[step, n] = decay
                level = decay * carry[n] + value * in_maps[step, n]
                levels[step + 1, n] = level
                new.append(level)
            return tuple(new)

        lax.fori_loop(0, steps, ahead, tuple(begin), unroll=4)
        link_size = link_size_ref[:, lanes]
        tail = []
        for n in range(states):
            tail.append(
                link_ref[n, :, lanes] + jnp.exp2(link_size * rates[n]) * entering_ref[n : n + 1, lanes])
            grad_rate[n] = jnp.zeros((CHUNKS, LANES), jnp.float32)

        def retreat(at, carry):
            step = steps - 1 - at
            plain, act, grad, value = (
                ref[step, :, lanes] for ref in (size_ref, acted, grad_ref, pushed))
            by_rate = jnp.zeros((CHUNKS, LANES), jnp.float32)
            by_input = jnp.zeros((CHUNKS, LANES), jnp.float32)
            new = []
            for n in range(states):
                spot = slice(n * LANES, (n + 1) * LANES)
                back = out_maps[step, n] * grad + carry[n]
                grad_out[step, :, spot] += grad * levels[step + 1, n]
                grad_in[step, :, spot] += back * value
                by_input = by_input + back * in_maps[step, n]
                passed = decays[step, n] * back
                new.append(passed)
                pull = passed * levels[step, n]
                by_rate = by_rate + pull * rates[n]
                grad_rate[n] += pull * plain
            grad_size[step, :, lanes] = by_rate * (1.0 / LOG2E) + act * by_input
            grad_act_ref[step, :, lanes] = plain * by_input
            return tuple(new)

        lax.fori_loop(0, steps, retreat, tuple(tail), unroll=2)
        for n in range(states):
            grad_decay_ref[n : n + 1, lanes] = (
                jnp.sum(grad_rate[n], axis=0, keepdims=True) * true_rates[n : n + 1, :]
            )

    each_part(scan)
    grad_act_ref[...] += grad_ref[...] * skip
    tile = pl.program_id(0)
    grad_all[:, pl.ds(pl.multiple_of(tile * TILE, TILE), TILE)] = grad_size[...].reshape(tokens, TILE)

    @pl.when(pl.program_id(0) == tiles - 1)
    def _():
        rank_low = selection_ref[...].reshape(tokens, selection_ref.shape[2])[:, :rank].astype(jnp.bfloat16)
        linear = dot_nn(rank_low, step_ref[...]) + step_bias_ref[...]
        grad_linear = grad_all[...] * jax.nn.sigmoid(linear)
        grad_bias_ref[...] = jnp.sum(grad_linear, axis=0, keepdims=True)
        grad_low = grad_linear.astype(jnp.bfloat16)
        grad_step_ref[...] = dot_tn(rank_low, grad_low)
        grad_rank = dot_nt(grad_low, step_ref[...])
        size = states * LANES
        row = lax.broadcasted_iota(jnp.int32, (size, states), 0)
        column = lax.broadcasted_iota(jnp.int32, (size, states), 1)
        pick = ((row >= column * LANES) & (row < (column + 1) * LANES)).astype(jnp.float32)
        pick = pick.astype(jnp.bfloat16)
        found = [grad_rank]
        for ref in (grad_in, grad_out):
            full = ref[...].reshape(tokens, size)
            high = full.astype(jnp.bfloat16)
            rest = (full - high.astype(jnp.float32)).astype(jnp.bfloat16)
            found.append(dot_nn(high, pick) + dot_nn(rest, pick))
        grad_selection_ref[...] = jnp.concatenate(found, axis=1).astype(jnp.bfloat16)


def mixer_back(layer, size, act, grad_y, decay_log, selection, reset, begin, link, link_size, entering,
               step_weight, step_bias, skip_weight):
    steps, _, channels = size.shape
    tokens = steps * CHUNKS
    states = decay_log.shape[1]
    columns = selection.shape[2]
    rank = columns - 2 * states
    tiles = channels // TILE
    f32 = jnp.float32
    maps = VMEM((steps, states, CHUNKS, LANES), f32)
    return plain_call(
        functools.partial(back_kernel, (rank, states, steps, tiles)),
        (tiles,),
        [slab(steps), rows_of(tokens), slab(steps), layer_rows(layer, states), whole(selection.shape),
         whole(reset.shape), slab(states), slab(states), rows_of(CHUNKS), rows_of(states),
         layer_whole(layer, (rank, channels)), layer_whole(layer, (1, channels)), layer_rows(layer, 1)],
        [slab(steps), rows_of(states), whole((1, channels)), whole((rank, channels)),
         whole((tokens, columns))],
        [
            shaped((steps, CHUNKS, channels)),
            shaped((states, channels)),
            shaped((1, channels)),
            shaped((rank, channels)),
            shaped((tokens, columns), jnp.bfloat16),
        ],
        [maps, maps, VMEM((steps + 1, states, CHUNKS, LANES), f32), maps,
         VMEM((steps, CHUNKS, states * LANES), f32), VMEM((steps, CHUNKS, states * LANES), f32),
         VMEM((steps, CHUNKS, TILE), f32), VMEM((states, CHUNKS, LANES), f32), VMEM((tokens, channels), f32)]
        + [VMEM((steps, CHUNKS, TILE), f32)] * 2,
        (size, act, grad_y, decay_log, selection, reset, begin, link, link_size, entering, step_weight,
         step_bias, skip_weight),
        35,
    )


def conv_back_kernel(dims, grad_act_ref, grad_selection_ref, state_ref, value_ref, rim_ref, mask_ref,
                     conv_ref, conv_bias_ref, act_ref, grad_step_ref, grad_decay_ref, grad_bias_ref,
                     grad_skip_ref, half_ref, grad_value_ref, edge_ref, rim_grad_ref, channel_ref,
                     extended, passed):
    taps, states, steps = dims
    lanes = grad_act_ref.shape[2]
    extend(value_ref, rim_ref, extended, taps)
    bias = conv_bias_ref[...]
    grad_selection = grad_selection_ref[...]
    from_selection = dot_nt(grad_selection, state_ref[...]).reshape(steps, CHUNKS, lanes)
    passed[:steps] = grad_act_ref[...] + from_selection
    passed[steps:] = jnp.zeros((taps - 1, CHUNKS, lanes), jnp.float32)
    zero = jnp.zeros((CHUNKS, lanes), jnp.float32)

    def keep(offset, step):
        return jnp.concatenate([mask_ref[offset - 1, step]] * (lanes // LANES), axis=1)

    def ahead(step, carry):
        convolved = conv_slab(extended, step, mask_ref, conv_ref, bias, taps)
        share = jax.nn.sigmoid(convolved)
        grad = passed[step] * (share * (1.0 + convolved * (1.0 - share)))
        passed[step] = grad
        new = [carry[0] + grad, carry[1] + grad * extended[step + taps - 1]]
        for offset in range(1, taps):
            kept = grad * keep(offset, step)
            new.append(carry[offset + 1] + kept * extended[step + taps - 1 - offset])
        return tuple(new)

    sums = lax.fori_loop(0, steps, ahead, (zero,) * (taps + 1), unroll=2)

    def reach(step, last):
        total = zero
        for offset in range(last):
            at = step + offset
            part = conv_ref[offset : offset + 1, :] * passed[at]
            if offset:
                part = part * keep(offset, at)
            total = total + part
        return total

    def back(pair, carry):
        both = [reach(2 * pair + half, taps) for half in (0, 1)]
        rows = pl.ds(pl.multiple_of(pair * 2 * CHUNKS, 2 * CHUNKS), 2 * CHUNKS)
        grad_value_ref[rows, :] = jnp.concatenate(both, axis=0).astype(jnp.bfloat16)
        return carry

    safe = (steps - taps + 1) // 2
    lax.fori_loop(0, safe, back, 0, unroll=2)
    place = lax.broadcasted_iota(jnp.int32, (CHUNKS, lanes), 0)
    ends = {}
    for j in range(taps - 1):
        before = zero
        for offset in range(taps - 1 - j, taps):
            at = j - taps + 1 + offset
            before = before + conv_ref[offset : offset + 1, :] * (
                passed[at] * keep(offset, at)
            )
        rim_grad_ref[j : j + 1, :] = before[0:1]
        ends[steps - taps + 1 + j] = jnp.where(
            place < CHUNKS - 1, pltpu.roll(before, CHUNKS - 1, axis=0), 0.0
        )
    for pair in range(safe, steps // 2):
        both = []
        for step in (2 * pair, 2 * pair + 1):
            total = reach(step, min(taps, steps - step))
            if step in ends:
                total = total + ends[step]
                j = step - steps + taps - 1
                edge_ref[j : j + 1, :] = total[CHUNKS - 1 : CHUNKS]
            both.append(total)
        grad_value_ref[2 * pair * CHUNKS : (2 * pair + 2) * CHUNKS, :] = jnp.concatenate(
            both, axis=0
        ).astype(jnp.bfloat16)
    small = jnp.zeros((CHUNKS, lanes), jnp.float32)
    rows = [jnp.sum(part, axis=0, keepdims=True) for part in sums[1:] + sums[:1]]
    rows += [grad_bias_ref[...], grad_skip_ref[...]]
    for index, row in enumerate(rows):
        small = jnp.where(place == index, row, small)
    grad_state = dot_tn(grad_selection, act_ref[...])
    parts = [grad_state, grad_step_ref[...], grad_decay_ref[...], small]
    used = sum(part.shape[0] for part in parts)
    parts.append(jnp.zeros((2 * LANES - used, lanes), jnp.float32))
    channel_ref[...] = jnp.concatenate(parts, axis=0).T.astype(jnp.bfloat16)


def mixer_conv_back(layer, grad_act, grad_selection, state_weight, projected, rim, masks, conv_weight,
                    conv_bias, act, grad_step, grad_decay, grad_bias, grad_skip, halved):
    steps, _, channels = grad_act.shape
    tokens = steps * CHUNKS
    taps, columns = conv_weight.shape[1], state_weight.shape[2]
    states, rank = grad_decay.shape[0], grad_step.shape[0]
    lanes = 2 * LANES
    f32 = jnp.float32

    def cubes(count):
        return pl.BlockSpec((count, CHUNKS, lanes), lambda c: (0, 0, c))

    def rows(count):
        return pl.BlockSpec((count, lanes), lambda c: (0, c))

    def weight_rows(count):
        return pl.BlockSpec((None, count, lanes), lambda c: (layer, 0, c))

    return plain_call(
        functools.partial(conv_back_kernel, (taps, states, steps)),
        (channels // lanes,),
        [cubes(steps), whole(grad_selection.shape),
         pl.BlockSpec((None, lanes, columns), lambda c: (layer, c, 0)), cubes(steps),
         rows(taps - 1), whole(masks.shape), weight_rows(taps), weight_rows(1),
         rows(tokens), rows(rank), rows(states), rows(1), rows(1), ANYWHERE],
        [rows(tokens), rows(taps - 1), rows(taps - 1),
         pl.BlockSpec((lanes, 2 * LANES), lambda c: (c, 0))],
        [
            shaped((tokens, 2 * channels), jnp.bfloat16),
            shaped((taps - 1, channels)),
            shaped((taps - 1, channels)),
            shaped((channels, 2 * LANES), jnp.bfloat16),
        ],
        [VMEM((steps + taps - 1, CHUNKS, lanes), f32), VMEM((steps + taps - 1, CHUNKS, lanes), f32)],
        (grad_act, grad_selection, state_weight, projected, rim, masks, conv_weight, conv_bias, act, grad_step,
         grad_decay, grad_bias, grad_skip, halved),
        10,
        {13: 0},
    )


def hand_on(layer, count, reverse, total_ref, size_ref, decay_ref, out_ref, scratch, between, after):
    (mine, mine_length, near, near_length, both, both_length, far, far_length,
     send, recv, send_length, recv_length) = scratch
    here = lax.axis_index("wide")
    group = lax.axis_index("narrow")
    pairs = count // 2
    pair, side = here // 2, lax.rem(here, 2)
    partner = here + 1 - 2 * side
    others = [lax.rem(pair + k, pairs) for k in range(1, pairs)]
    f32 = jnp.float32
    barrier = pltpu.get_barrier_semaphore()
    pl.semaphore_signal(barrier, inc=1, device_id=(partner, group), device_id_type=MESH)
    for other in others:
        pl.semaphore_signal(barrier, inc=1, device_id=(2 * other + side, group), device_id_type=MESH)
    mine[...] = total_ref[...].astype(mine.dtype)
    mine_length[...] = size_ref[...]
    rate = rates_of(decay_ref[layer])
    pl.semaphore_wait(barrier, pairs)

    def hand(index, source, source_length, target, target_length, window):
        copies = []
        for src, dst, out, back in (
            (source, target, send, recv), (source_length, target_length, send_length, recv_length)):
            copies.append(pltpu.make_async_remote_copy(
                src_ref=src, dst_ref=dst, send_sem=out.at[index], recv_sem=back.at[index],
                device_id=(window, group), device_id_type=MESH))
            copies[-1].start()
        return copies

    first = hand(0, mine, mine_length, near, near_length, partner)
    between()
    for copy in first:
        copy.wait_recv()
    second_here = (side == 0) if reverse else (side == 1)
    own, own_length = total_ref[...], size_ref[...]
    met, met_length = near[...].astype(f32), near_length[...]
    late_length = jnp.where(second_here, own_length, met_length)
    early = jnp.where(second_here, met, own)
    late = jnp.where(second_here, own, met)
    both[...] = (jnp.exp2(late_length * rate) * early + late).astype(both.dtype)
    both_length[...] = own_length + met_length
    sent = []
    for k, other in enumerate(others):
        sent.append(hand(
            1 + k, both, both_length, far.at[pair], far_length.at[pair], 2 * other + side))
    after()
    for copies in sent:
        for copy in copies:
            copy.wait_recv()
    level = jnp.zeros(own.shape, f32)
    for at in range(pairs - 1, -1, -1) if reverse else range(pairs):
        valid = (pair < at) if reverse else (pair > at)
        step = jnp.exp2(far_length[at] * rate) * level + far[at].astype(f32)
        level = jnp.where(valid, step, level)
    step = jnp.exp2(met_length * rate) * level + met
    out_ref[...] = jnp.where(second_here, step, level)
    for copies in [first] + sent:
        for copy in copies:
            copy.wait_send()


LINK_REFS = 12


def link_scratch(count, states, channels):
    pairs = count // 2
    f32, low = jnp.float32, jnp.bfloat16
    dma = pltpu.SemaphoreType.DMA((pairs,))
    return [
        VMEM((states, channels), low), VMEM((1, channels), f32),
        VMEM((states, channels), low), VMEM((1, channels), f32),
        VMEM((states, channels), low), VMEM((1, channels), f32),
        VMEM((pairs, states, channels), low), VMEM((pairs, 1, channels), f32),
        dma, dma, dma, dma,
    ]


def link_call(kernel, total, size, decay_log, beside, out_shapes, scratch, identity):
    states, channels = total.shape
    inside = pl.BlockSpec(memory_space=VMEM)
    return pl.pallas_call(
        kernel,
        out_shape=[shaped((states, channels))] + out_shapes,
        in_specs=[inside] * 3 + [ANYWHERE] * len(beside),
        out_specs=[inside] + [ANYWHERE] * len(out_shapes),
        scratch_shapes=link_scratch(lax.axis_size("wide"), states, channels) + scratch,
        compiler_params=pltpu.CompilerParams(
            collective_id=identity, has_side_effects=True, vmem_limit_bytes=60 * MIB
        ),
        cost_estimate=microseconds(12),
    )(total, size, decay_log, *beside)


def ahead_kernel(layer, count, wanted, total_ref, size_ref, decay_ref, *refs):
    arrays = len(wanted)
    sources, out_ref, targets = refs[:arrays], refs[arrays], refs[arrays + 1 : 2 * arrays + 1]
    scratch, (*held, got, put) = refs[2 * arrays + 1 :][:LINK_REFS], refs[2 * arrays + 1 + LINK_REFS :]
    into = [
        pltpu.make_async_copy(sources[i].at[wanted[i]], held[i], got.at[i]) for i in range(arrays)]
    out = [pltpu.make_async_copy(held[i], targets[i], put.at[i]) for i in range(arrays)]
    for copy in into:
        copy.start()

    def after():
        for i in range(arrays):
            into[i].wait()
            out[i].start()

    hand_on(layer, count, False, total_ref, size_ref, decay_ref, out_ref, scratch, lambda: None, after)
    for copy in out:
        copy.wait()


def handed_ahead(layer, total, size, decay_log, wanted, identity):
    shapes = [array.shape[1:] for array, _ in wanted]
    dma = pltpu.SemaphoreType.DMA((len(wanted),))
    return link_call(
        functools.partial(ahead_kernel, layer, lax.axis_size("wide"), tuple(which for _, which in wanted)),
        total, size, decay_log, [array for array, _ in wanted],
        [shaped(shape, array.dtype) for shape, (array, _) in zip(shapes, wanted)],
        [VMEM(shape, array.dtype) for shape, (array, _) in zip(shapes, wanted)] + [dma, dma],
        identity)


def behind_kernel(layer, count, total_ref, size_ref, decay_ref, rows_hbm, pre_hbm, hidden_hbm, grad_hbm,
                  out_ref, *refs):
    outs = len(refs) - LINK_REFS - 6
    outs //= 2
    targets, scratch = refs[:outs], refs[outs : outs + LINK_REFS]
    rows, pre, hidden_rows, grad, *found = refs[outs + LINK_REFS : -2]
    got, put = refs[-2:]
    members, _, hidden = pre.shape
    width = rows.shape[1]
    low = jnp.bfloat16
    loads = [
        pltpu.make_async_copy(source, target, got.at[i])
        for i, (source, target) in enumerate(
            ((rows_hbm, rows), (pre_hbm, pre), (hidden_hbm, hidden_rows), (grad_hbm, grad)))
    ]
    for load in loads:
        load.start()
    stores = [
        [pltpu.make_async_copy(found[i].at[s], targets[i].at[s], put.at[i, s]) for i in range(outs)]
        for s in range(members)
    ]

    def weights(s):
        up = dot_tn(rows[...], pre[s]).astype(low)
        down = dot_tn(hidden_rows[s], grad[...]).astype(low)
        if outs == 2:
            found[0][s], found[1][s] = up, down
        else:
            found[0][s, :width] = up
            for f in range(width // hidden):
                found[0][s, width + f * hidden : width + (f + 1) * hidden] = down[
                    :, f * hidden : (f + 1) * hidden]
        for store in stores[s]:
            store.start()

    def between():
        for load in loads:
            load.wait()
        weights(0)

    def after():
        for s in range(1, members):
            weights(s)

    hand_on(layer, count, True, total_ref, size_ref, decay_ref, out_ref, scratch, between, after)
    for pair in stores:
        for store in pair:
            store.wait()


def handed_back(layer, total, size, decay_log, rows, pre, hidden_rows, grad_rows, identity):
    members, _, hidden = pre.shape
    width = rows.shape[1]
    low = jnp.bfloat16
    sizes = [(2 * width, hidden)] if folds(width, hidden) else [(width, hidden), (hidden, width)]
    shapes = [(members,) + size for size in sizes]
    return link_call(
        functools.partial(behind_kernel, layer, lax.axis_size("wide")),
        total, size, decay_log, [rows, pre, hidden_rows, grad_rows],
        [shaped(shape, low) for shape in shapes],
        [VMEM(array.shape, low) for array in (rows, pre, hidden_rows, grad_rows)]
        + [VMEM(shape, low) for shape in shapes]
        + [pltpu.SemaphoreType.DMA((4,)), pltpu.SemaphoreType.DMA((len(shapes), members))],
        identity)


def bell(values):
    return 0.5 * (1.0 + lax.erf(values * 0.7071067811865476))


def expert_kernel(dims, backward, beside, which, *refs):
    count, groups, members, block, share, width, hidden = dims
    out_ref, perm_ref, up_hbm, down_hbm, *refs = refs
    if backward:
        pre_hbm, *refs = refs
    if beside:
        next_hbm, *refs = refs
    ret_ref, rows_hbm, *refs = refs
    if not backward:
        pre_hbm, *refs = refs
    low_hbm, *scratch = refs
    if beside:
        met_hbm, *scratch, leaving, met, next_send, next_recv, next_local = scratch
    (arrived, own, rows, pre, low, part, got, final, landed, up, down, total,
     there_send, there_recv, row_send, row_recv, sum_send, sum_recv, back_send, back_recv, local) = scratch
    f32, bf16 = jnp.float32, jnp.bfloat16
    here = lax.axis_index("wide")
    group = lax.axis_index("narrow")
    quads = count // members
    quad, member = here // members, lax.rem(here, members)
    lines = groups // 2
    line, core = group // 2, lax.rem(group, 2)
    near_group = group + 1 - 2 * core
    others = [(2 * away + c, 2 * lax.rem(line + away, lines) + c) for away in range(1, lines) for c in (0, 1)]
    early = 2 * (share // groups) // 16 * 16
    head, tail = pl.ds(0, early), pl.ds(early, share - early)

    loads = [
        pltpu.make_async_copy(up_hbm, up, local.at[0]),
        pltpu.make_async_copy(down_hbm, down, local.at[1]),
    ]
    if backward:
        loads.append(pltpu.make_async_copy(pre_hbm, pre, local.at[2]))
    for load in loads:
        load.start()
    if beside:
        source = next_hbm if which is None else next_hbm.at[which]
        next_load = pltpu.make_async_copy(source, leaving, next_local.at[0])
        next_load.start()

    def window_at(away, turn):
        return lax.rem(quad + away, quads) * members + lax.rem(member + turn, members)

    barrier = pltpu.get_barrier_semaphore()
    for peer in [near_group] + [other for _, other in others]:
        pl.semaphore_signal(barrier, inc=1, device_id=(here, peer), device_id_type=MESH)
    for away in range(quads):
        for turn in range(members):
            if away or turn:
                pl.semaphore_signal(
                    barrier, inc=1, device_id=(window_at(away, turn), group), device_id_type=MESH)
    pl.semaphore_wait(barrier, groups - 1 + count - 1)

    there = []

    def hand_over(k, source, target, send, recv):
        if k:
            place, peer = others[k - 1]
            away = place // 2
            landing, signal = (lines - away) * 2 + core, 2 * away - 1 + core
        else:
            peer, landing, signal = near_group, core, 0
        copy = pltpu.make_async_remote_copy(
            src_ref=source, dst_ref=target.at[landing], send_sem=send.at[k], recv_sem=recv.at[signal],
            device_id=(here, peer), device_id_type=MESH)
        copy.start()
        return copy

    def taken(k, target, send, recv):
        pltpu.make_async_remote_copy(
            src_ref=out_ref.at[group], dst_ref=target.at[0], send_sem=send.at[k], recv_sem=recv.at[k],
            device_id=(here, near_group), device_id_type=MESH).wait_recv()

    there = [hand_over(0, out_ref.at[near_group], arrived, there_send, there_recv)]
    for k, (_, other) in enumerate(others):
        there.append(hand_over(1 + k, out_ref.at[other], arrived, there_send, there_recv))
    arrived[core] = out_ref[group]

    def span(window, part=None):
        start, size = (0, share) if part is None else ((0, early), (early, share - early))[part]
        return pl.ds(pl.multiple_of(window * share + start, 16), size)

    sent = []
    ways = [(away, turn) for turn in range(members) for away in list(range(1, quads)) + [0] if away or turn]

    def carry(away, turn, part):
        window = window_at(away, turn)
        copy = pltpu.make_async_remote_copy(
            src_ref=own.at[lax.rem(member + turn, members), (head, tail)[part]],
            dst_ref=rows.at[span(here, part), :],
            send_sem=row_send.at[away, turn, part], recv_sem=row_recv.at[away, turn, part],
            device_id=(window, group), device_id_type=MESH)
        copy.start()
        sent.append(copy)

    taken(0, arrived, there_send, there_recv)
    order = perm_ref[...].reshape(members, share, groups * block)
    first = arrived[pl.ds(0, 2)].reshape(2 * block, width)
    own[:, head] = dot_nn(
        order[:, :early, : 2 * block].reshape(members * early, 2 * block), first
    ).astype(bf16).reshape(members, early, width)
    for away, turn in ways:
        carry(away, turn, 0)
    for k in range(1, groups - 1):
        taken(k, arrived, there_send, there_recv)
    own[:, tail] = dot_nn(
        order[:, early:].reshape(members * (share - early), groups * block),
        arrived[...].reshape(groups * block, width),
    ).astype(bf16).reshape(members, share - early, width)
    for away, turn in ways:
        carry(away, turn, 1)
    rows[span(here), :] = own[member]
    beside_copies = []

    def send_beside(turns):
        for turn in turns if beside else ():
            copy = pltpu.make_async_remote_copy(
                src_ref=leaving.at[lax.rem(member + turn, members)], dst_ref=met.at[member],
                send_sem=next_send.at[turn], recv_sem=next_recv.at[turn],
                device_id=(window_at(0, turn), group), device_id_type=MESH)
            copy.start()
            beside_copies.append(copy)

    if beside:
        next_load.wait()
        met[member] = leaving[member]
    send_beside([1])

    def arrive(away, turn):
        window = lax.rem(quad + quads - away, quads) * members + lax.rem(member + members - turn, members)
        for part in (0, 1):
            pltpu.make_async_remote_copy(
                src_ref=own.at[member, (head, tail)[part]], dst_ref=rows.at[span(window, part), :],
                send_sem=row_send.at[away, turn, part], recv_sem=row_recv.at[away, turn, part],
                device_id=(window, group), device_id_type=MESH).wait_recv()
        return window

    def compute(windows):
        size = len(windows) * share

        def one(s, carry):
            x = jnp.concatenate([rows[span(w), :] for w in windows], axis=0)
            if backward:
                grad_hidden = dot_nt(x, down[s])
                before = jnp.concatenate([pre[s, span(w), :] for w in windows], axis=0)
                slope = bell(before) + before * (0.3989422804014327 * jnp.exp(-0.5 * before * before))
                middle = (grad_hidden * slope).astype(bf16)
                y = dot_nt(middle, up[s])
            else:
                before = dot_nn(x, up[s])
                middle = (before * bell(before)).astype(bf16)
                y = dot_nn(middle, down[s])
            for index, w in enumerate(windows):
                piece = slice(index * share, (index + 1) * share)
                if not backward:
                    pre[s, span(w), :] = before[piece]
                low[s, span(w), :] = middle[piece]

            @pl.when(s == 0)
            def _():
                total[:size] = y

            @pl.when(s > 0)
            def _():
                total[:size] += y

            return carry

        lax.fori_loop(0, members, one, 0)
        for index, w in enumerate(windows):
            part[w] = total[index * share : (index + 1) * share].astype(bf16)

    def give_back(away, turn, window, part):
        copy = pltpu.make_async_remote_copy(
            src_ref=part_rows(window, part), dst_ref=got.at[here, (head, tail)[part]],
            send_sem=sum_send.at[away, turn, part], recv_sem=sum_recv.at[away, turn, part],
            device_id=(window, group), device_id_type=MESH)
        copy.start()
        sent.append(copy)

    def part_rows(window, which):
        return part.at[window, (head, tail)[which]]

    for load in loads:
        load.wait()
    windows = [here] + [arrive(0, turn) for turn in range(1, members)]
    compute(windows)
    for which in (1, 0):
        for turn in range(1, members):
            give_back(0, turn, windows[turn], which)
    got[here] = part[here]
    late = []
    for away in range(1, quads):
        for first in range(0, members, 2):
            windows = [arrive(away, turn) for turn in (first, first + 1)]
            compute(windows)
            for turn in (first, first + 1):
                give_back(away, turn, windows[turn - first], 1)
                late.append((away, turn, windows[turn - first]))
    for away, turn, window in late:
        give_back(away, turn, window, 0)
    send_beside(range(2, members))

    saves = [
        pltpu.make_async_copy(rows, rows_hbm, local.at[3]),
        pltpu.make_async_copy(low, low_hbm, local.at[4]),
    ]
    if not backward:
        saves.append(pltpu.make_async_copy(pre, pre_hbm, local.at[2]))
    for save in saves:
        save.start()

    def returned(which):
        for away, turn in ways:
            window = window_at(away, turn)
            pltpu.make_async_remote_copy(
                src_ref=part_rows(here, which), dst_ref=got.at[window, (head, tail)[which]],
                send_sem=sum_send.at[away, turn, which], recv_sem=sum_recv.at[away, turn, which],
                device_id=(window, group), device_id_type=MESH).wait_recv()
        place = (head, tail)[which]
        summed = got[pl.ds(0, members), place].astype(f32)
        for q in range(1, quads):
            summed = summed + got[pl.ds(q * members, members), place].astype(f32)
        return summed.astype(bf16)

    later = returned(1)
    rest = groups - 2
    final[pl.ds(2, rest)] = dot_tn(
        order[:, early:, 2 * block :].reshape(members * (share - early), rest * block),
        later.reshape(members * (share - early), width),
    ).astype(bf16).reshape(rest, block, width)
    home = []
    for k, (place, _) in enumerate(others):
        home.append(hand_over(1 + k, final.at[place], landed, back_send, back_recv))
    sooner = returned(0)
    final[pl.ds(0, 2)] = (
        dot_tn(order[:, :early, : 2 * block].reshape(members * early, 2 * block),
               sooner.reshape(members * early, width))
        + dot_tn(order[:, early:, : 2 * block].reshape(members * (share - early), 2 * block),
                 later.reshape(members * (share - early), width))
    ).astype(bf16).reshape(2, block, width)
    home.append(hand_over(0, final.at[1 - core], landed, back_send, back_recv))
    ret_ref[group] = final[core]
    for k in range(groups - 1):
        taken(k, landed, back_send, back_recv)
    ret_ref[near_group] = landed[1 - core]
    for place, other in others:
        ret_ref[other] = landed[place]
    if beside:
        for copy in beside_copies:
            copy.wait_recv()
        saves.append(pltpu.make_async_copy(met, met_hbm, next_local.at[1]))
        saves[-1].start()
    for copy in there + sent + home + beside_copies:
        copy.wait_send()
    for save in saves:
        save.wait()


def expert_pass(outbound, perm, weights, pre, identity, beside=None, which=None):
    count, groups = lax.axis_size("wide"), lax.axis_size("narrow")
    backward = pre is not None
    _, block, width = outbound.shape
    members, _, hidden = weights[0].shape
    share = perm.shape[0] // members
    quads = count // members
    total = count * share
    low, f32 = jnp.bfloat16, jnp.float32
    dims = (count, groups, members, block, share, width, hidden)
    inside = pl.BlockSpec(memory_space=VMEM)
    args = (outbound, perm) + tuple(weights) + ((pre,) if backward else ())
    args += () if beside is None else (beside,)
    outs = [shaped((groups, block, width), low), shaped((total, width), low)]
    outs += ([] if backward else [shaped((members, total, hidden))]) + [shaped((members, total, hidden), low)]
    dma = pltpu.SemaphoreType.DMA
    more = []
    if beside is not None:
        shape = beside.shape[-3:]
        outs.append(shaped(shape, low))
        more = [VMEM(shape, low), VMEM(shape, low), dma((members,)), dma((members,)), dma((2,))]
    return pl.pallas_call(
        functools.partial(expert_kernel, dims, backward, beside is not None, which),
        out_shape=outs,
        in_specs=[inside, inside] + [ANYWHERE] * (len(args) - 2),
        out_specs=[inside] + [ANYWHERE] * (len(outs) - 1),
        scratch_shapes=[
            VMEM((groups, block, width), low),
            VMEM((members, share, width), low),
            VMEM((total, width), low),
            VMEM((members, total, hidden), f32),
            VMEM((members, total, hidden), low),
            VMEM((count, share, width), low),
            VMEM((count, share, width), low),
            VMEM((groups, block, width), low),
            VMEM((groups, block, width), low),
            VMEM((members, width, hidden), low),
            VMEM((members, hidden, width), low),
            VMEM((members * share, width), f32),
            dma((groups - 1,)), dma((groups - 1,)),
            dma((quads, members, 2)), dma((quads, members, 2)),
            dma((quads, members, 2)), dma((quads, members, 2)),
            dma((groups - 1,)), dma((groups - 1,)),
            dma((5,)),
        ] + more,
        compiler_params=pltpu.CompilerParams(
            collective_id=identity, has_side_effects=True, vmem_limit_bytes=60 * MIB
        ),
        cost_estimate=microseconds(65),
    )(*args)


def expert_order(experts, groups, block, capacity):
    share = groups * capacity
    row = jnp.arange(experts * share, dtype=jnp.int32)
    expert, rest = row // share, row % share
    source = (rest // capacity) * block + expert * capacity + rest % capacity
    return (source[:, None] == jnp.arange(groups * block, dtype=jnp.int32)[None, :]).astype(jnp.bfloat16)


def between_members(arrays):
    count, members = lax.axis_size("wide"), arrays[0].shape[0]
    quads = [list(range(first, first + members)) for first in range(0, count, members)]
    return [
        lax.all_to_all(values, "wide", split_axis=0, concat_axis=0, tiled=True, axis_index_groups=quads)
        for values in arrays
    ]


def slice_kernel(layer, from_ref, to_ref, held, got, put):
    count = held.shape[0]
    incoming = [pltpu.make_async_copy(from_ref.at[layer, e], held.at[e], got.at[e]) for e in range(count)]
    outgoing = [pltpu.make_async_copy(held.at[e], to_ref.at[e], put.at[e]) for e in range(count)]
    for copy in incoming:
        copy.start()
    for into, out in zip(incoming, outgoing):
        into.wait()
        out.start()
    for out in outgoing:
        out.wait()


def layer_of(values, layer):
    shape = values.shape[1:]
    return pl.pallas_call(
        functools.partial(slice_kernel, layer),
        out_shape=shaped(shape, values.dtype),
        in_specs=[ANYWHERE],
        out_specs=ANYWHERE,
        scratch_shapes=[
            VMEM(shape, values.dtype), pltpu.SemaphoreType.DMA(shape[:1]), pltpu.SemaphoreType.DMA(shape[:1])],
        compiler_params=pltpu.CompilerParams(vmem_limit_bytes=60 * MIB),
        cost_estimate=microseconds(2),
    )(values)


def folds(width, hidden):
    return 0 if hidden % LANES else width // hidden


def widen_kernel(arrays, *refs):
    refs, (up_ref, down_ref) = refs[:arrays], refs[-2:]
    width, hidden = up_ref.shape
    if arrays == 2:
        up_ref[...] = refs[0][...].astype(jnp.float32)
        down_ref[...] = refs[1][...].astype(jnp.float32)
        return
    up_ref[...] = refs[0][:width].astype(jnp.float32)
    for f in range(width // hidden):
        down_ref[:, f * hidden : (f + 1) * hidden] = refs[0][
            width + f * hidden : width + (f + 1) * hidden].astype(jnp.float32)


def widened(layer, layers, arrays, width, hidden, held):
    experts = arrays[0].shape[0]
    count = len(arrays)
    return plain_call(
        functools.partial(widen_kernel, count),
        (experts,),
        [pl.BlockSpec((None,) + array.shape[1:], lambda e: (e, 0, 0)) for array in arrays]
        + [ANYWHERE] * len(held),
        [pl.BlockSpec((None, None, width, hidden), lambda e: (layer, e, 0, 0)),
         pl.BlockSpec((None, None, hidden, width), lambda e: (layer, e, 0, 0))],
        [shaped((layers, experts, width, hidden)), shaped((layers, experts, hidden, width))],
        [],
        tuple(arrays) + tuple(held),
        60,
        {count + k: k for k in range(len(held))},
    )


def sum_kernel(dims, *refs):
    count, lines, sizes, first_rows, width = dims
    total = len(sizes)
    arrays, out_ref = refs[:total], refs[total]
    (own, near, over, spun, spun_first, home, core_send, core_recv, load, over_send, over_recv,
     spin_send, spin_recv, spin_first_send, spin_first_recv, home_send, home_recv) = refs[total + 1 :]
    rows = sum(sizes)
    later = rows - first_rows
    here = lax.axis_index("wide")
    group = lax.axis_index("narrow")
    line, core = group // 2, lax.rem(group, 2)
    half = count // 2
    low, f32 = jnp.bfloat16, jnp.float32

    def window_of(position):
        position = lax.rem(position + 2 * count, count)
        upper = position // half
        return 2 * position * (1 - upper) + (2 * (count - 1 - position) + 1) * upper

    odd = lax.rem(here, 2)
    spot = (here // 2) * (1 - odd) + (count - 1 - here // 2) * odd
    ring = (window_of(spot + 1), window_of(spot - 1))
    peer = 2 * line + 1 - core
    lines_away = [lax.rem(line + k, lines) for k in range(1, lines)]

    barrier = pltpu.get_barrier_semaphore()
    for window in ring:
        pl.semaphore_signal(barrier, inc=1, device_id=(window, group), device_id_type=MESH)
    pl.semaphore_signal(barrier, inc=1, device_id=(here, peer), device_id_type=MESH)
    for other in lines_away:
        pl.semaphore_signal(barrier, inc=1, device_id=(here, 2 * other + core), device_id_type=MESH)
    pl.semaphore_wait(barrier, 2 + lines)

    order = [spot + half]
    for away in range(half - 1, 0, -1):
        order += [spot + away, spot - away]
    order = [window_of(position) for position in order + [spot]]
    sent, held = [], []
    for k, window in enumerate(order):
        held.append([])
        start = 0
        for i, size in enumerate(sizes):
            place = pl.ds(start, size)
            start += size
            copy = pltpu.make_async_remote_copy(
                src_ref=arrays[i].at[window, :, 1 - core], dst_ref=near.at[window, :, place],
                send_sem=core_send.at[k, i], recv_sem=core_recv.at[k, i],
                device_id=(here, peer), device_id_type=MESH)
            copy.start()
            mine = pltpu.make_async_copy(
                arrays[i].at[window, :, core], own.at[window, :, place], load.at[k, i])
            mine.start()
            sent.append(copy)
            held[-1].append((copy, mine))

    ahead, behind = pl.ds(0, first_rows), pl.ds(first_rows, later)
    cut_first = first_rows // 32 * 16
    cut_later = later // 32 * 16
    parts_first = (pl.ds(0, cut_first), pl.ds(cut_first, first_rows - cut_first))
    parts_later = (
        pl.ds(first_rows, cut_later), pl.ds(first_rows + cut_later, later - cut_later))
    parts_got = (pl.ds(0, cut_later), pl.ds(cut_later, later - cut_later))

    def meet(k):
        window = order[k]
        for copy, mine in held[k]:
            copy.wait_recv()
            mine.wait()

        def one(at, carry):
            place = pl.ds(pl.multiple_of(at * 16, 16), 16)
            for x in range(lines):
                own[window, x, place] = (
                    own[window, x, place].astype(f32) + near[window, x, place].astype(f32)
                ).astype(low)
            return carry

        lax.fori_loop(0, rows // 16, one, 0)
        for j, other in enumerate(lines_away):
            copy = pltpu.make_async_remote_copy(
                src_ref=own.at[window, other, ahead], dst_ref=over.at[j, window],
                send_sem=over_send.at[j, k], recv_sem=over_recv.at[j, k],
                device_id=(here, 2 * other + core), device_id_type=MESH)
            copy.start()
            sent.append(copy)
            crossing[k].append(copy)

    crossing = [[] for _ in order]

    def spin_later(step):
        for way, sign in ((0, 1), (1, -1)):
            window = window_of(spot + sign * (half - step))
            if step == 0:
                which, got_which = parts_later[way], parts_got[way]
                if not (later - cut_later if way else cut_later):
                    continue
            else:
                which, got_which = behind, pl.ds(0, later)
                add_which, add_got = (
                    (parts_later[way], parts_got[way]) if step == 1 else (which, got_which))
                if turns[way]:
                    turns[way][-1].wait_recv()
                    own[window, :, add_which] = (
                        own[window, :, add_which].astype(f32)
                        + spun[way, step - 1, :, add_got].astype(f32)
                    ).astype(low)
            copy = pltpu.make_async_remote_copy(
                src_ref=own.at[window, :, which], dst_ref=spun.at[way, step, :, got_which],
                send_sem=spin_send.at[way, step], recv_sem=spin_recv.at[way, step],
                device_id=(ring[way], group), device_id_type=MESH)
            copy.start()
            sent.append(copy)
            turns[way].append(copy)

    def cross(k):
        window = order[k]
        value = own[window, line, ahead].astype(f32)
        for j, copy in enumerate(crossing[k]):
            copy.wait_recv()
            value = value + over[j, window].astype(f32)
        return value

    first_turns = ([], [])

    def spin_first(step):
        for way, sign in ((0, 1), (1, -1)):
            k = 0 if step == 0 else 2 * step - 1 + way
            window = order[k]
            if step or way == 0:
                own[window, line, ahead] = cross(k).astype(low)
            if step == 0:
                which = parts_first[way]
            else:
                which = ahead
                add_which = parts_first[way] if step == 1 else which
                first_turns[way][-1].wait_recv()
                own[window, line, add_which] = (
                    own[window, line, add_which].astype(f32)
                    + spun_first[way, step - 1, add_which].astype(f32)
                ).astype(low)
            copy = pltpu.make_async_remote_copy(
                src_ref=own.at[window, line, which], dst_ref=spun_first.at[way, step, which],
                send_sem=spin_first_send.at[way, step], recv_sem=spin_first_recv.at[way, step],
                device_id=(ring[way], group), device_id_type=MESH)
            copy.start()
            sent.append(copy)
            first_turns[way].append(copy)

    turns = ([], [])
    meet(0)
    spin_later(0)
    for step in range(1, half):
        meet(2 * step - 1)
        meet(2 * step)
        spin_first(step - 1)
        spin_later(step)
    meet(len(order) - 1)
    spin_first(half - 1)
    summed = own[here, :, behind].astype(f32)
    for way in (0, 1):
        turns[way][-1].wait_recv()
        summed = summed + spun[way, half - 1].astype(f32)
    own[here, :, behind] = summed.astype(low)
    homes = []
    for j, other in enumerate(lines_away):
        copy = pltpu.make_async_remote_copy(
            src_ref=own.at[here, other, behind], dst_ref=home.at[j],
            send_sem=home_send.at[j], recv_sem=home_recv.at[j],
            device_id=(here, 2 * other + core), device_id_type=MESH)
        copy.start()
        sent.append(copy)
        homes.append(copy)

    summed = cross(len(order) - 1)
    for way in (0, 1):
        first_turns[way][-1].wait_recv()
        summed = summed + spun_first[way, half - 1].astype(f32)
    out_ref[ahead, :] = summed
    value = own[here, line, behind].astype(f32)
    for j, copy in enumerate(homes):
        copy.wait_recv()
        value = value + home[j].astype(f32)
    out_ref[behind, :] = value
    for copy in sent:
        copy.wait_send()


def summed_shares(arrays, identity):
    count, groups = lax.axis_size("wide"), lax.axis_size("narrow")
    lines, half = groups // 2, count // 2
    width = arrays[0].shape[2]
    if any(array.shape[1] % 16 for array in arrays):
        packed = jnp.concatenate(arrays, axis=1)
        arrays = [jnp.pad(packed, ((0, 0), (0, -packed.shape[1] % 16), (0, 0)))]
    sizes = tuple(array.shape[1] for array in arrays)
    rows = sum(sizes)
    first = max(32, rows * 11 // 20 // 16 * 16)
    later = rows - first
    low = jnp.bfloat16
    dma = pltpu.SemaphoreType.DMA
    return pl.pallas_call(
        functools.partial(sum_kernel, (count, lines, sizes, first, width)),
        out_shape=jax.ShapeDtypeStruct((rows, width), jnp.float32),
        in_specs=[ANYWHERE] * len(arrays),
        out_specs=pl.BlockSpec(memory_space=VMEM),
        scratch_shapes=[
            VMEM((count, lines, rows, width), low),
            VMEM((count, lines, rows, width), low),
            VMEM((lines - 1, count, first, width), low),
            VMEM((2, half, lines, later, width), low),
            VMEM((2, half, first, width), low),
            VMEM((lines - 1, later, width), low),
            dma((count, len(arrays))), dma((count, len(arrays))), dma((count, len(arrays))),
            dma((lines - 1, count)), dma((lines - 1, count)),
            dma((2, half)), dma((2, half)),
            dma((2, half)), dma((2, half)),
            dma((lines - 1,)), dma((lines - 1,)),
        ],
        compiler_params=pltpu.CompilerParams(
            collective_id=identity, has_side_effects=True, vmem_limit_bytes=60 * MIB
        ),
        cost_estimate=microseconds(60),
    )(*[array.reshape(count, lines, 2, array.shape[1], width) for array in arrays])


def inward_kernel(dims, grad_ref, weight_ref, edge_ref, handed_ref, normed_ref, begin_ref, gain_ref, passed_ref,
                  out_ref, channel_ref, router_ref, expert_ref, packed_ref, new_ref, rows, features, held_block):
    blocks, wide, tall, held, fold, marks, spare, steps = dims
    owners, count, _ = packed_ref.shape
    f32, low = jnp.float32, jnp.bfloat16
    step = pl.program_id(0)
    tokens = grad_ref.shape[0]
    last = edge_ref.shape[0]
    edited = (last + 1) // 2 * 2 * CHUNKS
    held_block[...] = grad_ref[...]

    @pl.when(lax.rem(step, blocks) < blocks // 2)
    def _():
        edge = edge_ref[...] + handed_ref[...]
        ends = grad_ref[tokens - edited :, :].astype(f32)
        place = lax.broadcasted_iota(jnp.int32, ends.shape, 0)
        for j in range(last):
            row = edited - (last - j) * CHUNKS + CHUNKS - 1
            ends = jnp.where(place == row, edge[j : j + 1], ends)
        held_block[tokens - edited :, :] = ends.astype(low)

    block = held_block[...]

    @pl.when(step == 0)
    def _():
        new_ref[...] = jnp.zeros_like(new_ref)
        rows[...] = jnp.zeros_like(rows)

    @pl.when(step < blocks)
    def _():
        new_ref[...] += dot_nt(block, weight_ref[...])

    @pl.when(step == blocks - 1)
    def _():
        grad, norm_grad = rms_back(begin_ref[...], gain_ref[...], new_ref[...])
        new_ref[...] = passed_ref[...] + grad
        experts = router_ref.shape[1]
        lane = lax.broadcasted_iota(jnp.int32, (experts, 2 * LANES), 1)
        row = lax.broadcasted_iota(jnp.int32, (experts, 2 * LANES), 0)
        pick = (lane == row + spare).astype(f32).astype(low)
        lane = lax.broadcasted_iota(jnp.int32, (2, 2 * LANES), 1)
        row = lax.broadcasted_iota(jnp.int32, (2, 2 * LANES), 0)
        pick_norms = (lane == row + spare + experts).astype(f32).astype(low)
        norms = jnp.concatenate([norm_grad[None], expert_ref[...]], axis=0).astype(low)
        features[...] = dot_nn(router_ref[...].astype(low), pick) + dot_tn(norms, pick_norms)

    @pl.when(step >= blocks)
    def _():
        grad = dot_tn(block, normed_ref[...])
        passed = out_ref[...]
        channel = channel_ref[...].astype(f32)
        start = pl.multiple_of((step - blocks) * owners * marks, 8)
        mine = features[pl.ds(start, owners * marks), :]
        thin = held // fold
        whole_tiles = not any(size % 16 for size in (wide, tall, thin))
        target = packed_ref if whole_tiles else rows
        kind = target.dtype
        for k in range(owners):
            target[k, :wide] = grad[k * wide : (k + 1) * wide].astype(kind)
            target[k, wide : wide + tall] = passed[k * tall : (k + 1) * tall].astype(kind)
            small = channel[k * held : (k + 1) * held]
            extra = mine[k * marks : (k + 1) * marks]
            small = small + jnp.concatenate([extra, jnp.zeros((held - marks, 2 * LANES), f32)], axis=0)
            for f in range(fold):
                target[k, wide + tall : wide + tall + thin, f * 2 * LANES : (f + 1) * 2 * LANES] = small[
                    f * thin : (f + 1) * thin].astype(kind)
            if whole_tiles and count > wide + tall + thin:
                packed_ref[k, wide + tall + thin :] = jnp.zeros((count - wide - tall - thin, grad.shape[1]), kind)
        if not whole_tiles:
            packed_ref[...] = rows[...].astype(low)


def mixer_inward(layer, grad_projected, in_weight, edge, handed, normed, begin, gain, passed, grad_out, channel,
                 grad_router, grad_expert, devices, spare):
    tokens, columns = grad_projected.shape
    width = normed.shape[1]
    wide, tall = columns // devices, grad_out.shape[0] // devices
    held, marks = channel.shape[0] // devices, width // devices
    fold = width // (2 * LANES)
    count = wide + tall + held // fold
    count += -count % 16
    owners = width // wide
    blocks = devices // owners
    span = owners * wide
    taps = edge.shape[0]
    inner = edge.shape[1] // span

    def at(i):
        return jnp.maximum(i - blocks, 0)

    return plain_call(
        functools.partial(inward_kernel, (blocks, wide, tall, held, fold, marks, spare, tokens // CHUNKS)),
        (2 * blocks,),
        [pl.BlockSpec((tokens, span), lambda i: (0, i % blocks)),
         pl.BlockSpec((None, width, span), lambda i: (layer, 0, jnp.minimum(i, blocks - 1))),
         pl.BlockSpec((taps, span), lambda i: (0, jnp.minimum(i % blocks, inner - 1))),
         pl.BlockSpec((taps, span), lambda i: (0, jnp.minimum(i % blocks, inner - 1))),
         whole(normed.shape), whole(begin.shape), layer_whole(layer, (1, width)), whole(passed.shape),
         pl.BlockSpec((owners * tall, width), lambda i: (at(i), 0)),
         pl.BlockSpec((owners * held, 2 * LANES), lambda i: (at(i), 0)),
         whole(grad_router.shape), whole(grad_expert.shape)],
        [pl.BlockSpec((owners, count, width), lambda i: (at(i), 0, 0)), whole((tokens, width))],
        [shaped((devices, count, width), jnp.bfloat16), shaped((tokens, width))],
        [VMEM((owners, count, width), jnp.float32), VMEM((width, 2 * LANES), jnp.float32),
         VMEM((tokens, span), jnp.bfloat16)],
        (grad_projected, in_weight, edge, handed, normed, begin, gain, passed, grad_out, channel, grad_router,
         grad_expert),
        9,
    )


def unfold_kernel(dims, *refs):
    layers, wide, tall, held, fold, marks, spare, sizes = dims
    inputs, outs = refs[:layers], refs[layers:]
    (in_ref, out_ref, state_ref, step_ref, decay_ref, conv_ref, conv_bias_ref, step_bias_ref, skip_ref,
     router_ref, mix_ref, expert_ref) = outs
    thin = held // fold
    for layer in range(layers):
        whole_rows = inputs[layer][...].astype(jnp.float32)
        in_ref[layer] = whole_rows[:wide]
        out_ref[layer] = whole_rows[wide : wide + tall]
        mine = whole_rows[wide + tall : wide + tall + thin]
        channel = jnp.concatenate(
            [mine[:, f * 2 * LANES : (f + 1) * 2 * LANES] for f in range(fold)], axis=0)
        state_ref[layer] = channel[:, : sizes[0]]
        turned = channel.T
        bounds = [0]
        for size in sizes:
            bounds.append(bounds[-1] + size)
        pieces = [turned[bounds[i] : bounds[i + 1]] for i in range(7)]
        step_ref[layer] = pieces[1]
        decay_ref[layer] = pieces[2]
        conv_ref[layer] = pieces[3]
        conv_bias_ref[layer : layer + 1] = pieces[4]
        step_bias_ref[layer : layer + 1] = pieces[5]
        skip_ref[layer : layer + 1] = pieces[6]
        experts = router_ref.shape[1]
        router_ref[layer] = turned[spare : spare + experts, :marks]
        mix_ref[layer : layer + 1] = turned[spare + experts : spare + experts + 1, :marks]
        expert_ref[layer : layer + 1] = turned[spare + experts + 1 : spare + experts + 2, :marks]


def unfolded(sums, wide, tall, held, marks, experts, spare, sizes):
    layers, width = len(sums), sums[0].shape[1]
    fold = width // (2 * LANES)
    shapes = [
        (wide, width), (tall, width), (held, sizes[0]), (sizes[1], held), (sizes[2], held), (sizes[3], held),
        (held,), (held,), (held,), (experts, marks), (marks,), (marks,),
    ]
    inside = pl.BlockSpec(memory_space=VMEM)
    return pl.pallas_call(
        functools.partial(unfold_kernel, (layers, wide, tall, held, fold, marks, spare, sizes)),
        out_shape=[shaped((layers,) + shape) for shape in shapes],
        in_specs=[inside] * layers,
        out_specs=[inside] * len(shapes),
        compiler_params=pltpu.CompilerParams(vmem_limit_bytes=60 * MIB),
        cost_estimate=microseconds(3),
    )(*sums)


def on_device(
    hidden,
    doc_start,
    expert_choice,
    slot_index,
    norm_mix,
    in_weight,
    conv_weight,
    conv_bias,
    state_weight,
    step_weight,
    step_bias,
    decay_log,
    skip_weight,
    out_weight,
    norm_expert,
    router,
    expert_up,
    expert_down,
    cotangent,
):
    layers = in_weight.shape[0]
    tokens = hidden.shape[1]
    width = hidden.shape[2]
    inner = skip_weight.shape[1]
    rank = step_weight.shape[1]
    states = decay_log.shape[1]
    experts = router.shape[2]
    taps = conv_weight.shape[1]
    steps = tokens // CHUNKS
    both = ("wide", "narrow")
    groups = lax.axis_size("narrow")
    devices = lax.axis_size("wide") * groups
    per_group = experts // groups
    capacity = max(2, 5 * tokens // (4 * experts))
    block = -(-per_group * capacity // 16) * 16
    low, f32 = jnp.bfloat16, jnp.float32
    keep_mask = rim_keep(doc_start[0], taps - 1)[:, None]
    order = expert_order(per_group, groups, block, capacity)
    norm_mix, conv_bias, step_bias, skip_weight, norm_expert = (
        values[:, None, :] for values in (norm_mix, conv_bias, step_bias, skip_weight, norm_expert))
    current = to_steps(hidden[0]).reshape(tokens, width).astype(f32)
    saved = []

    def cube(values):
        return values.reshape(steps, CHUNKS, values.shape[-1])

    tail = passed_along(hidden[0, tokens - taps + 1 :] * keep_mask.astype(low), 1)
    weights = [None] * layers
    ready, tail, slot_index = lax.optimization_barrier((layer_of(expert_up, 0), tail, slot_index))
    weights[0] = between_members([ready])
    reset, masks, fills, onehots, keeps = tables(
        doc_start, expert_choice, slot_index, taps, experts, groups, block, capacity)

    for layer in range(layers):
        begin = current
        normed = rms_scale(current, norm_mix[layer]).astype(low)
        projected = cube(dot_nn(normed, in_weight[layer]))
        if layer == 0:
            before = rms_scale(tail.astype(f32), norm_mix[layer]).astype(low)
            rim = dot_nn(before, in_weight[layer, :, :inner])
        else:
            rim = passed_along(projected[steps - taps + 1 :, CHUNKS - 1, :inner] * keep_mask, 1)
        act, selection, size, link, link_size, total, total_size = mixer_front(
            layer, projected, rim, masks, reset, conv_weight, conv_bias, state_weight, step_weight, step_bias,
            decay_log)
        if layer == 0:
            total, order = lax.optimization_barrier((total, order))
        entering, ready = handed_ahead(layer, total, total_size, decay_log, [(expert_down, layer)], layer)
        weights[layer] += between_members([ready])
        mixed, gated, begins, middle, routed, logits, outbound = mixer_run(
            layer, size, act, selection, reset, decay_log, link, link_size, entering, projected, skip_weight,
            out_weight, current, norm_expert, router, fills[layer])
        returned, kept_rows, pre_act, hidden_low, *following = expert_pass(
            outbound.reshape(groups, block, width), order, weights[layer], None, 4 + layer,
            expert_up if layer + 1 < layers else None, layer + 1)
        if following:
            weights[layer + 1] = following
        shares = jax.nn.softmax(logits, axis=-1)
        gate = jnp.sum(shares * onehots[layer], axis=1, keepdims=True)
        back_rows = dot_tn(fills[layer], returned.reshape(groups * block, width))
        current = middle + (keeps[layer] * gate) * back_rows
        saved.append(dict(
            begin=begin, normed=normed, projected=projected, rim=rim, act=act, selection=selection, size=size,
            begins=begins, mixed=mixed, gated=gated, middle=middle, routed=routed, shares=shares, gate=gate,
            kept_rows=kept_rows, pre_act=pre_act, hidden_low=hidden_low, back_rows=back_rows))
    output = to_tokens(cube(current.astype(low)))[None]
    grad = to_steps(cotangent[0]).reshape(tokens, width).astype(f32)
    sums = [None] * layers
    wide_grads = ()
    expert_grads = [None] * layers
    per_device = inner // devices
    norm_device = width // devices
    spare = 160
    for layer in range(layers - 1, -1, -1):
        entry = saved[layer]
        fill, keep, gate = fills[layer], keeps[layer], entry["gate"]
        grad_rows_low = ((keep * gate) * grad).astype(low)
        grad_gate = keep * jnp.sum(grad * entry["back_rows"], axis=1, keepdims=True)
        outbound = dot_nn(fill, grad_rows_low).astype(low).reshape(groups, block, width)
        inbound, grad_rows, grad_pre = expert_pass(
            outbound, order, weights[layer], entry["pre_act"], 6 + layer)
        grad_sent = dot_tn(fill, inbound.reshape(groups * block, width))
        grad_logits_low = ((grad_gate * gate) * (onehots[layer] - entry["shares"])).astype(low)
        grad_router = dot_tn(entry["routed"], grad_logits_low)
        grad_routed = grad_sent + dot_nt(grad_logits_low, router[layer])
        grad_middle, grad_norm_expert = rms_back(entry["middle"], norm_expert[layer], grad_routed)
        grad = grad + grad_middle
        grad_low = grad.astype(low)
        grad_y, grad_igate, grad_skip, grad_out, link, link_size, total, total_size = mixer_turn(
            layer, grad_low, out_weight, entry["projected"], entry["mixed"], entry["act"], entry["gated"],
            entry["size"], entry["selection"], reset, decay_log)
        entering, *ready = handed_back(
            layer, total, total_size, decay_log, entry["kept_rows"], grad_pre, entry["hidden_low"], grad_rows,
            2 + layer)
        expert_grads[layer] = between_members(ready)
        grad_act, grad_decay, grad_bias, grad_step, grad_selection = mixer_back(
            layer, entry["size"], entry["act"], grad_y, decay_log, entry["selection"], reset,
            entry["begins"], link, link_size, entering, step_weight, step_bias, skip_weight)
        grad_projected, edge, rim_grad, channel = mixer_conv_back(
            layer, grad_act, grad_selection, state_weight, entry["projected"], entry["rim"], masks, conv_weight,
            conv_bias, entry["act"], grad_step, grad_decay, grad_bias, grad_skip, grad_igate)
        handed = passed_along(rim_grad, -1) * keep_mask
        if layer + 1 < layers:
            wide_grads = widened(layer + 1, layers, expert_grads[layer + 1], width, expert_up.shape[3], wide_grads)
            handed, *wide_grads = lax.optimization_barrier((handed, *wide_grads))
        blocks, grad = mixer_inward(
            layer, grad_projected, in_weight, edge, handed, entry["normed"], entry["begin"], norm_mix, grad,
            grad_out, channel, grad_router, grad_norm_expert.reshape(1, width), devices, spare)
        if layer:
            blocks, grad = lax.optimization_barrier((blocks, grad))
            rows = blocks.shape[1]
            sums[layer] = lax.psum_scatter(
                blocks.reshape(devices * rows, width), both, scatter_dimension=0, tiled=True)
        else:
            sums[layer] = summed_shares([blocks], 8)
    (grad_in, grad_out, grad_state, grad_step, grad_decay, grad_conv, grad_conv_bias, grad_step_bias, grad_skip,
     grad_router, grad_norm_mix, grad_norm_expert) = unfolded(
        sums, 2 * inner // devices, per_device, per_device, norm_device, experts, spare,
        (rank + 2 * states, rank, states, taps, 1, 1, 1))
    shared = (
        grad_norm_mix, jnp.swapaxes(grad_in, 1, 2), grad_conv, grad_conv_bias, grad_state, grad_step,
        grad_step_bias, grad_decay, grad_skip, grad_out, grad_norm_expert, jnp.swapaxes(grad_router, 1, 2))
    up_grads, down_grads = widened(0, layers, expert_grads[0], width, expert_up.shape[3], wide_grads)
    output_grad = to_tokens(cube(grad))[None]
    return (output, output_grad, *shared, up_grads, down_grads)


def solution(mesh):
    both = ("wide", "narrow")
    placed = (
        P("narrow", "wide", None),
        P("narrow", "wide"),
        P(None, "narrow", "wide"),
        P(None, "narrow", "wide"),
    ) + (P(),) * 12 + (
        P(None, "narrow", None, "wide"),
        P(None, "narrow", "wide", None),
        P("narrow", "wide", None),
    )
    return jax.shard_map(
        on_device,
        mesh=mesh,
        in_specs=placed,
        out_specs=(
            P("narrow", "wide", None),
            P("narrow", "wide", None),
            P(None, both),
            P(None, None, both),
            P(None, None, both),
            P(None, both),
            P(None, both, None),
            P(None, None, both),
            P(None, both),
            P(None, None, both),
            P(None, both),
            P(None, both, None),
            P(None, both),
            P(None, both, None),
            P(None, "narrow", None, "wide"),
            P(None, "narrow", "wide", None),
        ),
        check_vma=False,
    )
```

```python
import functools

import jax
import jax.numpy as jnp
from jax import lax
from jax.experimental import pallas as pl
from jax.experimental.pallas import tpu as pltpu
from jax.sharding import PartitionSpec as P

EPS = 1e-05
CHUNKS = 8
LANES = 128
LOG2E = 1.4426950408889634
RESET = 1e9
MIB = 1024 * 1024
MESH = pl.DeviceIdType.MESH
VMEM = pltpu.VMEM


def to_steps(values):
    steps = values.shape[0] // CHUNKS
    return jnp.swapaxes(values.reshape((CHUNKS, steps) + values.shape[1:]), 0, 1)


def to_tokens(values):
    moved = jnp.swapaxes(values, 0, 1)
    return moved.reshape((-1,) + values.shape[2:])


def rms_scale(values, gain):
    return values * lax.rsqrt(jnp.mean(values * values, axis=-1, keepdims=True) + EPS) * gain


def rms_back(values, gain, grad):
    scale = lax.rsqrt(jnp.mean(values * values, axis=-1, keepdims=True) + EPS)
    weighted = grad * gain
    inner = jnp.mean(weighted * values, axis=-1, keepdims=True)
    return (
        scale * weighted - values * (scale * scale * scale) * inner,
        jnp.sum(grad * values * scale, axis=0),
    )


def dot_nn(left, right):
    return lax.dot_general(left, right, (((1,), (0,)), ((), ())), preferred_element_type=jnp.float32)


def dot_nt(left, right):
    return lax.dot_general(left, right, (((1,), (1,)), ((), ())), preferred_element_type=jnp.float32)


def dot_tn(left, right):
    return lax.dot_general(left, right, (((0,), (0,)), ((), ())), preferred_element_type=jnp.float32)


def passed_along(x, by):
    size = lax.axis_size("wide")
    return lax.ppermute(x, "wide", [(i, i + by) for i in range(size) if 0 <= i + by < size])


def tables_kernel(dims, doc_ref, choice_ref, slot_ref, reset_ref, mask_ref, *outs):
    layers, taps, per_group, block, capacity = dims
    tokens = doc_ref.shape[1]
    steps = tokens // CHUNKS
    f32, low = jnp.float32, jnp.bfloat16
    fills, onehots, keeps = outs[:layers], outs[layers : 2 * layers], outs[2 * layers :]
    rows = [doc_ref[...]] + [choice_ref[l] for l in range(layers)] + [slot_ref[l] for l in range(layers)]
    rows = jnp.concatenate([row.astype(f32) for row in rows], axis=0)
    rows = jnp.concatenate([rows, jnp.zeros((CHUNKS - rows.shape[0], tokens), f32)], axis=0).astype(low)
    place = lax.broadcasted_iota(jnp.int32, (tokens, tokens), 1)
    token = (place & (CHUNKS - 1)) * steps + lax.shift_right_logical(place, 3)
    order = (lax.broadcasted_iota(jnp.int32, (tokens, tokens), 0) == token).astype(f32).astype(low)
    along = dot_nn(rows, order)
    down = lax.dot_general(order, rows, (((0,), (1,)), ((), ())), preferred_element_type=f32)

    starts = jnp.broadcast_to(down[:, 0:1], (tokens, LANES)).reshape(steps, CHUNKS, LANES)
    reset_ref[...] = starts * RESET
    chunk = lax.broadcasted_iota(jnp.int32, (CHUNKS, LANES), 0)
    mask_ref[0] = 1.0 - starts
    for offset in range(2, taps):
        mask_ref[offset - 1, offset - 1 :] = mask_ref[offset - 2, offset - 1 :] * (
            1.0 - starts[: steps - offset + 1])
        for i in range(offset - 1):
            before = jnp.where(chunk == 0, 0.0, pltpu.roll(starts[steps - offset + 1 + i], 1, axis=0))
            mask_ref[offset - 1, i] = mask_ref[offset - 2, i] * (1.0 - before)

    for l in range(layers):
        chosen, slot = along[1 + l : 2 + l], along[1 + layers + l : 2 + layers + l]
        group = jnp.floor((chosen + 0.5) * (1.0 / per_group))
        spot = group * block + (chosen - group * per_group) * capacity + slot
        spot = jnp.where(slot >= 0.0, spot, -1.0).astype(jnp.int32)
        fills[l][...] = (
            lax.broadcasted_iota(jnp.int32, fills[l].shape, 0) == spot).astype(f32).astype(low)
        picked = down[:, 1 + l : 2 + l].astype(jnp.int32)
        onehots[l][...] = (lax.broadcasted_iota(jnp.int32, onehots[l].shape, 1) == picked).astype(f32)
        keeps[l][...] = jnp.where(down[:, 1 + layers + l : 2 + layers + l] >= 0.0, 1.0, 0.0)


def tables(doc_start, expert_choice, slot_index, taps, experts, groups, block, capacity):
    layers = expert_choice.shape[0]
    tokens = doc_start.shape[1]
    steps = tokens // CHUNKS
    f32 = jnp.float32
    shapes = [shaped((steps, CHUNKS, LANES)), shaped((taps - 1, steps, CHUNKS, LANES))]
    shapes += [shaped((groups * block, tokens), jnp.bfloat16)] * layers
    shapes += [shaped((tokens, experts))] * layers + [shaped((tokens, 1))] * layers
    inside = pl.BlockSpec(memory_space=VMEM)
    reset, masks, *rest = pl.pallas_call(
        functools.partial(tables_kernel, (layers, taps, experts // groups, block, capacity)),
        out_shape=shapes,
        in_specs=[inside] * 3,
        out_specs=[inside] * len(shapes),
        compiler_params=pltpu.CompilerParams(vmem_limit_bytes=60 * MIB),
        cost_estimate=microseconds(3),
    )(doc_start, expert_choice, slot_index)
    return reset, masks, rest[:layers], rest[layers : 2 * layers], rest[2 * layers :]


def rim_keep(doc_start, count):
    tail = 1.0 - doc_start[doc_start.shape[0] - count :].astype(jnp.float32)
    later = jnp.cumprod(tail[::-1])[::-1]
    return jnp.concatenate([later[1:], jnp.ones((1,), jnp.float32)])


TILE = 2 * LANES


def each_part(body):
    def one(at, carry):
        body(pl.ds(pl.multiple_of(at * LANES, LANES), LANES))
        return carry

    lax.fori_loop(0, TILE // LANES, one, 0)


def microseconds(count):
    return pl.CostEstimate(flops=int(count * 1.5e8), transcendentals=0, bytes_accessed=10000)


def plain_call(kernel, grid, in_specs, out_specs, out_shapes, scratch, args, cost, aliases=None):
    return pl.pallas_call(
        kernel,
        grid=grid,
        in_specs=in_specs,
        out_specs=out_specs,
        out_shape=out_shapes,
        scratch_shapes=scratch,
        input_output_aliases=aliases or {},
        compiler_params=pltpu.CompilerParams(
            dimension_semantics=("arbitrary",), vmem_limit_bytes=60 * MIB
        ),
        cost_estimate=microseconds(cost),
    )(*args)


def shaped(shape, kind=jnp.float32):
    return jax.ShapeDtypeStruct(shape, kind)


def slab(steps, first=0):
    return pl.BlockSpec((steps, CHUNKS, TILE), lambda c: (0, 0, first + c))


def rows_of(count):
    return pl.BlockSpec((count, TILE), lambda c: (0, c))


def layer_rows(layer, count):
    return pl.BlockSpec((None, count, TILE), lambda c: (layer, 0, c))


def layer_columns(layer, count):
    return pl.BlockSpec((None, TILE, count), lambda c: (layer, c, 0))


def layer_whole(layer, shape):
    return pl.BlockSpec((None,) + shape, lambda c: (layer,) + (0,) * len(shape))


def whole(shape):
    return pl.BlockSpec(shape, lambda c: (0,) * len(shape))


ANYWHERE = pl.BlockSpec(memory_space=pl.ANY)


def spread_columns(selection_ref, first, states, out_ref):
    def one(step, carry):
        tile = selection_ref[step]
        for n in range(states):
            out_ref[step, n] = jnp.broadcast_to(tile[:, first + n : first + n + 1], (CHUNKS, LANES))
        return carry

    lax.fori_loop(0, selection_ref.shape[0], one, 0, unroll=8)


def rate_rows(rate):
    return [jnp.broadcast_to(rate[n : n + 1, :], (CHUNKS, LANES)) for n in range(rate.shape[0])]


def rates_of(decay_log):
    return -jnp.exp(decay_log) * LOG2E


def two_steps(ref, pair, lanes=slice(None)):
    both = ref[pl.ds(pl.multiple_of(pair * 2 * CHUNKS, 2 * CHUNKS), 2 * CHUNKS), lanes]
    both = both.astype(jnp.float32)
    return both[:CHUNKS], both[CHUNKS:]


def chunk_links(found, sizes, rates, reverse):
    place = lax.broadcasted_iota(jnp.int32, (CHUNKS, LANES), 0)
    if reverse:
        place = CHUNKS - 1 - place
    last = 0 if reverse else CHUNKS - 1

    def shifted(values, by):
        turned = pltpu.roll(values, CHUNKS - by if reverse else by, axis=0)
        return jnp.where(place >= by, turned, 0.0)

    lengths = [sizes]
    for by in (1, 2, 4):
        lengths.append(lengths[-1] + shifted(lengths[-1], by))
    links, totals = [], []
    for n, rate in enumerate(rates):
        level = found[n]
        for index, by in enumerate((1, 2, 4)):
            level = level + jnp.exp2(lengths[index] * rate) * shifted(level, by)
        links.append(shifted(level, 1))
        totals.append(level[last : last + 1])
    return links, totals, shifted(lengths[-1], 1), lengths[-1][last : last + 1]


def conv_slab(extended, step, mask_ref, kernel_ref, bias, taps):
    total = bias + kernel_ref[0:1, :] * extended[step + taps - 1]
    tiles = total.shape[1] // LANES
    for offset in range(1, taps):
        mask = mask_ref[offset - 1, step]
        mask = jnp.concatenate([mask] * tiles, axis=1) if tiles > 1 else mask
        total = total + kernel_ref[offset : offset + 1, :] * (
            extended[step + taps - 1 - offset] * mask
        )
    return total


def extend(value_ref, rim_ref, extended, taps):
    steps = value_ref.shape[0]
    place = lax.broadcasted_iota(jnp.int32, value_ref.shape[1:], 0)
    for j in range(taps - 1):
        turned = pltpu.roll(value_ref[steps - taps + 1 + j], 1, axis=0)
        extended[j] = jnp.where(place == 0, rim_ref[j : j + 1, :], turned)
    extended[taps - 1 :] = value_ref[...]


def enter_kernel(first, gain_ref, weight_ref, *refs):
    low = jnp.bfloat16
    if first:
        current_ref, tail_ref, normed_ref, projected_ref, rim_ref, before = refs
    else:
        middle_ref, share_ref, fill_ref, returned_ref, current_ref, taken_ref, normed_ref, projected_ref = refs

    @pl.when(pl.program_id(0) == 0)
    def _():
        if first:
            before[...] = rms_scale(tail_ref[...], gain_ref[...]).astype(low)
        else:
            taken = dot_tn(fill_ref[...], returned_ref[...])
            taken_ref[...] = taken
            current_ref[...] = middle_ref[...] + share_ref[...] * taken
        normed_ref[...] = rms_scale(current_ref[...], gain_ref[...]).astype(low)

    projected_ref[...] = dot_nn(normed_ref[...], weight_ref[...])
    if first:
        rim_ref[...] = dot_nn(before[...], weight_ref[...])


def mixer_enter(layer, gain, in_weight, *arrays):
    first = len(arrays) == 2
    _, width, columns = in_weight.shape
    tokens = arrays[0].shape[0]
    span = 4 * LANES
    low = jnp.bfloat16
    normed = (whole((tokens, width)), shaped((tokens, width), low))
    projected = (pl.BlockSpec((tokens, span), lambda c: (0, c)), shaped((tokens, columns)))
    if first:
        rows = arrays[1].shape[0]
        outs = [normed, projected, (pl.BlockSpec((rows, span), lambda c: (0, c)), shaped((rows, columns)))]
        scratch = [VMEM((rows, width), low)]
    else:
        full = (whole((tokens, width)), shaped((tokens, width)))
        outs, scratch = [full, full, normed, projected], []
    return plain_call(
        functools.partial(enter_kernel, first),
        (columns // span,),
        [layer_whole(layer, (1, width)), pl.BlockSpec((None, width, span), lambda c: (layer, 0, c))]
        + [whole(array.shape) for array in arrays],
        [spec for spec, _ in outs],
        [shape for _, shape in outs],
        scratch,
        (gain, in_weight) + arrays,
        5,
    )


def front_kernel(dims, value_ref, rim_ref, mask_ref, reset_ref, conv_ref, conv_bias_ref, state_ref,
                 step_ref, step_bias_ref, decay_ref,
                 act_ref, selection_ref, size_ref, link_ref, link_size_ref, total_ref, total_size_ref,
                 extended, maps, sized, pushed):
    taps, rank, states, steps, channels = dims
    extend(value_ref, rim_ref, extended, taps)
    bias = conv_bias_ref[...]

    def conv_pair(pair, carry):
        both = []
        for step in (2 * pair, 2 * pair + 1):
            both.append(jax.nn.silu(conv_slab(extended, step, mask_ref, conv_ref, bias, taps)))
        at = pl.ds(pl.multiple_of(pair * 2 * CHUNKS, 2 * CHUNKS), 2 * CHUNKS)
        act_ref[at, :] = jnp.concatenate(both, axis=0).astype(jnp.bfloat16)
        return carry

    lax.fori_loop(0, steps // 2, conv_pair, 0)
    selection = dot_nn(act_ref[...], state_ref[...])
    selection_ref[...] = selection.reshape(steps, CHUNKS, selection.shape[1])
    rank_low = selection[:, :rank].astype(jnp.bfloat16)

    def size_tile(c, carry):
        lanes = pl.ds(pl.multiple_of(c * 256, 256), 256)
        linear = dot_nn(rank_low, step_ref[:, lanes]) + step_bias_ref[:, lanes]
        size_ref[:, :, lanes] = jax.nn.softplus(linear).reshape(steps, CHUNKS, 256)
        return carry

    lax.fori_loop(0, channels // 256, size_tile, 0)
    spread_columns(selection_ref, rank, states, maps)

    def end_tile(c, carry):
        lanes = pl.ds(pl.multiple_of(c * LANES, LANES), LANES)
        rates = rate_rows(rates_of(decay_ref[:, lanes]))
        size = size_ref[:, :, lanes]
        pushed[...] = size * act_ref[:, lanes].astype(jnp.float32).reshape(size.shape)
        sized[...] = size + reset_ref[...]

        def one(step, carry):
            size, value = sized[step], pushed[step]
            new = []
            for n in range(states):
                new.append(jnp.exp2(size * rates[n]) * carry[n] + value * maps[step, n])
            return tuple(new) + (carry[states] + size,)

        zero = jnp.zeros((CHUNKS, LANES), jnp.float32)
        found = lax.fori_loop(0, steps, one, (zero,) * (states + 1), unroll=4)
        links, totals, link_size, total_size = chunk_links(found, found[states], rates, False)
        link_size_ref[:, lanes] = link_size
        total_size_ref[:, lanes] = total_size
        for n in range(states):
            link_ref[n, :, lanes] = links[n]
            total_ref[n : n + 1, lanes] = totals[n]
        return carry

    lax.fori_loop(0, channels // LANES, end_tile, 0)


def mixer_front(layer, projected, rim, masks, reset, conv_weight, conv_bias, state_weight, step_weight,
                step_bias, decay_log):
    steps = projected.shape[0]
    channels = conv_weight.shape[2]
    taps, rank, states = conv_weight.shape[1], step_weight.shape[1], decay_log.shape[1]
    columns = state_weight.shape[2]
    value = pl.BlockSpec((steps, CHUNKS, channels), lambda c: (0, 0, 0))
    shapes = [
        shaped((steps * CHUNKS, channels), jnp.bfloat16),
        shaped((steps, CHUNKS, columns)),
        shaped((steps, CHUNKS, channels)),
        shaped((states, CHUNKS, channels)),
        shaped((CHUNKS, channels)),
        shaped((states, channels)),
        shaped((1, channels)),
    ]
    return plain_call(
        functools.partial(front_kernel, (taps, rank, states, steps, channels)),
        (1,),
        [value, whole((rim.shape[0], channels)), whole(masks.shape), whole(reset.shape),
         layer_whole(layer, conv_weight.shape[1:]), layer_whole(layer, conv_bias.shape[1:]),
         layer_whole(layer, state_weight.shape[1:]), layer_whole(layer, step_weight.shape[1:]),
         layer_whole(layer, step_bias.shape[1:]), layer_whole(layer, decay_log.shape[1:])],
        [whole(s.shape) for s in shapes],
        shapes,
        [VMEM((steps + taps - 1, CHUNKS, channels), jnp.float32),
         VMEM((steps, states, CHUNKS, LANES), jnp.float32),
         VMEM((steps, CHUNKS, LANES), jnp.float32), VMEM((steps, CHUNKS, LANES), jnp.float32)],
        (projected, rim, masks, reset, conv_weight, conv_bias, state_weight, step_weight, step_bias,
         decay_log),
        18,
    )


def run_kernel(dims, size_ref, act_ref, selection_ref, reset_ref, decay_ref, link_ref, link_size_ref,
               entering_ref, gate_ref, skip_ref, out_weight_ref, current_ref, norm_ref, router_ref, fill_ref,
               onehot_ref, keep_ref,
               mixed_ref, gated_ref, begin_ref, middle_ref, routed_ref, shares_ref, weight_ref, outbound_ref,
               in_maps, out_maps, pushed):
    rank, states, steps, tiles = dims

    @pl.when(pl.program_id(0) == 0)
    def _():
        spread_columns(selection_ref, rank, states, in_maps)
        spread_columns(selection_ref, rank + states, states, out_maps)
        middle_ref[...] = current_ref[...]

    size = size_ref[...]
    act = act_ref[...].astype(jnp.float32).reshape(size.shape)
    pushed[...] = size * act

    def scan(lanes):
        rates = rate_rows(rates_of(decay_ref[:, lanes]))
        link_size = link_size_ref[:, lanes]
        begin = []
        for n in range(states):
            first = link_ref[n, :, lanes] + jnp.exp2(link_size * rates[n]) * entering_ref[n : n + 1, lanes]
            begin_ref[n, :, lanes] = first
            begin.append(first)

        def one(step, carry):
            size, value = size_ref[step, :, lanes] + reset_ref[step], pushed[step, :, lanes]
            new = []
            sums = [None, None]
            for n in range(states):
                level = jnp.exp2(size * rates[n]) * carry[n] + value * in_maps[step, n]
                new.append(level)
                term = out_maps[step, n] * level
                sums[n % 2] = term if sums[n % 2] is None else sums[n % 2] + term
            mixed_ref[step, :, lanes] = sums[0] + sums[1]
            return tuple(new)

        lax.fori_loop(0, steps, one, tuple(begin), unroll=4)

    each_part(scan)
    mixed = mixed_ref[...] + skip_ref[...] * act
    mixed_ref[...] = mixed
    gated = mixed * jax.nn.silu(gate_ref[...])
    gated_ref[...] = gated.reshape(steps * CHUNKS, TILE).astype(jnp.bfloat16)
    middle_ref[...] += dot_nn(gated_ref[...], out_weight_ref[...])

    @pl.when(pl.program_id(0) == tiles - 1)
    def _():
        routed = rms_scale(middle_ref[...], norm_ref[...]).astype(jnp.bfloat16)
        routed_ref[...] = routed
        logits = dot_nn(routed, router_ref[...])
        raised = jnp.exp(logits - jnp.max(logits, axis=1, keepdims=True))
        shares = raised / jnp.sum(raised, axis=1, keepdims=True)
        shares_ref[...] = shares
        weight_ref[...] = keep_ref[...] * jnp.sum(shares * onehot_ref[...], axis=1, keepdims=True)
        outbound_ref[...] = dot_nn(fill_ref[...], routed).astype(jnp.bfloat16)


def mixer_run(layer, size, act, selection, reset, decay_log, link, link_size, entering, projected, skip_weight,
              out_weight, current, norm_expert, router, fill, onehot, keep):
    steps, _, channels = size.shape
    tokens = steps * CHUNKS
    states, width, experts = decay_log.shape[1], current.shape[1], router.shape[2]
    rank = selection.shape[2] - 2 * states
    tiles = channels // TILE
    low = jnp.bfloat16
    maps = VMEM((steps, states, CHUNKS, LANES), jnp.float32)
    return plain_call(
        functools.partial(run_kernel, (rank, states, steps, tiles)),
        (tiles,),
        [slab(steps), rows_of(tokens), whole(selection.shape), whole(reset.shape),
         layer_rows(layer, states), slab(states), rows_of(CHUNKS), rows_of(states), slab(steps, tiles),
         layer_rows(layer, 1), layer_columns(layer, width), whole(current.shape),
         layer_whole(layer, (1, width)), layer_whole(layer, (width, experts)), whole(fill.shape),
         whole(onehot.shape), whole(keep.shape)],
        [slab(steps), rows_of(tokens), slab(states), whole((tokens, width)), whole((tokens, width)),
         whole((tokens, experts)), whole((tokens, 1)), whole((fill.shape[0], width))],
        [
            shaped((steps, CHUNKS, channels)),
            shaped((tokens, channels), low),
            shaped((states, CHUNKS, channels)),
            shaped((tokens, width)),
            shaped((tokens, width), low),
            shaped((tokens, experts)),
            shaped((tokens, 1)),
            shaped((fill.shape[0], width), low),
        ],
        [maps, maps, VMEM((steps, CHUNKS, TILE), jnp.float32)],
        (size, act, selection, reset, decay_log, link, link_size, entering, projected, skip_weight, out_weight,
         current, norm_expert, router, fill, onehot, keep),
        22,
    )


def turn_kernel(dims, grad_ref, out_weight_ref, gate_ref, mixed_ref, act_ref, gated_ref, size_ref,
                selection_ref, reset_ref, decay_ref,
                grad_y_ref, grad_gate_ref, grad_skip_ref, grad_out_ref, link_ref, link_size_ref, total_ref,
                total_size_ref, maps):
    rank, states, steps = dims

    @pl.when(pl.program_id(0) == 0)
    def _():
        spread_columns(selection_ref, rank + states, states, maps)

    grad = grad_ref[...]
    grad_out_ref[...] = dot_tn(gated_ref[...], grad).astype(jnp.bfloat16)
    gated = dot_nt(grad, out_weight_ref[...]).reshape(steps, CHUNKS, TILE)
    gate = gate_ref[...]
    share = jax.nn.sigmoid(gate)
    grad_y = gated * (gate * share)
    grad_y_ref[...] = grad_y
    grad_gate = gated * mixed_ref[...] * (share * (1.0 + gate * (1.0 - share)))
    grad_gate_ref[...] = grad_gate.reshape(steps * CHUNKS, TILE).astype(jnp.bfloat16)
    by_skip = grad_y * act_ref[...].astype(jnp.float32).reshape(steps, CHUNKS, TILE)
    grad_skip_ref[...] = jnp.sum(jnp.sum(by_skip, axis=0), axis=0, keepdims=True)

    def scan(lanes):
        rates = rate_rows(rates_of(decay_ref[:, lanes]))

        def one(at, carry):
            step = steps - 1 - at
            size, grad_y = size_ref[step, :, lanes] + reset_ref[step], grad_y_ref[step, :, lanes]
            new = []
            for n in range(states):
                new.append(jnp.exp2(size * rates[n]) * (carry[n] + grad_y * maps[step, n]))
            return tuple(new) + (carry[states] + size,)

        zero = jnp.zeros((CHUNKS, LANES), jnp.float32)
        found = lax.fori_loop(0, steps, one, (zero,) * (states + 1), unroll=4)
        links, totals, link_size, total_size = chunk_links(found, found[states], rates, True)
        link_size_ref[:, lanes] = link_size
        total_size_ref[:, lanes] = total_size
        for n in range(states):
            link_ref[n, :, lanes] = links[n]
            total_ref[n : n + 1, lanes] = totals[n]

    each_part(scan)


def mixer_turn(layer, grad_low, out_weight, projected, mixed, act, gated, size, selection, reset, decay_log):
    steps, _, channels = size.shape
    tokens = steps * CHUNKS
    states, width = decay_log.shape[1], grad_low.shape[1]
    rank = selection.shape[2] - 2 * states
    tiles = channels // TILE
    low = jnp.bfloat16
    return plain_call(
        functools.partial(turn_kernel, (rank, states, steps)),
        (tiles,),
        [whole(grad_low.shape), layer_columns(layer, width), slab(steps, tiles), slab(steps), rows_of(tokens),
         rows_of(tokens), slab(steps), whole(selection.shape), whole(reset.shape), layer_rows(layer, states)],
        [slab(steps), pl.BlockSpec((tokens, TILE), lambda c: (0, tiles + c)), rows_of(1),
         pl.BlockSpec((TILE, width), lambda c: (c, 0)),
         slab(states), rows_of(CHUNKS), rows_of(states), rows_of(1)],
        [
            shaped((steps, CHUNKS, channels)),
            shaped((tokens, 2 * channels), low),
            shaped((1, channels)),
            shaped((channels, width), low),
            shaped((states, CHUNKS, channels)),
            shaped((CHUNKS, channels)),
            shaped((states, channels)),
            shaped((1, channels)),
        ],
        [VMEM((steps, states, CHUNKS, LANES), jnp.float32)],
        (grad_low, out_weight, projected, mixed, act, gated, size, selection, reset, decay_log),
        14,
    )


def back_kernel(dims, size_ref, act_ref, grad_ref, decay_ref, selection_ref, reset_ref, begin_ref, link_ref,
                link_size_ref, entering_ref, step_ref, step_bias_ref, skip_ref,
                grad_act_ref, grad_decay_ref, grad_bias_ref, grad_step_ref, grad_selection_ref,
                in_maps, out_maps, levels, decays, grad_in, grad_out, grad_size, grad_rate, grad_all, pushed, acted):
    rank, states, steps, tiles = dims
    tokens = steps * CHUNKS

    @pl.when(pl.program_id(0) == 0)
    def _():
        spread_columns(selection_ref, rank, states, in_maps)
        spread_columns(selection_ref, rank + states, states, out_maps)
        grad_in[...] = jnp.zeros_like(grad_in)
        grad_out[...] = jnp.zeros_like(grad_out)

    skip = skip_ref[...]
    size = size_ref[...]
    act = act_ref[...].astype(jnp.float32).reshape(size.shape)
    acted[...] = act
    pushed[...] = size * act

    def scan(lanes):
        true_rates = -jnp.exp(decay_ref[:, lanes])
        rates = rate_rows(true_rates * LOG2E)
        begin = []
        for n in range(states):
            levels[0, n] = begin_ref[n, :, lanes]
            begin.append(begin_ref[n, :, lanes])

        def ahead(step, carry):
            size, value = size_ref[step, :, lanes] + reset_ref[step], pushed[step, :, lanes]
            new = []
            for n in range(states):
                decay = jnp.exp2(size * rates[n])
                decays[step, n] = decay
                level = decay * carry[n] + value * in_maps[step, n]
                levels[step + 1, n] = level
                new.append(level)
            return tuple(new)

        lax.fori_loop(0, steps, ahead, tuple(begin), unroll=4)
        link_size = link_size_ref[:, lanes]
        tail = []
        for n in range(states):
            tail.append(
                link_ref[n, :, lanes] + jnp.exp2(link_size * rates[n]) * entering_ref[n : n + 1, lanes])
            grad_rate[n] = jnp.zeros((CHUNKS, LANES), jnp.float32)

        def retreat(at, carry):
            step = steps - 1 - at
            plain, act, grad, value = (
                ref[step, :, lanes] for ref in (size_ref, acted, grad_ref, pushed))
            by_rate = jnp.zeros((CHUNKS, LANES), jnp.float32)
            by_input = jnp.zeros((CHUNKS, LANES), jnp.float32)
            new = []
            for n in range(states):
                spot = slice(n * LANES, (n + 1) * LANES)
                back = out_maps[step, n] * grad + carry[n]
                grad_out[step, :, spot] += grad * levels[step + 1, n]
                grad_in[step, :, spot] += back * value
                by_input = by_input + back * in_maps[step, n]
                passed = decays[step, n] * back
                new.append(passed)
                pull = passed * levels[step, n]
                by_rate = by_rate + pull * rates[n]
                grad_rate[n] += pull * plain
            grad_size[step, :, lanes] = by_rate * (1.0 / LOG2E) + act * by_input
            grad_act_ref[step, :, lanes] = plain * by_input
            return tuple(new)

        lax.fori_loop(0, steps, retreat, tuple(tail), unroll=2)
        for n in range(states):
            grad_decay_ref[n : n + 1, lanes] = (
                jnp.sum(grad_rate[n], axis=0, keepdims=True) * true_rates[n : n + 1, :]
            )

    each_part(scan)
    grad_act_ref[...] += grad_ref[...] * skip
    tile = pl.program_id(0)
    grad_all[:, pl.ds(pl.multiple_of(tile * TILE, TILE), TILE)] = grad_size[...].reshape(tokens, TILE)

    @pl.when(pl.program_id(0) == tiles - 1)
    def _():
        rank_low = selection_ref[...].reshape(tokens, selection_ref.shape[2])[:, :rank].astype(jnp.bfloat16)
        linear = dot_nn(rank_low, step_ref[...]) + step_bias_ref[...]
        grad_linear = grad_all[...] * jax.nn.sigmoid(linear)
        grad_bias_ref[...] = jnp.sum(grad_linear, axis=0, keepdims=True)
        grad_low = grad_linear.astype(jnp.bfloat16)
        grad_step_ref[...] = dot_tn(rank_low, grad_low)
        grad_rank = dot_nt(grad_low, step_ref[...])
        size = states * LANES
        row = lax.broadcasted_iota(jnp.int32, (size, states), 0)
        column = lax.broadcasted_iota(jnp.int32, (size, states), 1)
        pick = ((row >= column * LANES) & (row < (column + 1) * LANES)).astype(jnp.float32)
        pick = pick.astype(jnp.bfloat16)
        found = [grad_rank]
        for ref in (grad_in, grad_out):
            full = ref[...].reshape(tokens, size)
            high = full.astype(jnp.bfloat16)
            rest = (full - high.astype(jnp.float32)).astype(jnp.bfloat16)
            found.append(dot_nn(high, pick) + dot_nn(rest, pick))
        grad_selection_ref[...] = jnp.concatenate(found, axis=1).astype(jnp.bfloat16)


def mixer_back(layer, size, act, grad_y, decay_log, selection, reset, begin, link, link_size, entering,
               step_weight, step_bias, skip_weight):
    steps, _, channels = size.shape
    tokens = steps * CHUNKS
    states = decay_log.shape[1]
    columns = selection.shape[2]
    rank = columns - 2 * states
    tiles = channels // TILE
    f32 = jnp.float32
    maps = VMEM((steps, states, CHUNKS, LANES), f32)
    return plain_call(
        functools.partial(back_kernel, (rank, states, steps, tiles)),
        (tiles,),
        [slab(steps), rows_of(tokens), slab(steps), layer_rows(layer, states), whole(selection.shape),
         whole(reset.shape), slab(states), slab(states), rows_of(CHUNKS), rows_of(states),
         layer_whole(layer, (rank, channels)), layer_whole(layer, (1, channels)), layer_rows(layer, 1)],
        [slab(steps), rows_of(states), whole((1, channels)), whole((rank, channels)),
         whole((tokens, columns))],
        [
            shaped((steps, CHUNKS, channels)),
            shaped((states, channels)),
            shaped((1, channels)),
            shaped((rank, channels)),
            shaped((tokens, columns), jnp.bfloat16),
        ],
        [maps, maps, VMEM((steps + 1, states, CHUNKS, LANES), f32), maps,
         VMEM((steps, CHUNKS, states * LANES), f32), VMEM((steps, CHUNKS, states * LANES), f32),
         VMEM((steps, CHUNKS, TILE), f32), VMEM((states, CHUNKS, LANES), f32), VMEM((tokens, channels), f32)]
        + [VMEM((steps, CHUNKS, TILE), f32)] * 2,
        (size, act, grad_y, decay_log, selection, reset, begin, link, link_size, entering, step_weight,
         step_bias, skip_weight),
        35,
    )


def conv_back_kernel(dims, grad_act_ref, grad_selection_ref, state_ref, value_ref, rim_ref, mask_ref,
                     conv_ref, conv_bias_ref, act_ref, grad_step_ref, grad_decay_ref, grad_bias_ref,
                     grad_skip_ref, half_ref, grad_value_ref, edge_ref, rim_grad_ref, channel_ref,
                     extended, passed):
    taps, states, steps = dims
    lanes = grad_act_ref.shape[2]
    extend(value_ref, rim_ref, extended, taps)
    bias = conv_bias_ref[...]
    grad_selection = grad_selection_ref[...]
    from_selection = dot_nt(grad_selection, state_ref[...]).reshape(steps, CHUNKS, lanes)
    passed[:steps] = grad_act_ref[...] + from_selection
    passed[steps:] = jnp.zeros((taps - 1, CHUNKS, lanes), jnp.float32)
    zero = jnp.zeros((CHUNKS, lanes), jnp.float32)

    def keep(offset, step):
        return jnp.concatenate([mask_ref[offset - 1, step]] * (lanes // LANES), axis=1)

    def ahead(step, carry):
        convolved = conv_slab(extended, step, mask_ref, conv_ref, bias, taps)
        share = jax.nn.sigmoid(convolved)
        grad = passed[step] * (share * (1.0 + convolved * (1.0 - share)))
        passed[step] = grad
        new = [carry[0] + grad, carry[1] + grad * extended[step + taps - 1]]
        for offset in range(1, taps):
            kept = grad * keep(offset, step)
            new.append(carry[offset + 1] + kept * extended[step + taps - 1 - offset])
        return tuple(new)

    sums = lax.fori_loop(0, steps, ahead, (zero,) * (taps + 1), unroll=2)

    def reach(step, last):
        total = zero
        for offset in range(last):
            at = step + offset
            part = conv_ref[offset : offset + 1, :] * passed[at]
            if offset:
                part = part * keep(offset, at)
            total = total + part
        return total

    def back(pair, carry):
        both = [reach(2 * pair + half, taps) for half in (0, 1)]
        rows = pl.ds(pl.multiple_of(pair * 2 * CHUNKS, 2 * CHUNKS), 2 * CHUNKS)
        grad_value_ref[rows, :] = jnp.concatenate(both, axis=0).astype(jnp.bfloat16)
        return carry

    safe = (steps - taps + 1) // 2
    lax.fori_loop(0, safe, back, 0, unroll=2)
    place = lax.broadcasted_iota(jnp.int32, (CHUNKS, lanes), 0)
    ends = {}
    for j in range(taps - 1):
        before = zero
        for offset in range(taps - 1 - j, taps):
            at = j - taps + 1 + offset
            before = before + conv_ref[offset : offset + 1, :] * (
                passed[at] * keep(offset, at)
            )
        rim_grad_ref[j : j + 1, :] = before[0:1]
        ends[steps - taps + 1 + j] = jnp.where(
            place < CHUNKS - 1, pltpu.roll(before, CHUNKS - 1, axis=0), 0.0
        )
    for pair in range(safe, steps // 2):
        both = []
        for step in (2 * pair, 2 * pair + 1):
            total = reach(step, min(taps, steps - step))
            if step in ends:
                total = total + ends[step]
                j = step - steps + taps - 1
                edge_ref[j : j + 1, :] = total[CHUNKS - 1 : CHUNKS]
            both.append(total)
        grad_value_ref[2 * pair * CHUNKS : (2 * pair + 2) * CHUNKS, :] = jnp.concatenate(
            both, axis=0
        ).astype(jnp.bfloat16)
    small = jnp.zeros((CHUNKS, lanes), jnp.float32)
    rows = [jnp.sum(part, axis=0, keepdims=True) for part in sums[1:] + sums[:1]]
    rows += [grad_bias_ref[...], grad_skip_ref[...]]
    for index, row in enumerate(rows):
        small = jnp.where(place == index, row, small)
    grad_state = dot_tn(grad_selection, act_ref[...])
    parts = [grad_state, grad_step_ref[...], grad_decay_ref[...], small]
    used = sum(part.shape[0] for part in parts)
    parts.append(jnp.zeros((2 * LANES - used, lanes), jnp.float32))
    channel_ref[...] = jnp.concatenate(parts, axis=0).T.astype(jnp.bfloat16)


def mixer_conv_back(layer, grad_act, grad_selection, state_weight, projected, rim, masks, conv_weight,
                    conv_bias, act, grad_step, grad_decay, grad_bias, grad_skip, halved):
    steps, _, channels = grad_act.shape
    tokens = steps * CHUNKS
    taps, columns = conv_weight.shape[1], state_weight.shape[2]
    states, rank = grad_decay.shape[0], grad_step.shape[0]
    lanes = 2 * LANES
    f32 = jnp.float32

    def cubes(count):
        return pl.BlockSpec((count, CHUNKS, lanes), lambda c: (0, 0, c))

    def rows(count):
        return pl.BlockSpec((count, lanes), lambda c: (0, c))

    def weight_rows(count):
        return pl.BlockSpec((None, count, lanes), lambda c: (layer, 0, c))

    return plain_call(
        functools.partial(conv_back_kernel, (taps, states, steps)),
        (channels // lanes,),
        [cubes(steps), whole(grad_selection.shape),
         pl.BlockSpec((None, lanes, columns), lambda c: (layer, c, 0)), cubes(steps),
         rows(taps - 1), whole(masks.shape), weight_rows(taps), weight_rows(1),
         rows(tokens), rows(rank), rows(states), rows(1), rows(1), ANYWHERE],
        [rows(tokens), rows(taps - 1), rows(taps - 1),
         pl.BlockSpec((lanes, 2 * LANES), lambda c: (c, 0))],
        [
            shaped((tokens, 2 * channels), jnp.bfloat16),
            shaped((taps - 1, channels)),
            shaped((taps - 1, channels)),
            shaped((channels, 2 * LANES), jnp.bfloat16),
        ],
        [VMEM((steps + taps - 1, CHUNKS, lanes), f32), VMEM((steps + taps - 1, CHUNKS, lanes), f32)],
        (grad_act, grad_selection, state_weight, projected, rim, masks, conv_weight, conv_bias, act, grad_step,
         grad_decay, grad_bias, grad_skip, halved),
        10,
        {13: 0},
    )


def hand_on(layer, count, reverse, total_ref, size_ref, decay_ref, out_ref, scratch, between, after):
    (mine, mine_length, near, near_length, both, both_length, far, far_length,
     send, recv, send_length, recv_length) = scratch
    here = lax.axis_index("wide")
    group = lax.axis_index("narrow")
    pairs = count // 2
    pair, side = here // 2, lax.rem(here, 2)
    partner = here + 1 - 2 * side
    others = [lax.rem(pair + k, pairs) for k in range(1, pairs)]
    f32 = jnp.float32
    barrier = pltpu.get_barrier_semaphore()
    pl.semaphore_signal(barrier, inc=1, device_id=(partner, group), device_id_type=MESH)
    for other in others:
        pl.semaphore_signal(barrier, inc=1, device_id=(2 * other + side, group), device_id_type=MESH)
    mine[...] = total_ref[...].astype(mine.dtype)
    mine_length[...] = size_ref[...]
    rate = rates_of(decay_ref[layer])
    pl.semaphore_wait(barrier, pairs)

    def hand(index, source, source_length, target, target_length, window):
        copies = []
        for src, dst, out, back in (
            (source, target, send, recv), (source_length, target_length, send_length, recv_length)):
            copies.append(pltpu.make_async_remote_copy(
                src_ref=src, dst_ref=dst, send_sem=out.at[index], recv_sem=back.at[index],
                device_id=(window, group), device_id_type=MESH))
            copies[-1].start()
        return copies

    first = hand(0, mine, mine_length, near, near_length, partner)
    between()
    for copy in first:
        copy.wait_recv()
    second_here = (side == 0) if reverse else (side == 1)
    own, own_length = total_ref[...], size_ref[...]
    met, met_length = near[...].astype(f32), near_length[...]
    late_length = jnp.where(second_here, own_length, met_length)
    early = jnp.where(second_here, met, own)
    late = jnp.where(second_here, own, met)
    both[...] = (jnp.exp2(late_length * rate) * early + late).astype(both.dtype)
    both_length[...] = own_length + met_length
    sent = []
    for k, other in enumerate(others):
        sent.append(hand(
            1 + k, both, both_length, far.at[pair], far_length.at[pair], 2 * other + side))
    after()
    for copies in sent:
        for copy in copies:
            copy.wait_recv()
    level = jnp.zeros(own.shape, f32)
    for at in range(pairs - 1, -1, -1) if reverse else range(pairs):
        valid = (pair < at) if reverse else (pair > at)
        step = jnp.exp2(far_length[at] * rate) * level + far[at].astype(f32)
        level = jnp.where(valid, step, level)
    step = jnp.exp2(met_length * rate) * level + met
    out_ref[...] = jnp.where(second_here, step, level)
    for copies in [first] + sent:
        for copy in copies:
            copy.wait_send()


LINK_REFS = 12


def link_scratch(count, states, channels):
    pairs = count // 2
    f32, low = jnp.float32, jnp.bfloat16
    dma = pltpu.SemaphoreType.DMA((pairs,))
    return [
        VMEM((states, channels), low), VMEM((1, channels), f32),
        VMEM((states, channels), low), VMEM((1, channels), f32),
        VMEM((states, channels), low), VMEM((1, channels), f32),
        VMEM((pairs, states, channels), low), VMEM((pairs, 1, channels), f32),
        dma, dma, dma, dma,
    ]


def link_call(kernel, total, size, decay_log, beside, out_shapes, scratch, identity):
    states, channels = total.shape
    inside = pl.BlockSpec(memory_space=VMEM)
    return pl.pallas_call(
        kernel,
        out_shape=[shaped((states, channels))] + out_shapes,
        in_specs=[inside] * 3 + [ANYWHERE] * len(beside),
        out_specs=[inside] + [ANYWHERE] * len(out_shapes),
        scratch_shapes=link_scratch(lax.axis_size("wide"), states, channels) + scratch,
        compiler_params=pltpu.CompilerParams(
            collective_id=identity, has_side_effects=True, vmem_limit_bytes=60 * MIB
        ),
        cost_estimate=microseconds(12),
    )(total, size, decay_log, *beside)


def ahead_kernel(layer, count, wanted, total_ref, size_ref, decay_ref, *refs):
    arrays = len(wanted)
    sources, out_ref, targets = refs[:arrays], refs[arrays], refs[arrays + 1 : 2 * arrays + 1]
    scratch, (*held, got, put) = refs[2 * arrays + 1 :][:LINK_REFS], refs[2 * arrays + 1 + LINK_REFS :]
    into = [
        pltpu.make_async_copy(sources[i].at[wanted[i]], held[i], got.at[i]) for i in range(arrays)]
    out = [pltpu.make_async_copy(held[i], targets[i], put.at[i]) for i in range(arrays)]
    for copy in into:
        copy.start()

    def after():
        for i in range(arrays):
            into[i].wait()
            out[i].start()

    hand_on(layer, count, False, total_ref, size_ref, decay_ref, out_ref, scratch, lambda: None, after)
    for copy in out:
        copy.wait()


def handed_ahead(layer, total, size, decay_log, wanted, identity):
    shapes = [array.shape[1:] for array, _ in wanted]
    dma = pltpu.SemaphoreType.DMA((len(wanted),))
    return link_call(
        functools.partial(ahead_kernel, layer, lax.axis_size("wide"), tuple(which for _, which in wanted)),
        total, size, decay_log, [array for array, _ in wanted],
        [shaped(shape, array.dtype) for shape, (array, _) in zip(shapes, wanted)],
        [VMEM(shape, array.dtype) for shape, (array, _) in zip(shapes, wanted)] + [dma, dma],
        identity)


def behind_kernel(layer, count, total_ref, size_ref, decay_ref, rows_hbm, pre_hbm, hidden_hbm, grad_hbm,
                  out_ref, *refs):
    outs = len(refs) - LINK_REFS - 6
    outs //= 2
    targets, scratch = refs[:outs], refs[outs : outs + LINK_REFS]
    rows, pre, hidden_rows, grad, *found = refs[outs + LINK_REFS : -2]
    got, put = refs[-2:]
    members, _, hidden = pre.shape
    width = rows.shape[1]
    low = jnp.bfloat16
    loads = [
        pltpu.make_async_copy(source, target, got.at[i])
        for i, (source, target) in enumerate(
            ((rows_hbm, rows), (pre_hbm, pre), (hidden_hbm, hidden_rows), (grad_hbm, grad)))
    ]
    for load in loads:
        load.start()
    stores = [
        [pltpu.make_async_copy(found[i].at[s], targets[i].at[s], put.at[i, s]) for i in range(outs)]
        for s in range(members)
    ]

    def weights(s):
        up = dot_tn(rows[...], pre[s]).astype(low)
        down = dot_tn(hidden_rows[s], grad[...]).astype(low)
        if outs == 2:
            found[0][s], found[1][s] = up, down
        else:
            found[0][s, :width] = up
            for f in range(width // hidden):
                found[0][s, width + f * hidden : width + (f + 1) * hidden] = down[
                    :, f * hidden : (f + 1) * hidden]
        for store in stores[s]:
            store.start()

    def between():
        for load in loads:
            load.wait()
        weights(0)

    def after():
        for s in range(1, members):
            weights(s)

    hand_on(layer, count, True, total_ref, size_ref, decay_ref, out_ref, scratch, between, after)
    for pair in stores:
        for store in pair:
            store.wait()


def handed_back(layer, total, size, decay_log, rows, pre, hidden_rows, grad_rows, identity):
    members, _, hidden = pre.shape
    width = rows.shape[1]
    low = jnp.bfloat16
    sizes = [(2 * width, hidden)] if folds(width, hidden) else [(width, hidden), (hidden, width)]
    shapes = [(members,) + size for size in sizes]
    return link_call(
        functools.partial(behind_kernel, layer, lax.axis_size("wide")),
        total, size, decay_log, [rows, pre, hidden_rows, grad_rows],
        [shaped(shape, low) for shape in shapes],
        [VMEM(array.shape, low) for array in (rows, pre, hidden_rows, grad_rows)]
        + [VMEM(shape, low) for shape in shapes]
        + [pltpu.SemaphoreType.DMA((4,)), pltpu.SemaphoreType.DMA((len(shapes), members))],
        identity)


def bell(values):
    return 0.5 * (1.0 + lax.erf(values * 0.7071067811865476))


def expert_kernel(dims, kinds, beside, which, *refs):
    count, groups, members, block, share, width, hidden = dims
    flows = len(kinds)
    out_refs, (perm_ref, up_hbm, down_hbm, *refs) = refs[:flows], refs[flows:]
    if kinds == (True,):
        pre_hbm, *refs = refs
    if beside:
        next_hbm, *refs = refs
    results, refs = [refs[3 * f : 3 * f + 3] for f in range(flows)], refs[3 * flows :]
    if kinds == (False,):
        pre_hbm, *refs = refs
    if beside:
        met_hbm, *refs = refs
        *refs, leaving, met, next_send, next_recv, next_local = refs
    pre, up, down, total, local, *refs = refs
    scratch = [refs[16 * f : 16 * f + 16] for f in range(flows)]
    f32, bf16 = jnp.float32, jnp.bfloat16
    here = lax.axis_index("wide")
    group = lax.axis_index("narrow")
    quads = count // members
    quad, member = here // members, lax.rem(here, members)
    lines = groups // 2
    line, core = group // 2, lax.rem(group, 2)
    near_group = group + 1 - 2 * core
    others = [(2 * away + c, 2 * lax.rem(line + away, lines) + c) for away in range(1, lines) for c in (0, 1)]
    early = 2 * (share // groups) // 16 * 16
    head, tail = pl.ds(0, early), pl.ds(early, share - early)
    ways = [(away, turn) for turn in range(members) for away in list(range(1, quads)) + [0] if away or turn]

    loads = [
        pltpu.make_async_copy(up_hbm, up, local.at[0]),
        pltpu.make_async_copy(down_hbm, down, local.at[1]),
    ]
    if kinds == (True,):
        loads.append(pltpu.make_async_copy(pre_hbm, pre, local.at[2]))
    for load in loads:
        load.start()
    if beside:
        source = next_hbm if which is None else next_hbm.at[which]
        next_load = pltpu.make_async_copy(source, leaving, next_local.at[0])
        next_load.start()

    def window_at(away, turn):
        return lax.rem(quad + away, quads) * members + lax.rem(member + turn, members)

    def span(window, part=None):
        start, size = (0, share) if part is None else ((0, early), (early, share - early))[part]
        return pl.ds(pl.multiple_of(window * share + start, 16), size)

    barrier = pltpu.get_barrier_semaphore()
    for peer in [near_group] + [other for _, other in others]:
        pl.semaphore_signal(barrier, inc=1, device_id=(here, peer), device_id_type=MESH)
    for away in range(quads):
        for turn in range(members):
            if away or turn:
                pl.semaphore_signal(
                    barrier, inc=1, device_id=(window_at(away, turn), group), device_id_type=MESH)
    pl.semaphore_wait(barrier, groups - 1 + count - 1)
    order = perm_ref[...].reshape(members, share, groups * block)
    sent, saves = [], []

    def hand_over(k, source, target, send, recv):
        if k:
            place, peer = others[k - 1]
            away = place // 2
            landing, signal = (lines - away) * 2 + core, 2 * away - 1 + core
        else:
            peer, landing, signal = near_group, core, 0
        copy = pltpu.make_async_remote_copy(
            src_ref=source, dst_ref=target.at[landing], send_sem=send.at[k], recv_sem=recv.at[signal],
            device_id=(here, peer), device_id_type=MESH)
        copy.start()
        sent.append(copy)

    def taken(k, like, target, send, recv):
        pltpu.make_async_remote_copy(
            src_ref=like, dst_ref=target.at[0], send_sem=send.at[k], recv_sem=recv.at[k],
            device_id=(here, near_group), device_id_type=MESH).wait_recv()

    class Flow:
        def __init__(self, backward, out_ref, result, scratch):
            self.backward, self.out_ref = backward, out_ref
            self.ret_ref, self.rows_hbm, self.low_hbm = result
            (self.arrived, self.own, self.rows, self.low, self.part, self.got, self.final, self.landed,
             self.there_send, self.there_recv, self.row_send, self.row_recv, self.sum_send, self.sum_recv,
             self.back_send, self.back_recv) = scratch

        def to_groups(self):
            there = self.there_send, self.there_recv
            hand_over(0, self.out_ref.at[near_group], self.arrived, *there)
            for k, (_, other) in enumerate(others):
                hand_over(1 + k, self.out_ref.at[other], self.arrived, *there)
            self.arrived[core] = self.out_ref[group]

        def carry(self, part):
            for away, turn in ways:
                copy = pltpu.make_async_remote_copy(
                    src_ref=self.own.at[lax.rem(member + turn, members), (head, tail)[part]],
                    dst_ref=self.rows.at[span(here, part), :],
                    send_sem=self.row_send.at[away, turn, part], recv_sem=self.row_recv.at[away, turn, part],
                    device_id=(window_at(away, turn), group), device_id_type=MESH)
                copy.start()
                sent.append(copy)

        def to_experts(self):
            there = self.there_send, self.there_recv
            taken(0, self.out_ref.at[group], self.arrived, *there)
            first = self.arrived[pl.ds(0, 2)].reshape(2 * block, width)
            self.own[:, head] = dot_nn(
                order[:, :early, : 2 * block].reshape(members * early, 2 * block), first
            ).astype(bf16).reshape(members, early, width)
            self.carry(0)
            for k in range(1, groups - 1):
                taken(k, self.out_ref.at[group], self.arrived, *there)
            self.own[:, tail] = dot_nn(
                order[:, early:].reshape(members * (share - early), groups * block),
                self.arrived[...].reshape(groups * block, width),
            ).astype(bf16).reshape(members, share - early, width)
            self.carry(1)
            self.rows[span(here), :] = self.own[member]

        def arrive(self, away, turn):
            window = lax.rem(quad + quads - away, quads) * members + lax.rem(member + members - turn, members)
            for part in (0, 1):
                pltpu.make_async_remote_copy(
                    src_ref=self.own.at[member, (head, tail)[part]], dst_ref=self.rows.at[span(window, part), :],
                    send_sem=self.row_send.at[away, turn, part], recv_sem=self.row_recv.at[away, turn, part],
                    device_id=(window, group), device_id_type=MESH).wait_recv()
            return window

        def compute(self, windows):
            size = len(windows) * share

            def one(s, carry):
                x = jnp.concatenate([self.rows[span(w), :] for w in windows], axis=0)
                if self.backward:
                    grad_hidden = dot_nt(x, down[s])
                    before = jnp.concatenate([pre[s, span(w), :] for w in windows], axis=0)
                    slope = bell(before) + before * (
                        0.3989422804014327 * jnp.exp(-0.5 * before * before))
                    middle = (grad_hidden * slope).astype(bf16)
                    y = dot_nt(middle, up[s])
                else:
                    before = dot_nn(x, up[s])
                    middle = (before * bell(before)).astype(bf16)
                    y = dot_nn(middle, down[s])
                for index, w in enumerate(windows):
                    piece = slice(index * share, (index + 1) * share)
                    if not self.backward:
                        pre[s, span(w), :] = before[piece]
                    self.low[s, span(w), :] = middle[piece]

                @pl.when(s == 0)
                def _():
                    total[:size] = y

                @pl.when(s > 0)
                def _():
                    total[:size] += y

                return carry

            lax.fori_loop(0, members, one, 0)
            for index, w in enumerate(windows):
                self.part[w] = total[index * share : (index + 1) * share].astype(bf16)

        def give_back(self, away, turn, window, part):
            copy = pltpu.make_async_remote_copy(
                src_ref=self.part.at[window, (head, tail)[part]], dst_ref=self.got.at[here, (head, tail)[part]],
                send_sem=self.sum_send.at[away, turn, part], recv_sem=self.sum_recv.at[away, turn, part],
                device_id=(window, group), device_id_type=MESH)
            copy.start()
            sent.append(copy)

        def work(self, first_save):
            windows = [here] + [self.arrive(0, turn) for turn in range(1, members)]
            self.compute(windows)
            for part in (1, 0):
                for turn in range(1, members):
                    self.give_back(0, turn, windows[turn], part)
            self.got[here] = self.part[here]
            late = []
            for away in range(1, quads):
                for first in range(0, members, 2):
                    windows = [self.arrive(away, turn) for turn in (first, first + 1)]
                    self.compute(windows)
                    for turn in (first, first + 1):
                        self.give_back(away, turn, windows[turn - first], 1)
                        late.append((away, turn, windows[turn - first]))
            for away, turn, window in late:
                self.give_back(away, turn, window, 0)
            for k, (source, target) in enumerate(((self.rows, self.rows_hbm), (self.low, self.low_hbm))):
                saves.append(pltpu.make_async_copy(source, target, local.at[first_save + k]))
                saves[-1].start()

        def returned(self, part):
            place = (head, tail)[part]
            for away, turn in ways:
                window = window_at(away, turn)
                pltpu.make_async_remote_copy(
                    src_ref=self.part.at[here, place], dst_ref=self.got.at[window, place],
                    send_sem=self.sum_send.at[away, turn, part], recv_sem=self.sum_recv.at[away, turn, part],
                    device_id=(window, group), device_id_type=MESH).wait_recv()
            summed = self.got[pl.ds(0, members), place].astype(f32)
            for q in range(1, quads):
                summed = summed + self.got[pl.ds(q * members, members), place].astype(f32)
            return summed.astype(bf16)

        def leave(self):
            back = self.back_send, self.back_recv
            later = self.returned(1)
            rest = groups - 2
            self.final[pl.ds(2, rest)] = dot_tn(
                order[:, early:, 2 * block :].reshape(members * (share - early), rest * block),
                later.reshape(members * (share - early), width),
            ).astype(bf16).reshape(rest, block, width)
            for k, (place, _) in enumerate(others):
                hand_over(1 + k, self.final.at[place], self.landed, *back)
            sooner = self.returned(0)
            self.final[pl.ds(0, 2)] = (
                dot_tn(order[:, :early, : 2 * block].reshape(members * early, 2 * block),
                       sooner.reshape(members * early, width))
                + dot_tn(order[:, early:, : 2 * block].reshape(members * (share - early), 2 * block),
                         later.reshape(members * (share - early), width))
            ).astype(bf16).reshape(2, block, width)
            hand_over(0, self.final.at[1 - core], self.landed, *back)
            self.ret_ref[group] = self.final[core]

        def land(self):
            for k in range(groups - 1):
                taken(k, self.out_ref.at[group], self.landed, self.back_send, self.back_recv)
            self.ret_ref[near_group] = self.landed[1 - core]
            for place, other in others:
                self.ret_ref[other] = self.landed[place]

    travels = [Flow(*parts) for parts in zip(kinds, out_refs, results, scratch)]
    for flow in travels:
        flow.to_groups()
    for flow in travels:
        flow.to_experts()

    def send_beside(turns):
        for turn in turns if beside else ():
            copy = pltpu.make_async_remote_copy(
                src_ref=leaving.at[lax.rem(member + turn, members)], dst_ref=met.at[member],
                send_sem=next_send.at[turn], recv_sem=next_recv.at[turn],
                device_id=(window_at(0, turn), group), device_id_type=MESH)
            copy.start()
            beside_copies.append(copy)

    beside_copies = []
    if beside:
        next_load.wait()
        met[member] = leaving[member]
    send_beside([1])
    for load in loads:
        load.wait()
    for f, flow in enumerate(travels):
        flow.work(3 + 2 * f)
    send_beside(range(2, members))
    if kinds == (False,):
        saves.append(pltpu.make_async_copy(pre, pre_hbm, local.at[2]))
        saves[-1].start()
    for flow in travels:
        flow.leave()
    for flow in travels:
        flow.land()
    if beside:
        for copy in beside_copies:
            copy.wait_recv()
        saves.append(pltpu.make_async_copy(met, met_hbm, next_local.at[1]))
        saves[-1].start()
    for copy in sent + beside_copies:
        copy.wait_send()
    for save in saves:
        save.wait()


def expert_pass(outbounds, kinds, perm, weights, pre, identity, beside=None, which=None):
    count, groups = lax.axis_size("wide"), lax.axis_size("narrow")
    _, block, width = outbounds[0].shape
    members, _, hidden = weights[0].shape
    share = perm.shape[0] // members
    quads = count // members
    total = count * share
    low, f32 = jnp.bfloat16, jnp.float32
    dims = (count, groups, members, block, share, width, hidden)
    inside = pl.BlockSpec(memory_space=VMEM)
    args = tuple(outbounds) + (perm,) + tuple(weights) + (() if pre is None else (pre,))
    args += () if beside is None else (beside,)
    out_specs, outs = [], []
    for _ in kinds:
        out_specs += [inside, ANYWHERE, ANYWHERE]
        outs += [shaped((groups, block, width), low), shaped((total, width), low),
                 shaped((members, total, hidden), low)]
    if kinds == (False,):
        outs.append(shaped((members, total, hidden)))
    dma = pltpu.SemaphoreType.DMA
    scratch = [
        VMEM((members, total, hidden), f32),
        VMEM((members, width, hidden), low),
        VMEM((members, hidden, width), low),
        VMEM((members * share, width), f32),
        dma((3 + 2 * len(kinds),)),
    ]
    for _ in kinds:
        scratch += [
            VMEM((groups, block, width), low),
            VMEM((members, share, width), low),
            VMEM((total, width), low),
            VMEM((members, total, hidden), low),
            VMEM((count, share, width), low),
            VMEM((count, share, width), low),
            VMEM((groups, block, width), low),
            VMEM((groups, block, width), low),
            dma((groups - 1,)), dma((groups - 1,)),
            dma((quads, members, 2)), dma((quads, members, 2)),
            dma((quads, members, 2)), dma((quads, members, 2)),
            dma((groups - 1,)), dma((groups - 1,)),
        ]
    if beside is not None:
        shape = beside.shape[-3:]
        outs.append(shaped(shape, low))
        scratch += [VMEM(shape, low), VMEM(shape, low), dma((members,)), dma((members,)), dma((2,))]
    out_specs += [ANYWHERE] * (len(outs) - len(out_specs))
    return pl.pallas_call(
        functools.partial(expert_kernel, dims, tuple(kinds), beside is not None, which),
        out_shape=outs,
        in_specs=[inside] * (len(kinds) + 1) + [ANYWHERE] * (len(args) - len(kinds) - 1),
        out_specs=out_specs,
        scratch_shapes=scratch,
        compiler_params=pltpu.CompilerParams(
            collective_id=identity, has_side_effects=True, vmem_limit_bytes=60 * MIB
        ),
        cost_estimate=microseconds(65),
    )(*args)


def expert_order(experts, groups, block, capacity):
    share = groups * capacity
    row = jnp.arange(experts * share, dtype=jnp.int32)
    expert, rest = row // share, row % share
    source = (rest // capacity) * block + expert * capacity + rest % capacity
    return (source[:, None] == jnp.arange(groups * block, dtype=jnp.int32)[None, :]).astype(jnp.bfloat16)


def between_members(arrays):
    count, members = lax.axis_size("wide"), arrays[0].shape[0]
    quads = [list(range(first, first + members)) for first in range(0, count, members)]
    return [
        lax.all_to_all(values, "wide", split_axis=0, concat_axis=0, tiled=True, axis_index_groups=quads)
        for values in arrays
    ]


def slice_kernel(layer, from_ref, to_ref, held, got, put):
    count = held.shape[0]
    incoming = [pltpu.make_async_copy(from_ref.at[layer, e], held.at[e], got.at[e]) for e in range(count)]
    outgoing = [pltpu.make_async_copy(held.at[e], to_ref.at[e], put.at[e]) for e in range(count)]
    for copy in incoming:
        copy.start()
    for into, out in zip(incoming, outgoing):
        into.wait()
        out.start()
    for out in outgoing:
        out.wait()


def layer_of(values, layer):
    shape = values.shape[1:]
    return pl.pallas_call(
        functools.partial(slice_kernel, layer),
        out_shape=shaped(shape, values.dtype),
        in_specs=[ANYWHERE],
        out_specs=ANYWHERE,
        scratch_shapes=[
            VMEM(shape, values.dtype), pltpu.SemaphoreType.DMA(shape[:1]), pltpu.SemaphoreType.DMA(shape[:1])],
        compiler_params=pltpu.CompilerParams(vmem_limit_bytes=60 * MIB),
        cost_estimate=microseconds(2),
    )(values)


def folds(width, hidden):
    return 0 if hidden % LANES else width // hidden


def widen_kernel(arrays, *refs):
    refs, (up_ref, down_ref) = refs[:arrays], refs[-2:]
    width, hidden = up_ref.shape
    if arrays == 2:
        up_ref[...] = refs[0][...].astype(jnp.float32)
        down_ref[...] = refs[1][...].astype(jnp.float32)
        return
    up_ref[...] = refs[0][:width].astype(jnp.float32)
    for f in range(width // hidden):
        down_ref[:, f * hidden : (f + 1) * hidden] = refs[0][
            width + f * hidden : width + (f + 1) * hidden].astype(jnp.float32)


def widened(layer, layers, arrays, width, hidden, held):
    experts = arrays[0].shape[0]
    count = len(arrays)
    return plain_call(
        functools.partial(widen_kernel, count),
        (experts,),
        [pl.BlockSpec((None,) + array.shape[1:], lambda e: (e, 0, 0)) for array in arrays]
        + [ANYWHERE] * len(held),
        [pl.BlockSpec((None, None, width, hidden), lambda e: (layer, e, 0, 0)),
         pl.BlockSpec((None, None, hidden, width), lambda e: (layer, e, 0, 0))],
        [shaped((layers, experts, width, hidden)), shaped((layers, experts, hidden, width))],
        [],
        tuple(arrays) + tuple(held),
        60,
        {count + k: k for k in range(len(held))},
    )


def sum_kernel(dims, *refs):
    count, lines, sizes, first_rows, width = dims
    total = len(sizes)
    arrays, out_ref = refs[:total], refs[total]
    (own, near, over, spun, spun_first, home, core_send, core_recv, load, over_send, over_recv,
     spin_send, spin_recv, spin_first_send, spin_first_recv, home_send, home_recv) = refs[total + 1 :]
    rows = sum(sizes)
    later = rows - first_rows
    here = lax.axis_index("wide")
    group = lax.axis_index("narrow")
    line, core = group // 2, lax.rem(group, 2)
    half = count // 2
    low, f32 = jnp.bfloat16, jnp.float32

    def window_of(position):
        position = lax.rem(position + 2 * count, count)
        upper = position // half
        return 2 * position * (1 - upper) + (2 * (count - 1 - position) + 1) * upper

    odd = lax.rem(here, 2)
    spot = (here // 2) * (1 - odd) + (count - 1 - here // 2) * odd
    ring = (window_of(spot + 1), window_of(spot - 1))
    peer = 2 * line + 1 - core
    lines_away = [lax.rem(line + k, lines) for k in range(1, lines)]

    barrier = pltpu.get_barrier_semaphore()
    for window in ring:
        pl.semaphore_signal(barrier, inc=1, device_id=(window, group), device_id_type=MESH)
    pl.semaphore_signal(barrier, inc=1, device_id=(here, peer), device_id_type=MESH)
    for other in lines_away:
        pl.semaphore_signal(barrier, inc=1, device_id=(here, 2 * other + core), device_id_type=MESH)
    pl.semaphore_wait(barrier, 2 + lines)

    order = [spot + half]
    for away in range(half - 1, 0, -1):
        order += [spot + away, spot - away]
    order = [window_of(position) for position in order + [spot]]
    sent, held = [], []
    for k, window in enumerate(order):
        held.append([])
        start = 0
        for i, size in enumerate(sizes):
            place = pl.ds(start, size)
            start += size
            copy = pltpu.make_async_remote_copy(
                src_ref=arrays[i].at[window, :, 1 - core], dst_ref=near.at[window, :, place],
                send_sem=core_send.at[k, i], recv_sem=core_recv.at[k, i],
                device_id=(here, peer), device_id_type=MESH)
            copy.start()
            mine = pltpu.make_async_copy(
                arrays[i].at[window, :, core], own.at[window, :, place], load.at[k, i])
            mine.start()
            sent.append(copy)
            held[-1].append((copy, mine))

    ahead, behind = pl.ds(0, first_rows), pl.ds(first_rows, later)
    cut_first = first_rows // 32 * 16
    cut_later = later // 32 * 16
    parts_first = (pl.ds(0, cut_first), pl.ds(cut_first, first_rows - cut_first))
    parts_later = (
        pl.ds(first_rows, cut_later), pl.ds(first_rows + cut_later, later - cut_later))
    parts_got = (pl.ds(0, cut_later), pl.ds(cut_later, later - cut_later))

    def meet(k):
        window = order[k]
        for copy, mine in held[k]:
            copy.wait_recv()
            mine.wait()

        def one(at, carry):
            place = pl.ds(pl.multiple_of(at * 16, 16), 16)
            for x in range(lines):
                own[window, x, place] = (
                    own[window, x, place].astype(f32) + near[window, x, place].astype(f32)
                ).astype(low)
            return carry

        lax.fori_loop(0, rows // 16, one, 0)
        for j, other in enumerate(lines_away):
            copy = pltpu.make_async_remote_copy(
                src_ref=own.at[window, other, ahead], dst_ref=over.at[j, window],
                send_sem=over_send.at[j, k], recv_sem=over_recv.at[j, k],
                device_id=(here, 2 * other + core), device_id_type=MESH)
            copy.start()
            sent.append(copy)
            crossing[k].append(copy)

    crossing = [[] for _ in order]

    def spin_later(step):
        for way, sign in ((0, 1), (1, -1)):
            window = window_of(spot + sign * (half - step))
            if step == 0:
                which, got_which = parts_later[way], parts_got[way]
                if not (later - cut_later if way else cut_later):
                    continue
            else:
                which, got_which = behind, pl.ds(0, later)
                add_which, add_got = (
                    (parts_later[way], parts_got[way]) if step == 1 else (which, got_which))
                if turns[way]:
                    turns[way][-1].wait_recv()
                    own[window, :, add_which] = (
                        own[window, :, add_which].astype(f32)
                        + spun[way, step - 1, :, add_got].astype(f32)
                    ).astype(low)
            copy = pltpu.make_async_remote_copy(
                src_ref=own.at[window, :, which], dst_ref=spun.at[way, step, :, got_which],
                send_sem=spin_send.at[way, step], recv_sem=spin_recv.at[way, step],
                device_id=(ring[way], group), device_id_type=MESH)
            copy.start()
            sent.append(copy)
            turns[way].append(copy)

    def cross(k):
        window = order[k]
        value = own[window, line, ahead].astype(f32)
        for j, copy in enumerate(crossing[k]):
            copy.wait_recv()
            value = value + over[j, window].astype(f32)
        return value

    first_turns = ([], [])

    def spin_first(step):
        for way, sign in ((0, 1), (1, -1)):
            k = 0 if step == 0 else 2 * step - 1 + way
            window = order[k]
            if step or way == 0:
                own[window, line, ahead] = cross(k).astype(low)
            if step == 0:
                which = parts_first[way]
            else:
                which = ahead
                add_which = parts_first[way] if step == 1 else which
                first_turns[way][-1].wait_recv()
                own[window, line, add_which] = (
                    own[window, line, add_which].astype(f32)
                    + spun_first[way, step - 1, add_which].astype(f32)
                ).astype(low)
            copy = pltpu.make_async_remote_copy(
                src_ref=own.at[window, line, which], dst_ref=spun_first.at[way, step, which],
                send_sem=spin_first_send.at[way, step], recv_sem=spin_first_recv.at[way, step],
                device_id=(ring[way], group), device_id_type=MESH)
            copy.start()
            sent.append(copy)
            first_turns[way].append(copy)

    turns = ([], [])
    meet(0)
    spin_later(0)
    for step in range(1, half):
        meet(2 * step - 1)
        meet(2 * step)
        spin_first(step - 1)
        spin_later(step)
    meet(len(order) - 1)
    spin_first(half - 1)
    summed = own[here, :, behind].astype(f32)
    for way in (0, 1):
        turns[way][-1].wait_recv()
        summed = summed + spun[way, half - 1].astype(f32)
    own[here, :, behind] = summed.astype(low)
    homes = []
    for j, other in enumerate(lines_away):
        copy = pltpu.make_async_remote_copy(
            src_ref=own.at[here, other, behind], dst_ref=home.at[j],
            send_sem=home_send.at[j], recv_sem=home_recv.at[j],
            device_id=(here, 2 * other + core), device_id_type=MESH)
        copy.start()
        sent.append(copy)
        homes.append(copy)

    summed = cross(len(order) - 1)
    for way in (0, 1):
        first_turns[way][-1].wait_recv()
        summed = summed + spun_first[way, half - 1].astype(f32)
    out_ref[ahead, :] = summed
    value = own[here, line, behind].astype(f32)
    for j, copy in enumerate(homes):
        copy.wait_recv()
        value = value + home[j].astype(f32)
    out_ref[behind, :] = value
    for copy in sent:
        copy.wait_send()


def summed_shares(arrays, identity):
    count, groups = lax.axis_size("wide"), lax.axis_size("narrow")
    lines, half = groups // 2, count // 2
    width = arrays[0].shape[2]
    if any(array.shape[1] % 16 for array in arrays):
        packed = jnp.concatenate(arrays, axis=1)
        arrays = [jnp.pad(packed, ((0, 0), (0, -packed.shape[1] % 16), (0, 0)))]
    sizes = tuple(array.shape[1] for array in arrays)
    rows = sum(sizes)
    first = max(32, rows * 11 // 20 // 16 * 16)
    later = rows - first
    low = jnp.bfloat16
    dma = pltpu.SemaphoreType.DMA
    return pl.pallas_call(
        functools.partial(sum_kernel, (count, lines, sizes, first, width)),
        out_shape=jax.ShapeDtypeStruct((rows, width), jnp.float32),
        in_specs=[ANYWHERE] * len(arrays),
        out_specs=pl.BlockSpec(memory_space=VMEM),
        scratch_shapes=[
            VMEM((count, lines, rows, width), low),
            VMEM((count, lines, rows, width), low),
            VMEM((lines - 1, count, first, width), low),
            VMEM((2, half, lines, later, width), low),
            VMEM((2, half, first, width), low),
            VMEM((lines - 1, later, width), low),
            dma((count, len(arrays))), dma((count, len(arrays))), dma((count, len(arrays))),
            dma((lines - 1, count)), dma((lines - 1, count)),
            dma((2, half)), dma((2, half)),
            dma((2, half)), dma((2, half)),
            dma((lines - 1,)), dma((lines - 1,)),
        ],
        compiler_params=pltpu.CompilerParams(
            collective_id=identity, has_side_effects=True, vmem_limit_bytes=60 * MIB
        ),
        cost_estimate=microseconds(60),
    )(*[array.reshape(count, lines, 2, array.shape[1], width) for array in arrays])


def inward_kernel(dims, grad_ref, weight_ref, edge_ref, handed_ref, keep_ref, normed_ref, begin_ref, gain_ref,
                  passed_ref, out_ref, channel_ref, router_ref, expert_ref, packed_ref, new_ref, *refs):
    blocks, wide, tall, held, fold, marks, spare, steps = dims
    *turned_ref, rows, features, held_block = refs
    owners, count, _ = packed_ref.shape
    f32, low = jnp.float32, jnp.bfloat16
    step = pl.program_id(0)
    tokens = grad_ref.shape[0]
    last = edge_ref.shape[0]
    edited = (last + 1) // 2 * 2 * CHUNKS
    held_block[...] = grad_ref[...]

    @pl.when(lax.rem(step, blocks) < blocks // 2)
    def _():
        edge = edge_ref[...] + handed_ref[...] * keep_ref[...]
        ends = grad_ref[tokens - edited :, :].astype(f32)
        place = lax.broadcasted_iota(jnp.int32, ends.shape, 0)
        for j in range(last):
            row = edited - (last - j) * CHUNKS + CHUNKS - 1
            ends = jnp.where(place == row, edge[j : j + 1], ends)
        held_block[tokens - edited :, :] = ends.astype(low)

    block = held_block[...]

    @pl.when(step == 0)
    def _():
        new_ref[...] = jnp.zeros_like(new_ref)
        rows[...] = jnp.zeros_like(rows)

    @pl.when(step < blocks)
    def _():
        new_ref[...] += dot_nt(block, weight_ref[...])

    @pl.when(step == blocks - 1)
    def _():
        grad, norm_grad = rms_back(begin_ref[...], gain_ref[...], new_ref[...])
        new_ref[...] = passed_ref[...] + grad
        if turned_ref:
            by_step = new_ref[...].reshape(steps, CHUNKS, grad.shape[1])
            for chunk in range(CHUNKS):
                turned_ref[0][chunk * steps : (chunk + 1) * steps, :] = by_step[:, chunk, :]
        experts = router_ref.shape[1]
        lane = lax.broadcasted_iota(jnp.int32, (experts, 2 * LANES), 1)
        row = lax.broadcasted_iota(jnp.int32, (experts, 2 * LANES), 0)
        pick = (lane == row + spare).astype(f32).astype(low)
        lane = lax.broadcasted_iota(jnp.int32, (2, 2 * LANES), 1)
        row = lax.broadcasted_iota(jnp.int32, (2, 2 * LANES), 0)
        pick_norms = (lane == row + spare + experts).astype(f32).astype(low)
        norms = jnp.concatenate([norm_grad[None], expert_ref[...]], axis=0).astype(low)
        features[...] = dot_nn(router_ref[...].astype(low), pick) + dot_tn(norms, pick_norms)

    @pl.when(step >= blocks)
    def _():
        grad = dot_tn(block, normed_ref[...])
        passed = out_ref[...]
        channel = channel_ref[...].astype(f32)
        start = pl.multiple_of((step - blocks) * owners * marks, 8)
        mine = features[pl.ds(start, owners * marks), :]
        thin = held // fold
        whole_tiles = not any(size % 16 for size in (wide, tall, thin))
        target = packed_ref if whole_tiles else rows
        kind = target.dtype
        for k in range(owners):
            target[k, :wide] = grad[k * wide : (k + 1) * wide].astype(kind)
            target[k, wide : wide + tall] = passed[k * tall : (k + 1) * tall].astype(kind)
            small = channel[k * held : (k + 1) * held]
            extra = mine[k * marks : (k + 1) * marks]
            small = small + jnp.concatenate([extra, jnp.zeros((held - marks, 2 * LANES), f32)], axis=0)
            for f in range(fold):
                target[k, wide + tall : wide + tall + thin, f * 2 * LANES : (f + 1) * 2 * LANES] = small[
                    f * thin : (f + 1) * thin].astype(kind)
            if whole_tiles and count > wide + tall + thin:
                packed_ref[k, wide + tall + thin :] = jnp.zeros((count - wide - tall - thin, grad.shape[1]), kind)
        if not whole_tiles:
            packed_ref[...] = rows[...].astype(low)


def mixer_inward(layer, grad_projected, in_weight, edge, handed, keep, normed, begin, gain, passed, grad_out, channel,
                 grad_router, grad_expert, devices, spare):
    tokens, columns = grad_projected.shape
    width = normed.shape[1]
    wide, tall = columns // devices, grad_out.shape[0] // devices
    held, marks = channel.shape[0] // devices, width // devices
    fold = width // (2 * LANES)
    count = wide + tall + held // fold
    count += -count % 16
    owners = width // wide
    blocks = devices // owners
    span = owners * wide
    taps = edge.shape[0]
    inner = edge.shape[1] // span
    turned = layer == 0

    def at(i):
        return jnp.maximum(i - blocks, 0)

    return plain_call(
        functools.partial(inward_kernel, (blocks, wide, tall, held, fold, marks, spare, tokens // CHUNKS)),
        (2 * blocks,),
        [pl.BlockSpec((tokens, span), lambda i: (0, i % blocks)),
         pl.BlockSpec((None, width, span), lambda i: (layer, 0, jnp.minimum(i, blocks - 1))),
         pl.BlockSpec((taps, span), lambda i: (0, jnp.minimum(i % blocks, inner - 1))),
         pl.BlockSpec((taps, span), lambda i: (0, jnp.minimum(i % blocks, inner - 1))),
         whole(keep.shape), whole(normed.shape), whole(begin.shape), layer_whole(layer, (1, width)), whole(passed.shape),
         pl.BlockSpec((owners * tall, width), lambda i: (at(i), 0)),
         pl.BlockSpec((owners * held, 2 * LANES), lambda i: (at(i), 0)),
         whole(grad_router.shape), whole(grad_expert.shape)],
        [pl.BlockSpec((owners, count, width), lambda i: (at(i), 0, 0)), whole((tokens, width))]
        + turned * [whole((tokens, width))],
        [shaped((devices, count, width), jnp.bfloat16), shaped((tokens, width))]
        + turned * [shaped((tokens, width))],
        [VMEM((owners, count, width), jnp.float32), VMEM((width, 2 * LANES), jnp.float32),
         VMEM((tokens, span), jnp.bfloat16)],
        (grad_projected, in_weight, edge, handed, keep, normed, begin, gain, passed, grad_out, channel, grad_router,
         grad_expert),
        9,
    )


def unfold_kernel(dims, *refs):
    layers, wide, tall, held, fold, marks, spare, sizes = dims
    inputs, outs = refs[:layers], refs[layers:]
    (in_ref, out_ref, state_ref, step_ref, decay_ref, conv_ref, conv_bias_ref, step_bias_ref, skip_ref,
     router_ref, mix_ref, expert_ref) = outs
    thin = held // fold
    for layer in range(layers):
        whole_rows = inputs[layer][...].astype(jnp.float32)
        in_ref[layer] = whole_rows[:wide]
        out_ref[layer] = whole_rows[wide : wide + tall]
        mine = whole_rows[wide + tall : wide + tall + thin]
        channel = jnp.concatenate(
            [mine[:, f * 2 * LANES : (f + 1) * 2 * LANES] for f in range(fold)], axis=0)
        state_ref[layer] = channel[:, : sizes[0]]
        turned = channel.T
        bounds = [0]
        for size in sizes:
            bounds.append(bounds[-1] + size)
        pieces = [turned[bounds[i] : bounds[i + 1]] for i in range(7)]
        step_ref[layer] = pieces[1]
        decay_ref[layer] = pieces[2]
        conv_ref[layer] = pieces[3]
        conv_bias_ref[layer : layer + 1] = pieces[4]
        step_bias_ref[layer : layer + 1] = pieces[5]
        skip_ref[layer : layer + 1] = pieces[6]
        experts = router_ref.shape[1]
        router_ref[layer] = turned[spare : spare + experts, :marks]
        mix_ref[layer : layer + 1] = turned[spare + experts : spare + experts + 1, :marks]
        expert_ref[layer : layer + 1] = turned[spare + experts + 1 : spare + experts + 2, :marks]


def unfolded(sums, wide, tall, held, marks, experts, spare, sizes):
    layers, width = len(sums), sums[0].shape[1]
    fold = width // (2 * LANES)
    shapes = [
        (wide, width), (tall, width), (held, sizes[0]), (sizes[1], held), (sizes[2], held), (sizes[3], held),
        (held,), (held,), (held,), (experts, marks), (marks,), (marks,),
    ]
    inside = pl.BlockSpec(memory_space=VMEM)
    return pl.pallas_call(
        functools.partial(unfold_kernel, (layers, wide, tall, held, fold, marks, spare, sizes)),
        out_shape=[shaped((layers,) + shape) for shape in shapes],
        in_specs=[inside] * layers,
        out_specs=[inside] * len(shapes),
        compiler_params=pltpu.CompilerParams(vmem_limit_bytes=60 * MIB),
        cost_estimate=microseconds(3),
    )(*sums)


def on_device(
    hidden,
    doc_start,
    expert_choice,
    slot_index,
    norm_mix,
    in_weight,
    conv_weight,
    conv_bias,
    state_weight,
    step_weight,
    step_bias,
    decay_log,
    skip_weight,
    out_weight,
    norm_expert,
    router,
    expert_up,
    expert_down,
    cotangent,
):
    layers = in_weight.shape[0]
    tokens = hidden.shape[1]
    width = hidden.shape[2]
    inner = skip_weight.shape[1]
    rank = step_weight.shape[1]
    states = decay_log.shape[1]
    experts = router.shape[2]
    taps = conv_weight.shape[1]
    steps = tokens // CHUNKS
    both = ("wide", "narrow")
    groups = lax.axis_size("narrow")
    devices = lax.axis_size("wide") * groups
    per_group = experts // groups
    capacity = max(2, 5 * tokens // (4 * experts))
    block = -(-per_group * capacity // 16) * 16
    low, f32 = jnp.bfloat16, jnp.float32
    keep_mask = rim_keep(doc_start[0], taps - 1)[:, None]
    order = expert_order(per_group, groups, block, capacity)
    norm_mix, conv_bias, step_bias, skip_weight, norm_expert = (
        values[:, None, :] for values in (norm_mix, conv_bias, step_bias, skip_weight, norm_expert))
    current = to_steps(hidden[0]).reshape(tokens, width).astype(f32)
    saved = []

    def cube(values):
        return values.reshape(steps, CHUNKS, values.shape[-1])

    tail = passed_along(hidden[0, tokens - taps + 1 :] * keep_mask.astype(low), 1)
    weights = [None] * layers
    ready, tail, slot_index = lax.optimization_barrier((layer_of(expert_up, 0), tail, slot_index))
    weights[0] = between_members([ready])
    reset, masks, fills, onehots, keeps = tables(
        doc_start, expert_choice, slot_index, taps, experts, groups, block, capacity)

    for layer in range(layers):
        if layer == 0:
            normed, projected, rim = mixer_enter(layer, norm_mix, in_weight, current, tail.astype(f32))
            projected = cube(projected)
        else:
            current, back_rows, normed, projected = mixer_enter(
                layer, norm_mix, in_weight, middle, weight, fills[layer - 1],
                returned.reshape(groups * block, width))
            saved[-1]["back_rows"] = back_rows
            projected = cube(projected)
            rim = passed_along(projected[steps - taps + 1 :, CHUNKS - 1, :inner] * keep_mask, 1)
        begin = current
        act, selection, size, link, link_size, total, total_size = mixer_front(
            layer, projected, rim, masks, reset, conv_weight, conv_bias, state_weight, step_weight, step_bias,
            decay_log)
        if layer == 0:
            total, order = lax.optimization_barrier((total, order))
        entering, ready = handed_ahead(layer, total, total_size, decay_log, [(expert_down, layer)], layer)
        weights[layer] += between_members([ready])
        mixed, gated, begins, middle, routed, shares, weight, outbound = mixer_run(
            layer, size, act, selection, reset, decay_log, link, link_size, entering, projected, skip_weight,
            out_weight, current, norm_expert, router, fills[layer], onehots[layer], keeps[layer])
        pre_act = None
        outbound = outbound.reshape(groups, block, width)
        if layer + 1 < layers:
            returned, kept_rows, hidden_low, pre_act, following = expert_pass(
                [outbound], (False,), order, weights[layer], None, 4 + layer, expert_up, layer + 1)
            weights[layer + 1] = [following]
        else:
            grad = to_steps(cotangent[0]).reshape(tokens, width).astype(f32)
            grad_rows_low = (weight * grad).astype(low)
            returning = dot_nn(fills[layer], grad_rows_low).astype(low).reshape(groups, block, width)
            returned, kept_rows, hidden_low, inbound, grad_rows, grad_pre = expert_pass(
                [outbound, returning], (False, True), order, weights[layer], None, 4 + layer)
        saved.append(dict(
            begin=begin, normed=normed, projected=projected, rim=rim, act=act, selection=selection, size=size,
            begins=begins, mixed=mixed, gated=gated, middle=middle, routed=routed, shares=shares, weight=weight,
            kept_rows=kept_rows, pre_act=pre_act, hidden_low=hidden_low))
    back_rows = dot_tn(fills[-1], returned.reshape(groups * block, width))
    saved[-1]["back_rows"] = back_rows
    current = middle + weight * back_rows
    output = to_tokens(cube(current.astype(low)))[None]
    sums = [None] * layers
    wide_grads = ()
    expert_grads = [None] * layers
    per_device = inner // devices
    norm_device = width // devices
    spare = 160
    for layer in range(layers - 1, -1, -1):
        entry = saved[layer]
        fill, weight = fills[layer], entry["weight"]
        weighted = weight * jnp.sum(grad * entry["back_rows"], axis=1, keepdims=True)
        if layer + 1 < layers:
            grad_rows_low = (weight * grad).astype(low)
            outbound = dot_nn(fill, grad_rows_low).astype(low).reshape(groups, block, width)
            inbound, grad_rows, grad_pre = expert_pass(
                [outbound], (True,), order, weights[layer], entry["pre_act"], 6 + layer)
        grad_sent = dot_tn(fill, inbound.reshape(groups * block, width))
        grad_logits_low = (weighted * (onehots[layer] - entry["shares"])).astype(low)
        grad_router = dot_tn(entry["routed"], grad_logits_low)
        grad_routed = grad_sent + dot_nt(grad_logits_low, router[layer])
        grad_middle, grad_norm_expert = rms_back(entry["middle"], norm_expert[layer], grad_routed)
        grad = grad + grad_middle
        grad_low = grad.astype(low)
        grad_y, grad_igate, grad_skip, grad_out, link, link_size, total, total_size = mixer_turn(
            layer, grad_low, out_weight, entry["projected"], entry["mixed"], entry["act"], entry["gated"],
            entry["size"], entry["selection"], reset, decay_log)
        entering, *ready = handed_back(
            layer, total, total_size, decay_log, entry["kept_rows"], grad_pre, entry["hidden_low"], grad_rows,
            2 + layer)
        expert_grads[layer] = between_members(ready)
        grad_act, grad_decay, grad_bias, grad_step, grad_selection = mixer_back(
            layer, entry["size"], entry["act"], grad_y, decay_log, entry["selection"], reset,
            entry["begins"], link, link_size, entering, step_weight, step_bias, skip_weight)
        grad_projected, edge, rim_grad, channel = mixer_conv_back(
            layer, grad_act, grad_selection, state_weight, entry["projected"], entry["rim"], masks, conv_weight,
            conv_bias, entry["act"], grad_step, grad_decay, grad_bias, grad_skip, grad_igate)
        handed = passed_along(rim_grad, -1)
        if layer + 1 < layers:
            wide_grads = widened(layer + 1, layers, expert_grads[layer + 1], width, expert_up.shape[3], wide_grads)
            edge, *wide_grads = lax.optimization_barrier((edge, *wide_grads))
        blocks, grad, *turned = mixer_inward(
            layer, grad_projected, in_weight, edge, handed, keep_mask, entry["normed"], entry["begin"], norm_mix, grad,
            grad_out, channel, grad_router, grad_norm_expert.reshape(1, width), devices, spare)
        if layer:
            blocks, grad = lax.optimization_barrier((blocks, grad))
            rows = blocks.shape[1]
            sums[layer] = lax.psum_scatter(
                blocks.reshape(devices * rows, width), both, scatter_dimension=0, tiled=True)
        else:
            sums[layer] = summed_shares([blocks], 8)
    (grad_in, grad_out, grad_state, grad_step, grad_decay, grad_conv, grad_conv_bias, grad_step_bias, grad_skip,
     grad_router, grad_norm_mix, grad_norm_expert) = unfolded(
        sums, 2 * inner // devices, per_device, per_device, norm_device, experts, spare,
        (rank + 2 * states, rank, states, taps, 1, 1, 1))
    shared = (
        grad_norm_mix, jnp.swapaxes(grad_in, 1, 2), grad_conv, grad_conv_bias, grad_state, grad_step,
        grad_step_bias, grad_decay, grad_skip, grad_out, grad_norm_expert, jnp.swapaxes(grad_router, 1, 2))
    up_grads, down_grads = widened(0, layers, expert_grads[0], width, expert_up.shape[3], wide_grads)
    output_grad = turned[0][None]
    return (output, output_grad, *shared, up_grads, down_grads)


def solution(mesh):
    both = ("wide", "narrow")
    placed = (
        P("narrow", "wide", None),
        P("narrow", "wide"),
        P(None, "narrow", "wide"),
        P(None, "narrow", "wide"),
    ) + (P(),) * 12 + (
        P(None, "narrow", None, "wide"),
        P(None, "narrow", "wide", None),
        P("narrow", "wide", None),
    )
    return jax.shard_map(
        on_device,
        mesh=mesh,
        in_specs=placed,
        out_specs=(
            P("narrow", "wide", None),
            P("narrow", "wide", None),
            P(None, both),
            P(None, None, both),
            P(None, None, both),
            P(None, both),
            P(None, both, None),
            P(None, None, both),
            P(None, both),
            P(None, None, both),
            P(None, both),
            P(None, both, None),
            P(None, both),
            P(None, both, None),
            P(None, "narrow", None, "wide"),
            P(None, "narrow", "wide", None),
        ),
        check_vma=False,
    )
```

```python
import functools

import jax
import jax.numpy as jnp
from jax import lax
from jax.experimental import pallas as pl
from jax.experimental.pallas import tpu as pltpu
from jax.sharding import PartitionSpec as P

EPS = 1e-05
CHUNKS = 8
LANES = 128
LOG2E = 1.4426950408889634
RESET = 1e9
MIB = 1024 * 1024
MESH = pl.DeviceIdType.MESH
VMEM = pltpu.VMEM


def to_steps(values):
    steps = values.shape[0] // CHUNKS
    return jnp.swapaxes(values.reshape((CHUNKS, steps) + values.shape[1:]), 0, 1)


def to_tokens(values):
    moved = jnp.swapaxes(values, 0, 1)
    return moved.reshape((-1,) + values.shape[2:])


def rms_scale(values, gain):
    return values * lax.rsqrt(jnp.mean(values * values, axis=-1, keepdims=True) + EPS) * gain


def rms_back(values, gain, grad):
    scale = lax.rsqrt(jnp.mean(values * values, axis=-1, keepdims=True) + EPS)
    weighted = grad * gain
    inner = jnp.mean(weighted * values, axis=-1, keepdims=True)
    return (
        scale * weighted - values * (scale * scale * scale) * inner,
        jnp.sum(grad * values * scale, axis=0),
    )


def dot_nn(left, right):
    return lax.dot_general(left, right, (((1,), (0,)), ((), ())), preferred_element_type=jnp.float32)


def dot_nt(left, right):
    return lax.dot_general(left, right, (((1,), (1,)), ((), ())), preferred_element_type=jnp.float32)


def dot_tn(left, right):
    return lax.dot_general(left, right, (((0,), (0,)), ((), ())), preferred_element_type=jnp.float32)


def passed_along(x, by):
    size = lax.axis_size("wide")
    return lax.ppermute(x, "wide", [(i, i + by) for i in range(size) if 0 <= i + by < size])


def tables_kernel(dims, doc_ref, choice_ref, slot_ref, reset_ref, mask_ref, *outs):
    layers, taps, per_group, block, capacity = dims
    tokens = doc_ref.shape[1]
    steps = tokens // CHUNKS
    f32, low = jnp.float32, jnp.bfloat16
    fills, onehots, keeps = outs[:layers], outs[layers : 2 * layers], outs[2 * layers :]
    rows = [doc_ref[...]] + [choice_ref[l] for l in range(layers)] + [slot_ref[l] for l in range(layers)]
    rows = jnp.concatenate([row.astype(f32) for row in rows], axis=0)
    rows = jnp.concatenate([rows, jnp.zeros((CHUNKS - rows.shape[0], tokens), f32)], axis=0).astype(low)
    place = lax.broadcasted_iota(jnp.int32, (tokens, tokens), 1)
    token = (place & (CHUNKS - 1)) * steps + lax.shift_right_logical(place, 3)
    order = (lax.broadcasted_iota(jnp.int32, (tokens, tokens), 0) == token).astype(f32).astype(low)
    along = dot_nn(rows, order)
    down = lax.dot_general(order, rows, (((0,), (1,)), ((), ())), preferred_element_type=f32)

    starts = jnp.broadcast_to(down[:, 0:1], (tokens, LANES)).reshape(steps, CHUNKS, LANES)
    reset_ref[...] = starts * RESET
    chunk = lax.broadcasted_iota(jnp.int32, (CHUNKS, LANES), 0)
    mask_ref[0] = 1.0 - starts
    for offset in range(2, taps):
        mask_ref[offset - 1, offset - 1 :] = mask_ref[offset - 2, offset - 1 :] * (
            1.0 - starts[: steps - offset + 1])
        for i in range(offset - 1):
            before = jnp.where(chunk == 0, 0.0, pltpu.roll(starts[steps - offset + 1 + i], 1, axis=0))
            mask_ref[offset - 1, i] = mask_ref[offset - 2, i] * (1.0 - before)

    for l in range(layers):
        chosen, slot = along[1 + l : 2 + l], along[1 + layers + l : 2 + layers + l]
        group = jnp.floor((chosen + 0.5) * (1.0 / per_group))
        spot = group * block + (chosen - group * per_group) * capacity + slot
        spot = jnp.where(slot >= 0.0, spot, -1.0).astype(jnp.int32)
        fills[l][...] = (
            lax.broadcasted_iota(jnp.int32, fills[l].shape, 0) == spot).astype(f32).astype(low)
        picked = down[:, 1 + l : 2 + l].astype(jnp.int32)
        onehots[l][...] = (lax.broadcasted_iota(jnp.int32, onehots[l].shape, 1) == picked).astype(f32)
        keeps[l][...] = jnp.where(down[:, 1 + layers + l : 2 + layers + l] >= 0.0, 1.0, 0.0)


def tables(doc_start, expert_choice, slot_index, taps, experts, groups, block, capacity):
    layers = expert_choice.shape[0]
    tokens = doc_start.shape[1]
    steps = tokens // CHUNKS
    f32 = jnp.float32
    shapes = [shaped((steps, CHUNKS, LANES)), shaped((taps - 1, steps, CHUNKS, LANES))]
    shapes += [shaped((groups * block, tokens), jnp.bfloat16)] * layers
    shapes += [shaped((tokens, experts))] * layers + [shaped((tokens, 1))] * layers
    inside = pl.BlockSpec(memory_space=VMEM)
    reset, masks, *rest = pl.pallas_call(
        functools.partial(tables_kernel, (layers, taps, experts // groups, block, capacity)),
        out_shape=shapes,
        in_specs=[inside] * 3,
        out_specs=[inside] * len(shapes),
        compiler_params=pltpu.CompilerParams(vmem_limit_bytes=63 * MIB),
        cost_estimate=microseconds(3),
    )(doc_start, expert_choice, slot_index)
    return reset, masks, rest[:layers], rest[layers : 2 * layers], rest[2 * layers :]


def rim_keep(doc_start, count):
    tail = 1.0 - doc_start[doc_start.shape[0] - count :].astype(jnp.float32)
    later = jnp.cumprod(tail[::-1])[::-1]
    return jnp.concatenate([later[1:], jnp.ones((1,), jnp.float32)])


TILE = 2 * LANES


def each_part(body):
    def one(at, carry):
        body(pl.ds(pl.multiple_of(at * LANES, LANES), LANES))
        return carry

    lax.fori_loop(0, TILE // LANES, one, 0)


def microseconds(count):
    return pl.CostEstimate(flops=int(count * 2.0e7), transcendentals=0, bytes_accessed=10000)


def plain_call(kernel, grid, in_specs, out_specs, out_shapes, scratch, args, cost, aliases=None):
    return pl.pallas_call(
        kernel,
        grid=grid,
        in_specs=in_specs,
        out_specs=out_specs,
        out_shape=out_shapes,
        scratch_shapes=scratch,
        input_output_aliases=aliases or {},
        compiler_params=pltpu.CompilerParams(
            dimension_semantics=("arbitrary",), vmem_limit_bytes=63 * MIB
        ),
        cost_estimate=microseconds(cost),
    )(*args)


def shaped(shape, kind=jnp.float32):
    return jax.ShapeDtypeStruct(shape, kind)


def slab(steps, first=0):
    return pl.BlockSpec((steps, CHUNKS, TILE), lambda c: (0, 0, first + c))


def rows_of(count):
    return pl.BlockSpec((count, TILE), lambda c: (0, c))


def layer_rows(layer, count):
    return pl.BlockSpec((None, count, TILE), lambda c: (layer, 0, c))


def layer_columns(layer, count):
    return pl.BlockSpec((None, TILE, count), lambda c: (layer, c, 0))


def layer_whole(layer, shape):
    return pl.BlockSpec((None,) + shape, lambda c: (layer,) + (0,) * len(shape))


def whole(shape):
    return pl.BlockSpec(shape, lambda c: (0,) * len(shape))


ANYWHERE = pl.BlockSpec(memory_space=pl.ANY)


def spread_columns(selection_ref, first, states, out_ref):
    def one(step, carry):
        tile = selection_ref[step]
        for n in range(states):
            out_ref[step, n] = jnp.broadcast_to(tile[:, first + n : first + n + 1], (CHUNKS, LANES))
        return carry

    lax.fori_loop(0, selection_ref.shape[0], one, 0, unroll=8)


def rate_rows(rate):
    return [jnp.broadcast_to(rate[n : n + 1, :], (CHUNKS, LANES)) for n in range(rate.shape[0])]


def rates_of(decay_log):
    return -jnp.exp(decay_log) * LOG2E


def two_steps(ref, pair, lanes=slice(None)):
    both = ref[pl.ds(pl.multiple_of(pair * 2 * CHUNKS, 2 * CHUNKS), 2 * CHUNKS), lanes]
    both = both.astype(jnp.float32)
    return both[:CHUNKS], both[CHUNKS:]


def chunk_links(found, sizes, rates, reverse):
    place = lax.broadcasted_iota(jnp.int32, (CHUNKS, LANES), 0)
    if reverse:
        place = CHUNKS - 1 - place
    last = 0 if reverse else CHUNKS - 1

    def shifted(values, by):
        turned = pltpu.roll(values, CHUNKS - by if reverse else by, axis=0)
        return jnp.where(place >= by, turned, 0.0)

    lengths = [sizes]
    for by in (1, 2, 4):
        lengths.append(lengths[-1] + shifted(lengths[-1], by))
    links, totals = [], []
    for n, rate in enumerate(rates):
        level = found[n]
        for index, by in enumerate((1, 2, 4)):
            level = level + jnp.exp2(lengths[index] * rate) * shifted(level, by)
        links.append(shifted(level, 1))
        totals.append(level[last : last + 1])
    return links, totals, shifted(lengths[-1], 1), lengths[-1][last : last + 1]


def conv_slab(extended, step, mask_ref, kernel_ref, bias, taps):
    total = bias + kernel_ref[0:1, :] * extended[step + taps - 1]
    tiles = total.shape[1] // LANES
    for offset in range(1, taps):
        mask = mask_ref[offset - 1, step]
        mask = jnp.concatenate([mask] * tiles, axis=1) if tiles > 1 else mask
        total = total + kernel_ref[offset : offset + 1, :] * (
            extended[step + taps - 1 - offset] * mask
        )
    return total


def extend(value_ref, rim_ref, extended, taps):
    steps = value_ref.shape[0]
    place = lax.broadcasted_iota(jnp.int32, value_ref.shape[1:], 0)
    for j in range(taps - 1):
        turned = pltpu.roll(value_ref[steps - taps + 1 + j], 1, axis=0)
        extended[j] = jnp.where(place == 0, rim_ref[j : j + 1, :], turned)
    extended[taps - 1 :] = value_ref[...]


def enter_kernel(first, gain_ref, weight_ref, *refs):
    low = jnp.bfloat16
    if first:
        current_ref, tail_ref, normed_ref, projected_ref, rim_ref, before = refs
    else:
        middle_ref, share_ref, fill_ref, returned_ref, current_ref, taken_ref, normed_ref, projected_ref = refs

    @pl.when(pl.program_id(0) == 0)
    def _():
        if first:
            before[...] = rms_scale(tail_ref[...], gain_ref[...]).astype(low)
        else:
            taken = dot_tn(fill_ref[...], returned_ref[...])
            taken_ref[...] = taken
            current_ref[...] = middle_ref[...] + share_ref[...] * taken
        normed_ref[...] = rms_scale(current_ref[...], gain_ref[...]).astype(low)

    projected_ref[...] = dot_nn(normed_ref[...], weight_ref[...])
    if first:
        rim_ref[...] = dot_nn(before[...], weight_ref[...])


def mixer_enter(layer, gain, in_weight, *arrays):
    first = len(arrays) == 2
    _, width, columns = in_weight.shape
    tokens = arrays[0].shape[0]
    span = 4 * LANES
    low = jnp.bfloat16
    normed = (whole((tokens, width)), shaped((tokens, width), low))
    projected = (pl.BlockSpec((tokens, span), lambda c: (0, c)), shaped((tokens, columns)))
    if first:
        rows = arrays[1].shape[0]
        outs = [normed, projected, (pl.BlockSpec((rows, span), lambda c: (0, c)), shaped((rows, columns)))]
        scratch = [VMEM((rows, width), low)]
    else:
        full = (whole((tokens, width)), shaped((tokens, width)))
        outs, scratch = [full, full, normed, projected], []
    return plain_call(
        functools.partial(enter_kernel, first),
        (columns // span,),
        [layer_whole(layer, (1, width)), pl.BlockSpec((None, width, span), lambda c: (layer, 0, c))]
        + [whole(array.shape) for array in arrays],
        [spec for spec, _ in outs],
        [shape for _, shape in outs],
        scratch,
        (gain, in_weight) + arrays,
        5,
    )


def front_kernel(dims, value_ref, rim_ref, mask_ref, reset_ref, conv_ref, conv_bias_ref, state_ref,
                 step_ref, step_bias_ref, decay_ref,
                 act_ref, selection_ref, size_ref, link_ref, link_size_ref, total_ref, total_size_ref,
                 extended, maps, sized, pushed):
    taps, rank, states, steps, channels = dims
    extend(value_ref, rim_ref, extended, taps)
    bias = conv_bias_ref[...]

    def conv_pair(pair, carry):
        both = []
        for step in (2 * pair, 2 * pair + 1):
            both.append(jax.nn.silu(conv_slab(extended, step, mask_ref, conv_ref, bias, taps)))
        at = pl.ds(pl.multiple_of(pair * 2 * CHUNKS, 2 * CHUNKS), 2 * CHUNKS)
        act_ref[at, :] = jnp.concatenate(both, axis=0).astype(jnp.bfloat16)
        return carry

    lax.fori_loop(0, steps // 2, conv_pair, 0)
    selection = dot_nn(act_ref[...], state_ref[...])
    selection_ref[...] = selection.reshape(steps, CHUNKS, selection.shape[1])
    rank_low = selection[:, :rank].astype(jnp.bfloat16)

    def size_tile(c, carry):
        lanes = pl.ds(pl.multiple_of(c * 256, 256), 256)
        linear = dot_nn(rank_low, step_ref[:, lanes]) + step_bias_ref[:, lanes]
        size_ref[:, :, lanes] = jax.nn.softplus(linear).reshape(steps, CHUNKS, 256)
        return carry

    lax.fori_loop(0, channels // 256, size_tile, 0)
    spread_columns(selection_ref, rank, states, maps)

    def end_tile(c, carry):
        lanes = pl.ds(pl.multiple_of(c * LANES, LANES), LANES)
        rates = rate_rows(rates_of(decay_ref[:, lanes]))
        size = size_ref[:, :, lanes]
        pushed[...] = size * act_ref[:, lanes].astype(jnp.float32).reshape(size.shape)
        sized[...] = size + reset_ref[...]

        def one(step, carry):
            size, value = sized[step], pushed[step]
            new = []
            for n in range(states):
                new.append(jnp.exp2(size * rates[n]) * carry[n] + value * maps[step, n])
            return tuple(new) + (carry[states] + size,)

        zero = jnp.zeros((CHUNKS, LANES), jnp.float32)
        found = lax.fori_loop(0, steps, one, (zero,) * (states + 1), unroll=4)
        links, totals, link_size, total_size = chunk_links(found, found[states], rates, False)
        link_size_ref[:, lanes] = link_size
        total_size_ref[:, lanes] = total_size
        for n in range(states):
            link_ref[n, :, lanes] = links[n]
            total_ref[n : n + 1, lanes] = totals[n]
        return carry

    lax.fori_loop(0, channels // LANES, end_tile, 0)


def mixer_front(layer, projected, rim, masks, reset, conv_weight, conv_bias, state_weight, step_weight,
                step_bias, decay_log):
    steps = projected.shape[0]
    channels = conv_weight.shape[2]
    taps, rank, states = conv_weight.shape[1], step_weight.shape[1], decay_log.shape[1]
    columns = state_weight.shape[2]
    value = pl.BlockSpec((steps, CHUNKS, channels), lambda c: (0, 0, 0))
    shapes = [
        shaped((steps * CHUNKS, channels), jnp.bfloat16),
        shaped((steps, CHUNKS, columns)),
        shaped((steps, CHUNKS, channels)),
        shaped((states, CHUNKS, channels)),
        shaped((CHUNKS, channels)),
        shaped((states, channels)),
        shaped((1, channels)),
    ]
    return plain_call(
        functools.partial(front_kernel, (taps, rank, states, steps, channels)),
        (1,),
        [value, whole((rim.shape[0], channels)), whole(masks.shape), whole(reset.shape),
         layer_whole(layer, conv_weight.shape[1:]), layer_whole(layer, conv_bias.shape[1:]),
         layer_whole(layer, state_weight.shape[1:]), layer_whole(layer, step_weight.shape[1:]),
         layer_whole(layer, step_bias.shape[1:]), layer_whole(layer, decay_log.shape[1:])],
        [whole(s.shape) for s in shapes],
        shapes,
        [VMEM((steps + taps - 1, CHUNKS, channels), jnp.float32),
         VMEM((steps, states, CHUNKS, LANES), jnp.float32),
         VMEM((steps, CHUNKS, LANES), jnp.float32), VMEM((steps, CHUNKS, LANES), jnp.float32)],
        (projected, rim, masks, reset, conv_weight, conv_bias, state_weight, step_weight, step_bias,
         decay_log),
        18,
    )


def run_kernel(dims, size_ref, act_ref, selection_ref, reset_ref, decay_ref, link_ref, link_size_ref,
               entering_ref, gate_ref, skip_ref, out_weight_ref, current_ref, norm_ref, router_ref, fill_ref,
               onehot_ref, keep_ref,
               mixed_ref, gated_ref, begin_ref, middle_ref, routed_ref, shares_ref, weight_ref, outbound_ref,
               in_maps, out_maps, pushed):
    rank, states, steps, tiles = dims

    @pl.when(pl.program_id(0) == 0)
    def _():
        spread_columns(selection_ref, rank, states, in_maps)
        spread_columns(selection_ref, rank + states, states, out_maps)
        middle_ref[...] = current_ref[...]

    size = size_ref[...]
    act = act_ref[...].astype(jnp.float32).reshape(size.shape)
    pushed[...] = size * act

    def scan(lanes):
        rates = rate_rows(rates_of(decay_ref[:, lanes]))
        link_size = link_size_ref[:, lanes]
        begin = []
        for n in range(states):
            first = link_ref[n, :, lanes] + jnp.exp2(link_size * rates[n]) * entering_ref[n : n + 1, lanes]
            begin_ref[n, :, lanes] = first
            begin.append(first)

        def one(step, carry):
            size, value = size_ref[step, :, lanes] + reset_ref[step], pushed[step, :, lanes]
            new = []
            sums = [None, None]
            for n in range(states):
                level = jnp.exp2(size * rates[n]) * carry[n] + value * in_maps[step, n]
                new.append(level)
                term = out_maps[step, n] * level
                sums[n % 2] = term if sums[n % 2] is None else sums[n % 2] + term
            mixed_ref[step, :, lanes] = sums[0] + sums[1]
            return tuple(new)

        lax.fori_loop(0, steps, one, tuple(begin), unroll=4)

    each_part(scan)
    mixed = mixed_ref[...] + skip_ref[...] * act
    mixed_ref[...] = mixed
    gated = mixed * jax.nn.silu(gate_ref[...])
    gated_ref[...] = gated.reshape(steps * CHUNKS, TILE).astype(jnp.bfloat16)
    middle_ref[...] += dot_nn(gated_ref[...], out_weight_ref[...])

    @pl.when(pl.program_id(0) == tiles - 1)
    def _():
        routed = rms_scale(middle_ref[...], norm_ref[...]).astype(jnp.bfloat16)
        routed_ref[...] = routed
        logits = dot_nn(routed, router_ref[...])
        raised = jnp.exp(logits - jnp.max(logits, axis=1, keepdims=True))
        shares = raised / jnp.sum(raised, axis=1, keepdims=True)
        shares_ref[...] = shares
        weight_ref[...] = keep_ref[...] * jnp.sum(shares * onehot_ref[...], axis=1, keepdims=True)
        outbound_ref[...] = dot_nn(fill_ref[...], routed).astype(jnp.bfloat16)


def mixer_run(layer, size, act, selection, reset, decay_log, link, link_size, entering, projected, skip_weight,
              out_weight, current, norm_expert, router, fill, onehot, keep):
    steps, _, channels = size.shape
    tokens = steps * CHUNKS
    states, width, experts = decay_log.shape[1], current.shape[1], router.shape[2]
    rank = selection.shape[2] - 2 * states
    tiles = channels // TILE
    low = jnp.bfloat16
    maps = VMEM((steps, states, CHUNKS, LANES), jnp.float32)
    return plain_call(
        functools.partial(run_kernel, (rank, states, steps, tiles)),
        (tiles,),
        [slab(steps), rows_of(tokens), whole(selection.shape), whole(reset.shape),
         layer_rows(layer, states), slab(states), rows_of(CHUNKS), rows_of(states), slab(steps, tiles),
         layer_rows(layer, 1), layer_columns(layer, width), whole(current.shape),
         layer_whole(layer, (1, width)), layer_whole(layer, (width, experts)), whole(fill.shape),
         whole(onehot.shape), whole(keep.shape)],
        [slab(steps), rows_of(tokens), slab(states), whole((tokens, width)), whole((tokens, width)),
         whole((tokens, experts)), whole((tokens, 1)), whole((fill.shape[0], width))],
        [
            shaped((steps, CHUNKS, channels)),
            shaped((tokens, channels), low),
            shaped((states, CHUNKS, channels)),
            shaped((tokens, width)),
            shaped((tokens, width), low),
            shaped((tokens, experts)),
            shaped((tokens, 1)),
            shaped((fill.shape[0], width), low),
        ],
        [maps, maps, VMEM((steps, CHUNKS, TILE), jnp.float32)],
        (size, act, selection, reset, decay_log, link, link_size, entering, projected, skip_weight, out_weight,
         current, norm_expert, router, fill, onehot, keep),
        22,
    )


def turn_kernel(dims, grad_ref, out_weight_ref, gate_ref, mixed_ref, act_ref, gated_ref, size_ref,
                selection_ref, reset_ref, decay_ref,
                grad_y_ref, grad_gate_ref, grad_skip_ref, grad_out_ref, link_ref, link_size_ref, total_ref,
                total_size_ref, maps):
    rank, states, steps = dims

    @pl.when(pl.program_id(0) == 0)
    def _():
        spread_columns(selection_ref, rank + states, states, maps)

    grad = grad_ref[...]
    grad_out_ref[...] = dot_tn(gated_ref[...], grad).astype(jnp.bfloat16)
    gated = dot_nt(grad, out_weight_ref[...]).reshape(steps, CHUNKS, TILE)
    gate = gate_ref[...]
    share = jax.nn.sigmoid(gate)
    grad_y = gated * (gate * share)
    grad_y_ref[...] = grad_y
    grad_gate = gated * mixed_ref[...] * (share * (1.0 + gate * (1.0 - share)))
    grad_gate_ref[...] = grad_gate.reshape(steps * CHUNKS, TILE).astype(jnp.bfloat16)
    by_skip = grad_y * act_ref[...].astype(jnp.float32).reshape(steps, CHUNKS, TILE)
    grad_skip_ref[...] = jnp.sum(jnp.sum(by_skip, axis=0), axis=0, keepdims=True)

    def scan(lanes):
        rates = rate_rows(rates_of(decay_ref[:, lanes]))

        def one(at, carry):
            step = steps - 1 - at
            size, grad_y = size_ref[step, :, lanes] + reset_ref[step], grad_y_ref[step, :, lanes]
            new = []
            for n in range(states):
                new.append(jnp.exp2(size * rates[n]) * (carry[n] + grad_y * maps[step, n]))
            return tuple(new) + (carry[states] + size,)

        zero = jnp.zeros((CHUNKS, LANES), jnp.float32)
        found = lax.fori_loop(0, steps, one, (zero,) * (states + 1), unroll=4)
        links, totals, link_size, total_size = chunk_links(found, found[states], rates, True)
        link_size_ref[:, lanes] = link_size
        total_size_ref[:, lanes] = total_size
        for n in range(states):
            link_ref[n, :, lanes] = links[n]
            total_ref[n : n + 1, lanes] = totals[n]

    each_part(scan)


def mixer_turn(layer, grad_low, out_weight, projected, mixed, act, gated, size, selection, reset, decay_log):
    steps, _, channels = size.shape
    tokens = steps * CHUNKS
    states, width = decay_log.shape[1], grad_low.shape[1]
    rank = selection.shape[2] - 2 * states
    tiles = channels // TILE
    low = jnp.bfloat16
    return plain_call(
        functools.partial(turn_kernel, (rank, states, steps)),
        (tiles,),
        [whole(grad_low.shape), layer_columns(layer, width), slab(steps, tiles), slab(steps), rows_of(tokens),
         rows_of(tokens), slab(steps), whole(selection.shape), whole(reset.shape), layer_rows(layer, states)],
        [slab(steps), pl.BlockSpec((tokens, TILE), lambda c: (0, tiles + c)), rows_of(1),
         pl.BlockSpec((TILE, width), lambda c: (c, 0)),
         slab(states), rows_of(CHUNKS), rows_of(states), rows_of(1)],
        [
            shaped((steps, CHUNKS, channels)),
            shaped((tokens, 2 * channels), low),
            shaped((1, channels)),
            shaped((channels, width), low),
            shaped((states, CHUNKS, channels)),
            shaped((CHUNKS, channels)),
            shaped((states, channels)),
            shaped((1, channels)),
        ],
        [VMEM((steps, states, CHUNKS, LANES), jnp.float32)],
        (grad_low, out_weight, projected, mixed, act, gated, size, selection, reset, decay_log),
        14,
    )


def back_kernel(dims, size_ref, act_ref, grad_ref, decay_ref, selection_ref, reset_ref, begin_ref, link_ref,
                link_size_ref, entering_ref, step_ref, step_bias_ref, skip_ref,
                grad_act_ref, grad_decay_ref, grad_bias_ref, grad_step_ref, grad_selection_ref,
                in_maps, out_maps, levels, decays, grad_in, grad_out, grad_size, grad_rate, grad_all, pushed, acted):
    rank, states, steps, tiles = dims
    tokens = steps * CHUNKS

    @pl.when(pl.program_id(0) == 0)
    def _():
        spread_columns(selection_ref, rank, states, in_maps)
        spread_columns(selection_ref, rank + states, states, out_maps)
        grad_in[...] = jnp.zeros_like(grad_in)
        grad_out[...] = jnp.zeros_like(grad_out)

    skip = skip_ref[...]
    size = size_ref[...]
    act = act_ref[...].astype(jnp.float32).reshape(size.shape)
    acted[...] = act
    pushed[...] = size * act

    def scan(lanes):
        true_rates = -jnp.exp(decay_ref[:, lanes])
        rates = rate_rows(true_rates * LOG2E)
        begin = []
        for n in range(states):
            levels[0, n] = begin_ref[n, :, lanes]
            begin.append(begin_ref[n, :, lanes])

        def ahead(step, carry):
            size, value = size_ref[step, :, lanes] + reset_ref[step], pushed[step, :, lanes]
            new = []
            for n in range(states):
                decay = jnp.exp2(size * rates[n])
                decays[step, n] = decay
                level = decay * carry[n] + value * in_maps[step, n]
                levels[step + 1, n] = level
                new.append(level)
            return tuple(new)

        lax.fori_loop(0, steps, ahead, tuple(begin), unroll=4)
        link_size = link_size_ref[:, lanes]
        tail = []
        for n in range(states):
            tail.append(
                link_ref[n, :, lanes] + jnp.exp2(link_size * rates[n]) * entering_ref[n : n + 1, lanes])
            grad_rate[n] = jnp.zeros((CHUNKS, LANES), jnp.float32)

        def retreat(at, carry):
            step = steps - 1 - at
            plain, act, grad, value = (
                ref[step, :, lanes] for ref in (size_ref, acted, grad_ref, pushed))
            by_rate = jnp.zeros((CHUNKS, LANES), jnp.float32)
            by_input = jnp.zeros((CHUNKS, LANES), jnp.float32)
            new = []
            for n in range(states):
                spot = slice(n * LANES, (n + 1) * LANES)
                back = out_maps[step, n] * grad + carry[n]
                grad_out[step, :, spot] += grad * levels[step + 1, n]
                grad_in[step, :, spot] += back * value
                by_input = by_input + back * in_maps[step, n]
                passed = decays[step, n] * back
                new.append(passed)
                pull = passed * levels[step, n]
                by_rate = by_rate + pull * rates[n]
                grad_rate[n] += pull * plain
            grad_size[step, :, lanes] = by_rate * (1.0 / LOG2E) + act * by_input
            grad_act_ref[step, :, lanes] = plain * by_input
            return tuple(new)

        lax.fori_loop(0, steps, retreat, tuple(tail), unroll=2)
        for n in range(states):
            grad_decay_ref[n : n + 1, lanes] = (
                jnp.sum(grad_rate[n], axis=0, keepdims=True) * true_rates[n : n + 1, :]
            )

    each_part(scan)
    grad_act_ref[...] += grad_ref[...] * skip
    tile = pl.program_id(0)
    grad_all[:, pl.ds(pl.multiple_of(tile * TILE, TILE), TILE)] = grad_size[...].reshape(tokens, TILE)

    @pl.when(pl.program_id(0) == tiles - 1)
    def _():
        rank_low = selection_ref[...].reshape(tokens, selection_ref.shape[2])[:, :rank].astype(jnp.bfloat16)
        linear = dot_nn(rank_low, step_ref[...]) + step_bias_ref[...]
        grad_linear = grad_all[...] * jax.nn.sigmoid(linear)
        grad_bias_ref[...] = jnp.sum(grad_linear, axis=0, keepdims=True)
        grad_low = grad_linear.astype(jnp.bfloat16)
        grad_step_ref[...] = dot_tn(rank_low, grad_low)
        grad_rank = dot_nt(grad_low, step_ref[...])
        size = states * LANES
        row = lax.broadcasted_iota(jnp.int32, (size, states), 0)
        column = lax.broadcasted_iota(jnp.int32, (size, states), 1)
        pick = ((row >= column * LANES) & (row < (column + 1) * LANES)).astype(jnp.float32)
        pick = pick.astype(jnp.bfloat16)
        found = [grad_rank]
        for ref in (grad_in, grad_out):
            full = ref[...].reshape(tokens, size)
            high = full.astype(jnp.bfloat16)
            rest = (full - high.astype(jnp.float32)).astype(jnp.bfloat16)
            found.append(dot_nn(high, pick) + dot_nn(rest, pick))
        grad_selection_ref[...] = jnp.concatenate(found, axis=1).astype(jnp.bfloat16)


def mixer_back(layer, size, act, grad_y, decay_log, selection, reset, begin, link, link_size, entering,
               step_weight, step_bias, skip_weight):
    steps, _, channels = size.shape
    tokens = steps * CHUNKS
    states = decay_log.shape[1]
    columns = selection.shape[2]
    rank = columns - 2 * states
    tiles = channels // TILE
    f32 = jnp.float32
    maps = VMEM((steps, states, CHUNKS, LANES), f32)
    return plain_call(
        functools.partial(back_kernel, (rank, states, steps, tiles)),
        (tiles,),
        [slab(steps), rows_of(tokens), slab(steps), layer_rows(layer, states), whole(selection.shape),
         whole(reset.shape), slab(states), slab(states), rows_of(CHUNKS), rows_of(states),
         layer_whole(layer, (rank, channels)), layer_whole(layer, (1, channels)), layer_rows(layer, 1)],
        [slab(steps), rows_of(states), whole((1, channels)), whole((rank, channels)),
         whole((tokens, columns))],
        [
            shaped((steps, CHUNKS, channels)),
            shaped((states, channels)),
            shaped((1, channels)),
            shaped((rank, channels)),
            shaped((tokens, columns), jnp.bfloat16),
        ],
        [maps, maps, VMEM((steps + 1, states, CHUNKS, LANES), f32), maps,
         VMEM((steps, CHUNKS, states * LANES), f32), VMEM((steps, CHUNKS, states * LANES), f32),
         VMEM((steps, CHUNKS, TILE), f32), VMEM((states, CHUNKS, LANES), f32), VMEM((tokens, channels), f32)]
        + [VMEM((steps, CHUNKS, TILE), f32)] * 2,
        (size, act, grad_y, decay_log, selection, reset, begin, link, link_size, entering, step_weight,
         step_bias, skip_weight),
        35,
    )


def conv_back_kernel(dims, grad_act_ref, grad_selection_ref, state_ref, value_ref, rim_ref, mask_ref,
                     conv_ref, conv_bias_ref, act_ref, grad_step_ref, grad_decay_ref, grad_bias_ref,
                     grad_skip_ref, half_ref, grad_value_ref, edge_ref, rim_grad_ref, channel_ref,
                     extended, passed):
    taps, states, steps = dims
    lanes = grad_act_ref.shape[2]
    extend(value_ref, rim_ref, extended, taps)
    bias = conv_bias_ref[...]
    grad_selection = grad_selection_ref[...]
    from_selection = dot_nt(grad_selection, state_ref[...]).reshape(steps, CHUNKS, lanes)
    passed[:steps] = grad_act_ref[...] + from_selection
    passed[steps:] = jnp.zeros((taps - 1, CHUNKS, lanes), jnp.float32)
    zero = jnp.zeros((CHUNKS, lanes), jnp.float32)

    def keep(offset, step):
        return jnp.concatenate([mask_ref[offset - 1, step]] * (lanes // LANES), axis=1)

    def ahead(step, carry):
        convolved = conv_slab(extended, step, mask_ref, conv_ref, bias, taps)
        share = jax.nn.sigmoid(convolved)
        grad = passed[step] * (share * (1.0 + convolved * (1.0 - share)))
        passed[step] = grad
        new = [carry[0] + grad, carry[1] + grad * extended[step + taps - 1]]
        for offset in range(1, taps):
            kept = grad * keep(offset, step)
            new.append(carry[offset + 1] + kept * extended[step + taps - 1 - offset])
        return tuple(new)

    sums = lax.fori_loop(0, steps, ahead, (zero,) * (taps + 1), unroll=2)

    def reach(step, last):
        total = zero
        for offset in range(last):
            at = step + offset
            part = conv_ref[offset : offset + 1, :] * passed[at]
            if offset:
                part = part * keep(offset, at)
            total = total + part
        return total

    def back(pair, carry):
        both = [reach(2 * pair + half, taps) for half in (0, 1)]
        rows = pl.ds(pl.multiple_of(pair * 2 * CHUNKS, 2 * CHUNKS), 2 * CHUNKS)
        grad_value_ref[rows, :] = jnp.concatenate(both, axis=0).astype(jnp.bfloat16)
        return carry

    safe = (steps - taps + 1) // 2
    lax.fori_loop(0, safe, back, 0, unroll=2)
    place = lax.broadcasted_iota(jnp.int32, (CHUNKS, lanes), 0)
    ends = {}
    for j in range(taps - 1):
        before = zero
        for offset in range(taps - 1 - j, taps):
            at = j - taps + 1 + offset
            before = before + conv_ref[offset : offset + 1, :] * (
                passed[at] * keep(offset, at)
            )
        rim_grad_ref[j : j + 1, :] = before[0:1]
        ends[steps - taps + 1 + j] = jnp.where(
            place < CHUNKS - 1, pltpu.roll(before, CHUNKS - 1, axis=0), 0.0
        )
    for pair in range(safe, steps // 2):
        both = []
        for step in (2 * pair, 2 * pair + 1):
            total = reach(step, min(taps, steps - step))
            if step in ends:
                total = total + ends[step]
                j = step - steps + taps - 1
                edge_ref[j : j + 1, :] = total[CHUNKS - 1 : CHUNKS]
            both.append(total)
        grad_value_ref[2 * pair * CHUNKS : (2 * pair + 2) * CHUNKS, :] = jnp.concatenate(
            both, axis=0
        ).astype(jnp.bfloat16)
    small = jnp.zeros((CHUNKS, lanes), jnp.float32)
    rows = [jnp.sum(part, axis=0, keepdims=True) for part in sums[1:] + sums[:1]]
    rows += [grad_bias_ref[...], grad_skip_ref[...]]
    for index, row in enumerate(rows):
        small = jnp.where(place == index, row, small)
    grad_state = dot_tn(grad_selection, act_ref[...])
    parts = [grad_state, grad_step_ref[...], grad_decay_ref[...], small]
    used = sum(part.shape[0] for part in parts)
    parts.append(jnp.zeros((2 * LANES - used, lanes), jnp.float32))
    channel_ref[...] = jnp.concatenate(parts, axis=0).T.astype(jnp.bfloat16)


def mixer_conv_back(layer, grad_act, grad_selection, state_weight, projected, rim, masks, conv_weight,
                    conv_bias, act, grad_step, grad_decay, grad_bias, grad_skip, halved):
    steps, _, channels = grad_act.shape
    tokens = steps * CHUNKS
    taps, columns = conv_weight.shape[1], state_weight.shape[2]
    states, rank = grad_decay.shape[0], grad_step.shape[0]
    lanes = 2 * LANES
    f32 = jnp.float32

    def cubes(count):
        return pl.BlockSpec((count, CHUNKS, lanes), lambda c: (0, 0, c))

    def rows(count):
        return pl.BlockSpec((count, lanes), lambda c: (0, c))

    def weight_rows(count):
        return pl.BlockSpec((None, count, lanes), lambda c: (layer, 0, c))

    return plain_call(
        functools.partial(conv_back_kernel, (taps, states, steps)),
        (channels // lanes,),
        [cubes(steps), whole(grad_selection.shape),
         pl.BlockSpec((None, lanes, columns), lambda c: (layer, c, 0)), cubes(steps),
         rows(taps - 1), whole(masks.shape), weight_rows(taps), weight_rows(1),
         rows(tokens), rows(rank), rows(states), rows(1), rows(1), ANYWHERE],
        [rows(tokens), rows(taps - 1), rows(taps - 1),
         pl.BlockSpec((lanes, 2 * LANES), lambda c: (c, 0))],
        [
            shaped((tokens, 2 * channels), jnp.bfloat16),
            shaped((taps - 1, channels)),
            shaped((taps - 1, channels)),
            shaped((channels, 2 * LANES), jnp.bfloat16),
        ],
        [VMEM((steps + taps - 1, CHUNKS, lanes), f32), VMEM((steps + taps - 1, CHUNKS, lanes), f32)],
        (grad_act, grad_selection, state_weight, projected, rim, masks, conv_weight, conv_bias, act, grad_step,
         grad_decay, grad_bias, grad_skip, halved),
        10,
        {13: 0},
    )


def hand_on(layer, count, reverse, total_ref, size_ref, decay_ref, out_ref, scratch, between, after):
    (mine, mine_length, near, near_length, both, both_length, far, far_length,
     send, recv, send_length, recv_length) = scratch
    here = lax.axis_index("wide")
    group = lax.axis_index("narrow")
    pairs = count // 2
    pair, side = here // 2, lax.rem(here, 2)
    partner = here + 1 - 2 * side
    others = [lax.rem(pair + k, pairs) for k in range(1, pairs)]
    f32 = jnp.float32
    barrier = pltpu.get_barrier_semaphore()
    pl.semaphore_signal(barrier, inc=1, device_id=(partner, group), device_id_type=MESH)
    for other in others:
        pl.semaphore_signal(barrier, inc=1, device_id=(2 * other + side, group), device_id_type=MESH)
    mine[...] = total_ref[...].astype(mine.dtype)
    mine_length[...] = size_ref[...]
    rate = rates_of(decay_ref[layer])
    pl.semaphore_wait(barrier, pairs)

    def hand(index, source, source_length, target, target_length, window):
        copies = []
        for src, dst, out, back in (
            (source, target, send, recv), (source_length, target_length, send_length, recv_length)):
            copies.append(pltpu.make_async_remote_copy(
                src_ref=src, dst_ref=dst, send_sem=out.at[index], recv_sem=back.at[index],
                device_id=(window, group), device_id_type=MESH))
            copies[-1].start()
        return copies

    first = hand(0, mine, mine_length, near, near_length, partner)
    between()
    for copy in first:
        copy.wait_recv()
    second_here = (side == 0) if reverse else (side == 1)
    own, own_length = total_ref[...], size_ref[...]
    met, met_length = near[...].astype(f32), near_length[...]
    late_length = jnp.where(second_here, own_length, met_length)
    early = jnp.where(second_here, met, own)
    late = jnp.where(second_here, own, met)
    both[...] = (jnp.exp2(late_length * rate) * early + late).astype(both.dtype)
    both_length[...] = own_length + met_length
    sent = []
    for k, other in enumerate(others):
        sent.append(hand(
            1 + k, both, both_length, far.at[pair], far_length.at[pair], 2 * other + side))
    after()
    for copies in sent:
        for copy in copies:
            copy.wait_recv()
    level = jnp.zeros(own.shape, f32)
    for at in range(pairs - 1, -1, -1) if reverse else range(pairs):
        valid = (pair < at) if reverse else (pair > at)
        step = jnp.exp2(far_length[at] * rate) * level + far[at].astype(f32)
        level = jnp.where(valid, step, level)
    step = jnp.exp2(met_length * rate) * level + met
    out_ref[...] = jnp.where(second_here, step, level)
    for copies in [first] + sent:
        for copy in copies:
            copy.wait_send()


LINK_REFS = 12


def link_scratch(count, states, channels):
    pairs = count // 2
    f32, low = jnp.float32, jnp.bfloat16
    dma = pltpu.SemaphoreType.DMA((pairs,))
    return [
        VMEM((states, channels), low), VMEM((1, channels), f32),
        VMEM((states, channels), low), VMEM((1, channels), f32),
        VMEM((states, channels), low), VMEM((1, channels), f32),
        VMEM((pairs, states, channels), low), VMEM((pairs, 1, channels), f32),
        dma, dma, dma, dma,
    ]


def link_call(kernel, total, size, decay_log, beside, out_shapes, scratch, identity):
    states, channels = total.shape
    inside = pl.BlockSpec(memory_space=VMEM)
    return pl.pallas_call(
        kernel,
        out_shape=[shaped((states, channels))] + out_shapes,
        in_specs=[inside] * 3 + [ANYWHERE] * len(beside),
        out_specs=[inside] + [ANYWHERE] * len(out_shapes),
        scratch_shapes=link_scratch(lax.axis_size("wide"), states, channels) + scratch,
        compiler_params=pltpu.CompilerParams(
            collective_id=identity, has_side_effects=True, vmem_limit_bytes=63 * MIB
        ),
        cost_estimate=microseconds(12),
    )(total, size, decay_log, *beside)


def ahead_kernel(layer, count, wanted, total_ref, size_ref, decay_ref, *refs):
    arrays = len(wanted)
    sources, out_ref, targets = refs[:arrays], refs[arrays], refs[arrays + 1 : 2 * arrays + 1]
    scratch, (*held, got, put) = refs[2 * arrays + 1 :][:LINK_REFS], refs[2 * arrays + 1 + LINK_REFS :]
    into = [
        pltpu.make_async_copy(sources[i].at[wanted[i]], held[i], got.at[i]) for i in range(arrays)]
    out = [pltpu.make_async_copy(held[i], targets[i], put.at[i]) for i in range(arrays)]
    for copy in into:
        copy.start()

    def after():
        for i in range(arrays):
            into[i].wait()
            out[i].start()

    hand_on(layer, count, False, total_ref, size_ref, decay_ref, out_ref, scratch, lambda: None, after)
    for copy in out:
        copy.wait()


def handed_ahead(layer, total, size, decay_log, wanted, identity):
    shapes = [array.shape[1:] for array, _ in wanted]
    dma = pltpu.SemaphoreType.DMA((len(wanted),))
    return link_call(
        functools.partial(ahead_kernel, layer, lax.axis_size("wide"), tuple(which for _, which in wanted)),
        total, size, decay_log, [array for array, _ in wanted],
        [shaped(shape, array.dtype) for shape, (array, _) in zip(shapes, wanted)],
        [VMEM(shape, array.dtype) for shape, (array, _) in zip(shapes, wanted)] + [dma, dma],
        identity)


def behind_kernel(layer, count, total_ref, size_ref, decay_ref, out_ref, *scratch):
    def nothing():
        pass

    hand_on(layer, count, True, total_ref, size_ref, decay_ref, out_ref, scratch, nothing, nothing)


def handed_back(layer, total, size, decay_log, identity):
    return link_call(
        functools.partial(behind_kernel, layer, lax.axis_size("wide")),
        total, size, decay_log, [], [], [], identity)[0]


def bell(values):
    return 0.5 * (1.0 + lax.erf(values * 0.7071067811865476))


def expert_kernel(dims, kinds, beside, which, *refs):
    count, groups, members, block, share, width, hidden = dims
    flows = len(kinds)
    out_refs, (perm_ref, up_hbm, down_hbm, *refs) = refs[:flows], refs[flows:]
    learns, outs = True in kinds, 1 if kinds == (True,) and folds(width, hidden) else 2
    if kinds == (True,):
        pre_hbm, kept_hbm, hidden_hbm, *refs = refs
    if beside:
        next_hbm, *refs = refs
    ret_refs, refs = refs[:flows], refs[flows:]
    if learns:
        targets, refs = refs[:outs], refs[outs:]
    else:
        rows_hbm, low_hbm, pre_hbm, *refs = refs
    if beside:
        met_hbm, *refs = refs
        *refs, leaving, met, next_send, next_recv, next_local = refs
    pre, up, down, total, local, *refs = refs
    scratch, refs = [refs[16 * f : 16 * f + 16] for f in range(flows)], refs[16 * flows :]
    if learns:
        *found, put = refs[: outs + 1]
        kept_rows, kept_hidden = refs[outs + 1 :] if kinds == (True,) else (scratch[0][2], scratch[0][3])
    f32, bf16 = jnp.float32, jnp.bfloat16
    here = lax.axis_index("wide")
    group = lax.axis_index("narrow")
    quads = count // members
    quad, member = here // members, lax.rem(here, members)
    lines = groups // 2
    line, core = group // 2, lax.rem(group, 2)
    near_group = group + 1 - 2 * core
    others = [(2 * away + c, 2 * lax.rem(line + away, lines) + c) for away in range(1, lines) for c in (0, 1)]
    early = 2 * (share // groups) // 16 * 16
    head, tail = pl.ds(0, early), pl.ds(early, share - early)
    ways = [(away, turn) for turn in range(members) for away in list(range(1, quads)) + [0] if away or turn]

    loads = [
        pltpu.make_async_copy(up_hbm, up, local.at[0]),
        pltpu.make_async_copy(down_hbm, down, local.at[1]),
    ]
    if kinds == (True,):
        loads.append(pltpu.make_async_copy(pre_hbm, pre, local.at[2]))
        loads.append(pltpu.make_async_copy(kept_hbm, kept_rows, local.at[3]))
        loads.append(pltpu.make_async_copy(hidden_hbm, kept_hidden, local.at[4]))
    for load in loads:
        load.start()
    if beside:
        source = next_hbm if which is None else next_hbm.at[which]
        next_load = pltpu.make_async_copy(source, leaving, next_local.at[0])
        next_load.start()

    def window_at(away, turn):
        return lax.rem(quad + away, quads) * members + lax.rem(member + turn, members)

    def span(window, part=None):
        start, size = (0, share) if part is None else ((0, early), (early, share - early))[part]
        return pl.ds(pl.multiple_of(window * share + start, 16), size)

    barrier = pltpu.get_barrier_semaphore()
    for peer in [near_group] + [other for _, other in others]:
        pl.semaphore_signal(barrier, inc=1, device_id=(here, peer), device_id_type=MESH)
    for away in range(quads):
        for turn in range(members):
            if away or turn:
                pl.semaphore_signal(
                    barrier, inc=1, device_id=(window_at(away, turn), group), device_id_type=MESH)
    pl.semaphore_wait(barrier, groups - 1 + count - 1)
    order = perm_ref[...].reshape(members, share, groups * block)
    sent, saves = [], []

    def hand_over(k, source, target, send, recv):
        if k:
            place, peer = others[k - 1]
            away = place // 2
            landing, signal = (lines - away) * 2 + core, 2 * away - 1 + core
        else:
            peer, landing, signal = near_group, core, 0
        copy = pltpu.make_async_remote_copy(
            src_ref=source, dst_ref=target.at[landing], send_sem=send.at[k], recv_sem=recv.at[signal],
            device_id=(here, peer), device_id_type=MESH)
        copy.start()
        sent.append(copy)

    def taken(k, like, target, send, recv):
        pltpu.make_async_remote_copy(
            src_ref=like, dst_ref=target.at[0], send_sem=send.at[k], recv_sem=recv.at[k],
            device_id=(here, near_group), device_id_type=MESH).wait_recv()

    class Flow:
        def __init__(self, backward, out_ref, ret_ref, scratch):
            self.backward, self.out_ref, self.ret_ref = backward, out_ref, ret_ref
            (self.arrived, self.own, self.rows, self.low, self.part, self.got, self.final, self.landed,
             self.there_send, self.there_recv, self.row_send, self.row_recv, self.sum_send, self.sum_recv,
             self.back_send, self.back_recv) = scratch

        def to_groups(self):
            there = self.there_send, self.there_recv
            hand_over(0, self.out_ref.at[near_group], self.arrived, *there)
            for k, (_, other) in enumerate(others):
                hand_over(1 + k, self.out_ref.at[other], self.arrived, *there)
            self.arrived[core] = self.out_ref[group]

        def carry(self, part):
            for away, turn in ways:
                copy = pltpu.make_async_remote_copy(
                    src_ref=self.own.at[lax.rem(member + turn, members), (head, tail)[part]],
                    dst_ref=self.rows.at[span(here, part), :],
                    send_sem=self.row_send.at[away, turn, part], recv_sem=self.row_recv.at[away, turn, part],
                    device_id=(window_at(away, turn), group), device_id_type=MESH)
                copy.start()
                sent.append(copy)

        def to_experts(self):
            there = self.there_send, self.there_recv
            taken(0, self.out_ref.at[group], self.arrived, *there)
            first = self.arrived[pl.ds(0, 2)].reshape(2 * block, width)
            self.own[:, head] = dot_nn(
                order[:, :early, : 2 * block].reshape(members * early, 2 * block), first
            ).astype(bf16).reshape(members, early, width)
            self.carry(0)
            for k in range(1, groups - 1):
                taken(k, self.out_ref.at[group], self.arrived, *there)
            self.own[:, tail] = dot_nn(
                order[:, early:].reshape(members * (share - early), groups * block),
                self.arrived[...].reshape(groups * block, width),
            ).astype(bf16).reshape(members, share - early, width)
            self.carry(1)
            self.rows[span(here), :] = self.own[member]

        def arrive(self, away, turn):
            window = lax.rem(quad + quads - away, quads) * members + lax.rem(member + members - turn, members)
            for part in (0, 1):
                pltpu.make_async_remote_copy(
                    src_ref=self.own.at[member, (head, tail)[part]], dst_ref=self.rows.at[span(window, part), :],
                    send_sem=self.row_send.at[away, turn, part], recv_sem=self.row_recv.at[away, turn, part],
                    device_id=(window, group), device_id_type=MESH).wait_recv()
            return window

        def compute(self, windows):
            size = len(windows) * share

            def one(s, carry):
                x = jnp.concatenate([self.rows[span(w), :] for w in windows], axis=0)
                if self.backward:
                    grad_hidden = dot_nt(x, down[s])
                    before = jnp.concatenate([pre[s, span(w), :] for w in windows], axis=0)
                    slope = bell(before) + before * (
                        0.3989422804014327 * jnp.exp(-0.5 * before * before))
                    middle = (grad_hidden * slope).astype(bf16)
                    y = dot_nt(middle, up[s])
                else:
                    before = dot_nn(x, up[s])
                    middle = (before * bell(before)).astype(bf16)
                    y = dot_nn(middle, down[s])
                for index, w in enumerate(windows):
                    piece = slice(index * share, (index + 1) * share)
                    if not self.backward:
                        pre[s, span(w), :] = before[piece]
                    self.low[s, span(w), :] = middle[piece]

                @pl.when(s == 0)
                def _():
                    total[:size] = y

                @pl.when(s > 0)
                def _():
                    total[:size] += y

                return carry

            lax.fori_loop(0, members, one, 0)
            for index, w in enumerate(windows):
                self.part[w] = total[index * share : (index + 1) * share].astype(bf16)

        def give_back(self, away, turn, window, part):
            copy = pltpu.make_async_remote_copy(
                src_ref=self.part.at[window, (head, tail)[part]], dst_ref=self.got.at[here, (head, tail)[part]],
                send_sem=self.sum_send.at[away, turn, part], recv_sem=self.sum_recv.at[away, turn, part],
                device_id=(window, group), device_id_type=MESH)
            copy.start()
            sent.append(copy)

        def work(self):
            windows = [here] + [self.arrive(0, turn) for turn in range(1, members)]
            self.compute(windows)
            for part in (1, 0):
                for turn in range(1, members):
                    self.give_back(0, turn, windows[turn], part)
            self.got[here] = self.part[here]
            late = []
            for away in range(1, quads):
                for first in range(0, members, 2):
                    windows = [self.arrive(away, turn) for turn in (first, first + 1)]
                    self.compute(windows)
                    for turn in (first, first + 1):
                        self.give_back(away, turn, windows[turn - first], 1)
                        late.append((away, turn, windows[turn - first]))
            for away, turn, window in late:
                self.give_back(away, turn, window, 0)

        def returned(self, part):
            place = (head, tail)[part]
            for away, turn in ways:
                window = window_at(away, turn)
                pltpu.make_async_remote_copy(
                    src_ref=self.part.at[here, place], dst_ref=self.got.at[window, place],
                    send_sem=self.sum_send.at[away, turn, part], recv_sem=self.sum_recv.at[away, turn, part],
                    device_id=(window, group), device_id_type=MESH).wait_recv()
            summed = self.got[pl.ds(0, members), place].astype(f32)
            for q in range(1, quads):
                summed = summed + self.got[pl.ds(q * members, members), place].astype(f32)
            return summed.astype(bf16)

        def leave(self):
            back = self.back_send, self.back_recv
            later = self.returned(1)
            rest = groups - 2
            self.final[pl.ds(2, rest)] = dot_tn(
                order[:, early:, 2 * block :].reshape(members * (share - early), rest * block),
                later.reshape(members * (share - early), width),
            ).astype(bf16).reshape(rest, block, width)
            for k, (place, _) in enumerate(others):
                hand_over(1 + k, self.final.at[place], self.landed, *back)
            sooner = self.returned(0)
            self.final[pl.ds(0, 2)] = (
                dot_tn(order[:, :early, : 2 * block].reshape(members * early, 2 * block),
                       sooner.reshape(members * early, width))
                + dot_tn(order[:, early:, : 2 * block].reshape(members * (share - early), 2 * block),
                         later.reshape(members * (share - early), width))
            ).astype(bf16).reshape(2, block, width)
            hand_over(0, self.final.at[1 - core], self.landed, *back)
            self.ret_ref[group] = self.final[core]

        def land(self):
            for k in range(groups - 1):
                taken(k, self.out_ref.at[group], self.landed, self.back_send, self.back_recv)
            self.ret_ref[near_group] = self.landed[1 - core]
            for place, other in others:
                self.ret_ref[other] = self.landed[place]

    travels = [Flow(*parts) for parts in zip(kinds, out_refs, ret_refs, scratch)]
    for flow in travels:
        flow.to_groups()
    for flow in travels:
        flow.to_experts()

    def send_beside(turns):
        for turn in turns if beside else ():
            copy = pltpu.make_async_remote_copy(
                src_ref=leaving.at[lax.rem(member + turn, members)], dst_ref=met.at[member],
                send_sem=next_send.at[turn], recv_sem=next_recv.at[turn],
                device_id=(window_at(0, turn), group), device_id_type=MESH)
            copy.start()
            beside_copies.append(copy)

    beside_copies = []
    if beside:
        next_load.wait()
        met[member] = leaving[member]
    send_beside([1])
    for load in loads:
        load.wait()
    for flow in travels:
        flow.work()
    send_beside(range(2, members))
    if learns:
        back = travels[-1]
        for s in range(members):
            grads = [dot_tn(kept_rows[...], back.low[s]).astype(bf16),
                     dot_tn(kept_hidden[s], back.rows[...]).astype(bf16)]
            if outs == 2:
                found[0][s], found[1][s] = grads
            else:
                found[0][s, :width] = grads[0]
                for f in range(width // hidden):
                    found[0][s, width + f * hidden : width + (f + 1) * hidden] = grads[1][
                        :, f * hidden : (f + 1) * hidden]
            for i in range(outs):
                saves.append(pltpu.make_async_copy(found[i].at[s], targets[i].at[s], put.at[i, s]))
                saves[-1].start()
    else:
        held = ((travels[0].rows, rows_hbm), (travels[0].low, low_hbm), (pre, pre_hbm))
        for k, (source, target) in enumerate(held):
            saves.append(pltpu.make_async_copy(source, target, local.at[2 + k]))
            saves[-1].start()
    for flow in travels:
        flow.leave()
    for flow in travels:
        flow.land()
    if beside:
        for copy in beside_copies:
            copy.wait_recv()
        saves.append(pltpu.make_async_copy(met, met_hbm, next_local.at[1]))
        saves[-1].start()
    for copy in sent + beside_copies:
        copy.wait_send()
    for save in saves:
        save.wait()


def expert_pass(outbounds, kinds, perm, weights, identity, known=(), beside=None, which=None):
    count, groups = lax.axis_size("wide"), lax.axis_size("narrow")
    _, block, width = outbounds[0].shape
    members, _, hidden = weights[0].shape
    share = perm.shape[0] // members
    quads = count // members
    total = count * share
    low, f32 = jnp.bfloat16, jnp.float32
    dims = (count, groups, members, block, share, width, hidden)
    inside = pl.BlockSpec(memory_space=VMEM)
    args = tuple(outbounds) + (perm,) + tuple(weights) + tuple(known)
    args += () if beside is None else (beside,)
    outs = [shaped((groups, block, width), low) for _ in kinds]
    dma = pltpu.SemaphoreType.DMA
    scratch = [
        VMEM((members, total, hidden), f32),
        VMEM((members, width, hidden), low),
        VMEM((members, hidden, width), low),
        VMEM((members * share, width), f32),
        dma((5,)),
    ]
    for _ in kinds:
        scratch += [
            VMEM((groups, block, width), low),
            VMEM((members, share, width), low),
            VMEM((total, width), low),
            VMEM((members, total, hidden), low),
            VMEM((count, share, width), low),
            VMEM((count, share, width), low),
            VMEM((groups, block, width), low),
            VMEM((groups, block, width), low),
            dma((groups - 1,)), dma((groups - 1,)),
            dma((quads, members, 2)), dma((quads, members, 2)),
            dma((quads, members, 2)), dma((quads, members, 2)),
            dma((groups - 1,)), dma((groups - 1,)),
        ]
    if True in kinds:
        sizes = [(width, hidden), (hidden, width)]
        if len(kinds) == 1 and folds(width, hidden):
            sizes = [(2 * width, hidden)]
        outs += [shaped((members,) + size, low) for size in sizes]
        scratch += [VMEM((members,) + size, low) for size in sizes] + [dma((len(sizes), members))]
        if len(kinds) == 1:
            scratch += [VMEM((total, width), low), VMEM((members, total, hidden), low)]
    else:
        outs += [shaped((total, width), low), shaped((members, total, hidden), low),
                 shaped((members, total, hidden))]
    if beside is not None:
        shape = beside.shape[-3:]
        outs.append(shaped(shape, low))
        scratch += [VMEM(shape, low), VMEM(shape, low), dma((members,)), dma((members,)), dma((2,))]
    return pl.pallas_call(
        functools.partial(expert_kernel, dims, tuple(kinds), beside is not None, which),
        out_shape=outs,
        in_specs=[inside] * (len(kinds) + 1) + [ANYWHERE] * (len(args) - len(kinds) - 1),
        out_specs=[inside] * len(kinds) + [ANYWHERE] * (len(outs) - len(kinds)),
        scratch_shapes=scratch,
        compiler_params=pltpu.CompilerParams(
            collective_id=identity, has_side_effects=True, vmem_limit_bytes=63 * MIB
        ),
        cost_estimate=microseconds(65),
    )(*args)


def expert_order(experts, groups, block, capacity):
    share = groups * capacity
    row = jnp.arange(experts * share, dtype=jnp.int32)
    expert, rest = row // share, row % share
    source = (rest // capacity) * block + expert * capacity + rest % capacity
    return (source[:, None] == jnp.arange(groups * block, dtype=jnp.int32)[None, :]).astype(jnp.bfloat16)


def between_members(arrays):
    count, members = lax.axis_size("wide"), arrays[0].shape[0]
    quads = [list(range(first, first + members)) for first in range(0, count, members)]
    return [
        lax.all_to_all(values, "wide", split_axis=0, concat_axis=0, tiled=True, axis_index_groups=quads)
        for values in arrays
    ]


def slice_kernel(layer, from_ref, to_ref, held, got, put):
    count = held.shape[0]
    incoming = [pltpu.make_async_copy(from_ref.at[layer, e], held.at[e], got.at[e]) for e in range(count)]
    outgoing = [pltpu.make_async_copy(held.at[e], to_ref.at[e], put.at[e]) for e in range(count)]
    for copy in incoming:
        copy.start()
    for into, out in zip(incoming, outgoing):
        into.wait()
        out.start()
    for out in outgoing:
        out.wait()


def layer_of(values, layer):
    shape = values.shape[1:]
    return pl.pallas_call(
        functools.partial(slice_kernel, layer),
        out_shape=shaped(shape, values.dtype),
        in_specs=[ANYWHERE],
        out_specs=ANYWHERE,
        scratch_shapes=[
            VMEM(shape, values.dtype), pltpu.SemaphoreType.DMA(shape[:1]), pltpu.SemaphoreType.DMA(shape[:1])],
        compiler_params=pltpu.CompilerParams(vmem_limit_bytes=63 * MIB),
        cost_estimate=microseconds(2),
    )(values)


def folds(width, hidden):
    return 0 if hidden % LANES else width // hidden


def widen_kernel(arrays, *refs):
    refs, (up_ref, down_ref) = refs[:arrays], refs[-2:]
    width, hidden = up_ref.shape
    if arrays == 2:
        up_ref[...] = refs[0][...].astype(jnp.float32)
        down_ref[...] = refs[1][...].astype(jnp.float32)
        return
    up_ref[...] = refs[0][:width].astype(jnp.float32)
    for f in range(width // hidden):
        down_ref[:, f * hidden : (f + 1) * hidden] = refs[0][
            width + f * hidden : width + (f + 1) * hidden].astype(jnp.float32)


def widened(layer, layers, arrays, width, hidden, held):
    experts = arrays[0].shape[0]
    count = len(arrays)
    return plain_call(
        functools.partial(widen_kernel, count),
        (experts,),
        [pl.BlockSpec((None,) + array.shape[1:], lambda e: (e, 0, 0)) for array in arrays]
        + [ANYWHERE] * len(held),
        [pl.BlockSpec((None, None, width, hidden), lambda e: (layer, e, 0, 0)),
         pl.BlockSpec((None, None, hidden, width), lambda e: (layer, e, 0, 0))],
        [shaped((layers, experts, width, hidden)), shaped((layers, experts, hidden, width))],
        [],
        tuple(arrays) + tuple(held),
        450,
        {count + k: k for k in range(len(held))},
    )


def sum_kernel(dims, *refs):
    count, lines, sizes, first_rows, width = dims
    total = len(sizes)
    arrays, out_ref = refs[:total], refs[total]
    (own, near, over, spun, spun_first, home, core_send, core_recv, load, over_send, over_recv,
     spin_send, spin_recv, spin_first_send, spin_first_recv, home_send, home_recv) = refs[total + 1 :]
    rows = sum(sizes)
    later = rows - first_rows
    here = lax.axis_index("wide")
    group = lax.axis_index("narrow")
    line, core = group // 2, lax.rem(group, 2)
    half = count // 2
    low, f32 = jnp.bfloat16, jnp.float32

    def window_of(position):
        position = lax.rem(position + 2 * count, count)
        upper = position // half
        return 2 * position * (1 - upper) + (2 * (count - 1 - position) + 1) * upper

    odd = lax.rem(here, 2)
    spot = (here // 2) * (1 - odd) + (count - 1 - here // 2) * odd
    ring = (window_of(spot + 1), window_of(spot - 1))
    peer = 2 * line + 1 - core
    lines_away = [lax.rem(line + k, lines) for k in range(1, lines)]

    barrier = pltpu.get_barrier_semaphore()
    for window in ring:
        pl.semaphore_signal(barrier, inc=1, device_id=(window, group), device_id_type=MESH)
    pl.semaphore_signal(barrier, inc=1, device_id=(here, peer), device_id_type=MESH)
    for other in lines_away:
        pl.semaphore_signal(barrier, inc=1, device_id=(here, 2 * other + core), device_id_type=MESH)
    pl.semaphore_wait(barrier, 2 + lines)

    order = [spot + half]
    for away in range(half - 1, 0, -1):
        order += [spot + away, spot - away]
    order = [window_of(position) for position in order + [spot]]
    sent, held = [], []
    for k, window in enumerate(order):
        held.append([])
        start = 0
        for i, size in enumerate(sizes):
            place = pl.ds(start, size)
            start += size
            copy = pltpu.make_async_remote_copy(
                src_ref=arrays[i].at[window, :, 1 - core], dst_ref=near.at[window, :, place],
                send_sem=core_send.at[k, i], recv_sem=core_recv.at[k, i],
                device_id=(here, peer), device_id_type=MESH)
            copy.start()
            mine = pltpu.make_async_copy(
                arrays[i].at[window, :, core], own.at[window, :, place], load.at[k, i])
            mine.start()
            sent.append(copy)
            held[-1].append((copy, mine))

    ahead, behind = pl.ds(0, first_rows), pl.ds(first_rows, later)
    cut_first = first_rows // 32 * 16
    cut_later = later // 32 * 16
    parts_first = (pl.ds(0, cut_first), pl.ds(cut_first, first_rows - cut_first))
    parts_later = (
        pl.ds(first_rows, cut_later), pl.ds(first_rows + cut_later, later - cut_later))
    parts_got = (pl.ds(0, cut_later), pl.ds(cut_later, later - cut_later))

    def meet(k):
        window = order[k]
        for copy, mine in held[k]:
            copy.wait_recv()
            mine.wait()

        def one(at, carry):
            place = pl.ds(pl.multiple_of(at * 16, 16), 16)
            for x in range(lines):
                own[window, x, place] = (
                    own[window, x, place].astype(f32) + near[window, x, place].astype(f32)
                ).astype(low)
            return carry

        lax.fori_loop(0, rows // 16, one, 0)
        for j, other in enumerate(lines_away):
            copy = pltpu.make_async_remote_copy(
                src_ref=own.at[window, other, ahead], dst_ref=over.at[j, window],
                send_sem=over_send.at[j, k], recv_sem=over_recv.at[j, k],
                device_id=(here, 2 * other + core), device_id_type=MESH)
            copy.start()
            sent.append(copy)
            crossing[k].append(copy)

    crossing = [[] for _ in order]

    def spin_later(step):
        for way, sign in ((0, 1), (1, -1)):
            window = window_of(spot + sign * (half - step))
            if step == 0:
                which, got_which = parts_later[way], parts_got[way]
                if not (later - cut_later if way else cut_later):
                    continue
            else:
                which, got_which = behind, pl.ds(0, later)
                add_which, add_got = (
                    (parts_later[way], parts_got[way]) if step == 1 else (which, got_which))
                if turns[way]:
                    turns[way][-1].wait_recv()
                    own[window, :, add_which] = (
                        own[window, :, add_which].astype(f32)
                        + spun[way, step - 1, :, add_got].astype(f32)
                    ).astype(low)
            copy = pltpu.make_async_remote_copy(
                src_ref=own.at[window, :, which], dst_ref=spun.at[way, step, :, got_which],
                send_sem=spin_send.at[way, step], recv_sem=spin_recv.at[way, step],
                device_id=(ring[way], group), device_id_type=MESH)
            copy.start()
            sent.append(copy)
            turns[way].append(copy)

    def cross(k):
        window = order[k]
        value = own[window, line, ahead].astype(f32)
        for j, copy in enumerate(crossing[k]):
            copy.wait_recv()
            value = value + over[j, window].astype(f32)
        return value

    first_turns = ([], [])

    def spin_first(step):
        for way, sign in ((0, 1), (1, -1)):
            k = 0 if step == 0 else 2 * step - 1 + way
            window = order[k]
            if step or way == 0:
                own[window, line, ahead] = cross(k).astype(low)
            if step == 0:
                which = parts_first[way]
            else:
                which = ahead
                add_which = parts_first[way] if step == 1 else which
                first_turns[way][-1].wait_recv()
                own[window, line, add_which] = (
                    own[window, line, add_which].astype(f32)
                    + spun_first[way, step - 1, add_which].astype(f32)
                ).astype(low)
            copy = pltpu.make_async_remote_copy(
                src_ref=own.at[window, line, which], dst_ref=spun_first.at[way, step, which],
                send_sem=spin_first_send.at[way, step], recv_sem=spin_first_recv.at[way, step],
                device_id=(ring[way], group), device_id_type=MESH)
            copy.start()
            sent.append(copy)
            first_turns[way].append(copy)

    turns = ([], [])
    meet(0)
    spin_later(0)
    for step in range(1, half):
        meet(2 * step - 1)
        meet(2 * step)
        spin_first(step - 1)
        spin_later(step)
    meet(len(order) - 1)
    spin_first(half - 1)
    summed = own[here, :, behind].astype(f32)
    for way in (0, 1):
        turns[way][-1].wait_recv()
        summed = summed + spun[way, half - 1].astype(f32)
    own[here, :, behind] = summed.astype(low)
    homes = []
    for j, other in enumerate(lines_away):
        copy = pltpu.make_async_remote_copy(
            src_ref=own.at[here, other, behind], dst_ref=home.at[j],
            send_sem=home_send.at[j], recv_sem=home_recv.at[j],
            device_id=(here, 2 * other + core), device_id_type=MESH)
        copy.start()
        sent.append(copy)
        homes.append(copy)

    summed = cross(len(order) - 1)
    for way in (0, 1):
        first_turns[way][-1].wait_recv()
        summed = summed + spun_first[way, half - 1].astype(f32)
    out_ref[ahead, :] = summed
    value = own[here, line, behind].astype(f32)
    for j, copy in enumerate(homes):
        copy.wait_recv()
        value = value + home[j].astype(f32)
    out_ref[behind, :] = value
    for copy in sent:
        copy.wait_send()


def summed_shares(arrays, identity):
    count, groups = lax.axis_size("wide"), lax.axis_size("narrow")
    lines, half = groups // 2, count // 2
    width = arrays[0].shape[2]
    if any(array.shape[1] % 16 for array in arrays):
        packed = jnp.concatenate(arrays, axis=1)
        arrays = [jnp.pad(packed, ((0, 0), (0, -packed.shape[1] % 16), (0, 0)))]
    sizes = tuple(array.shape[1] for array in arrays)
    rows = sum(sizes)
    first = max(32, rows * 12 // 20 // 16 * 16)
    later = rows - first
    low = jnp.bfloat16
    dma = pltpu.SemaphoreType.DMA
    return pl.pallas_call(
        functools.partial(sum_kernel, (count, lines, sizes, first, width)),
        out_shape=jax.ShapeDtypeStruct((rows, width), jnp.float32),
        in_specs=[ANYWHERE] * len(arrays),
        out_specs=pl.BlockSpec(memory_space=VMEM),
        scratch_shapes=[
            VMEM((count, lines, rows, width), low),
            VMEM((count, lines, rows, width), low),
            VMEM((lines - 1, count, first, width), low),
            VMEM((2, half, lines, later, width), low),
            VMEM((2, half, first, width), low),
            VMEM((lines - 1, later, width), low),
            dma((count, len(arrays))), dma((count, len(arrays))), dma((count, len(arrays))),
            dma((lines - 1, count)), dma((lines - 1, count)),
            dma((2, half)), dma((2, half)),
            dma((2, half)), dma((2, half)),
            dma((lines - 1,)), dma((lines - 1,)),
        ],
        compiler_params=pltpu.CompilerParams(
            collective_id=identity, has_side_effects=True, vmem_limit_bytes=63 * MIB
        ),
        cost_estimate=microseconds(60),
    )(*[array.reshape(count, lines, 2, array.shape[1], width) for array in arrays])


def inward_kernel(dims, grad_ref, weight_ref, edge_ref, handed_ref, keep_ref, normed_ref, begin_ref, gain_ref,
                  passed_ref, out_ref, channel_ref, router_ref, expert_ref, packed_ref, new_ref, *refs):
    blocks, wide, tall, held, fold, marks, spare, steps = dims
    *turned_ref, rows, features, held_block = refs
    owners, count, _ = packed_ref.shape
    f32, low = jnp.float32, jnp.bfloat16
    step = pl.program_id(0)
    tokens = grad_ref.shape[0]
    last = edge_ref.shape[0]
    edited = (last + 1) // 2 * 2 * CHUNKS
    held_block[...] = grad_ref[...]

    @pl.when(lax.rem(step, blocks) < blocks // 2)
    def _():
        edge = edge_ref[...] + handed_ref[...] * keep_ref[...]
        ends = grad_ref[tokens - edited :, :].astype(f32)
        place = lax.broadcasted_iota(jnp.int32, ends.shape, 0)
        for j in range(last):
            row = edited - (last - j) * CHUNKS + CHUNKS - 1
            ends = jnp.where(place == row, edge[j : j + 1], ends)
        held_block[tokens - edited :, :] = ends.astype(low)

    block = held_block[...]

    @pl.when(step == 0)
    def _():
        new_ref[...] = jnp.zeros_like(new_ref)
        rows[...] = jnp.zeros_like(rows)

    @pl.when(step < blocks)
    def _():
        new_ref[...] += dot_nt(block, weight_ref[...])

    @pl.when(step == blocks - 1)
    def _():
        grad, norm_grad = rms_back(begin_ref[...], gain_ref[...], new_ref[...])
        new_ref[...] = passed_ref[...] + grad
        if turned_ref:
            by_step = new_ref[...].reshape(steps, CHUNKS, grad.shape[1])
            for chunk in range(CHUNKS):
                turned_ref[0][chunk * steps : (chunk + 1) * steps, :] = by_step[:, chunk, :]
        experts = router_ref.shape[1]
        lane = lax.broadcasted_iota(jnp.int32, (experts, 2 * LANES), 1)
        row = lax.broadcasted_iota(jnp.int32, (experts, 2 * LANES), 0)
        pick = (lane == row + spare).astype(f32).astype(low)
        lane = lax.broadcasted_iota(jnp.int32, (2, 2 * LANES), 1)
        row = lax.broadcasted_iota(jnp.int32, (2, 2 * LANES), 0)
        pick_norms = (lane == row + spare + experts).astype(f32).astype(low)
        norms = jnp.concatenate([norm_grad[None], expert_ref[...]], axis=0).astype(low)
        features[...] = dot_nn(router_ref[...].astype(low), pick) + dot_tn(norms, pick_norms)

    @pl.when(step >= blocks)
    def _():
        grad = dot_tn(block, normed_ref[...])
        passed = out_ref[...]
        channel = channel_ref[...].astype(f32)
        start = pl.multiple_of((step - blocks) * owners * marks, 8)
        mine = features[pl.ds(start, owners * marks), :]
        thin = held // fold
        whole_tiles = not any(size % 16 for size in (wide, tall, thin))
        target = packed_ref if whole_tiles else rows
        kind = target.dtype
        for k in range(owners):
            target[k, :wide] = grad[k * wide : (k + 1) * wide].astype(kind)
            target[k, wide : wide + tall] = passed[k * tall : (k + 1) * tall].astype(kind)
            small = channel[k * held : (k + 1) * held]
            extra = mine[k * marks : (k + 1) * marks]
            small = small + jnp.concatenate([extra, jnp.zeros((held - marks, 2 * LANES), f32)], axis=0)
            for f in range(fold):
                target[k, wide + tall : wide + tall + thin, f * 2 * LANES : (f + 1) * 2 * LANES] = small[
                    f * thin : (f + 1) * thin].astype(kind)
            if whole_tiles and count > wide + tall + thin:
                packed_ref[k, wide + tall + thin :] = jnp.zeros((count - wide - tall - thin, grad.shape[1]), kind)
        if not whole_tiles:
            packed_ref[...] = rows[...].astype(low)


def mixer_inward(layer, grad_projected, in_weight, edge, handed, keep, normed, begin, gain, passed, grad_out, channel,
                 grad_router, grad_expert, devices, spare):
    tokens, columns = grad_projected.shape
    width = normed.shape[1]
    wide, tall = columns // devices, grad_out.shape[0] // devices
    held, marks = channel.shape[0] // devices, width // devices
    fold = width // (2 * LANES)
    count = wide + tall + held // fold
    count += -count % 16
    owners = width // wide
    blocks = devices // owners
    span = owners * wide
    taps = edge.shape[0]
    inner = edge.shape[1] // span
    turned = layer == 0

    def at(i):
        return jnp.maximum(i - blocks, 0)

    return plain_call(
        functools.partial(inward_kernel, (blocks, wide, tall, held, fold, marks, spare, tokens // CHUNKS)),
        (2 * blocks,),
        [pl.BlockSpec((tokens, span), lambda i: (0, i % blocks)),
         pl.BlockSpec((None, width, span), lambda i: (layer, 0, jnp.minimum(i, blocks - 1))),
         pl.BlockSpec((taps, span), lambda i: (0, jnp.minimum(i % blocks, inner - 1))),
         pl.BlockSpec((taps, span), lambda i: (0, jnp.minimum(i % blocks, inner - 1))),
         whole(keep.shape), whole(normed.shape), whole(begin.shape), layer_whole(layer, (1, width)), whole(passed.shape),
         pl.BlockSpec((owners * tall, width), lambda i: (at(i), 0)),
         pl.BlockSpec((owners * held, 2 * LANES), lambda i: (at(i), 0)),
         whole(grad_router.shape), whole(grad_expert.shape)],
        [pl.BlockSpec((owners, count, width), lambda i: (at(i), 0, 0)), whole((tokens, width))]
        + turned * [whole((tokens, width))],
        [shaped((devices, count, width), jnp.bfloat16), shaped((tokens, width))]
        + turned * [shaped((tokens, width))],
        [VMEM((owners, count, width), jnp.float32), VMEM((width, 2 * LANES), jnp.float32),
         VMEM((tokens, span), jnp.bfloat16)],
        (grad_projected, in_weight, edge, handed, keep, normed, begin, gain, passed, grad_out, channel, grad_router,
         grad_expert),
        9,
    )


def unfold_kernel(dims, *refs):
    layers, wide, tall, held, fold, marks, spare, sizes = dims
    inputs, outs = refs[:layers], refs[layers:]
    (in_ref, out_ref, state_ref, step_ref, decay_ref, conv_ref, conv_bias_ref, step_bias_ref, skip_ref,
     router_ref, mix_ref, expert_ref) = outs
    thin = held // fold
    for layer in range(layers):
        whole_rows = inputs[layer][...].astype(jnp.float32)
        in_ref[layer] = whole_rows[:wide]
        out_ref[layer] = whole_rows[wide : wide + tall]
        mine = whole_rows[wide + tall : wide + tall + thin]
        channel = jnp.concatenate(
            [mine[:, f * 2 * LANES : (f + 1) * 2 * LANES] for f in range(fold)], axis=0)
        state_ref[layer] = channel[:, : sizes[0]]
        turned = channel.T
        bounds = [0]
        for size in sizes:
            bounds.append(bounds[-1] + size)
        pieces = [turned[bounds[i] : bounds[i + 1]] for i in range(7)]
        step_ref[layer] = pieces[1]
        decay_ref[layer] = pieces[2]
        conv_ref[layer] = pieces[3]
        conv_bias_ref[layer : layer + 1] = pieces[4]
        step_bias_ref[layer : layer + 1] = pieces[5]
        skip_ref[layer : layer + 1] = pieces[6]
        experts = router_ref.shape[1]
        router_ref[layer] = turned[spare : spare + experts, :marks]
        mix_ref[layer : layer + 1] = turned[spare + experts : spare + experts + 1, :marks]
        expert_ref[layer : layer + 1] = turned[spare + experts + 1 : spare + experts + 2, :marks]


def unfolded(sums, wide, tall, held, marks, experts, spare, sizes):
    layers, width = len(sums), sums[0].shape[1]
    fold = width // (2 * LANES)
    shapes = [
        (wide, width), (tall, width), (held, sizes[0]), (sizes[1], held), (sizes[2], held), (sizes[3], held),
        (held,), (held,), (held,), (experts, marks), (marks,), (marks,),
    ]
    inside = pl.BlockSpec(memory_space=VMEM)
    return pl.pallas_call(
        functools.partial(unfold_kernel, (layers, wide, tall, held, fold, marks, spare, sizes)),
        out_shape=[shaped((layers,) + shape) for shape in shapes],
        in_specs=[inside] * layers,
        out_specs=[inside] * len(shapes),
        compiler_params=pltpu.CompilerParams(vmem_limit_bytes=63 * MIB),
        cost_estimate=microseconds(3),
    )(*sums)


def on_device(
    hidden,
    doc_start,
    expert_choice,
    slot_index,
    norm_mix,
    in_weight,
    conv_weight,
    conv_bias,
    state_weight,
    step_weight,
    step_bias,
    decay_log,
    skip_weight,
    out_weight,
    norm_expert,
    router,
    expert_up,
    expert_down,
    cotangent,
):
    layers = in_weight.shape[0]
    tokens = hidden.shape[1]
    width = hidden.shape[2]
    inner = skip_weight.shape[1]
    rank = step_weight.shape[1]
    states = decay_log.shape[1]
    experts = router.shape[2]
    taps = conv_weight.shape[1]
    steps = tokens // CHUNKS
    both = ("wide", "narrow")
    groups = lax.axis_size("narrow")
    devices = lax.axis_size("wide") * groups
    per_group = experts // groups
    capacity = max(2, 5 * tokens // (4 * experts))
    block = -(-per_group * capacity // 16) * 16
    low, f32 = jnp.bfloat16, jnp.float32
    keep_mask = rim_keep(doc_start[0], taps - 1)[:, None]
    order = expert_order(per_group, groups, block, capacity)
    norm_mix, conv_bias, step_bias, skip_weight, norm_expert = (
        values[:, None, :] for values in (norm_mix, conv_bias, step_bias, skip_weight, norm_expert))
    current = to_steps(hidden[0]).reshape(tokens, width).astype(f32)
    saved = []

    def cube(values):
        return values.reshape(steps, CHUNKS, values.shape[-1])

    tail = passed_along(hidden[0, tokens - taps + 1 :] * keep_mask.astype(low), 1)
    weights = [None] * layers
    ready, tail, slot_index = lax.optimization_barrier((layer_of(expert_up, 0), tail, slot_index))
    weights[0] = between_members([ready])
    reset, masks, fills, onehots, keeps = tables(
        doc_start, expert_choice, slot_index, taps, experts, groups, block, capacity)

    for layer in range(layers):
        if layer == 0:
            normed, projected, rim = mixer_enter(layer, norm_mix, in_weight, current, tail.astype(f32))
            projected = cube(projected)
        else:
            current, back_rows, normed, projected = mixer_enter(
                layer, norm_mix, in_weight, middle, weight, fills[layer - 1],
                returned.reshape(groups * block, width))
            saved[-1]["back_rows"] = back_rows
            projected = cube(projected)
            rim = passed_along(projected[steps - taps + 1 :, CHUNKS - 1, :inner] * keep_mask, 1)
        begin = current
        act, selection, size, link, link_size, total, total_size = mixer_front(
            layer, projected, rim, masks, reset, conv_weight, conv_bias, state_weight, step_weight, step_bias,
            decay_log)
        if layer == 0:
            total, order = lax.optimization_barrier((total, order))
        entering, ready = handed_ahead(layer, total, total_size, decay_log, [(expert_down, layer)], layer)
        weights[layer] += between_members([ready])
        mixed, gated, begins, middle, routed, shares, weight, outbound = mixer_run(
            layer, size, act, selection, reset, decay_log, link, link_size, entering, projected, skip_weight,
            out_weight, current, norm_expert, router, fills[layer], onehots[layer], keeps[layer])
        outbound = outbound.reshape(groups, block, width)
        if layer + 1 < layers:
            returned, kept_rows, hidden_low, pre_act, following = expert_pass(
                [outbound], (False,), order, weights[layer], 4 + layer, (), expert_up, layer + 1)
            known = (pre_act, kept_rows, hidden_low)
            weights[layer + 1] = [following]
        else:
            grad = to_steps(cotangent[0]).reshape(tokens, width).astype(f32)
            grad_rows_low = (weight * grad).astype(low)
            returning = dot_nn(fills[layer], grad_rows_low).astype(low).reshape(groups, block, width)
            returned, inbound, *ready = expert_pass(
                [outbound, returning], (False, True), order, weights[layer], 4 + layer)
            known = None
        saved.append(dict(
            begin=begin, normed=normed, projected=projected, rim=rim, act=act, selection=selection, size=size,
            begins=begins, mixed=mixed, gated=gated, middle=middle, routed=routed, shares=shares, weight=weight,
            known=known))
    back_rows = dot_tn(fills[-1], returned.reshape(groups * block, width))
    saved[-1]["back_rows"] = back_rows
    current = middle + weight * back_rows
    output = to_tokens(cube(current.astype(low)))[None]
    sums = [None] * layers
    wide_grads = ()
    expert_grads = [None] * layers
    per_device = inner // devices
    norm_device = width // devices
    spare = 160
    for layer in range(layers - 1, -1, -1):
        entry = saved[layer]
        fill, weight = fills[layer], entry["weight"]
        weighted = weight * jnp.sum(grad * entry["back_rows"], axis=1, keepdims=True)
        if layer + 1 < layers:
            grad_rows_low = (weight * grad).astype(low)
            outbound = dot_nn(fill, grad_rows_low).astype(low).reshape(groups, block, width)
            inbound, *ready = expert_pass(
                [outbound], (True,), order, weights[layer], 6 + layer, entry["known"])
        grad_sent = dot_tn(fill, inbound.reshape(groups * block, width))
        grad_logits_low = (weighted * (onehots[layer] - entry["shares"])).astype(low)
        grad_router = dot_tn(entry["routed"], grad_logits_low)
        grad_routed = grad_sent + dot_nt(grad_logits_low, router[layer])
        grad_middle, grad_norm_expert = rms_back(entry["middle"], norm_expert[layer], grad_routed)
        grad = grad + grad_middle
        grad_low = grad.astype(low)
        grad_y, grad_igate, grad_skip, grad_out, link, link_size, total, total_size = mixer_turn(
            layer, grad_low, out_weight, entry["projected"], entry["mixed"], entry["act"], entry["gated"],
            entry["size"], entry["selection"], reset, decay_log)
        entering = handed_back(layer, total, total_size, decay_log, 2 + layer)
        at_once = ready[: len(ready) // 2] if layer + 1 == layers else []
        *later, entering = lax.optimization_barrier((*ready[len(at_once) :], entering))
        expert_grads[layer] = between_members(at_once + later)
        grad_act, grad_decay, grad_bias, grad_step, grad_selection = mixer_back(
            layer, entry["size"], entry["act"], grad_y, decay_log, entry["selection"], reset,
            entry["begins"], link, link_size, entering, step_weight, step_bias, skip_weight)
        grad_projected, edge, rim_grad, channel = mixer_conv_back(
            layer, grad_act, grad_selection, state_weight, entry["projected"], entry["rim"], masks, conv_weight,
            conv_bias, entry["act"], grad_step, grad_decay, grad_bias, grad_skip, grad_igate)
        handed = passed_along(rim_grad, -1)
        if layer + 1 < layers:
            wide_grads = widened(layer + 1, layers, expert_grads[layer + 1], width, expert_up.shape[3], wide_grads)
            edge, *wide_grads = lax.optimization_barrier((edge, *wide_grads))
        blocks, grad, *turned = mixer_inward(
            layer, grad_projected, in_weight, edge, handed, keep_mask, entry["normed"], entry["begin"], norm_mix, grad,
            grad_out, channel, grad_router, grad_norm_expert.reshape(1, width), devices, spare)
        if layer:
            blocks, grad = lax.optimization_barrier((blocks, grad))
            rows = blocks.shape[1]
            sums[layer] = lax.psum_scatter(
                blocks.reshape(devices * rows, width), both, scatter_dimension=0, tiled=True)
        else:
            sums[layer] = summed_shares([blocks], 8)
    (grad_in, grad_out, grad_state, grad_step, grad_decay, grad_conv, grad_conv_bias, grad_step_bias, grad_skip,
     grad_router, grad_norm_mix, grad_norm_expert) = unfolded(
        sums, 2 * inner // devices, per_device, per_device, norm_device, experts, spare,
        (rank + 2 * states, rank, states, taps, 1, 1, 1))
    shared = (
        grad_norm_mix, jnp.swapaxes(grad_in, 1, 2), grad_conv, grad_conv_bias, grad_state, grad_step,
        grad_step_bias, grad_decay, grad_skip, grad_out, grad_norm_expert, jnp.swapaxes(grad_router, 1, 2))
    up_grads, down_grads = widened(0, layers, expert_grads[0], width, expert_up.shape[3], wide_grads)
    output_grad = turned[0][None]
    return (output, output_grad, *shared, up_grads, down_grads)


def solution(mesh):
    both = ("wide", "narrow")
    placed = (
        P("narrow", "wide", None),
        P("narrow", "wide"),
        P(None, "narrow", "wide"),
        P(None, "narrow", "wide"),
    ) + (P(),) * 12 + (
        P(None, "narrow", None, "wide"),
        P(None, "narrow", "wide", None),
        P("narrow", "wide", None),
    )
    return jax.shard_map(
        on_device,
        mesh=mesh,
        in_specs=placed,
        out_specs=(
            P("narrow", "wide", None),
            P("narrow", "wide", None),
            P(None, both),
            P(None, None, both),
            P(None, None, both),
            P(None, both),
            P(None, both, None),
            P(None, None, both),
            P(None, both),
            P(None, None, both),
            P(None, both),
            P(None, both, None),
            P(None, both),
            P(None, both, None),
            P(None, "narrow", None, "wide"),
            P(None, "narrow", "wide", None),
        ),
        check_vma=False,
    )
```
